32 devices in a mesh: dp: 8 (over z, y), seq: 4 (over x, core).
Axes of the slice: x: 2, y: 2, z: 4, core: 2. Of those that a mesh axis runs over, the one named last changes fastest.
Arguments:
- tokens: bfloat16 [8, 1024, 1152], P('dp', 'seq'), may hold values from -6 to 6
- condition: bfloat16 [8, 1024, 1152], P('dp', 'seq'), may hold values from -6 to 6
- cotangent: bfloat16 [8, 1024, 1152], P('dp', 'seq'), may hold values from -6 to 6
- w_qkv: bfloat16 [1152, 3456], P('seq'), may hold values from -0.1875 to 0.1875
- w_out: bfloat16 [1152, 1152], P('seq'), may hold values from -3 to 3
- w_gate: bfloat16 [1152, 3072], P('seq'), may hold values from -0.1875 to 0.1875
- w_up: bfloat16 [1152, 3072], P('seq'), may hold values from -0.1875 to 0.1875
- w_down: bfloat16 [3072, 1152], P('seq'), may hold values from -0.109375 to 0.109375
- w_mod: bfloat16 [1152, 6912], P('seq'), may hold values from -0.1875 to 0.1875
- b_mod: float32 [6912], replicated, may hold values from -3 to 3
- q_gain: float32 [72], replicated, may hold values from 0.25 to 1.75
- k_gain: float32 [72], replicated, may hold values from 0.25 to 1.75
- noise_counts: int32 [4], replicated, may hold values from 1 to 4, 8 in all
- time_steps: int32 [8], P('dp'), may hold values from 0 to 999
- positions: int32 [2, 8, 1024], P(None, 'dp', 'seq'), may hold values from 0 to 62, as said below
Outputs:
- block_out: bfloat16 [8, 1024, 1152], P('dp', 'seq')
- grad_tokens: float32 [8, 1024, 1152], P('dp', 'seq')
- grad_condition: float32 [8, 1024, 1152], P('dp', 'seq')
- grad_w_qkv: float32 [1152, 3456], P(('dp', 'seq'))
- grad_w_out: float32 [1152, 1152], P(('dp', 'seq'))
- grad_w_gate: float32 [1152, 3072], P(('dp', 'seq'))
- grad_w_up: float32 [1152, 3072], P(('dp', 'seq'))
- grad_w_down: float32 [3072, 1152], P(('dp', 'seq'))
- grad_w_mod: float32 [1152, 6912], P(('dp', 'seq'))
- grad_b_mod: float32 [6912], P(('dp', 'seq'))
- grad_q_gain: float32 [72], replicated
- grad_k_gain: float32 [72], replicated
The draws below stay inside these ranges and needn't reach their ends.
Inputs may be any that keep to these rules, and one draw needn't show every extreme that they name: Image m owns the next noise_counts[m] items in order, so the counts sum to 8. `positions`: each item's rows hold every cell of its 32 x 32 patch grid once, in an order of that item, rows and columns both shifted by an offset of that item of 0 to 31; some item has offset 0 and another offset 32 - 1.
All inputs are finite; a program needn't handle non-finite values.
Results may differ from the reference program's by a relative error of at most 0.014.
Values may be sent and summed in bfloat16 or wider, within the bound.
A program may use at most 448 MiB of HBM per device.

```python
import math
import jax
import jax.numpy as jnp
import numpy as np
from jax import lax

D = 1152
HEADS = 16
HD = 72
FF = 3072
GRID = 32
PATCHES = 1024
ITEMS = 8
IMAGES = 4


def draw_positions(key, part):
    key = jax.random.fold_in(key, 7)
    key_off, key_low, key_high, key_order = jax.random.split(key, 4)
    offsets = jax.random.randint(key_off, (2, ITEMS, 1), 0, GRID)
    low_item = jax.random.randint(key_low, (), 0, ITEMS)
    high_item = (low_item + 1 + jax.random.randint(key_high, (), 0, ITEMS - 1)) % ITEMS
    item_ids = jnp.arange(ITEMS, dtype=jnp.int32)[None, :, None]
    offsets = jnp.where(item_ids == low_item, 0, offsets)
    offsets = jnp.where(item_ids == high_item, GRID - 1, offsets)
    order_keys = jax.random.split(key_order, ITEMS)
    cells = jax.vmap(lambda one_key: jax.random.permutation(one_key, PATCHES))(order_keys).astype(jnp.int32)
    layout = jnp.stack([cells // GRID, cells % GRID])
    return (layout + offsets).astype(jnp.int32)


def with_ends(values, own_key, least, high):
    dims = values.shape
    spot = [jax.random.randint(jax.random.fold_in(own_key, axis), (), 0, dims[axis]) for axis in range(len(dims))]
    values = values.at[tuple(spot)].set(least)
    longest = dims.index(max(dims))
    spot[longest] = (spot[longest] + 1) % dims[longest]
    return values.at[tuple(spot)].set(high)


def shard_levels(rng, shape, cuts, low, top_value):
    loudness = 1.0
    for dim, blocks in cuts:
        draws = jax.random.uniform(jax.random.fold_in(jax.random.fold_in(rng, 6), dim), (blocks,), jnp.float32, low / len(cuts), top_value / len(cuts))
        loudness = loudness * jnp.repeat(jnp.exp(draws), shape[dim] // blocks).reshape((-1,) + (1,) * (len(shape) - 1 - dim))
    return loudness


def profile(count, total, reach, skew):
    weights = [(1 << 20) // math.isqrt(rank ** skew) + 1 for rank in range(2, count + 1)]
    rest, counts = total - reach - (count - 1), [1] * (count - 1)
    while rest > 0:
        candidates = [i for i in range(count - 1) if counts[i] < reach]
        pool, budget = sum([weights[i] for i in candidates]), rest
        for i in candidates:
            more = min(reach - counts[i], max(1, budget * weights[i] // pool), rest)
            counts[i] = counts[i] + more
            rest = rest - more
    return np.array([reach] + counts)


def ragged(key, amount, total, limit, skew):
    if amount == 2:
        one = jax.random.randint(key, (), max(1, total - limit), min(limit, total - 1) + 1)
        return jnp.stack([one, total - one])
    lengths = jnp.asarray(profile(amount, total, limit, skew), jnp.int32)
    twos = (amount - 1) // 2
    source_of, taker = lengths[1:1 + 2 * twos:2], lengths[2:2 + 2 * twos:2]
    slack = jnp.minimum(source_of - 1, limit - taker)
    passed = jax.random.randint(jax.random.fold_in(key, 1), (twos,), 0, 1 << 20) % (slack + 1)
    lengths = lengths.at[1:1 + 2 * twos:2].set(source_of - passed).at[2:2 + 2 * twos:2].set(taker + passed)
    return lengths[jax.random.permutation(jax.random.fold_in(key, 2), amount)]


def scatter_about(key, shape, spread, limit, shards=(), kind=jnp.bfloat16):
    drawn = spread * jax.random.normal(key, shape, jnp.float32)
    if shards:
        drawn = drawn * shard_levels(key, shape, shards, -0.22, 0.18)
    return jnp.clip(drawn, -limit, limit).astype(kind)


def setup_inputs(seed: int = 0) -> dict:
    arg_keys = jax.random.split(jax.random.key(seed), 16)
    return {
        "tokens": scatter_about(arg_keys[0], (ITEMS, PATCHES, D), 1.0, 6.0, ((0, 8), (1, 4))),
        "condition": scatter_about(arg_keys[1], (ITEMS, PATCHES, D), 1.0, 6.0, ((0, 8), (1, 4))),
        "cotangent": scatter_about(arg_keys[2], (ITEMS, PATCHES, D), 1.0, 6.0, ((0, 8), (1, 4))),
        "w_qkv": scatter_about(arg_keys[3], (D, 3 * D), D ** -0.5, 0.1875, ((0, 4),)),
        "w_out": scatter_about(arg_keys[4], (D, D), 4 ** -0.5, 3.0, ((0, 4),)),
        "w_gate": scatter_about(arg_keys[5], (D, FF), D ** -0.5, 0.1875, ((0, 4),)),
        "w_up": scatter_about(arg_keys[6], (D, FF), D ** -0.5, 0.1875, ((0, 4),)),
        "w_down": scatter_about(arg_keys[7], (FF, D), FF ** -0.5, 0.109375, ((0, 4),)),
        "w_mod": scatter_about(arg_keys[8], (D, 6 * D), D ** -0.5, 0.1875, ((0, 4),)),
        "b_mod": scatter_about(arg_keys[9], (6 * D,), 0.5, 3.0, (), jnp.float32),
        "q_gain": jnp.clip(1.0 + 0.15 * jax.random.normal(arg_keys[10], (HD,), jnp.float32), 0.25, 1.75),
        "k_gain": jnp.clip(1.0 + 0.15 * jax.random.normal(arg_keys[11], (HD,), jnp.float32), 0.25, 1.75),
        "noise_counts": ragged(arg_keys[12], IMAGES, ITEMS, 4, 0).astype(jnp.int32),
        "time_steps": with_ends(jax.random.randint(arg_keys[13], (ITEMS,), 0, 1000), jax.random.fold_in(arg_keys[13], 1), 0, 999).astype(jnp.int32),
        "positions": draw_positions(jax.random.fold_in(arg_keys[15], 71), 0),
    }


@jax.custom_vjp
def low(v):
    return lax.optimization_barrier(v.astype(jnp.bfloat16)).astype(jnp.float32)

@jax.custom_vjp
def low_back(v):
    return v

def low_keep(v):
    return (low(v), None)

def low_pass(kept, grad):
    return (grad,)

def back_keep(v):
    return (v, None)

def back_low(kept, grad):
    return (low(grad),)
low.defvjp(low_keep, low_pass)
low_back.defvjp(back_keep, back_low)
EPSILON = 1e-06
HIGHEST = lax.Precision.HIGHEST

def product(left, right):
    return jnp.dot(left, right, precision=HIGHEST)

def rms_norm(values):
    return values * lax.rsqrt(lax.optimization_barrier(jnp.mean(values * values, axis=-1, keepdims=True)) + EPSILON)

def time_embed(steps, width):
    half_width = width // 2
    frequency = jnp.exp(-math.log(10000.0) * jnp.arange(half_width, dtype=jnp.float32) / half_width)
    angles = steps.astype(jnp.float32)[:, None] * frequency[None, :]
    return jnp.concatenate([jnp.cos(angles), jnp.sin(angles)], axis=-1)

def rope_tables(positions, head_size):
    quarter = head_size // 4
    frequency = jnp.exp(-math.log(10000.0) * jnp.arange(quarter, dtype=jnp.float32) / quarter)
    along_rows = positions[0].astype(jnp.float32)[..., None] * frequency
    along_cols = positions[1].astype(jnp.float32)[..., None] * frequency
    angles = jnp.concatenate([along_rows, along_rows, along_cols, along_cols], axis=-1)
    return (jnp.cos(angles)[..., None, :], jnp.sin(angles)[..., None, :])

def quarter_turn(values):
    first, second, third, fourth = jnp.split(values, 4, axis=-1)
    return jnp.concatenate([-second, first, -fourth, third], axis=-1)

def rotate_heads(values, cosine, sine):
    return values * cosine + quarter_turn(values) * sine

def forward(tokens_f, condition_f, w_qkv, w_out, w_gate, w_up, w_down, w_mod, b_mod, q_gain, k_gain, embed, cosine, sine):
    number, length, width = tokens_f.shape
    lifted = jax.nn.silu(condition_f + embed[:, None, :])
    modulation = low_back(product(low(lifted), w_mod) + b_mod)
    shift_a, scale_a, gate_a, shift_b, scale_b, gate_b = jnp.split(modulation, 6, axis=-1)
    hidden_a = low(rms_norm(tokens_f) * (1.0 + scale_a) + shift_a)
    projected = low_back(product(hidden_a, w_qkv)).reshape(number, length, 3, HEADS, HD)
    query_rows = low(rotate_heads(rms_norm(projected[:, :, 0]) * q_gain, cosine, sine))
    key_rows = low(rotate_heads(rms_norm(projected[:, :, 1]) * k_gain, cosine, sine))
    value_rows = low(projected[:, :, 2])
    scores = low_back(jnp.einsum('nqhd,nkhd->nhqk', query_rows, key_rows, precision=HIGHEST) * HD ** (-0.5))
    exp_scores = jnp.exp(scores)
    weights_low = low(exp_scores / lax.optimization_barrier(jnp.sum(exp_scores, axis=-1, keepdims=True)))
    attended = jnp.einsum('nhqk,nkhd->nqhd', weights_low, value_rows, precision=HIGHEST).reshape(number, length, width)
    attended = low(low_back(attended))
    branch_a = low_back(product(attended, w_out))
    middle = tokens_f + gate_a * branch_a
    hidden_b = low(rms_norm(middle) * (1.0 + scale_b) + shift_b)
    gate_in = low_back(product(hidden_b, w_gate))
    up_in = low_back(product(hidden_b, w_up))
    inner = low(jax.nn.silu(gate_in) * up_in)
    branch_b = low_back(product(inner, w_down))
    return middle + gate_b * branch_b

def reference(tokens, condition, cotangent, w_qkv, w_out, w_gate, w_up, w_down, w_mod, b_mod, q_gain, k_gain, noise_counts, time_steps, positions):
    running = jnp.cumsum(noise_counts)
    item_ids = jnp.arange(ITEMS, dtype=jnp.int32)
    image_ids = lax.optimization_barrier(jnp.sum((running[None, :] <= item_ids[:, None]).astype(jnp.int32), axis=1))
    chosen = jnp.arange(IMAGES, dtype=jnp.int32)[None, :] == image_ids[:, None]
    share = 1.0 / lax.optimization_barrier(jnp.sum(jnp.where(chosen, noise_counts[None, :], 0), axis=1)).astype(jnp.float32)
    embed = time_embed(time_steps, D)
    cosine, sine = rope_tables(positions, HD)
    params = tuple((weight.astype(jnp.float32) for weight in (w_qkv, w_out, w_gate, w_up, w_down, w_mod, b_mod, q_gain, k_gain)))
    groups = ITEMS // 4

    def regroup(array):
        return array.reshape((groups, 4) + array.shape[1:])
    blocks = (regroup(tokens), regroup(condition), regroup(cotangent), regroup(share), regroup(embed), regroup(cosine), regroup(sine))

    def scan_step(running_sums, block_in):
        tokens_b, condition_b, cotangent_b, share_b, embed_b, cosine_b, sine_b = block_in

        def local_forward(tokens_f, condition_f, *weights):
            return forward(tokens_f, condition_f, *weights, embed_b, cosine_b, sine_b)
        outputs, pullback = jax.vjp(local_forward, tokens_b.astype(jnp.float32), condition_b.astype(jnp.float32), *params)
        gradients = pullback(cotangent_b.astype(jnp.float32) * share_b[:, None, None])
        summed = tuple((total + grad for total, grad in zip(running_sums, gradients[2:])))
        return (summed, (outputs.astype(jnp.bfloat16), gradients[0], gradients[1]))
    initial = tuple((jnp.zeros_like(weight) for weight in params))
    sums, (block_out, grad_tokens, grad_condition) = lax.scan(scan_step, initial, blocks)
    shape_out = (ITEMS, PATCHES, D)
    return (block_out.reshape(shape_out), grad_tokens.reshape(shape_out), grad_condition.reshape(shape_out), sums[0], sums[1], sums[2], sums[3], sums[4], sums[5], sums[6], sums[7], sums[8])
```

```python
import math

import jax
import jax.numpy as jnp
from jax import lax
from jax.sharding import PartitionSpec as P

HEADS = 16
HD = 72
EPSILON = 1e-06
BF16 = jnp.bfloat16
F32 = jnp.float32


def inverse_rms(values):
    return lax.rsqrt(jnp.mean(values * values, axis=-1, keepdims=True) + EPSILON)


def rms_back(grad_in, normed, inverse):
    return inverse * (grad_in - normed * jnp.mean(grad_in * normed, axis=-1, keepdims=True))


def silu_slope(values):
    logistic = jax.nn.sigmoid(values)
    return logistic * (1.0 + values * (1.0 - logistic))


def time_embed(steps, width):
    half_width = width // 2
    frequency = jnp.exp(-math.log(10000.0) * jnp.arange(half_width, dtype=F32) / half_width)
    angles = steps.astype(F32)[:, None] * frequency[None, :]
    return jnp.concatenate([jnp.cos(angles), jnp.sin(angles)], axis=-1)


def rope_tables(positions, head_size):
    quarter = head_size // 4
    frequency = jnp.exp(-math.log(10000.0) * jnp.arange(quarter, dtype=F32) / quarter)
    along_rows = positions[0].astype(F32)[..., None] * frequency
    along_cols = positions[1].astype(F32)[..., None] * frequency
    angles = jnp.concatenate([along_rows, along_rows, along_cols, along_cols], axis=-1)
    return (jnp.cos(angles)[..., None, :], jnp.sin(angles)[..., None, :])


def quarter_turn(values):
    first, second, third, fourth = jnp.split(values, 4, axis=-1)
    return jnp.concatenate([-second, first, -fourth, third], axis=-1)


def rotate_heads(values, cosine, sine):
    return values * cosine + quarter_turn(values) * sine


def unrotate(grad_in, cosine, sine):
    return grad_in * cosine - quarter_turn(grad_in * sine)


def matmul(left, right):
    return jnp.dot(left, right, preferred_element_type=F32)


def outer_sum(left, right):
    return jnp.einsum("ra,rb->ab", left, right, preferred_element_type=F32)


def times_transpose(left, right):
    return jnp.einsum("rb,ab->ra", left, right, preferred_element_type=F32)


def gather_rows(values):
    return lax.all_gather(values, "seq", axis=0, tiled=True)


def scatter_rows(partial):
    return lax.psum_scatter(
        partial.astype(BF16), "seq", scatter_dimension=0, tiled=True
    ).astype(F32)


def rows_to_columns(values, blocks):
    rows, columns = values.shape
    ways = lax.axis_size("seq")
    values = values.reshape(rows, blocks, ways, columns // (blocks * ways))
    moved = lax.all_to_all(values, "seq", split_axis=2, concat_axis=0, tiled=True)
    return moved.reshape(rows * ways, columns // ways)


def columns_to_rows(values, blocks):
    rows, columns = values.shape
    ways = lax.axis_size("seq")
    values = values.reshape(rows, blocks, 1, columns // blocks)
    moved = lax.all_to_all(values, "seq", split_axis=0, concat_axis=2, tiled=True)
    return moved.reshape(rows // ways, columns * ways)


def sum_columns(partial, blocks):
    mine = lax.psum_scatter(partial.astype(BF16), "dp", scatter_dimension=0, tiled=True)
    return columns_to_rows(mine, blocks).astype(F32)


def sum_rows(partial):
    mine = lax.psum_scatter(partial.astype(BF16), "dp", scatter_dimension=0, tiled=True)
    n_dp, n_seq = lax.axis_size("dp"), lax.axis_size("seq")
    pairs = []
    for d in range(n_dp):
        for s in range(n_seq):
            pairs.append((d * n_seq + s, s * n_dp + d))
    return lax.ppermute(mine, ("dp", "seq"), pairs).astype(F32)


def shards(
    tokens,
    condition,
    cotangent,
    w_qkv,
    w_out,
    w_gate,
    w_up,
    w_down,
    w_mod,
    b_mod,
    q_gain,
    k_gain,
    noise_counts,
    time_steps,
    positions,
):
    local_rows, width = tokens.shape[1:]
    ways = lax.axis_size("seq")
    patches = local_rows * ways
    local_heads = HEADS // ways
    factor = HD ** (-0.5)
    mod_full = gather_rows(w_mod)
    qkv_cols = rows_to_columns(w_qkv, 3)
    gate_cols = rows_to_columns(w_gate, 1)
    up_cols = rows_to_columns(w_up, 1)
    all_positions = lax.all_gather(positions[:, 0], "seq", axis=1, tiled=True)
    cosine, sine = rope_tables(all_positions, HD)

    item = lax.axis_index("dp")
    running = jnp.cumsum(noise_counts)
    image_id = jnp.sum((running <= item).astype(jnp.int32))
    chosen = jnp.arange(noise_counts.shape[0], dtype=jnp.int32) == image_id
    share = 1.0 / jnp.sum(jnp.where(chosen, noise_counts, 0)).astype(F32)

    condition_in = condition[0].astype(F32) + time_embed(time_steps, width)
    lifted_low = jax.nn.silu(condition_in).astype(BF16)
    modulation = matmul(lifted_low, mod_full) + b_mod
    shift_a, scale_a, gate_a, shift_b, scale_b, gate_b = jnp.split(modulation, 6, axis=-1)
    tokens_f = tokens[0].astype(F32)
    inverse_a = inverse_rms(tokens_f)
    normed_a = tokens_f * inverse_a
    hidden_a = gather_rows((normed_a * (1.0 + scale_a) + shift_a).astype(BF16))
    lifted_full = gather_rows(lifted_low)
    grad_out = cotangent[0].astype(F32) * share
    grad_branch_b = gather_rows((grad_out * gate_b).astype(BF16))

    projected = matmul(hidden_a, qkv_cols).reshape(patches, 3, local_heads, HD)
    query_inv = inverse_rms(projected[:, 0])
    query_norm = projected[:, 0] * query_inv
    query_rows = rotate_heads(query_norm * q_gain, cosine, sine).astype(BF16)
    key_inv = inverse_rms(projected[:, 1])
    key_norm = projected[:, 1] * key_inv
    key_rows = rotate_heads(key_norm * k_gain, cosine, sine).astype(BF16)
    value_rows = projected[:, 2].astype(BF16)

    scores = jnp.einsum("qhd,khd->hqk", query_rows, key_rows, preferred_element_type=F32) * factor
    exp_scores = jnp.exp(scores)
    totals = jnp.sum(exp_scores, axis=-1, keepdims=True)
    weights_low = (exp_scores / totals).astype(BF16)
    mixed = jnp.einsum("hqk,khd->qhd", weights_low, value_rows, preferred_element_type=F32)
    attended = mixed.reshape(patches, local_heads * HD).astype(BF16)

    branch_a = scatter_rows(matmul(attended, w_out))
    middle = tokens_f + gate_a * branch_a
    inverse_b = inverse_rms(middle)
    normed_b = middle * inverse_b
    hidden_b = gather_rows((normed_b * (1.0 + scale_b) + shift_b).astype(BF16))
    gate_in = matmul(hidden_b, gate_cols)
    up_in = matmul(hidden_b, up_cols)
    activated = jax.nn.silu(gate_in)
    inner = (activated * up_in).astype(BF16)
    branch_b = scatter_rows(matmul(inner, w_down))
    block_out = (middle + gate_b * branch_b).astype(BF16)

    grad_gate_b = grad_out * branch_b
    grad_w_down = sum_rows(outer_sum(inner, grad_branch_b))
    grad_inner = times_transpose(grad_branch_b, w_down)
    grad_gate_in = (grad_inner * up_in * silu_slope(gate_in)).astype(BF16)
    grad_up_in = (grad_inner * activated).astype(BF16)
    grad_w_gate = sum_columns(outer_sum(hidden_b, grad_gate_in), 1)
    grad_w_up = sum_columns(outer_sum(hidden_b, grad_up_in), 1)
    grad_hidden_b = scatter_rows(
        times_transpose(grad_gate_in, gate_cols) + times_transpose(grad_up_in, up_cols)
    )
    grad_middle = grad_out + rms_back(grad_hidden_b * (1.0 + scale_b), normed_b, inverse_b)
    grad_gate_a = grad_middle * branch_a
    grad_branch_a = gather_rows((grad_middle * gate_a).astype(BF16))
    grad_w_out = sum_rows(outer_sum(attended, grad_branch_a))
    grad_attended = (
        times_transpose(grad_branch_a, w_out).astype(BF16).reshape(patches, local_heads, HD)
    )

    scores = jnp.einsum("qhd,khd->hqk", query_rows, key_rows, preferred_element_type=F32) * factor
    probs = jnp.exp(scores) / totals
    grad_probs = jnp.einsum("qhd,khd->hqk", grad_attended, value_rows, preferred_element_type=F32)
    row_inner = jnp.sum(probs * grad_probs, axis=-1, keepdims=True)
    grad_scores = (probs * (grad_probs - row_inner)).astype(BF16)
    grad_query = (
        jnp.einsum("hqk,khd->qhd", grad_scores, key_rows, preferred_element_type=F32) * factor
    )
    grad_key = (
        jnp.einsum("hqk,qhd->khd", grad_scores, query_rows, preferred_element_type=F32) * factor
    )
    grad_value = jnp.einsum(
        "hqk,qhd->khd", probs.astype(BF16), grad_attended, preferred_element_type=F32
    )
    grad_query_norm = unrotate(grad_query, cosine, sine)
    grad_key_norm = unrotate(grad_key, cosine, sine)
    grad_q_gain = jnp.sum(grad_query_norm * query_norm, axis=(0, 1))
    grad_k_gain = jnp.sum(grad_key_norm * key_norm, axis=(0, 1))
    grad_query_raw = rms_back(grad_query_norm * q_gain, query_norm, query_inv)
    grad_key_raw = rms_back(grad_key_norm * k_gain, key_norm, key_inv)
    grad_project = jnp.stack([grad_query_raw, grad_key_raw, grad_value], axis=1)
    grad_project = grad_project.reshape(patches, 3 * local_heads * HD).astype(BF16)
    grad_w_qkv = sum_columns(outer_sum(hidden_a, grad_project), 3)
    grad_hidden_a = scatter_rows(times_transpose(grad_project, qkv_cols))
    grad_tokens = grad_middle + rms_back(grad_hidden_a * (1.0 + scale_a), normed_a, inverse_a)
    grad_mod_rows = jnp.concatenate(
        [
            grad_hidden_a,
            grad_hidden_a * normed_a,
            grad_gate_a,
            grad_hidden_b,
            grad_hidden_b * normed_b,
            grad_gate_b,
        ],
        axis=-1,
    ).astype(BF16)
    grad_b_mod = jnp.sum(grad_mod_rows, axis=0, dtype=F32)
    grad_mod_cols = rows_to_columns(grad_mod_rows, 6)
    grad_w_mod = sum_columns(outer_sum(lifted_full, grad_mod_cols), 6)
    grad_condition = times_transpose(grad_mod_rows, mod_full) * silu_slope(condition_in)
    sum_bias = lax.psum_scatter(grad_b_mod, ("dp", "seq"), scatter_dimension=0, tiled=True)
    sum_q_gain, sum_k_gain = lax.psum((grad_q_gain, grad_k_gain), ("dp", "seq"))
    return (
        block_out[None],
        grad_tokens[None],
        grad_condition[None],
        grad_w_qkv,
        grad_w_out,
        grad_w_gate,
        grad_w_up,
        grad_w_down,
        grad_w_mod,
        sum_bias,
        sum_q_gain,
        sum_k_gain,
    )


def solution(mesh):
    placed = (
        P("dp", "seq", None),
        P("dp", "seq", None),
        P("dp", "seq", None),
        P("seq", None),
        P("seq", None),
        P("seq", None),
        P("seq", None),
        P("seq", None),
        P("seq", None),
        P(),
        P(),
        P(),
        P(),
        P("dp"),
        P(None, "dp", "seq"),
    )
    return jax.shard_map(
        shards,
        mesh=mesh,
        in_specs=placed,
        out_specs=(
            P("dp", "seq", None),
            P("dp", "seq", None),
            P("dp", "seq", None),
            P(("dp", "seq"), None),
            P(("dp", "seq"), None),
            P(("dp", "seq"), None),
            P(("dp", "seq"), None),
            P(("dp", "seq"), None),
            P(("dp", "seq"), None),
            P(("dp", "seq")),
            P(),
            P(),
        ),
        check_vma=False,
    )
```

```python
import math

import jax
import jax.numpy as jnp
from jax import lax
from jax.experimental import pallas as pl
from jax.experimental.pallas import tpu as pltpu
from jax.sharding import PartitionSpec as P

HEADS = 16
HD = 72
EPSILON = 1e-06
BF16 = jnp.bfloat16
F32 = jnp.float32


def inverse_rms(values):
    return lax.rsqrt(jnp.mean(values * values, axis=-1, keepdims=True) + EPSILON)


def rms_back(grad_in, normed, inverse):
    return inverse * (grad_in - normed * jnp.mean(grad_in * normed, axis=-1, keepdims=True))


def silu_slope(values):
    logistic = jax.nn.sigmoid(values)
    return logistic * (1.0 + values * (1.0 - logistic))


def time_embed(steps, width):
    half_width = width // 2
    frequency = jnp.exp(-math.log(10000.0) * jnp.arange(half_width, dtype=F32) / half_width)
    angles = steps.astype(F32)[:, None] * frequency[None, :]
    return jnp.concatenate([jnp.cos(angles), jnp.sin(angles)], axis=-1)


def rope_tables(positions, head_size):
    quarter = head_size // 4
    frequency = jnp.exp(-math.log(10000.0) * jnp.arange(quarter, dtype=F32) / quarter)
    along_rows = positions[0].astype(F32)[..., None] * frequency
    along_cols = positions[1].astype(F32)[..., None] * frequency
    angles = jnp.concatenate([along_rows, along_rows, along_cols, along_cols], axis=-1)
    return (jnp.cos(angles)[..., None, :], jnp.sin(angles)[..., None, :])


def quarter_turn(values):
    first, second, third, fourth = jnp.split(values, 4, axis=-1)
    return jnp.concatenate([-second, first, -fourth, third], axis=-1)


def rotate_heads(values, cosine, sine):
    return values * cosine + quarter_turn(values) * sine


def unrotate(grad_in, cosine, sine):
    return grad_in * cosine - quarter_turn(grad_in * sine)


def matmul(left, right):
    return jnp.dot(left, right, preferred_element_type=F32)


def outer_sum(left, right):
    return jnp.einsum("ra,rb->ab", left, right, preferred_element_type=F32)


def times_transpose(left, right):
    return jnp.einsum("rb,ab->ra", left, right, preferred_element_type=F32)


MESH = pl.DeviceIdType.MESH
SUM_ID, GATHER_ID, SCATTER_ID, WEIGHT_ID = 1, 2, 3, 4


def greet(partners):
    barrier = pltpu.get_barrier_semaphore()
    for partner in partners:
        pl.semaphore_signal(barrier, inc=1, device_id=partner, device_id_type=MESH)
    pl.semaphore_wait(barrier, len(partners))


def group_partners():
    item, column = lax.axis_index("dp"), lax.axis_index("seq")
    core = lax.rem(column, 2)
    return (item, column + 1 - 2 * core), (item, lax.rem(column + 2, 4))


GATHER_PIECES = 4


def gather_kernel(own_ref, out_ref, local_sem, send_sem, recv_sem):
    column = lax.axis_index("seq")
    sibling, across = group_partners()
    greet([sibling, across])
    local = pltpu.make_async_copy(own_ref, out_ref.at[column], local_sem)
    local.start()
    rows = own_ref.shape[0] // GATHER_PIECES

    def remote(source, place, piece, kind, target):
        part = pl.ds(piece * rows, rows)
        return pltpu.make_async_remote_copy(
            src_ref=source.at[part],
            dst_ref=out_ref.at[place, part],
            send_sem=send_sem.at[kind, piece],
            recv_sem=recv_sem.at[kind, piece],
            device_id=target,
            device_id_type=MESH,
        )

    far = lax.rem(column + 2, 4)
    pieces = range(GATHER_PIECES)
    over = [remote(own_ref, column, piece, 0, across) for piece in pieces]
    beside = [remote(own_ref, column, piece, 1, sibling) for piece in pieces]
    onward = [remote(out_ref.at[far], far, piece, 2, sibling) for piece in pieces]
    for copy in over:
        copy.start()
    for copy in beside:
        copy.start()
    for piece in pieces:
        over[piece].wait_recv()
        onward[piece].start()
    for piece in pieces:
        over[piece].wait_send()
        beside[piece].wait()
        onward[piece].wait()
    local.wait()


def gather_rows(values):
    rows, columns = values.shape
    gathered = pl.pallas_call(
        gather_kernel,
        out_shape=jax.ShapeDtypeStruct((4, rows, columns), values.dtype),
        in_specs=[pl.BlockSpec(memory_space=pltpu.VMEM)],
        out_specs=pl.BlockSpec(memory_space=pltpu.VMEM),
        scratch_shapes=[
            pltpu.SemaphoreType.DMA,
            pltpu.SemaphoreType.DMA((3, GATHER_PIECES)),
            pltpu.SemaphoreType.DMA((3, GATHER_PIECES)),
        ],
        compiler_params=pltpu.CompilerParams(
            collective_id=GATHER_ID, has_side_effects=True, vmem_limit_bytes=48 * 2**20
        ),
        name="gather_rows",
    )(values)
    return gathered.reshape(4 * rows, columns)


def scatter_kernel(parts_ref, out_ref, near, low, far, send_sem, recv_sem):
    column = lax.axis_index("seq")
    core, chip = lax.rem(column, 2), column // 2
    sibling, across = group_partners()
    greet([sibling, across])
    rows = out_ref.shape[0] // 2

    def remote(source, target_ref, index, target):
        return pltpu.make_async_remote_copy(
            src_ref=source,
            dst_ref=target_ref,
            send_sem=send_sem.at[index],
            recv_sem=recv_sem.at[index],
            device_id=target,
            device_id_type=MESH,
        )

    parts = [pl.ds(piece * rows, rows) for piece in range(2)]
    beside = [
        remote(parts_ref.at[1 - chip, 1 - core, part], near.at[0, part], i, sibling)
        for i, part in enumerate(parts)
    ]
    beside.append(remote(parts_ref.at[chip, 1 - core], near.at[1], 2, sibling))
    for copy in beside:
        copy.start()
    over = [remote(low.at[part], far.at[part], 3 + i, across) for i, part in enumerate(parts)]
    for i, part in enumerate(parts):
        beside[i].wait_recv()
        pair = parts_ref[1 - chip, core, part].astype(F32) + near[0, part].astype(F32)
        low[part] = pair.astype(BF16)
        over[i].start()
    beside[2].wait_recv()
    out_ref[...] = parts_ref[chip, core].astype(F32) + near[1].astype(F32)
    for i, part in enumerate(parts):
        over[i].wait()
        out_ref[part] += far[part].astype(F32)
    for copy in beside:
        copy.wait_send()


def scatter_rows(partial):
    rows, columns = partial.shape[0] // 4, partial.shape[1]
    return pl.pallas_call(
        scatter_kernel,
        out_shape=jax.ShapeDtypeStruct((rows, columns), F32),
        in_specs=[pl.BlockSpec(memory_space=pltpu.VMEM)],
        out_specs=pl.BlockSpec(memory_space=pltpu.VMEM),
        scratch_shapes=[
            pltpu.VMEM((2, rows, columns), BF16),
            pltpu.VMEM((rows, columns), BF16),
            pltpu.VMEM((rows, columns), BF16),
            pltpu.SemaphoreType.DMA((5,)),
            pltpu.SemaphoreType.DMA((5,)),
        ],
        compiler_params=pltpu.CompilerParams(
            collective_id=SCATTER_ID, has_side_effects=True, vmem_limit_bytes=48 * 2**20
        ),
        name="scatter_rows",
    )(partial.astype(BF16).reshape(2, 2, rows, columns))


def weight_blocks():
    blocks = [(0, None, 0, 1152), (1, 0, 0, 512), (1, 1, 0, 512), (0, None, 2304, 1152)]
    blocks += [(k, j, 0, 384) for k in (2, 3) for j in (0, 1)]
    return blocks + [(0, None, 4608, 1152)]


FIRST_ROWS = 80


def weights_kernel(*refs):
    ins, outs = refs[:4], refs[4:8]
    held, (local_sem, send_sem, recv_sem) = refs[8:12], refs[12:]
    item, column = lax.axis_index("dp"), lax.axis_index("seq")
    core, chip = lax.rem(column, 2), column // 2
    y_bit, z_bit = lax.rem(item, 2), lax.rem(item // 2, 2)
    sibling = (item, column + 1 - 2 * core)
    y_near = (item + 1 - 2 * y_bit, column)
    z_near = (item + 2 - 4 * z_bit, column)
    cores = [core, 1 - core]
    far = [(1 - chip) * 2 + k for k in cores]
    greet([(item, far[0]), (item, far[1]), sibling, y_near, z_near])
    blocks = weight_blocks()
    count = len(blocks)
    half_rows = ins[0].shape[0] // 2

    def copy(source, target_ref, block, kind, target):
        return pltpu.make_async_remote_copy(
            src_ref=source,
            dst_ref=target_ref,
            send_sem=send_sem.at[block, kind],
            recv_sem=recv_sem.at[block, kind],
            device_id=target,
            device_id_type=MESH,
        )

    def piece(ref, block, y_pick, z_pick, first_row=0, rows=half_rows):
        _, _, start, columns = blocks[block]
        return ref.at[
            pl.ds(pl.multiple_of(z_pick * half_rows + first_row, 16), rows),
            pl.ds(pl.multiple_of(start + y_pick * columns, 128), columns),
        ]

    def mine_for(array, target):
        if array == 0:
            return ins[0]
        if array == 1:
            return ins[1].at[target]
        columns = outs[array].shape[2]
        return ins[array].at[:, pl.ds(pl.multiple_of(target * columns, 128), columns)]

    def over(block):
        array, offset, _, _ = blocks[block]
        goal = far[offset or 0]
        if array >= 2:
            columns = blocks[block][3]
            source = ins[array].at[
                pl.ds(pl.multiple_of(z_bit * half_rows, 16), half_rows),
                pl.ds(pl.multiple_of(goal * 2 * columns + y_bit * columns, 128), columns),
            ]
        else:
            source = piece(mine_for(array, goal), block, y_bit, z_bit)
        return copy(source, piece(outs[array].at[column], block, y_bit, z_bit), block, 0, (item, goal))

    def onward(block, kind):
        array, offset, _, _ = blocks[block]
        ref = outs[array].at[far[offset or 0]]
        if kind == 1:
            part, target = piece(ref, block, y_bit, z_bit), y_near
        elif kind == 2:
            part, target = piece(ref, block, y_bit, z_bit), z_near
        elif kind == 3:
            part, target = piece(ref, block, 1 - y_bit, z_bit, 0, FIRST_ROWS), z_near
        else:
            rest = half_rows - FIRST_ROWS
            part, target = piece(ref, block, y_bit, 1 - z_bit, FIRST_ROWS, rest), y_near
        return copy(part, part, block, kind, target)

    def share(block):
        _, _, start, columns = blocks[block]
        part = outs[0].at[far[0], :, pl.ds(start, 2 * columns)]
        return copy(part, part, block, 5, sibling)

    beside = [
        copy(mine_for(k, sibling[1]), outs[k].at[column], k, 6, sibling) for k in range(4)
    ]
    load = [
        pltpu.make_async_copy(mine_for(k, column), held[k], local_sem.at[0, k]) for k in range(4)
    ]
    store = [
        pltpu.make_async_copy(held[k], outs[k].at[column], local_sem.at[1, k]) for k in range(4)
    ]
    over(0).start()
    over(1).start()
    for k in range(4):
        beside[k].start()
        load[k].start()
    for k in range(4):
        load[k].wait()
        store[k].start()
    for step in range(count + 2):
        if step < count:
            over(step).wait_recv()
            if step + 2 < count:
                over(step + 2).start()
            onward(step, 1).start()
            onward(step, 2).start()
        if 0 <= step - 1 < count:
            onward(step - 1, 1).wait_recv()
            onward(step - 1, 3).start()
            onward(step - 1, 2).wait_recv()
            onward(step - 1, 4).start()
        if 0 <= step - 2 < count:
            onward(step - 2, 3).wait_recv()
            onward(step - 2, 4).wait_recv()
            if blocks[step - 2][0] == 0:
                share(step - 2).start()
    for block in range(count):
        over(block).wait_send()
        for kind in range(1, 5):
            onward(block, kind).wait_send()
        if blocks[block][0] == 0:
            share(block).wait()
    for k in range(4):
        beside[k].wait()
        store[k].wait()


def gather_weights(w_mod, w_qkv, w_gate, w_up):
    rows, width = w_mod.shape[0], w_qkv.shape[1] // 3
    head_cols = 3 * width // 4
    qkv = jnp.transpose(w_qkv.reshape(rows, 3, 4, width // 4), (2, 0, 1, 3))
    qkv = jnp.pad(qkv.reshape(4, rows, head_cols), ((0, 0), (0, 0), (0, -head_cols % 256)))
    shapes = [
        w_mod.shape,
        qkv.shape[1:],
        (rows, w_gate.shape[1] // 4),
        (rows, w_up.shape[1] // 4),
    ]
    count = len(weight_blocks())
    gathered = pl.pallas_call(
        weights_kernel,
        out_shape=[jax.ShapeDtypeStruct((4,) + shape, BF16) for shape in shapes],
        in_specs=[pl.BlockSpec(memory_space=pl.ANY)] * 4,
        out_specs=[pl.BlockSpec(memory_space=pl.ANY)] * 4,
        scratch_shapes=[pltpu.VMEM(shape, BF16) for shape in shapes]
        + [
            pltpu.SemaphoreType.DMA((2, 4)),
            pltpu.SemaphoreType.DMA((count, 7)),
            pltpu.SemaphoreType.DMA((count, 7)),
        ],
        compiler_params=pltpu.CompilerParams(
            collective_id=WEIGHT_ID, has_side_effects=True, vmem_limit_bytes=56 * 2**20
        ),
        name="gather_weights",
    )(w_mod, qkv, w_gate, w_up)
    mod, qkv, gate, up = [part.reshape(4 * rows, part.shape[2]) for part in gathered]
    return mod, qkv[:, :head_cols], gate, up


def rows_to_columns(values, blocks):
    rows, columns = values.shape
    ways = lax.axis_size("seq")
    values = values.reshape(rows, blocks, ways, columns // (blocks * ways))
    moved = lax.all_to_all(values, "seq", split_axis=2, concat_axis=0, tiled=True)
    return moved.reshape(rows * ways, columns // ways)


def columns_to_rows(values, blocks):
    rows, columns = values.shape
    ways = lax.axis_size("seq")
    values = values.reshape(rows, blocks, 1, columns // blocks)
    moved = lax.all_to_all(values, "seq", split_axis=0, concat_axis=2, tiled=True)
    return moved.reshape(rows // ways, columns * ways)


TILE = 128


def first_tile(place, tiles):
    return (tiles * place) // 4


def padded_rows(rows):
    return -(-rows // 16) * 16


class Part:
    def __init__(self, left, right, rows, columns, order, by_rows=False):
        self.left, self.right, self.rows, self.columns = left, right, rows, columns
        self.order, self.by_rows = order, by_rows
        self.slab = padded_rows(rows)


def grads_kernel(parts, names, groups, n_out, *refs):
    refs = list(refs)

    def take(count):
        taken = refs[:count]
        del refs[:count]
        return taken

    ins = dict(zip(names, take(len(names)), strict=True))
    shared = take(groups)
    small_in = take(1)[0]
    count = len(parts)
    outs = take(count)
    small_out = take(1)[0]
    held = dict(zip(names, take(len(names)), strict=True))
    gathered = take(groups)
    own, first_in, second_in, third_in = take(count), take(count), take(count), take(count)
    slabs, slab_in = take(count), take(count)
    total, small, small_came = take(3)
    load_sem, share_send, share_recv, own_sem, send_sem, recv_sem = take(6)
    last_send, last_recv, small_send, small_recv = take(4)

    item, column = lax.axis_index("dp"), lax.axis_index("seq")
    bits = [lax.rem(item, 2), lax.rem(item // 2, 2), item // 4]
    partners = [(item + (1 - 2 * bits[k]) * (1 << k), column) for k in range(3)]
    peers = [(item, lax.rem(column + k, 4)) for k in range(1, 4)]
    owner = (2 * column + item // 4, lax.rem(item, 4))
    feeder = (4 * lax.rem(item, 2) + column, item // 2)
    elsewhere = jnp.logical_or(owner[0] != item, owner[1] != column)

    loads = {
        name: pltpu.make_async_copy(ins[name], held[name], load_sem.at[i])
        for i, name in enumerate(names)
    }
    for name in names:
        loads[name].start()

    barrier = pltpu.get_barrier_semaphore()
    for partner in partners + peers:
        pl.semaphore_signal(barrier, inc=1, device_id=partner, device_id_type=MESH)
    waits = 6
    if any(part.by_rows for part in parts):
        waits = 6 + elsewhere.astype(jnp.int32)

        @pl.when(elsewhere)
        def _():
            pl.semaphore_signal(barrier, inc=1, device_id=feeder, device_id_type=MESH)

    pl.semaphore_wait(barrier, waits)

    def remote(source, target_ref, send, recv, target):
        return pltpu.make_async_remote_copy(
            src_ref=source,
            dst_ref=target_ref,
            send_sem=send,
            recv_sem=recv,
            device_id=target,
            device_id_type=MESH,
        )

    def columns_of(group, place):
        wide, narrow = shared[group].shape[1], gathered[group].shape[2]
        if wide == narrow:
            return shared[group]
        start = first_tile(place, wide // TILE) * TILE
        return shared[group].at[:, pl.ds(pl.multiple_of(start, TILE), narrow)]

    shares = [
        [
            remote(
                columns_of(group, peer[1]),
                gathered[group].at[column],
                share_send.at[group, k],
                share_recv.at[group, k],
                peer,
            )
            for k, peer in enumerate(peers)
        ]
        for group in range(groups)
    ]
    own_shares = [
        pltpu.make_async_copy(columns_of(g, column), gathered[g].at[column], own_sem.at[g])
        for g in range(groups)
    ]
    for group in range(groups):
        own_shares[group].start()
        for copy in shares[group]:
            copy.start()
    ready = set()

    def operand(name):
        if isinstance(name, int):
            if name not in ready:
                own_shares[name].wait()
                for copy in shares[name]:
                    copy.wait()
            ready.add(name)
            ref = gathered[name]
            return ref[...].reshape(4 * ref.shape[1], ref.shape[2])
        if name not in ready:
            loads[name].wait()
        ready.add(name)
        return held[name][...]

    def multiply(index):
        part = parts[index]
        left, right = operand(part.left), operand(part.right)
        if isinstance(part.right, int):
            sums = jnp.sum(right.astype(F32), axis=0, keepdims=True)
            for tile in range(part.columns // TILE):
                row = 8 * (part.right - 1) + tile
                small[0, row : row + 1] = sums[:, tile * TILE : (tile + 1) * TILE]
        step = 384 if part.slab == part.rows else left.shape[1]
        for start in range(0, left.shape[1], step):
            product = lax.dot_general(
                left[:, start : start + step],
                right,
                (((0,), (0,)), ((), ())),
                preferred_element_type=F32,
            )
            if part.slab == part.rows:
                product = product.astype(BF16)
                for d in range(8):
                    low = max(start, d * part.rows)
                    high = min(start + step, (d + 1) * part.rows)
                    if low < high:
                        own[index][
                            d // 4, d // 2 % 2, d % 2, low - d * part.rows : high - d * part.rows
                        ] = product[low - start : high - start]
            else:
                total[: left.shape[1], : part.columns] = product
                for d in range(8):
                    own[index][d // 4, d // 2 % 2, d % 2] = cut(
                        d * part.rows, part.rows, part.slab, part.columns
                    )

    def cut(start, rows, padded, columns):
        values = total[start : start + rows, :columns]
        if padded > rows:
            values = jnp.concatenate([values, jnp.zeros((padded - rows, columns), F32)], axis=0)
        return values.astype(BF16)

    def half(index, mine):
        order = parts[index].order
        pick = bits[order] if mine else 1 - bits[order]
        return (slice(None), slice(None), pick) if order == 0 else (slice(None), pick)

    def pick_own(index, high, low):
        order = parts[index].order
        return (high, low, bits[0]) if order == 0 else (high, bits[1], low)

    def stage(index, step):
        part = parts[index]
        sems = send_sem.at[index, step], recv_sem.at[index, step]
        other = 1 - part.order
        if step == 0:
            source, target = own[index].at[half(index, False)], first_in[index]
            return remote(source, target, *sems, partners[part.order])
        if step == 1:
            place = pick_own(index, slice(None), 1 - bits[other])
            return remote(own[index].at[place], second_in[index], *sems, partners[other])
        place = pick_own(index, 1 - bits[2], bits[other])
        return remote(own[index].at[place], third_in[index], *sems, partners[2])

    def begin(index):
        multiply(index)
        stage(index, 0).start()

    def end_first(index):
        stage(index, 0).wait()
        for high in range(2):
            for low in range(2):
                place = pick_own(index, high, low)
                mine = own[index][place].astype(F32)
                own[index][place] = (mine + first_in[index][high, low].astype(F32)).astype(BF16)
        stage(index, 1).start()

    def end_second(index):
        stage(index, 1).wait()
        for high in range(2):
            place = pick_own(index, high, bits[1 - parts[index].order])
            mine = own[index][place].astype(F32)
            own[index][place] = (mine + second_in[index][high].astype(F32)).astype(BF16)
        stage(index, 2).start()

    def last(index):
        if parts[index].by_rows:
            sems = last_send.at[index, 0], last_recv.at[index, 0]
            return [remote(slabs[index], slab_in[index], *sems, owner)]
        return [
            remote(
                slabs[index].at[peer[1]],
                slab_in[index].at[column],
                last_send.at[index, k],
                last_recv.at[index, k],
                peer,
            )
            for k, peer in enumerate(peers)
        ]

    def end_third(index):
        part = parts[index]
        stage(index, 2).wait()
        place = pick_own(index, bits[2], bits[1 - part.order])
        sums = own[index][place].astype(F32) + third_in[index][...].astype(F32)
        if part.by_rows:
            slabs[index][...] = sums.astype(BF16)

            @pl.when(elsewhere)
            def _():
                last(index)[0].start()

            @pl.when(jnp.logical_not(elsewhere))
            def _():
                slab_in[index][...] = slabs[index][...]

            return
        total[: part.rows, : part.columns] = sums
        rows = part.rows // 4
        for k in range(4):
            slabs[index][k] = cut(k * rows, rows, padded_rows(rows), part.columns)
        for copy in last(index):
            copy.start()
        slab_in[index][column] = slabs[index][column]

    def end_last(index):
        part = parts[index]
        if part.by_rows:

            @pl.when(elsewhere)
            def _():
                last(index)[0].wait()

            outs[index][...] = slab_in[index][...].astype(F32)[: part.rows]
            return
        for copy in last(index):
            copy.wait()
        rows = part.rows // 4
        wide = outs[index].shape[-1]
        for k in range(4):
            values = slab_in[index][k].astype(F32)[:rows]
            if len(outs[index].shape) == 3:
                outs[index][k] = values
            else:
                start = first_tile(k, wide // TILE) * TILE
                outs[index][:, start : start + part.columns] = values

    def small_step(step):
        if step < 3:
            sems = small_send.at[step], small_recv.at[step]
            return [remote(small.at[step], small_came.at[step], *sems, partners[step])]
        return [
            remote(small.at[3], small_out.at[column], small_send.at[3 + k], small_recv.at[3 + k], peer)
            for k, peer in enumerate(peers)
        ]

    small[0] = small_in[...]
    ahead = 2
    for index in range(min(ahead, count)):
        begin(index)
    for step in range(count + 3):
        if step < count:
            end_first(step)
            if step + ahead < count:
                begin(step + ahead)
        if 0 <= step - 1 < count:
            end_second(step - 1)
        if 0 <= step - 2 < count:
            end_third(step - 2)
        if 0 <= step - 3 < count:
            end_last(step - 3)
        at = step - (count - ahead)
        if at == 0:
            small_step(0)[0].start()
        if 1 <= at <= 3:
            small_step(at - 1)[0].wait()
            small[at] = small[at - 1] + small_came[at - 1]
            for copy in small_step(at):
                copy.start()
    small_out[column] = small[3]
    for copy in small_step(3):
        copy.wait()


def weight_grads(parts, arrays, shared, small, out_shapes):
    count, groups = len(parts), len(shared)
    names = tuple(arrays)
    tokens_all = 4 * shared[0].shape[0]
    scratch = [pltpu.VMEM(value.shape, BF16) for value in arrays.values()]
    for index, value in enumerate(shared):
        columns = value.shape[1] if index == 0 else -(-value.shape[1] // (4 * TILE)) * TILE
        scratch.append(pltpu.VMEM((4, tokens_all // 4, columns), BF16))
    for lead in ((2, 2, 2), (2, 2), (2,), ()):
        scratch += [pltpu.VMEM(lead + (part.slab, part.columns), BF16) for part in parts]
    for _ in range(2):
        for part in parts:
            if part.by_rows:
                scratch.append(pltpu.VMEM((part.slab, part.columns), BF16))
            else:
                scratch.append(pltpu.VMEM((4, padded_rows(part.rows // 4), part.columns), BF16))
    widest = max(part.columns for part in parts)
    tallest = max(8 * part.rows if part.by_rows and part.slab > part.rows else part.rows for part in parts)
    scratch += [
        pltpu.VMEM((tallest, widest), F32),
        pltpu.VMEM((4,) + small.shape, F32),
        pltpu.VMEM((3,) + small.shape, F32),
        pltpu.SemaphoreType.DMA((len(names),)),
        pltpu.SemaphoreType.DMA((groups, 3)),
        pltpu.SemaphoreType.DMA((groups, 3)),
        pltpu.SemaphoreType.DMA((groups,)),
        pltpu.SemaphoreType.DMA((count, 3)),
        pltpu.SemaphoreType.DMA((count, 3)),
        pltpu.SemaphoreType.DMA((count, 3)),
        pltpu.SemaphoreType.DMA((count, 3)),
        pltpu.SemaphoreType.DMA((6,)),
        pltpu.SemaphoreType.DMA((6,)),
    ]

    def kernel(*refs):
        grads_kernel(parts, names, groups, count, *refs)

    return pl.pallas_call(
        kernel,
        out_shape=[jax.ShapeDtypeStruct(shape, F32) for shape in out_shapes]
        + [jax.ShapeDtypeStruct((4,) + small.shape, F32)],
        in_specs=[pl.BlockSpec(memory_space=pl.ANY)] * (len(names) + groups)
        + [pl.BlockSpec(memory_space=pltpu.VMEM)],
        out_specs=[pl.BlockSpec(memory_space=pltpu.VMEM)] * (count + 1),
        scratch_shapes=scratch,
        compiler_params=pltpu.CompilerParams(
            collective_id=SUM_ID, has_side_effects=True, vmem_limit_bytes=63 * 2**20
        ),
        name="weight_grads",
    )(*arrays.values(), *shared, small)


def to_owners(rows):
    n_dp, n_seq = lax.axis_size("dp"), lax.axis_size("seq")
    pairs = []
    for d in range(n_dp):
        for s in range(n_seq):
            pairs.append((d * n_seq + s, s * n_dp + d))
    return lax.ppermute(rows, ("dp", "seq"), pairs)


def columns_to_rows(values, blocks):
    rows, columns = values.shape
    ways = lax.axis_size("seq")
    values = values.reshape(rows, blocks, 1, columns // blocks)
    moved = lax.all_to_all(values, "seq", split_axis=0, concat_axis=2, tiled=True)
    return moved.reshape(rows // ways, columns * ways)


def plain_weight_grads(arrays, shared, bias_rows, gains):
    def share(partial):
        return lax.psum_scatter(partial.astype(BF16), "dp", scatter_dimension=0, tiled=True)

    def by_columns(left, right, blocks):
        return columns_to_rows(share(outer_sum(left, right)), blocks).astype(F32)

    def by_rows(left, right):
        return to_owners(share(outer_sum(left, right))).astype(F32)

    lifted = gather_rows(shared[0])
    mod_rows = jnp.concatenate([shared[1], shared[2]], axis=1)
    mod = by_columns(lifted, rows_to_columns(mod_rows, 6), 6)
    bias = lax.psum_scatter(bias_rows, ("dp", "seq"), scatter_dimension=0, tiled=True)
    return (
        by_columns(arrays["hidden_a"], arrays["grad_project"], 3),
        by_rows(arrays["attended"], arrays["grad_branch_a"]),
        by_columns(arrays["hidden_b"], arrays["grad_gate_in"], 1),
        by_columns(arrays["hidden_b"], arrays["grad_up_in"], 1),
        by_rows(arrays["inner"], arrays["grad_branch_b"]),
        mod,
        bias,
        lax.psum(gains, ("dp", "seq")),
    )


def all_weight_grads(arrays, shared, gains):
    if lax.axis_size("dp") != 8:
        bias_rows = jnp.concatenate([jnp.sum(part.astype(F32), axis=0) for part in shared[1:]])
        return plain_weight_grads(arrays, shared, bias_rows, gains)
    width, wide = arrays["hidden_a"].shape[1], shared[1].shape[1]
    ff, heads = arrays["inner"].shape[1], arrays["attended"].shape[1]
    mod = -(-wide // (4 * TILE)) * TILE
    rows = width // 8
    parts = [
        Part("inner", "grad_branch_b", ff // 8, width, 0, True),
        Part("hidden_b", "grad_gate_in", rows, ff, 1),
        Part("hidden_b", "grad_up_in", rows, ff, 0),
        Part("attended", "grad_branch_a", heads // 8, width, 1, True),
        Part("hidden_a", "grad_project", rows, 3 * heads, 0),
        Part(0, 2, rows, mod, 0),
        Part(0, 1, rows, mod, 0),
    ]
    small = jnp.pad(gains, ((0, 0), (0, TILE - gains.shape[1])))
    small = jnp.concatenate([jnp.zeros((16, TILE), F32), small, jnp.zeros((6, TILE), F32)])
    own = rows // 4
    shapes = [
        (ff // 8, width),
        (own, 4 * ff),
        (own, 4 * ff),
        (heads // 8, width),
        (4, own, 3 * heads),
        (own, wide),
        (own, wide),
    ]
    down, gate, up, out, qkv, mod_b, mod_a, small = weight_grads(parts, arrays, shared, small, shapes)
    qkv = jnp.transpose(qkv.reshape(4, own, 3, heads), (1, 2, 0, 3)).reshape(own, 3 * width)
    sums = small[:, :16].reshape(4, 2, 8 * TILE)
    tiles = wide // TILE
    edges = [first_tile(k, tiles) for k in range(4)] + [tiles]
    bias = jnp.concatenate(
        [sums[k, g, : (edges[k + 1] - edges[k]) * TILE] for g in range(2) for k in range(4)]
    )
    own_bias = bias.shape[0] // 32
    place = lax.axis_index("dp") * 4 + lax.axis_index("seq")
    bias = lax.dynamic_slice(bias, (place * own_bias,), (own_bias,))
    gains = jnp.sum(small[:, 16:18, :HD], axis=0)
    return qkv, out, gate, up, down, jnp.concatenate([mod_a, mod_b], axis=1), bias, gains


def shards(
    tokens,
    condition,
    cotangent,
    w_qkv,
    w_out,
    w_gate,
    w_up,
    w_down,
    w_mod,
    b_mod,
    q_gain,
    k_gain,
    noise_counts,
    time_steps,
    positions,
):
    local_rows, width = tokens.shape[1:]
    ways = lax.axis_size("seq")
    patches = local_rows * ways
    local_heads = HEADS // ways
    factor = HD ** (-0.5)
    mod_full, qkv_cols, gate_cols, up_cols = gather_weights(w_mod, w_qkv, w_gate, w_up)
    all_positions = lax.all_gather(positions[:, 0], "seq", axis=1, tiled=True)
    cosine, sine = rope_tables(all_positions, HD)

    item = lax.axis_index("dp")
    running = jnp.cumsum(noise_counts)
    image_id = jnp.sum((running <= item).astype(jnp.int32))
    chosen = jnp.arange(noise_counts.shape[0], dtype=jnp.int32) == image_id
    share = 1.0 / jnp.sum(jnp.where(chosen, noise_counts, 0)).astype(F32)

    condition_in = condition[0].astype(F32) + time_embed(time_steps, width)
    lifted_low = jax.nn.silu(condition_in).astype(BF16)
    modulation = matmul(lifted_low, mod_full) + b_mod
    shift_a, scale_a, gate_a, shift_b, scale_b, gate_b = jnp.split(modulation, 6, axis=-1)
    tokens_f = tokens[0].astype(F32)
    inverse_a = inverse_rms(tokens_f)
    normed_a = tokens_f * inverse_a
    hidden_a = gather_rows((normed_a * (1.0 + scale_a) + shift_a).astype(BF16))
    grad_out = cotangent[0].astype(F32) * share
    grad_branch_b = gather_rows((grad_out * gate_b).astype(BF16))

    projected = matmul(hidden_a, qkv_cols).reshape(patches, 3, local_heads, HD)
    query_inv = inverse_rms(projected[:, 0])
    query_norm = projected[:, 0] * query_inv
    query_rows = rotate_heads(query_norm * q_gain, cosine, sine).astype(BF16)
    key_inv = inverse_rms(projected[:, 1])
    key_norm = projected[:, 1] * key_inv
    key_rows = rotate_heads(key_norm * k_gain, cosine, sine).astype(BF16)
    value_rows = projected[:, 2].astype(BF16)

    scores = jnp.einsum("qhd,khd->hqk", query_rows, key_rows, preferred_element_type=F32) * factor
    exp_scores = jnp.exp(scores)
    totals = jnp.sum(exp_scores, axis=-1, keepdims=True)
    weights_low = (exp_scores / totals).astype(BF16)
    mixed = jnp.einsum("hqk,khd->qhd", weights_low, value_rows, preferred_element_type=F32)
    attended = mixed.reshape(patches, local_heads * HD).astype(BF16)

    branch_a = scatter_rows(matmul(attended, w_out))
    middle = tokens_f + gate_a * branch_a
    inverse_b = inverse_rms(middle)
    normed_b = middle * inverse_b
    hidden_b = gather_rows((normed_b * (1.0 + scale_b) + shift_b).astype(BF16))
    gate_in = matmul(hidden_b, gate_cols)
    up_in = matmul(hidden_b, up_cols)
    activated = jax.nn.silu(gate_in)
    inner = (activated * up_in).astype(BF16)
    branch_b = scatter_rows(matmul(inner, w_down))
    block_out = (middle + gate_b * branch_b).astype(BF16)

    grad_gate_b = grad_out * branch_b
    grad_inner = times_transpose(grad_branch_b, w_down)
    grad_gate_in = (grad_inner * up_in * silu_slope(gate_in)).astype(BF16)
    grad_up_in = (grad_inner * activated).astype(BF16)
    grad_hidden_b = scatter_rows(
        times_transpose(grad_gate_in, gate_cols) + times_transpose(grad_up_in, up_cols)
    )
    grad_middle = grad_out + rms_back(grad_hidden_b * (1.0 + scale_b), normed_b, inverse_b)
    grad_gate_a = grad_middle * branch_a
    grad_branch_a = gather_rows((grad_middle * gate_a).astype(BF16))
    grad_attended = (
        times_transpose(grad_branch_a, w_out).astype(BF16).reshape(patches, local_heads, HD)
    )

    scores = jnp.einsum("qhd,khd->hqk", query_rows, key_rows, preferred_element_type=F32) * factor
    probs = jnp.exp(scores) / totals
    grad_probs = jnp.einsum("qhd,khd->hqk", grad_attended, value_rows, preferred_element_type=F32)
    row_inner = jnp.sum(probs * grad_probs, axis=-1, keepdims=True)
    grad_scores = (probs * (grad_probs - row_inner)).astype(BF16)
    grad_query = (
        jnp.einsum("hqk,khd->qhd", grad_scores, key_rows, preferred_element_type=F32) * factor
    )
    grad_key = (
        jnp.einsum("hqk,qhd->khd", grad_scores, query_rows, preferred_element_type=F32) * factor
    )
    grad_value = jnp.einsum(
        "hqk,qhd->khd", probs.astype(BF16), grad_attended, preferred_element_type=F32
    )
    grad_query_norm = unrotate(grad_query, cosine, sine)
    grad_key_norm = unrotate(grad_key, cosine, sine)
    grad_q_gain = jnp.sum(grad_query_norm * query_norm, axis=(0, 1))
    grad_k_gain = jnp.sum(grad_key_norm * key_norm, axis=(0, 1))
    grad_query_raw = rms_back(grad_query_norm * q_gain, query_norm, query_inv)
    grad_key_raw = rms_back(grad_key_norm * k_gain, key_norm, key_inv)
    grad_project = jnp.stack([grad_query_raw, grad_key_raw, grad_value], axis=1)
    grad_project = grad_project.reshape(patches, 3 * local_heads * HD).astype(BF16)
    grad_hidden_a = scatter_rows(times_transpose(grad_project, qkv_cols))
    grad_tokens = grad_middle + rms_back(grad_hidden_a * (1.0 + scale_a), normed_a, inverse_a)
    grad_mod_a = jnp.concatenate(
        [grad_hidden_a, grad_hidden_a * normed_a, grad_gate_a], axis=-1
    ).astype(BF16)
    grad_mod_b = jnp.concatenate(
        [grad_hidden_b, grad_hidden_b * normed_b, grad_gate_b], axis=-1
    ).astype(BF16)
    half = grad_mod_a.shape[1]
    grad_condition = (
        times_transpose(grad_mod_a, mod_full[:, :half])
        + times_transpose(grad_mod_b, mod_full[:, half:])
    ) * silu_slope(condition_in)
    arrays = {
        "inner": inner,
        "grad_branch_b": grad_branch_b,
        "hidden_b": hidden_b,
        "grad_gate_in": grad_gate_in,
        "grad_up_in": grad_up_in,
        "attended": attended,
        "grad_branch_a": grad_branch_a,
        "hidden_a": hidden_a,
        "grad_project": grad_project,
    }
    gains = jnp.stack([grad_q_gain, grad_k_gain])
    shared = [lifted_low, grad_mod_a, grad_mod_b]
    (grad_w_qkv, grad_w_out, grad_w_gate, grad_w_up, grad_w_down, grad_w_mod, sum_bias, gains) = (
        all_weight_grads(arrays, shared, gains)
    )
    sum_q_gain, sum_k_gain = gains[0], gains[1]
    return (
        block_out[None],
        grad_tokens[None],
        grad_condition[None],
        grad_w_qkv,
        grad_w_out,
        grad_w_gate,
        grad_w_up,
        grad_w_down,
        grad_w_mod,
        sum_bias,
        sum_q_gain,
        sum_k_gain,
    )


def solution(mesh):
    placed = (
        P("dp", "seq", None),
        P("dp", "seq", None),
        P("dp", "seq", None),
        P("seq", None),
        P("seq", None),
        P("seq", None),
        P("seq", None),
        P("seq", None),
        P("seq", None),
        P(),
        P(),
        P(),
        P(),
        P("dp"),
        P(None, "dp", "seq"),
    )
    return jax.shard_map(
        shards,
        mesh=mesh,
        in_specs=placed,
        out_specs=(
            P("dp", "seq", None),
            P("dp", "seq", None),
            P("dp", "seq", None),
            P(("dp", "seq"), None),
            P(("dp", "seq"), None),
            P(("dp", "seq"), None),
            P(("dp", "seq"), None),
            P(("dp", "seq"), None),
            P(("dp", "seq"), None),
            P(("dp", "seq")),
            P(),
            P(),
        ),
        check_vma=False,
    )
```

```python
import math

import jax
import jax.numpy as jnp
from jax import lax
from jax.experimental import pallas as pl
from jax.experimental.pallas import tpu as pltpu
from jax.sharding import PartitionSpec as P

HEADS = 16
HD = 72
EPSILON = 1e-06
BF16 = jnp.bfloat16
F32 = jnp.float32


def inverse_rms(values):
    return lax.rsqrt(jnp.mean(values * values, axis=-1, keepdims=True) + EPSILON)


def rms_back(grad_in, normed, inverse):
    return inverse * (grad_in - normed * jnp.mean(grad_in * normed, axis=-1, keepdims=True))


def silu_slope(values):
    logistic = jax.nn.sigmoid(values)
    return logistic * (1.0 + values * (1.0 - logistic))


def time_embed(steps, width):
    half_width = width // 2
    frequency = jnp.exp(-math.log(10000.0) * jnp.arange(half_width, dtype=F32) / half_width)
    angles = steps.astype(F32)[:, None] * frequency[None, :]
    return jnp.concatenate([jnp.cos(angles), jnp.sin(angles)], axis=-1)


def rope_tables(positions, head_size):
    quarter = head_size // 4
    frequency = jnp.exp(-math.log(10000.0) * jnp.arange(quarter, dtype=F32) / quarter)
    along_rows = positions[0].astype(F32)[..., None] * frequency
    along_cols = positions[1].astype(F32)[..., None] * frequency
    angles = jnp.concatenate([along_rows, along_rows, along_cols, along_cols], axis=-1)
    return (jnp.cos(angles)[..., None, :], jnp.sin(angles)[..., None, :])


def quarter_turn(values):
    first, second, third, fourth = jnp.split(values, 4, axis=-1)
    return jnp.concatenate([-second, first, -fourth, third], axis=-1)


def rotate_heads(values, cosine, sine):
    return values * cosine + quarter_turn(values) * sine


def unrotate(grad_in, cosine, sine):
    return grad_in * cosine - quarter_turn(grad_in * sine)


def matmul(left, right):
    return jnp.dot(left, right, preferred_element_type=F32)


def outer_sum(left, right):
    return jnp.einsum("ra,rb->ab", left, right, preferred_element_type=F32)


def times_transpose(left, right):
    return jnp.einsum("rb,ab->ra", left, right, preferred_element_type=F32)


MESH = pl.DeviceIdType.MESH
SUM_ID, GATHER_ID, SCATTER_ID, WEIGHT_ID, ATTEND_ID, BACK_ID = 1, 2, 3, 4, 5, 6


def greet(partners):
    barrier = pltpu.get_barrier_semaphore()
    for partner in partners:
        pl.semaphore_signal(barrier, inc=1, device_id=partner, device_id_type=MESH)
    pl.semaphore_wait(barrier, len(partners))


def group_partners():
    item, column = lax.axis_index("dp"), lax.axis_index("seq")
    core = lax.rem(column, 2)
    return (item, column + 1 - 2 * core), (item, lax.rem(column + 2, 4))


GATHER_PIECES = 4


def gather_kernel(own_ref, out_ref, local_sem, send_sem, recv_sem):
    column = lax.axis_index("seq")
    sibling, across = group_partners()
    greet([sibling, across])
    local = pltpu.make_async_copy(own_ref, out_ref.at[column], local_sem)
    local.start()
    rows = own_ref.shape[0] // GATHER_PIECES

    def remote(source, place, piece, kind, target):
        part = pl.ds(piece * rows, rows)
        return pltpu.make_async_remote_copy(
            src_ref=source.at[part],
            dst_ref=out_ref.at[place, part],
            send_sem=send_sem.at[kind, piece],
            recv_sem=recv_sem.at[kind, piece],
            device_id=target,
            device_id_type=MESH,
        )

    far = lax.rem(column + 2, 4)
    pieces = range(GATHER_PIECES)
    over = [remote(own_ref, column, piece, 0, across) for piece in pieces]
    beside = [remote(own_ref, column, piece, 1, sibling) for piece in pieces]
    onward = [remote(out_ref.at[far], far, piece, 2, sibling) for piece in pieces]
    for copy in over:
        copy.start()
    for copy in beside:
        copy.start()
    for piece in pieces:
        over[piece].wait_recv()
        onward[piece].start()
    for piece in pieces:
        over[piece].wait_send()
        beside[piece].wait()
        onward[piece].wait()
    local.wait()


def gather_rows(values):
    rows, columns = values.shape
    gathered = pl.pallas_call(
        gather_kernel,
        out_shape=jax.ShapeDtypeStruct((4, rows, columns), values.dtype),
        in_specs=[pl.BlockSpec(memory_space=pltpu.VMEM)],
        out_specs=pl.BlockSpec(memory_space=pltpu.VMEM),
        scratch_shapes=[
            pltpu.SemaphoreType.DMA,
            pltpu.SemaphoreType.DMA((3, GATHER_PIECES)),
            pltpu.SemaphoreType.DMA((3, GATHER_PIECES)),
        ],
        compiler_params=pltpu.CompilerParams(
            collective_id=GATHER_ID, has_side_effects=True, vmem_limit_bytes=48 * 2**20
        ),
        name="gather_rows",
    )(values)
    return gathered.reshape(4 * rows, columns)


def scatter_kernel(parts_ref, out_ref, near, low, far, send_sem, recv_sem):
    column = lax.axis_index("seq")
    core, chip = lax.rem(column, 2), column // 2
    sibling, across = group_partners()
    greet([sibling, across])
    rows = out_ref.shape[0] // 2

    def remote(source, target_ref, index, target):
        return pltpu.make_async_remote_copy(
            src_ref=source,
            dst_ref=target_ref,
            send_sem=send_sem.at[index],
            recv_sem=recv_sem.at[index],
            device_id=target,
            device_id_type=MESH,
        )

    parts = [pl.ds(piece * rows, rows) for piece in range(2)]
    beside = [
        remote(parts_ref.at[1 - chip, 1 - core, part], near.at[0, part], i, sibling)
        for i, part in enumerate(parts)
    ]
    beside.append(remote(parts_ref.at[chip, 1 - core], near.at[1], 2, sibling))
    for copy in beside:
        copy.start()
    over = [remote(low.at[part], far.at[part], 3 + i, across) for i, part in enumerate(parts)]
    for i, part in enumerate(parts):
        beside[i].wait_recv()
        pair = parts_ref[1 - chip, core, part].astype(F32) + near[0, part].astype(F32)
        low[part] = pair.astype(BF16)
        over[i].start()
    beside[2].wait_recv()
    out_ref[...] = parts_ref[chip, core].astype(F32) + near[1].astype(F32)
    for i, part in enumerate(parts):
        over[i].wait()
        out_ref[part] += far[part].astype(F32)
    for copy in beside:
        copy.wait_send()


def scatter_rows(partial):
    rows, columns = partial.shape[0] // 4, partial.shape[1]
    return pl.pallas_call(
        scatter_kernel,
        out_shape=jax.ShapeDtypeStruct((rows, columns), F32),
        in_specs=[pl.BlockSpec(memory_space=pltpu.VMEM)],
        out_specs=pl.BlockSpec(memory_space=pltpu.VMEM),
        scratch_shapes=[
            pltpu.VMEM((2, rows, columns), BF16),
            pltpu.VMEM((rows, columns), BF16),
            pltpu.VMEM((rows, columns), BF16),
            pltpu.SemaphoreType.DMA((5,)),
            pltpu.SemaphoreType.DMA((5,)),
        ],
        compiler_params=pltpu.CompilerParams(
            collective_id=SCATTER_ID, has_side_effects=True, vmem_limit_bytes=48 * 2**20
        ),
        name="scatter_rows",
    )(partial.astype(BF16).reshape(2, 2, rows, columns))


TILE = 128
LANES = 128
QUARTER = HD // 4
FIRST_ROWS = 80


class WeightImport:
    def __init__(self, blocks, base):
        self.blocks, self.base = blocks, base
        self.arrays = sorted({block[0] for block in blocks})

    def scratch(self):
        count = len(self.blocks)
        return [
            pltpu.SemaphoreType.DMA((4,)),
            pltpu.SemaphoreType.DMA((count, 7)),
            pltpu.SemaphoreType.DMA((count, 7)),
        ]

    def bind(self, ins, outs, scratch):
        self.ins, self.outs = ins, outs
        self.own_sem, self.send_sem, self.recv_sem = scratch
        item, column = lax.axis_index("dp"), lax.axis_index("seq")
        core, chip = lax.rem(column, 2), column // 2
        self.item, self.column = item, column
        self.y_bit, self.z_bit = lax.rem(item, 2), lax.rem(item // 2, 2)
        self.sibling = (item, column + 1 - 2 * core)
        self.y_near = (item + 1 - 2 * self.y_bit, column)
        self.z_near = (item + 2 - 4 * self.z_bit, column)
        self.far = [(1 - chip) * 2 + k for k in (core, 1 - core)]
        self.half_rows = ins[0].shape[0] // 2

    def partners(self):
        across = [(self.item, place) for place in self.far]
        return across + [self.sibling, self.y_near, self.z_near]

    def copy(self, source, target_ref, block, kind, target):
        return pltpu.make_async_remote_copy(
            src_ref=source,
            dst_ref=target_ref,
            send_sem=self.send_sem.at[block, kind],
            recv_sem=self.recv_sem.at[block, kind],
            device_id=target,
            device_id_type=MESH,
        )

    def piece(self, ref, block, y_pick, z_pick, first_row=0, rows=None, base=0):
        _, _, start, columns = self.blocks[block]
        rows = self.half_rows if rows is None else rows
        return ref.at[
            pl.ds(pl.multiple_of(z_pick * self.half_rows + first_row, 16), rows),
            pl.ds(pl.multiple_of(base + start + y_pick * columns, TILE), columns),
        ]

    def mine_for(self, array, place):
        ref = self.ins[array]
        if len(ref.shape) == 3:
            return ref.at[place], 0
        return ref, self.base if array == 0 else place * self.outs[array].shape[2]

    def whole(self, array, place):
        ref, base = self.mine_for(array, place)
        columns = self.outs[array].shape[2]
        if ref.shape[-1] == columns:
            return ref
        return ref.at[:, pl.ds(pl.multiple_of(base, TILE), columns)]

    def over(self, block):
        array, offset, _, _ = self.blocks[block]
        goal = self.far[offset or 0]
        ref, base = self.mine_for(array, goal)
        source = self.piece(ref, block, self.y_bit, self.z_bit, base=base)
        target = self.piece(self.outs[array].at[self.column], block, self.y_bit, self.z_bit)
        return self.copy(source, target, block, 0, (self.item, goal))

    def onward(self, block, kind):
        array, offset, _, _ = self.blocks[block]
        ref = self.outs[array].at[self.far[offset or 0]]
        if kind == 1:
            part, target = self.piece(ref, block, self.y_bit, self.z_bit), self.y_near
        elif kind == 2:
            part, target = self.piece(ref, block, self.y_bit, self.z_bit), self.z_near
        elif kind == 3:
            part = self.piece(ref, block, 1 - self.y_bit, self.z_bit, 0, FIRST_ROWS)
            target = self.z_near
        else:
            rest = self.half_rows - FIRST_ROWS
            part = self.piece(ref, block, self.y_bit, 1 - self.z_bit, FIRST_ROWS, rest)
            target = self.y_near
        return self.copy(part, part, block, kind, target)

    def share(self, block):
        _, _, start, columns = self.blocks[block]
        part = self.outs[0].at[self.far[0], :, pl.ds(start, 2 * columns)]
        return self.copy(part, part, block, 5, self.sibling)

    def beside(self, array):
        source = self.whole(array, self.sibling[1])
        index = self.arrays.index(array)
        return self.copy(source, self.outs[array].at[self.column], index, 6, self.sibling)

    def own(self, array):
        source = self.whole(array, self.column)
        return pltpu.make_async_copy(source, self.outs[array].at[self.column], self.own_sem.at[array])

    def steps(self):
        count = len(self.blocks)
        todo = []
        for step in range(count + 3):
            if step < count:
                todo.append(lambda step=step: self.arrive(step))
            if 0 <= step - 1 < count:
                todo.append(lambda step=step: self.pass_on(step - 1))
            if 0 <= step - 2 < count:
                todo.append(lambda step=step: self.complete(step - 2))
        return todo

    def arrive(self, step):
        self.over(step).wait_recv()
        self.onward(step, 1).start()
        self.onward(step, 2).start()

    def pass_on(self, step):
        self.onward(step, 1).wait_recv()
        self.onward(step, 3).start()
        self.onward(step, 2).wait_recv()
        self.onward(step, 4).start()

    def complete(self, step):
        self.onward(step, 3).wait_recv()
        self.onward(step, 4).wait_recv()
        if self.blocks[step][0] == 0:
            self.share(step).start()

    def end(self):
        for block in range(len(self.blocks)):
            self.over(block).wait_send()
            for kind in range(1, 5):
                self.onward(block, kind).wait_send()
            if self.blocks[block][0] == 0:
                self.share(block).wait_send()


class RowGather:
    def __init__(self, own, everyone, local_sem, send_sem, recv_sem):
        self.own, self.everyone = own, everyone
        self.local_sem, self.send_sem, self.recv_sem = local_sem, send_sem, recv_sem
        self.column = lax.axis_index("seq")
        self.far = lax.rem(self.column + 2, 4)
        self.sibling, self.across = group_partners()

    def remote(self, source, place, piece, kind, target):
        rows = self.own.shape[0] // GATHER_PIECES
        part = pl.ds(piece * rows, rows)
        return pltpu.make_async_remote_copy(
            src_ref=source.at[part],
            dst_ref=self.everyone.at[place, part],
            send_sem=self.send_sem.at[kind, piece],
            recv_sem=self.recv_sem.at[kind, piece],
            device_id=target,
            device_id_type=MESH,
        )

    def over(self, piece):
        return self.remote(self.own, self.column, piece, 0, self.across)

    def beside(self, piece):
        return self.remote(self.own, self.column, piece, 1, self.sibling)

    def onward(self, piece):
        return self.remote(self.everyone.at[self.far], self.far, piece, 2, self.sibling)

    def local(self):
        return pltpu.make_async_copy(self.own, self.everyone.at[self.column], self.local_sem)

    def start(self):
        for piece in range(GATHER_PIECES):
            self.over(piece).start()
        for piece in range(GATHER_PIECES):
            self.beside(piece).start()
        self.local().start()

    def pass_on(self):
        for piece in range(GATHER_PIECES):
            self.over(piece).wait_recv()
            self.onward(piece).start()

    def end(self):
        for piece in range(GATHER_PIECES):
            self.over(piece).wait_send()
            self.beside(piece).wait()
            self.onward(piece).wait()
        self.local().wait()

    @staticmethod
    def scratch():
        return [
            pltpu.SemaphoreType.DMA,
            pltpu.SemaphoreType.DMA((3, GATHER_PIECES)),
            pltpu.SemaphoreType.DMA((3, GATHER_PIECES)),
        ]


MOD_BLOCK = 2304


def first_import():
    wide = 3 * HEADS // 4 * LANES
    return WeightImport([(0, None, 0, MOD_BLOCK // 2), (1, 0, 0, wide // 2), (1, 1, 0, wide // 2)], 0)


def second_import(ff):
    blocks = [(0, None, 0, MOD_BLOCK // 2)]
    blocks += [(k, j, 0, ff // 2) for k in (2, 3) for j in (0, 1)]
    return WeightImport(blocks + [(0, None, MOD_BLOCK, MOD_BLOCK // 2)], MOD_BLOCK)


def spread_heads(w_ref, lanes_ref):
    rows = w_ref.shape[0]
    valid = lax.broadcasted_iota(jnp.int32, (rows, LANES), 1) < HD
    for head in range(3 * HEADS):
        kind, device, place = head // HEADS, head % HEADS // 4, head % 4
        start = head * HD // LANES * LANES
        stop = min(start + 2 * LANES, w_ref.shape[1])
        window = w_ref[:, start:stop].astype(F32)
        shift = head * HD - start
        if shift:
            window = pltpu.roll(window, window.shape[1] - shift, 1)
        target = (kind * 4 + place) * LANES
        lanes_ref[device, :, target : target + LANES] = jnp.where(
            valid, window[:, :LANES], 0.0
        ).astype(BF16)


def first_kernel(imports, *refs):
    (w_mod, w_qkv, condition, tokens, embed, bias, positions), refs = refs[:7], refs[7:]
    (mod_out, qkv_out, modulation_out, hidden_all, lifted, positions_all), refs = refs[:6], refs[6:]
    (mod_all, lanes, hidden, mod_sem, spot_send, spot_recv), refs = refs[:6], refs[6:]
    imports.bind({0: w_mod, 1: lanes}, {0: mod_all, 1: qkv_out}, refs[:3])
    gather = RowGather(hidden, hidden_all, *refs[3:6])
    item, column = lax.axis_index("dp"), lax.axis_index("seq")
    greet(imports.partners())
    imports.over(0).start()
    imports.own(0).start()
    imports.beside(0).start()
    peers = [(item, lax.rem(column + k, 4)) for k in range(1, 4)]
    spot_copies = [
        pltpu.make_async_remote_copy(
            src_ref=positions,
            dst_ref=positions_all.at[column],
            send_sem=spot_send.at[k],
            recv_sem=spot_recv.at[k],
            device_id=peer,
            device_id_type=MESH,
        )
        for k, peer in enumerate(peers)
    ]
    for copy in spot_copies:
        copy.start()
    positions_all[column] = positions[...]
    spread_heads(w_qkv, lanes)
    imports.over(1).start()
    imports.over(2).start()
    imports.own(1).start()
    imports.beside(1).start()
    values = condition[...].astype(F32) + embed[...]
    lifted[...] = (values * jax.nn.sigmoid(values)).astype(BF16)
    todo = imports.steps()
    for step in todo[:5]:
        step()
    imports.complete(0)
    imports.own(0).wait()
    imports.beside(0).wait_recv()
    imports.share(0).wait_recv()
    store = pltpu.make_async_copy(mod_all, mod_out, mod_sem)
    store.start()
    weights = mod_all[...].reshape(-1, mod_all.shape[2])
    modulation = jnp.dot(lifted[...], weights, preferred_element_type=F32)
    modulation = modulation + bias[:, : mod_all.shape[2]]
    modulation_out[...] = modulation
    width = tokens.shape[1]
    values = tokens[...].astype(F32)
    normed = values * inverse_rms(values)
    hidden[...] = (normed * (1.0 + modulation[:, width:]) + modulation[:, :width]).astype(BF16)
    gather.start()
    for step in todo[6:]:
        step()
    gather.pass_on()
    imports.end()
    imports.beside(0).wait_send()
    imports.beside(1).wait()
    imports.own(1).wait()
    gather.end()
    for copy in spot_copies:
        copy.wait()
    store.wait()


def first_stage(w_mod, w_qkv, condition, tokens, embed, bias, positions):
    rows, width = tokens.shape
    depth, lanes = w_mod.shape[0], 3 * HEADS // 4 * LANES
    imports = first_import()
    vmem, anywhere = pl.BlockSpec(memory_space=pltpu.VMEM), pl.BlockSpec(memory_space=pl.ANY)

    def kernel(*refs):
        first_kernel(imports, *refs)

    return pl.pallas_call(
        kernel,
        out_shape=[
            jax.ShapeDtypeStruct((4, depth, MOD_BLOCK), BF16),
            jax.ShapeDtypeStruct((4, depth, lanes), BF16),
            jax.ShapeDtypeStruct((rows, MOD_BLOCK), F32),
            jax.ShapeDtypeStruct((4, rows, width), BF16),
            jax.ShapeDtypeStruct((rows, width), BF16),
            jax.ShapeDtypeStruct((4,) + positions.shape, jnp.int32),
        ],
        in_specs=[anywhere] + [vmem] * 6,
        out_specs=[anywhere, anywhere] + [vmem] * 4,
        scratch_shapes=[
            pltpu.VMEM((4, depth, MOD_BLOCK), BF16),
            pltpu.VMEM((4, depth, lanes), BF16),
            pltpu.VMEM((rows, width), BF16),
            pltpu.SemaphoreType.DMA,
            pltpu.SemaphoreType.DMA((3,)),
            pltpu.SemaphoreType.DMA((3,)),
        ]
        + imports.scratch()
        + RowGather.scratch(),
        compiler_params=pltpu.CompilerParams(
            collective_id=WEIGHT_ID, has_side_effects=True, vmem_limit_bytes=60 * 2**20
        ),
        name="first_stage",
    )(w_mod, w_qkv, condition, tokens, embed, bias, positions)


def rotated(values, tables, sign):
    cosine, ahead, behind = tables
    turned = pltpu.roll(values, LANES - QUARTER, 1) * ahead + pltpu.roll(values, QUARTER, 1) * behind
    return values * cosine + turned if sign > 0 else values * cosine - turned


def lane_tables(positions):
    cosine, sine = rope_tables(positions, HD)
    cosine, sine = cosine[:, 0], sine[:, 0]
    takes_ahead = (jnp.arange(HD) // QUARTER % 2 == 0)[None, :]
    tables = (cosine, jnp.where(takes_ahead, -sine, 0.0), jnp.where(takes_ahead, 0.0, sine))
    return [jnp.pad(table, ((0, 0), (0, LANES - HD))) for table in tables]


def head_inverse(values):
    return lax.rsqrt(jnp.sum(values * values, axis=-1, keepdims=True) * (1.0 / HD) + EPSILON)


def over_rows(left, right):
    return lax.dot_general(left, right, (((1,), (1,)), ((), ())), preferred_element_type=F32)


def over_first(left, right):
    return lax.dot_general(left, right, (((0,), (0,)), ((), ())), preferred_element_type=F32)


class RowSums:
    def __init__(self, blocks, near, low, far, send_sem, recv_sem):
        column = lax.axis_index("seq")
        self.column = column
        self.core, self.chip = lax.rem(column, 2), column // 2
        self.sibling, self.across = group_partners()
        self.blocks, self.near, self.low, self.far = blocks, near, low, far
        self.send_sem, self.recv_sem = send_sem, recv_sem
        self.order = [
            (1 - self.chip) * 2 + 1 - self.core,
            (1 - self.chip) * 2 + self.core,
            self.chip * 2 + 1 - self.core,
            column,
        ]

    def copy(self, source, target_ref, index, target):
        return pltpu.make_async_remote_copy(
            src_ref=source,
            dst_ref=target_ref,
            send_sem=self.send_sem.at[index],
            recv_sem=self.recv_sem.at[index],
            device_id=target,
            device_id_type=MESH,
        )

    def beside(self, index):
        return self.copy(self.blocks.at[index], self.near.at[index], index, self.sibling)

    def over(self):
        return self.copy(self.low, self.far, 2, self.across)

    def put(self, index, values):
        if index == 0 or index == 2:
            self.blocks[index // 2] = values.astype(BF16)
            self.beside(index // 2).start()
        elif index == 1:
            self.beside(0).wait_recv()
            self.low[...] = (values + self.near[0].astype(F32)).astype(BF16)
            self.over().start()
        else:
            self.own = values

    def sums(self):
        self.beside(1).wait_recv()
        total = self.own + self.near[1].astype(F32)
        self.over().wait()
        total = total + self.far[...].astype(F32)
        self.beside(0).wait_send()
        self.beside(1).wait_send()
        return total

    @staticmethod
    def scratch(rows, columns):
        return [
            pltpu.VMEM((2, rows, columns), BF16),
            pltpu.VMEM((2, rows, columns), BF16),
            pltpu.VMEM((rows, columns), BF16),
            pltpu.VMEM((rows, columns), BF16),
            pltpu.SemaphoreType.DMA((3,)),
            pltpu.SemaphoreType.DMA((3,)),
        ]


def attend_kernel(imports, *refs):
    (hidden, w_qkv, w_out, cosine, ahead, behind, q_gain, k_gain), refs = refs[:8], refs[8:]
    (w_mod, w_gate, w_up, lifted, bias), refs = refs[:5], refs[5:]
    (heads_out, rows_out, attended_out, branch_out), refs = refs[:4], refs[4:]
    (mod_out, gate_out, up_out, modulation_out), refs = refs[:4], refs[4:]
    (mod_all, gate_own, up_own, mod_sem, load_sem), refs = refs[:5], refs[5:]
    sums = RowSums(*refs[:6])
    imports.bind({0: w_mod, 2: w_gate, 3: w_up}, {0: mod_all, 2: gate_out, 3: up_out}, refs[6:])
    greet(imports.partners())
    for block in range(len(imports.blocks)):
        imports.over(block).start()
    imports.own(0).start()
    loads = [
        pltpu.make_async_copy(imports.whole(k, sums.column), ref, load_sem.at[k - 2])
        for k, ref in ((2, gate_own), (3, up_own))
    ]
    stores = [
        pltpu.make_async_copy(ref, imports.outs[k].at[sums.column], load_sem.at[k])
        for k, ref in ((2, gate_own), (3, up_own))
    ]
    for copy in loads:
        copy.start()
    for array in imports.arrays:
        imports.beside(array).start()
    todo = imports.steps()

    def aside(number):
        for _ in range(min(number, len(todo))):
            todo.pop(0)()

    factor = HD ** (-0.5)
    rows = branch_out.shape[0]
    heads = attended_out.shape[1] // LANES
    tables = cosine[...], ahead[...], behind[...]
    for pair in range(3 * heads // 2):
        span = slice(pair * 2 * LANES, (pair + 1) * 2 * LANES)
        projected = jnp.dot(hidden[...], w_qkv[:, span], preferred_element_type=F32)
        if pair >= heads:
            rows_out[:, span] = projected.astype(BF16)
            continue
        heads_out[:, span] = projected
        gain = (q_gain if pair < heads // 2 else k_gain)[...]
        for half in range(2):
            values = projected[:, half * LANES : (half + 1) * LANES]
            values = values * head_inverse(values) * gain
            start = pair * 2 * LANES + half * LANES
            rows_out[:, start : start + LANES] = rotated(values, tables, 1).astype(BF16)
        if pair == heads - 1:
            aside(1)
    aside(1)
    for copy in loads:
        copy.wait()
    for copy in stores:
        copy.start()
    for index in range(4):
        block = pl.ds(pl.multiple_of(sums.order[index] * rows, rows), rows)
        for head in range(heads):
            spans = [slice((k * heads + head) * LANES, (k * heads + head + 1) * LANES) for k in range(3)]
            exp_scores = jnp.exp(over_rows(rows_out[block, spans[0]], rows_out[:, spans[1]]) * factor)
            scale = 1.0 / jnp.sum(exp_scores, axis=1, keepdims=True)
            mixed = jnp.dot(
                (exp_scores * scale).astype(BF16),
                rows_out[:, spans[2]],
                preferred_element_type=F32,
            )
            attended_out[block, spans[0]] = mixed.astype(BF16)
            aside(1)
        sums.put(index, jnp.dot(attended_out[block, :], w_out[...], preferred_element_type=F32))
    aside(6)
    imports.own(0).wait()
    imports.beside(0).wait_recv()
    arrays = [block[0] for block in imports.blocks]
    mod_blocks = [index for index, array in enumerate(arrays) if array == 0]

    def modulate(number):
        imports.share(mod_blocks[number]).wait_recv()
        span = slice(number * MOD_BLOCK, (number + 1) * MOD_BLOCK)
        weights = mod_all[:, :, span].reshape(-1, MOD_BLOCK)
        modulation = jnp.dot(lifted[...], weights, preferred_element_type=F32)
        start = imports.base + number * MOD_BLOCK
        modulation_out[:, span] = modulation + bias[:, start : start + MOD_BLOCK]

    modulate(0)
    aside(len(todo))
    branch_out[...] = sums.sums()
    modulate(1)
    store = pltpu.make_async_copy(mod_all, mod_out, mod_sem)
    store.start()
    imports.end()
    imports.beside(0).wait_send()
    for array in imports.arrays[1:]:
        imports.beside(array).wait()
    for copy in stores:
        copy.wait()
    store.wait()


def attend(hidden, w_qkv, w_out, tables, q_gain, k_gain, w_mod, w_gate, w_up, lifted, bias):
    patches, wide = hidden.shape[0], w_qkv.shape[1]
    rows, width = patches // 4, hidden.shape[1]
    depth, ff = w_mod.shape[0], w_gate.shape[1] // 4
    rest = w_mod.shape[1] - MOD_BLOCK
    imports = second_import(ff)
    vmem, anywhere = pl.BlockSpec(memory_space=pltpu.VMEM), pl.BlockSpec(memory_space=pl.ANY)

    def kernel(*refs):
        attend_kernel(imports, *refs)

    return pl.pallas_call(
        kernel,
        out_shape=[
            jax.ShapeDtypeStruct((patches, wide * 2 // 3), F32),
            jax.ShapeDtypeStruct((patches, wide), BF16),
            jax.ShapeDtypeStruct((patches, wide // 3), BF16),
            jax.ShapeDtypeStruct((rows, width), F32),
            jax.ShapeDtypeStruct((4, depth, rest), BF16),
            jax.ShapeDtypeStruct((4, depth, ff), BF16),
            jax.ShapeDtypeStruct((4, depth, ff), BF16),
            jax.ShapeDtypeStruct((rows, rest), F32),
        ],
        in_specs=[vmem] * 8 + [anywhere] * 3 + [vmem] * 2,
        out_specs=[vmem] * 4 + [anywhere] * 3 + [vmem],
        scratch_shapes=[
            pltpu.VMEM((4, depth, rest), BF16),
            pltpu.VMEM((depth, ff), BF16),
            pltpu.VMEM((depth, ff), BF16),
            pltpu.SemaphoreType.DMA,
            pltpu.SemaphoreType.DMA((4,)),
        ]
        + RowSums.scratch(rows, width)
        + imports.scratch(),
        compiler_params=pltpu.CompilerParams(
            collective_id=ATTEND_ID, has_side_effects=True, vmem_limit_bytes=63 * 2**20
        ),
        name="attend",
    )(hidden, w_qkv, w_out, *tables, q_gain, k_gain, w_mod, w_gate, w_up, lifted, bias)


def rows_to_columns(values, blocks):
    rows, columns = values.shape
    ways = lax.axis_size("seq")
    values = values.reshape(rows, blocks, ways, columns // (blocks * ways))
    moved = lax.all_to_all(values, "seq", split_axis=2, concat_axis=0, tiled=True)
    return moved.reshape(rows * ways, columns // ways)


def columns_to_rows(values, blocks):
    rows, columns = values.shape
    ways = lax.axis_size("seq")
    values = values.reshape(rows, blocks, 1, columns // blocks)
    moved = lax.all_to_all(values, "seq", split_axis=0, concat_axis=2, tiled=True)
    return moved.reshape(rows // ways, columns * ways)


def first_tile(place, tiles):
    return (tiles * place) // 4


def padded_rows(rows):
    return -(-rows // 16) * 16


class Part:
    def __init__(self, left, right, rows, span, out, order, by_rows=False, in_lanes=False, bias=False):
        self.left, self.right, self.rows = left, right, rows
        self.start, self.columns, self.out = span[0], span[1] - span[0], out
        self.order, self.by_rows, self.in_lanes, self.bias = order, by_rows, in_lanes, bias
        self.slab = padded_rows(rows)


def split_part(left, right, rows, columns, out, order, **kinds):
    middle = -(-columns // (2 * TILE)) * TILE
    return [
        Part(left, right, rows, span, out, order, **kinds)
        for span in ((0, middle), (middle, columns))
    ]


class GradSums:
    def __init__(self, parts, names, shared_shapes, small_shape):
        self.parts, self.names = parts, names
        self.shared_shapes, self.small_shape = shared_shapes, small_shape
        self.has_rows = any(part.by_rows for part in parts)

    def spread(self, group):
        rows, columns, whole = self.shared_shapes[group]
        return rows, columns if whole else -(-columns // (4 * TILE)) * TILE

    def scratch(self, array_shapes):
        parts, count, groups = self.parts, len(self.parts), len(self.shared_shapes)
        shapes = [pltpu.VMEM(shape, BF16) for shape in array_shapes]
        shapes += [pltpu.VMEM((4,) + self.spread(group), BF16) for group in range(groups)]
        for lead in ((2, 2, 2), (2, 2), (2,), ()):
            shapes += [pltpu.VMEM(lead + (part.slab, part.columns), BF16) for part in parts]
        for _ in range(2):
            for part in parts:
                if part.by_rows:
                    shapes.append(pltpu.VMEM((part.slab, part.columns), BF16))
                else:
                    shapes.append(pltpu.VMEM((4, padded_rows(part.rows // 4), part.columns), BF16))
        widest = max(part.columns for part in parts)
        tallest = max(4 * LANES if part.in_lanes else part.rows for part in parts)
        return shapes + [
            pltpu.VMEM((tallest, widest), F32),
            pltpu.VMEM((4,) + self.small_shape, F32),
            pltpu.VMEM((3,) + self.small_shape, F32),
            pltpu.SemaphoreType.DMA((len(self.names),)),
            pltpu.SemaphoreType.DMA((groups, 3)),
            pltpu.SemaphoreType.DMA((groups, 3)),
            pltpu.SemaphoreType.DMA((groups,)),
            pltpu.SemaphoreType.DMA((count, 3)),
            pltpu.SemaphoreType.DMA((count, 3)),
            pltpu.SemaphoreType.DMA((count, 3)),
            pltpu.SemaphoreType.DMA((count, 3)),
            pltpu.SemaphoreType.DMA((6,)),
            pltpu.SemaphoreType.DMA((6,)),
        ]

    def bind(self, ins, shared, small_in, outs, small_out, scratch):
        count, groups, names = len(self.parts), len(self.shared_shapes), self.names
        refs = list(scratch)

        def take(number):
            taken = refs[:number]
            del refs[:number]
            return taken

        self.shared, self.small_in, self.outs, self.small_out = shared, small_in, outs, small_out
        self.held = dict(zip(names, take(len(names)), strict=True))
        self.gathered = take(groups)
        self.own, self.first_in = take(count), take(count)
        self.second_in, self.third_in = take(count), take(count)
        self.slabs, self.slab_in = take(count), take(count)
        self.total, self.small, self.small_came = take(3)
        load_sem, self.share_send, self.share_recv, own_sem, self.send_sem, self.recv_sem = take(6)
        self.last_send, self.last_recv, self.small_send, self.small_recv = take(4)
        item, column = lax.axis_index("dp"), lax.axis_index("seq")
        self.column = column
        self.bits = [lax.rem(item, 2), lax.rem(item // 2, 2), item // 4]
        self.partners = [(item + (1 - 2 * self.bits[k]) * (1 << k), column) for k in range(3)]
        self.peers = [(item, lax.rem(column + k, 4)) for k in range(1, 4)]
        self.owner = (2 * column + item // 4, lax.rem(item, 4))
        self.feeder = (4 * lax.rem(item, 2) + column, item // 2)
        self.elsewhere = jnp.logical_or(self.owner[0] != item, self.owner[1] != column)
        self.loads = {
            name: pltpu.make_async_copy(ins[i], self.held[name], load_sem.at[i])
            for i, name in enumerate(names)
        }
        self.own_shares = [
            pltpu.make_async_copy(
                self.columns_of(g, column), self.gathered[g].at[column], own_sem.at[g]
            )
            for g in range(groups)
        ]
        self.ready = set()
        self.others = {}

    def greet(self):
        barrier = pltpu.get_barrier_semaphore()
        for partner in self.partners + self.peers:
            pl.semaphore_signal(barrier, inc=1, device_id=partner, device_id_type=MESH)
        waits = 6
        if self.has_rows:
            waits = 6 + self.elsewhere.astype(jnp.int32)

            @pl.when(self.elsewhere)
            def _():
                pl.semaphore_signal(barrier, inc=1, device_id=self.feeder, device_id_type=MESH)

        pl.semaphore_wait(barrier, waits)

    def load(self):
        for name in self.names:
            self.loads[name].start()

    def remote(self, source, target_ref, send, recv, target):
        return pltpu.make_async_remote_copy(
            src_ref=source,
            dst_ref=target_ref,
            send_sem=send,
            recv_sem=recv,
            device_id=target,
            device_id_type=MESH,
        )

    def columns_of(self, group, place):
        wide, narrow = self.shared_shapes[group][1], self.spread(group)[1]
        if wide == narrow:
            return self.shared[group]
        start = first_tile(place, wide // TILE) * TILE
        return self.shared[group].at[:, pl.ds(pl.multiple_of(start, TILE), narrow)]

    def shares(self, group):
        return [
            self.remote(
                self.columns_of(group, peer[1]),
                self.gathered[group].at[self.column],
                self.share_send.at[group, k],
                self.share_recv.at[group, k],
                peer,
            )
            for k, peer in enumerate(self.peers)
        ]

    def share(self):
        for group in range(len(self.shared_shapes)):
            self.own_shares[group].start()
            for copy in self.shares(group):
                copy.start()

    def operand(self, name):
        if isinstance(name, int):
            if name not in self.ready:
                self.own_shares[name].wait()
                for copy in self.shares(name):
                    copy.wait()
            self.ready.add(name)
            ref = self.gathered[name]
            return ref[...].reshape(4 * ref.shape[1], ref.shape[2])
        first = name not in self.ready
        self.ready.add(name)
        if name in self.others:
            ref, wait = self.others[name]
            if first:
                wait()
            return ref[...].reshape(4 * ref.shape[1], ref.shape[2])
        if first:
            self.loads[name].wait()
        return self.held[name][...]

    def multiply(self, index):
        part = self.parts[index]
        left, right = self.operand(part.left), self.operand(part.right)
        right = right[:, part.start : part.start + part.columns]
        if part.bias:
            sums = jnp.sum(right.astype(F32), axis=0, keepdims=True)
            for tile in range(part.columns // TILE):
                row = part.start // TILE + tile
                self.small[0, row : row + 1] = sums[:, tile * TILE : (tile + 1) * TILE]
        own, rows = self.own[index], part.rows
        if part.in_lanes:
            self.total[: left.shape[1], : part.columns] = over_first(left, right)
            for d in range(8):
                start = d // 2 * LANES + d % 2 * rows
                own[d // 4, d // 2 % 2, d % 2] = self.cut(start, rows, part.slab, part.columns)
            return
        step = 3 * TILE
        for start in range(0, left.shape[1], step):
            product = over_first(left[:, start : start + step], right).astype(BF16)
            for d in range(8):
                low, high = max(start, d * rows), min(start + step, (d + 1) * rows)
                if low < high:
                    place = slice(low - d * rows, high - d * rows)
                    own[d // 4, d // 2 % 2, d % 2, place] = product[low - start : high - start]

    def cut(self, start, rows, padded, columns):
        values = self.total[start : start + rows, :columns]
        if padded > rows:
            values = jnp.concatenate([values, jnp.zeros((padded - rows, columns), F32)], axis=0)
        return values.astype(BF16)

    def place(self, index, high, low):
        if self.parts[index].order == 0:
            return (high, low, self.bits[0])
        return (high, self.bits[1], low)

    def stage(self, index, step):
        order = self.parts[index].order
        other = 1 - order
        sems = self.send_sem.at[index, step], self.recv_sem.at[index, step]
        own = self.own[index]
        if step == 0:
            pick = 1 - self.bits[order]
            half = (slice(None), slice(None), pick) if order == 0 else (slice(None), pick)
            return self.remote(own.at[half], self.first_in[index], *sems, self.partners[order])
        if step == 1:
            place = self.place(index, slice(None), 1 - self.bits[other])
            return self.remote(own.at[place], self.second_in[index], *sems, self.partners[other])
        place = self.place(index, 1 - self.bits[2], self.bits[other])
        return self.remote(own.at[place], self.third_in[index], *sems, self.partners[2])

    def begin(self, index):
        self.multiply(index)
        self.stage(index, 0).start()

    def end_first(self, index):
        self.stage(index, 0).wait()
        for high in range(2):
            for low in range(2):
                place = self.place(index, high, low)
                came = self.first_in[index][high, low].astype(F32)
                self.own[index][place] = (self.own[index][place].astype(F32) + came).astype(BF16)
        self.stage(index, 1).start()

    def end_second(self, index):
        self.stage(index, 1).wait()
        for high in range(2):
            place = self.place(index, high, self.bits[1 - self.parts[index].order])
            came = self.second_in[index][high].astype(F32)
            self.own[index][place] = (self.own[index][place].astype(F32) + came).astype(BF16)
        self.stage(index, 2).start()

    def last(self, index):
        if self.parts[index].by_rows:
            sems = self.last_send.at[index, 0], self.last_recv.at[index, 0]
            return [self.remote(self.slabs[index], self.slab_in[index], *sems, self.owner)]
        return [
            self.remote(
                self.slabs[index].at[peer[1]],
                self.slab_in[index].at[self.column],
                self.last_send.at[index, k],
                self.last_recv.at[index, k],
                peer,
            )
            for k, peer in enumerate(self.peers)
        ]

    def end_third(self, index):
        part = self.parts[index]
        self.stage(index, 2).wait()
        place = self.place(index, self.bits[2], self.bits[1 - part.order])
        sums = self.own[index][place].astype(F32) + self.third_in[index][...].astype(F32)
        if part.by_rows:
            self.slabs[index][...] = sums.astype(BF16)

            @pl.when(self.elsewhere)
            def _():
                self.last(index)[0].start()

            @pl.when(jnp.logical_not(self.elsewhere))
            def _():
                self.slab_in[index][...] = self.slabs[index][...]

            return
        self.total[: part.rows, : part.columns] = sums
        rows = part.rows // 4
        for k in range(4):
            self.slabs[index][k] = self.cut(k * rows, rows, padded_rows(rows), part.columns)
        for copy in self.last(index):
            copy.start()
        self.slab_in[index][self.column] = self.slabs[index][self.column]

    def end_last(self, index):
        part = self.parts[index]
        out, stop = self.outs[part.out], part.start + part.columns
        if part.by_rows:

            @pl.when(self.elsewhere)
            def _():
                self.last(index)[0].wait()

            out[:, part.start : stop] = self.slab_in[index][...].astype(F32)[: part.rows]
            return
        for copy in self.last(index):
            copy.wait()
        rows = part.rows // 4
        wide = out.shape[-1]
        for k in range(4):
            values = self.slab_in[index][k].astype(F32)[:rows]
            if len(out.shape) == 3:
                out[k, :, part.start : stop] = values
            else:
                start = first_tile(k, wide // TILE) * TILE
                out[:, start + part.start : start + stop] = values

    def small_step(self, step):
        if step < 3:
            sems = self.small_send.at[step], self.small_recv.at[step]
            return [
                self.remote(self.small.at[step], self.small_came.at[step], *sems, self.partners[step])
            ]
        return [
            self.remote(
                self.small.at[3],
                self.small_out.at[self.column],
                self.small_send.at[3 + k],
                self.small_recv.at[3 + k],
                peer,
            )
            for k, peer in enumerate(self.peers)
        ]

    def end_small(self, at):
        self.small_step(at - 1)[0].wait()
        self.small[at] = self.small[at - 1] + self.small_came[at - 1]
        for copy in self.small_step(at):
            copy.start()

    def steps(self, ahead=2):
        count = len(self.parts)
        todo = [lambda: self.small.__setitem__(0, self.small_in[...])]
        todo += [lambda index=index: self.begin(index) for index in range(min(ahead, count))]
        for step in range(count + 3):
            if step < count:
                todo.append(lambda step=step: self.end_first(step))
                if step + ahead < count:
                    todo.append(lambda step=step: self.begin(step + ahead))
            if 0 <= step - 1 < count:
                todo.append(lambda step=step: self.end_second(step - 1))
            if 0 <= step - 2 < count:
                todo.append(lambda step=step: self.end_third(step - 2))
            if 0 <= step - 3 < count:
                todo.append(lambda step=step: self.end_last(step - 3))
            at = step - max(count - ahead, 0)
            if at == 0:
                todo.append(lambda: self.small_step(0)[0].start())
            if 1 <= at <= 3:
                todo.append(lambda at=at: self.end_small(at))
        todo.append(self.end)
        return todo

    def end(self):
        self.small_out[self.column] = self.small[3]
        for copy in self.small_step(3):
            copy.wait()


def split(refs, *counts):
    groups, start = [], 0
    for number in counts:
        groups.append(refs[start : start + number])
        start += number
    return groups + [refs[start:]]


def weight_grads(parts, arrays, shared, small, out_shapes):
    names = tuple(arrays)
    sums = GradSums(parts, names, [value.shape + (whole,) for value, whole in shared], small.shape)
    count = len(out_shapes)

    def kernel(*refs):
        ins, given, (small_in,), outs, (small_out,), scratch = split(
            refs, len(names), len(shared), 1, count, 1
        )
        sums.bind(ins, given, small_in, outs, small_out, scratch)
        sums.load()
        sums.greet()
        sums.share()
        for step in sums.steps(ahead=3):
            step()

    return pl.pallas_call(
        kernel,
        out_shape=[jax.ShapeDtypeStruct(shape, F32) for shape in out_shapes]
        + [jax.ShapeDtypeStruct((4,) + small.shape, F32)],
        in_specs=[pl.BlockSpec(memory_space=pl.ANY)] * (len(names) + len(shared))
        + [pl.BlockSpec(memory_space=pltpu.VMEM)],
        out_specs=[pl.BlockSpec(memory_space=pltpu.VMEM)] * (count + 1),
        scratch_shapes=sums.scratch([value.shape for value in arrays.values()]),
        compiler_params=pltpu.CompilerParams(
            collective_id=SUM_ID, has_side_effects=True, vmem_limit_bytes=63 * 2**20
        ),
        name="weight_grads",
    )(*arrays.values(), *[value for value, _ in shared], small)


BACK_INPUTS = ("rows", "heads", "w_qkv", "w_out", "cosine", "ahead", "behind", "q_gain", "k_gain")


def back_kernel(sums, grad_in, lifted, given, lifted_all, project_out, hidden_out, gains_out, refs):
    branch_in, loads_into, pieces, scratch = split(refs, 1, 4, 1)
    (branch_all,), (rows, heads, w_qkv, w_out), (grad_heads,) = branch_in, loads_into, pieces
    load_sem = scratch[0]
    gather, gather_lifted = RowGather(grad_in, branch_all, *scratch[1:4]), RowGather(lifted, lifted_all, *scratch[4:7])
    row_sums = RowSums(*scratch[7:])
    cosine, ahead, behind, q_gain, k_gain = given[4:]
    local_rows = grad_in.shape[0]
    count = grad_heads.shape[1] // LANES
    factor = HD ** (-0.5)
    loads = [
        pltpu.make_async_copy(source, target, load_sem.at[k])
        for k, (source, target) in enumerate(zip(given[:4], (rows, heads, w_qkv, w_out), strict=True))
    ]
    for k in (3, 0, 1, 2):
        loads[k].start()
    sums.load()
    sums.greet()

    gather.start()
    gather_lifted.start()
    sums.share()

    def lifted_ready():
        gather_lifted.pass_on()
        gather_lifted.end()

    sums.others["lifted"] = (lifted_all, lifted_ready)
    todo = sums.steps(ahead=3)

    def aside(number):
        for _ in range(min(number, len(todo))):
            todo.pop(0)()

    aside(4)
    gather.pass_on()
    gather.end()
    loads[3].wait()
    grad_branch = branch_all[...].reshape(4 * local_rows, branch_all.shape[2])
    grad_heads[...] = over_rows(grad_branch, w_out[...]).astype(BF16)
    loads[0].wait()
    loads[1].wait()
    tables = cosine[...], ahead[...], behind[...]
    block = 256
    gain_sums = [jnp.zeros((1, LANES), F32), jnp.zeros((1, LANES), F32)]
    counts = (1, 3, 3, 3)
    for head in range(count):
        spans = [slice((k * count + head) * LANES, (k * count + head + 1) * LANES) for k in range(3)]
        keys, values = rows[:, spans[1]], rows[:, spans[2]]
        grad_query, grad_key, grad_value = [], None, None
        for start in range(0, rows.shape[0], block):
            queries = rows[start : start + block, spans[0]]
            grads = grad_heads[start : start + block, spans[0]]
            exp_scores = jnp.exp(over_rows(keys, queries) * factor)
            probs = exp_scores * (1.0 / jnp.sum(exp_scores, axis=0, keepdims=True))
            grad_probs = over_rows(values, grads)
            inner = jnp.sum(probs * grad_probs, axis=0, keepdims=True)
            grad_scores = (probs * (grad_probs - inner)).astype(BF16)
            grad_query.append(over_first(grad_scores, keys))
            key_term = jnp.dot(grad_scores, queries, preferred_element_type=F32)
            value_term = jnp.dot(probs.astype(BF16), grads, preferred_element_type=F32)
            grad_key = key_term if grad_key is None else grad_key + key_term
            grad_value = value_term if grad_value is None else grad_value + value_term
        project_out[:, spans[2]] = grad_value.astype(BF16)
        terms = (jnp.concatenate(grad_query, axis=0) * factor, grad_key * factor)
        for k, (term, gain) in enumerate(zip(terms, (q_gain, k_gain), strict=True)):
            raw = heads[:, spans[k]]
            inverse = head_inverse(raw)
            normed = raw * inverse
            back = rotated(term, tables, -1)
            gain_sums[k] = gain_sums[k] + jnp.sum(back * normed, axis=0, keepdims=True)
            back = back * gain[...]
            mean = jnp.sum(back * normed, axis=-1, keepdims=True) * (1.0 / HD)
            project_out[:, spans[k]] = (inverse * (back - normed * mean)).astype(BF16)
        aside(counts[head])
    gains_out[...] = jnp.concatenate(gain_sums + [jnp.zeros((6, LANES), F32)], axis=0)
    loads[2].wait()
    for index in range(4):
        part = pl.ds(pl.multiple_of(row_sums.order[index] * local_rows, local_rows), local_rows)
        row_sums.put(index, over_rows(project_out[part, :], w_qkv[...]))
        if index == 1:
            aside(1)
    aside(3)
    hidden_out[...] = row_sums.sums()
    aside(len(todo))


def attention_back(grad_in, lifted, given, parts, arrays, shared, small, out_shapes):
    names = tuple(arrays)
    sums = GradSums(parts, names, [value.shape + (whole,) for value, whole in shared], small.shape)
    count = len(out_shapes)
    rows, width = grad_in.shape
    kept, heads, w_qkv, w_out = given[:4]
    vmem, anywhere = pl.BlockSpec(memory_space=pltpu.VMEM), pl.BlockSpec(memory_space=pl.ANY)

    def kernel(*refs):
        ins, exchanged, (small_in, grad, low), held, outs, (small_out, low_all), results, refs = split(
            refs, len(names), len(shared), 3, len(given), count, 2, 4
        )
        own, scratch = split(refs, OWN_SCRATCH)
        sums.bind(ins, exchanged, small_in, outs, small_out, scratch)
        branch_all, project, hidden, gains = results
        back_kernel(sums, grad, low, held, low_all, project, hidden, gains, [branch_all] + list(own))

    own_scratch = [
        pltpu.VMEM(kept.shape, BF16),
        pltpu.VMEM(heads.shape, F32),
        pltpu.VMEM(w_qkv.shape, BF16),
        pltpu.VMEM(w_out.shape, BF16),
        pltpu.VMEM((4 * rows, w_out.shape[0]), BF16),
        pltpu.SemaphoreType.DMA((4,)),
        *RowGather.scratch(),
        *RowGather.scratch(),
    ] + RowSums.scratch(rows, width)
    return pl.pallas_call(
        kernel,
        out_shape=[jax.ShapeDtypeStruct(shape, F32) for shape in out_shapes]
        + [
            jax.ShapeDtypeStruct((4,) + small.shape, F32),
            jax.ShapeDtypeStruct((4, rows, width), BF16),
            jax.ShapeDtypeStruct((4, rows, width), BF16),
            jax.ShapeDtypeStruct(kept.shape, BF16),
            jax.ShapeDtypeStruct((rows, width), F32),
            jax.ShapeDtypeStruct((8, LANES), F32),
        ],
        in_specs=[anywhere] * (len(names) + len(shared)) + [vmem] * 3 + [anywhere] * 4 + [vmem] * 5,
        out_specs=[vmem] * (count + 6),
        scratch_shapes=own_scratch + sums.scratch([value.shape for value in arrays.values()]),
        compiler_params=pltpu.CompilerParams(
            collective_id=BACK_ID, has_side_effects=True, vmem_limit_bytes=63 * 2**20
        ),
        name="attention_back",
    )(*arrays.values(), *[value for value, _ in shared], small, grad_in, lifted, *given)


OWN_SCRATCH = 18


def to_owners(rows):
    n_dp, n_seq = lax.axis_size("dp"), lax.axis_size("seq")
    pairs = []
    for d in range(n_dp):
        for s in range(n_seq):
            pairs.append((d * n_seq + s, s * n_dp + d))
    return lax.ppermute(rows, ("dp", "seq"), pairs)


def plain_sums(left, right, blocks):
    mine = lax.psum_scatter(outer_sum(left, right).astype(BF16), "dp", scatter_dimension=0, tiled=True)
    return (columns_to_rows(mine, blocks) if blocks else to_owners(mine)).astype(F32)


def padded_small(values):
    values = jnp.pad(values, ((0, 8 - values.shape[0]), (0, TILE - values.shape[1])))
    return jnp.concatenate([jnp.zeros((8, TILE), F32), values])


def bias_columns(small, tiles):
    edges = [first_tile(k, tiles) for k in range(4)] + [tiles]
    sums = small[:, :8].reshape(4, 8 * TILE)
    return [sums[k, : (edges[k + 1] - edges[k]) * TILE] for k in range(4)]


def in_lanes(values, axis):
    shape = values.shape
    values = values.reshape(shape[:axis] + (shape[axis] // HD, HD) + shape[axis + 1 :])
    pads = [(0, 0)] * len(values.shape)
    pads[axis + 1] = (0, LANES - HD)
    return jnp.pad(values, pads).reshape(shape[:axis] + (-1,) + shape[axis + 1 :])


def out_of_lanes(values):
    return values.reshape(values.shape[0], -1, LANES)[:, :, :HD]


def plain_back(grad_branch_a, given):
    kept, projected, w_qkv, w_out, cosine, ahead, behind, q_gain, k_gain = given
    patches, count = kept.shape[0], w_out.shape[0] // LANES
    factor = HD ** (-0.5)
    tables = [table[:, None, :] for table in (cosine, ahead, behind)]

    def turn(values):
        turned = jnp.roll(values, -QUARTER, -1) * tables[1] + jnp.roll(values, QUARTER, -1) * tables[2]
        return values * tables[0] - turned

    query, key, value = jnp.split(kept.reshape(patches, 3 * count, LANES), 3, axis=1)
    grads = times_transpose(grad_branch_a, w_out).astype(BF16).reshape(patches, count, LANES)
    scores = jnp.einsum("qhd,khd->hqk", query, key, preferred_element_type=F32) * factor
    exp_scores = jnp.exp(scores)
    probs = exp_scores / jnp.sum(exp_scores, axis=-1, keepdims=True)
    grad_probs = jnp.einsum("qhd,khd->hqk", grads, value, preferred_element_type=F32)
    inner = jnp.sum(probs * grad_probs, axis=-1, keepdims=True)
    grad_scores = (probs * (grad_probs - inner)).astype(BF16)
    terms = (
        jnp.einsum("hqk,khd->qhd", grad_scores, key, preferred_element_type=F32) * factor,
        jnp.einsum("hqk,qhd->khd", grad_scores, query, preferred_element_type=F32) * factor,
    )
    grad_value = jnp.einsum("hqk,qhd->khd", probs.astype(BF16), grads, preferred_element_type=F32)
    raws = jnp.split(projected.reshape(patches, 2 * count, LANES), 2, axis=1)
    results, gains = [], []
    for term, raw, gain in zip(terms, raws, (q_gain, k_gain), strict=True):
        inverse = head_inverse(raw)
        normed = raw * inverse
        back = turn(term)
        gains.append(jnp.sum(back * normed, axis=(0, 1)))
        back = back * gain[0]
        mean = jnp.sum(back * normed, axis=-1, keepdims=True) * (1.0 / HD)
        results.append(inverse * (back - normed * mean))
    grad_lanes = jnp.concatenate(results + [grad_value], axis=1).reshape(kept.shape).astype(BF16)
    return grad_lanes, times_transpose(grad_lanes, w_qkv), jnp.stack(gains)


def shards(
    tokens,
    condition,
    cotangent,
    w_qkv,
    w_out,
    w_gate,
    w_up,
    w_down,
    w_mod,
    b_mod,
    q_gain,
    k_gain,
    noise_counts,
    time_steps,
    positions,
):
    local_rows, width = tokens.shape[1:]
    ways = lax.axis_size("seq")
    patches = local_rows * ways
    local_heads = HEADS // ways
    item = lax.axis_index("dp")
    running = jnp.cumsum(noise_counts)
    image_id = jnp.sum((running <= item).astype(jnp.int32))
    chosen = jnp.arange(noise_counts.shape[0], dtype=jnp.int32) == image_id
    share = 1.0 / jnp.sum(jnp.where(chosen, noise_counts, 0)).astype(F32)

    embed = time_embed(time_steps, width)
    condition_in = condition[0].astype(F32) + embed
    bias_row = b_mod[None]
    mod_first, w_qkv_lanes, modulation_first, hidden_a, lifted_low, all_positions = first_stage(
        w_mod, w_qkv, condition[0], tokens[0], embed, bias_row, positions[:, 0]
    )
    shift_a, scale_a = jnp.split(modulation_first, 2, axis=-1)
    hidden_a = hidden_a.reshape(patches, width)
    w_qkv_lanes = w_qkv_lanes.reshape(width, w_qkv_lanes.shape[2])
    tables = lane_tables(jnp.transpose(all_positions, (1, 0, 2)).reshape(2, patches))
    w_out_lanes = in_lanes(w_out, 0)
    gain_lanes = [jnp.pad(gain, (0, LANES - HD))[None] for gain in (q_gain, k_gain)]
    (
        projected_lanes,
        rows_lanes,
        attended_lanes,
        branch_a,
        mod_rest,
        gate_cols,
        up_cols,
        modulation_rest,
    ) = attend(
        hidden_a, w_qkv_lanes, w_out_lanes, tables, *gain_lanes, w_mod, w_gate, w_up, lifted_low, bias_row
    )
    gate_a, shift_b, scale_b, gate_b = jnp.split(modulation_rest, 4, axis=-1)
    mod_first, mod_rest = mod_first.reshape(width, -1), mod_rest.reshape(width, -1)
    gate_cols, up_cols = gate_cols.reshape(width, -1), up_cols.reshape(width, -1)
    tokens_f = tokens[0].astype(F32)
    inverse_a = inverse_rms(tokens_f)
    normed_a = tokens_f * inverse_a
    grad_out = cotangent[0].astype(F32) * share
    grad_branch_b = gather_rows((grad_out * gate_b).astype(BF16))

    middle = tokens_f + gate_a * branch_a
    inverse_b = inverse_rms(middle)
    normed_b = middle * inverse_b
    hidden_b = gather_rows((normed_b * (1.0 + scale_b) + shift_b).astype(BF16))
    gate_in = matmul(hidden_b, gate_cols)
    up_in = matmul(hidden_b, up_cols)
    activated = jax.nn.silu(gate_in)
    inner = (activated * up_in).astype(BF16)
    branch_b = scatter_rows(matmul(inner, w_down))
    block_out = (middle + gate_b * branch_b).astype(BF16)

    grad_gate_b = grad_out * branch_b
    grad_inner = times_transpose(grad_branch_b, w_down)
    grad_gate_in = (grad_inner * up_in * silu_slope(gate_in)).astype(BF16)
    grad_up_in = (grad_inner * activated).astype(BF16)
    grad_hidden_b = scatter_rows(
        times_transpose(grad_gate_in, gate_cols) + times_transpose(grad_up_in, up_cols)
    )
    grad_middle = grad_out + rms_back(grad_hidden_b * (1.0 + scale_b), normed_b, inverse_b)
    grad_gate_a = grad_middle * branch_a
    own_branch_a = (grad_middle * gate_a).astype(BF16)
    grad_mod_b = jnp.concatenate(
        [grad_hidden_b, grad_hidden_b * normed_b, grad_gate_b], axis=-1
    ).astype(BF16)
    wide = grad_mod_b.shape[1]
    ff, heads_wide, own_rows = gate_cols.shape[1], local_heads * HD, width // 8
    mod_cols = -(-wide // (4 * TILE)) * TILE
    pieces = lax.axis_size("dp") == 8
    parts_b, arrays_b, shared_b, shapes_b = [], {}, [], []
    if pieces:
        parts_b = [
            *split_part("inner", "grad_branch_b", ff // 8, width, 0, 0, by_rows=True),
            *split_part("hidden_b", "grad_gate_in", own_rows, ff, 1, 1),
            *split_part("hidden_b", "grad_up_in", own_rows, ff, 2, 0),
            *split_part("lifted", 0, own_rows, mod_cols, 3, 0, bias=True),
        ]
        parts_b = [parts_b[k] for k in (0, 2, 1, 3, 4, 5, 6, 7)]
        arrays_b = {
            "inner": inner,
            "grad_branch_b": grad_branch_b,
            "hidden_b": hidden_b,
            "grad_gate_in": grad_gate_in,
            "grad_up_in": grad_up_in,
        }
        shared_b = [(grad_mod_b, False)]
        shapes_b = [
            (ff // 8, width),
            (own_rows // 4, 4 * ff),
            (own_rows // 4, 4 * ff),
            (own_rows // 4, wide),
        ]
    given = [rows_lanes, projected_lanes, w_qkv_lanes, w_out_lanes, *tables, *gain_lanes]
    empty = jnp.zeros((16, TILE), F32)
    if pieces:
        (*sums_b, small_b, lifted_full, grad_branch_a, grad_lanes, grad_hidden_a, gain_sums) = (
            attention_back(own_branch_a, lifted_low, given, parts_b, arrays_b, shared_b, empty, shapes_b)
        )
        grad_branch_a = grad_branch_a.reshape(patches, width)
        lifted_full = lifted_full.reshape(patches, width)
    else:
        grad_branch_a = gather_rows(own_branch_a)
        grad_lanes, partial, gain_sums = plain_back(grad_branch_a, given)
        grad_hidden_a = scatter_rows(partial)
    grad_tokens = grad_middle + rms_back(grad_hidden_a * (1.0 + scale_a), normed_a, inverse_a)
    grad_mod_a = jnp.concatenate(
        [grad_hidden_a, grad_hidden_a * normed_a, grad_gate_a], axis=-1
    ).astype(BF16)
    first = mod_first.shape[1]
    grad_condition = (
        times_transpose(grad_mod_a[:, :first], mod_first)
        + times_transpose(
            jnp.concatenate([grad_mod_a[:, first:], grad_mod_b], axis=1), mod_rest
        )
    ) * silu_slope(condition_in)
    grad_project = out_of_lanes(grad_lanes).reshape(patches, 3 * heads_wide)
    gain_sums = gain_sums[:2, :HD]
    if pieces:
        parts_a = [
            *split_part("hidden_a", "grad_project", own_rows, 3 * heads_wide, 0, 0),
            Part(
                "attended", "grad_branch_a", heads_wide // 8, (0, width), 1, 1, by_rows=True, in_lanes=True
            ),
            *split_part("lifted", 0, own_rows, mod_cols, 2, 0, bias=True),
        ]
        parts_a = [parts_a[k] for k in (0, 2, 1, 3, 4)]
        arrays_a = {
            "hidden_a": hidden_a,
            "grad_project": grad_project,
            "attended": attended_lanes,
            "grad_branch_a": grad_branch_a,
            "lifted": lifted_full,
        }
        shapes_a = [
            (4, own_rows // 4, 3 * heads_wide),
            (heads_wide // 8, width),
            (own_rows // 4, wide),
        ]
        qkv_sum, grad_w_out, mod_a, small_a = weight_grads(
            parts_a, arrays_a, [(grad_mod_a, False)], padded_small(gain_sums), shapes_a
        )
        grad_w_down, grad_w_gate, grad_w_up, mod_b = sums_b
        grad_w_qkv = jnp.transpose(
            qkv_sum.reshape(4, own_rows // 4, 3, heads_wide), (1, 2, 0, 3)
        ).reshape(own_rows // 4, 3 * width)
        grad_w_mod = jnp.concatenate([mod_a, mod_b], axis=1)
        tiles = wide // TILE
        bias = jnp.concatenate(bias_columns(small_a, tiles) + bias_columns(small_b, tiles))
        own_bias = bias.shape[0] // (8 * ways)
        sum_bias = lax.dynamic_slice(
            bias, ((item * ways + lax.axis_index("seq")) * own_bias,), (own_bias,)
        )
        gains = jnp.sum(small_a[:, 8:10, :HD], axis=0)
    else:
        mod_rows = jnp.concatenate([grad_mod_a, grad_mod_b], axis=1)
        grad_w_down = plain_sums(inner, grad_branch_b, 0)
        grad_w_gate = plain_sums(hidden_b, grad_gate_in, 1)
        grad_w_up = plain_sums(hidden_b, grad_up_in, 1)
        grad_w_qkv = plain_sums(hidden_a, grad_project, 3)
        attended = out_of_lanes(attended_lanes).reshape(patches, heads_wide)
        grad_w_out = plain_sums(attended, grad_branch_a, 0)
        grad_w_mod = plain_sums(gather_rows(lifted_low), rows_to_columns(mod_rows, 6), 6)
        bias_rows = jnp.sum(mod_rows, axis=0, dtype=F32)
        sum_bias = lax.psum_scatter(bias_rows, ("dp", "seq"), scatter_dimension=0, tiled=True)
        gains = lax.psum(gain_sums, ("dp", "seq"))
    sum_q_gain, sum_k_gain = gains[0], gains[1]
    return (
        block_out[None],
        grad_tokens[None],
        grad_condition[None],
        grad_w_qkv,
        grad_w_out,
        grad_w_gate,
        grad_w_up,
        grad_w_down,
        grad_w_mod,
        sum_bias,
        sum_q_gain,
        sum_k_gain,
    )


def solution(mesh):
    placed = (
        P("dp", "seq", None),
        P("dp", "seq", None),
        P("dp", "seq", None),
        P("seq", None),
        P("seq", None),
        P("seq", None),
        P("seq", None),
        P("seq", None),
        P("seq", None),
        P(),
        P(),
        P(),
        P(),
        P("dp"),
        P(None, "dp", "seq"),
    )
    return jax.shard_map(
        shards,
        mesh=mesh,
        in_specs=placed,
        out_specs=(
            P("dp", "seq", None),
            P("dp", "seq", None),
            P("dp", "seq", None),
            P(("dp", "seq"), None),
            P(("dp", "seq"), None),
            P(("dp", "seq"), None),
            P(("dp", "seq"), None),
            P(("dp", "seq"), None),
            P(("dp", "seq"), None),
            P(("dp", "seq")),
            P(),
            P(),
        ),
        check_vma=False,
    )
```

```python
import math

import jax
import jax.numpy as jnp
from jax import lax
from jax.experimental import pallas as pl
from jax.experimental.pallas import tpu as pltpu
from jax.sharding import PartitionSpec as P

HEADS = 16
HD = 72
EPSILON = 1e-06
BF16 = jnp.bfloat16
F32 = jnp.float32


def inverse_rms(values):
    return lax.rsqrt(jnp.mean(values * values, axis=-1, keepdims=True) + EPSILON)


def rms_back(grad_in, normed, inverse):
    return inverse * (grad_in - normed * jnp.mean(grad_in * normed, axis=-1, keepdims=True))


def silu_slope(values):
    logistic = jax.nn.sigmoid(values)
    return logistic * (1.0 + values * (1.0 - logistic))


def time_embed(steps, width):
    half_width = width // 2
    frequency = jnp.exp(-math.log(10000.0) * jnp.arange(half_width, dtype=F32) / half_width)
    angles = steps.astype(F32)[:, None] * frequency[None, :]
    return jnp.concatenate([jnp.cos(angles), jnp.sin(angles)], axis=-1)


def rope_tables(positions, head_size):
    quarter = head_size // 4
    frequency = jnp.exp(-math.log(10000.0) * jnp.arange(quarter, dtype=F32) / quarter)
    along_rows = positions[0].astype(F32)[..., None] * frequency
    along_cols = positions[1].astype(F32)[..., None] * frequency
    angles = jnp.concatenate([along_rows, along_rows, along_cols, along_cols], axis=-1)
    return (jnp.cos(angles)[..., None, :], jnp.sin(angles)[..., None, :])


def quarter_turn(values):
    first, second, third, fourth = jnp.split(values, 4, axis=-1)
    return jnp.concatenate([-second, first, -fourth, third], axis=-1)


def rotate_heads(values, cosine, sine):
    return values * cosine + quarter_turn(values) * sine


def unrotate(grad_in, cosine, sine):
    return grad_in * cosine - quarter_turn(grad_in * sine)


def matmul(left, right):
    return jnp.dot(left, right, preferred_element_type=F32)


def outer_sum(left, right):
    return jnp.einsum("ra,rb->ab", left, right, preferred_element_type=F32)


def times_transpose(left, right):
    return jnp.einsum("rb,ab->ra", left, right, preferred_element_type=F32)


MESH = pl.DeviceIdType.MESH
SUM_ID, GATHER_ID, SCATTER_ID, WEIGHT_ID, ATTEND_ID, BACK_ID, MLP_ID = 1, 2, 3, 4, 5, 6, 7


def greet(partners):
    barrier = pltpu.get_barrier_semaphore()
    for partner in partners:
        pl.semaphore_signal(barrier, inc=1, device_id=partner, device_id_type=MESH)
    pl.semaphore_wait(barrier, len(partners))


def group_partners():
    item, column = lax.axis_index("dp"), lax.axis_index("seq")
    core = lax.rem(column, 2)
    return (item, column + 1 - 2 * core), (item, lax.rem(column + 2, 4))


GATHER_PIECES = 4


def gather_kernel(own_ref, out_ref, local_sem, send_sem, recv_sem):
    column = lax.axis_index("seq")
    sibling, across = group_partners()
    greet([sibling, across])
    local = pltpu.make_async_copy(own_ref, out_ref.at[column], local_sem)
    local.start()
    rows = own_ref.shape[0] // GATHER_PIECES

    def remote(source, place, piece, kind, target):
        part = pl.ds(piece * rows, rows)
        return pltpu.make_async_remote_copy(
            src_ref=source.at[part],
            dst_ref=out_ref.at[place, part],
            send_sem=send_sem.at[kind, piece],
            recv_sem=recv_sem.at[kind, piece],
            device_id=target,
            device_id_type=MESH,
        )

    far = lax.rem(column + 2, 4)
    pieces = range(GATHER_PIECES)
    over = [remote(own_ref, column, piece, 0, across) for piece in pieces]
    beside = [remote(own_ref, column, piece, 1, sibling) for piece in pieces]
    onward = [remote(out_ref.at[far], far, piece, 2, sibling) for piece in pieces]
    for copy in over:
        copy.start()
    for copy in beside:
        copy.start()
    for piece in pieces:
        over[piece].wait_recv()
        onward[piece].start()
    for piece in pieces:
        over[piece].wait_send()
        beside[piece].wait()
        onward[piece].wait()
    local.wait()


def gather_rows(values):
    rows, columns = values.shape
    gathered = pl.pallas_call(
        gather_kernel,
        out_shape=jax.ShapeDtypeStruct((4, rows, columns), values.dtype),
        in_specs=[pl.BlockSpec(memory_space=pltpu.VMEM)],
        out_specs=pl.BlockSpec(memory_space=pltpu.VMEM),
        scratch_shapes=[
            pltpu.SemaphoreType.DMA,
            pltpu.SemaphoreType.DMA((3, GATHER_PIECES)),
            pltpu.SemaphoreType.DMA((3, GATHER_PIECES)),
        ],
        compiler_params=pltpu.CompilerParams(
            collective_id=GATHER_ID, has_side_effects=True, vmem_limit_bytes=48 * 2**20
        ),
        name="gather_rows",
    )(values)
    return gathered.reshape(4 * rows, columns)


def scatter_kernel(parts_ref, out_ref, near, low, far, send_sem, recv_sem):
    column = lax.axis_index("seq")
    core, chip = lax.rem(column, 2), column // 2
    sibling, across = group_partners()
    greet([sibling, across])
    rows = out_ref.shape[0] // 2

    def remote(source, target_ref, index, target):
        return pltpu.make_async_remote_copy(
            src_ref=source,
            dst_ref=target_ref,
            send_sem=send_sem.at[index],
            recv_sem=recv_sem.at[index],
            device_id=target,
            device_id_type=MESH,
        )

    parts = [pl.ds(piece * rows, rows) for piece in range(2)]
    beside = [
        remote(parts_ref.at[1 - chip, 1 - core, part], near.at[0, part], i, sibling)
        for i, part in enumerate(parts)
    ]
    beside.append(remote(parts_ref.at[chip, 1 - core], near.at[1], 2, sibling))
    for copy in beside:
        copy.start()
    over = [remote(low.at[part], far.at[part], 3 + i, across) for i, part in enumerate(parts)]
    for i, part in enumerate(parts):
        beside[i].wait_recv()
        pair = parts_ref[1 - chip, core, part].astype(F32) + near[0, part].astype(F32)
        low[part] = pair.astype(BF16)
        over[i].start()
    beside[2].wait_recv()
    out_ref[...] = parts_ref[chip, core].astype(F32) + near[1].astype(F32)
    for i, part in enumerate(parts):
        over[i].wait()
        out_ref[part] += far[part].astype(F32)
    for copy in beside:
        copy.wait_send()


def scatter_rows(partial):
    rows, columns = partial.shape[0] // 4, partial.shape[1]
    return pl.pallas_call(
        scatter_kernel,
        out_shape=jax.ShapeDtypeStruct((rows, columns), F32),
        in_specs=[pl.BlockSpec(memory_space=pltpu.VMEM)],
        out_specs=pl.BlockSpec(memory_space=pltpu.VMEM),
        scratch_shapes=[
            pltpu.VMEM((2, rows, columns), BF16),
            pltpu.VMEM((rows, columns), BF16),
            pltpu.VMEM((rows, columns), BF16),
            pltpu.SemaphoreType.DMA((5,)),
            pltpu.SemaphoreType.DMA((5,)),
        ],
        compiler_params=pltpu.CompilerParams(
            collective_id=SCATTER_ID, has_side_effects=True, vmem_limit_bytes=48 * 2**20
        ),
        name="scatter_rows",
    )(partial.astype(BF16).reshape(2, 2, rows, columns))


TILE = 128
LANES = 128
QUARTER = HD // 4
FIRST_ROWS = 80


class WeightImport:
    def __init__(self, blocks, ranges):
        self.blocks, self.ranges = blocks, ranges
        self.arrays = sorted({block[0] for block in blocks})

    def scratch(self):
        count = len(self.blocks)
        return [
            pltpu.SemaphoreType.DMA((8,)),
            pltpu.SemaphoreType.DMA((count, 7)),
            pltpu.SemaphoreType.DMA((count, 7)),
        ]

    def bind(self, ins, outs, scratch):
        self.ins, self.outs = ins, outs
        self.own_sem, self.send_sem, self.recv_sem = scratch
        item, column = lax.axis_index("dp"), lax.axis_index("seq")
        core, chip = lax.rem(column, 2), column // 2
        self.item, self.column = item, column
        self.y_bit, self.z_bit = lax.rem(item, 2), lax.rem(item // 2, 2)
        self.sibling = (item, column + 1 - 2 * core)
        self.y_near = (item + 1 - 2 * self.y_bit, column)
        self.z_near = (item + 2 - 4 * self.z_bit, column)
        self.far = [(1 - chip) * 2 + k for k in (core, 1 - core)]
        self.half_rows = ins[0].shape[0] // 2

    def partners(self):
        across = [(self.item, place) for place in self.far]
        return across + [self.sibling, self.y_near, self.z_near]

    def copy(self, source, target_ref, block, kind, target):
        return pltpu.make_async_remote_copy(
            src_ref=source,
            dst_ref=target_ref,
            send_sem=self.send_sem.at[block, kind],
            recv_sem=self.recv_sem.at[block, kind],
            device_id=target,
            device_id_type=MESH,
        )

    def source_column(self, column):
        for start, stop in self.ranges:
            if column < stop - start:
                return start + column
            column -= stop - start

    def piece(self, ref, block, y_pick, z_pick, first_row=0, rows=None, base=0, outside=False):
        array, _, start, columns = self.blocks[block]
        step = columns
        if array == 0 and outside:
            step = self.source_column(start + columns) - self.source_column(start)
            start = self.source_column(start)
        rows = self.half_rows if rows is None else rows
        return ref.at[
            pl.ds(pl.multiple_of(z_pick * self.half_rows + first_row, 16), rows),
            pl.ds(pl.multiple_of(base + start + y_pick * step, TILE), columns),
        ]

    def mine_for(self, array, place):
        ref = self.ins[array]
        if len(ref.shape) == 3:
            return ref.at[place], 0
        return ref, 0 if array == 0 else place * self.outs[array].shape[2]

    def whole(self, array, place):
        ref, base = self.mine_for(array, place)
        columns = self.outs[array].shape[2]
        if ref.shape[-1] == columns:
            return ref
        return ref.at[:, pl.ds(pl.multiple_of(base, TILE), columns)]

    def over(self, block):
        array, offset, _, _ = self.blocks[block]
        goal = self.far[offset or 0]
        ref, base = self.mine_for(array, goal)
        source = self.piece(ref, block, self.y_bit, self.z_bit, base=base, outside=True)
        target = self.piece(self.outs[array].at[self.column], block, self.y_bit, self.z_bit)
        return self.copy(source, target, block, 0, (self.item, goal))

    def onward(self, block, kind):
        array, offset, _, _ = self.blocks[block]
        ref = self.outs[array].at[self.far[offset or 0]]
        if kind == 1:
            part, target = self.piece(ref, block, self.y_bit, self.z_bit), self.y_near
        elif kind == 2:
            part, target = self.piece(ref, block, self.y_bit, self.z_bit), self.z_near
        elif kind == 3:
            part = self.piece(ref, block, 1 - self.y_bit, self.z_bit, 0, FIRST_ROWS)
            target = self.z_near
        else:
            rest = self.half_rows - FIRST_ROWS
            part = self.piece(ref, block, self.y_bit, 1 - self.z_bit, FIRST_ROWS, rest)
            target = self.y_near
        return self.copy(part, part, block, kind, target)

    def share(self, block):
        _, _, start, columns = self.blocks[block]
        part = self.outs[0].at[self.far[0], :, pl.ds(start, 2 * columns)]
        return self.copy(part, part, block, 5, self.sibling)

    def spans(self, array, place):
        target = self.outs[array].at[self.column]
        if array:
            return [(self.whole(array, place), target)]
        pairs, at = [], 0
        for start, stop in self.ranges:
            columns = stop - start
            pairs.append((self.ins[0].at[:, pl.ds(start, columns)], target.at[:, pl.ds(at, columns)]))
            at += columns
        return pairs

    def beside(self, array):
        index = self.arrays.index(array)
        return [
            self.copy(source, target, index + 2 * k, 6, self.sibling)
            for k, (source, target) in enumerate(self.spans(array, self.sibling[1]))
        ]

    def own(self, array):
        return [
            pltpu.make_async_copy(source, target, self.own_sem.at[array + 4 * k])
            for k, (source, target) in enumerate(self.spans(array, self.column))
        ]

    def steps(self):
        count = len(self.blocks)
        todo = []
        for step in range(count + 3):
            if step < count:
                todo.append(lambda step=step: self.arrive(step))
            if 0 <= step - 1 < count:
                todo.append(lambda step=step: self.pass_on(step - 1))
            if 0 <= step - 2 < count:
                todo.append(lambda step=step: self.complete(step - 2))
        return todo

    def arrive(self, step):
        self.over(step).wait_recv()
        self.onward(step, 1).start()
        self.onward(step, 2).start()

    def pass_on(self, step):
        self.onward(step, 1).wait_recv()
        self.onward(step, 3).start()
        self.onward(step, 2).wait_recv()
        self.onward(step, 4).start()

    def complete(self, step):
        self.onward(step, 3).wait_recv()
        self.onward(step, 4).wait_recv()
        if self.blocks[step][0] == 0:
            self.share(step).start()

    def end(self):
        for block in range(len(self.blocks)):
            self.over(block).wait_send()
            for kind in range(1, 5):
                self.onward(block, kind).wait_send()
            if self.blocks[block][0] == 0:
                self.share(block).wait_send()


class RowGather:
    def __init__(self, own, everyone, local_sem, send_sem, recv_sem):
        self.own, self.everyone = own, everyone
        self.local_sem, self.send_sem, self.recv_sem = local_sem, send_sem, recv_sem
        self.column = lax.axis_index("seq")
        self.far = lax.rem(self.column + 2, 4)
        self.sibling, self.across = group_partners()

    def remote(self, source, place, piece, kind, target):
        rows = self.own.shape[0] // GATHER_PIECES
        part = pl.ds(piece * rows, rows)
        return pltpu.make_async_remote_copy(
            src_ref=source.at[part],
            dst_ref=self.everyone.at[place, part],
            send_sem=self.send_sem.at[kind, piece],
            recv_sem=self.recv_sem.at[kind, piece],
            device_id=target,
            device_id_type=MESH,
        )

    def over(self, piece):
        return self.remote(self.own, self.column, piece, 0, self.across)

    def beside(self, piece):
        return self.remote(self.own, self.column, piece, 1, self.sibling)

    def onward(self, piece):
        return self.remote(self.everyone.at[self.far], self.far, piece, 2, self.sibling)

    def local(self):
        return pltpu.make_async_copy(self.own, self.everyone.at[self.column], self.local_sem)

    def start(self):
        for piece in range(GATHER_PIECES):
            self.over(piece).start()
        for piece in range(GATHER_PIECES):
            self.beside(piece).start()
        self.local().start()

    def pass_on(self):
        for piece in range(GATHER_PIECES):
            self.over(piece).wait_recv()
            self.onward(piece).start()

    def end(self):
        for piece in range(GATHER_PIECES):
            self.over(piece).wait_send()
            self.beside(piece).wait()
            self.onward(piece).wait()
        self.local().wait()

    @staticmethod
    def scratch():
        return [
            pltpu.SemaphoreType.DMA,
            pltpu.SemaphoreType.DMA((3, GATHER_PIECES)),
            pltpu.SemaphoreType.DMA((3, GATHER_PIECES)),
        ]


def first_import(width):
    wide = 3 * HEADS // 4 * LANES
    blocks = [(0, None, 0, width), (0, None, 2 * width, width), (1, 0, 0, wide // 2), (1, 1, 0, wide // 2)]
    return WeightImport(blocks, [(0, 3 * width), (5 * width, 6 * width)])


def second_import(width, ff):
    blocks = [(0, None, 0, width)] + [(k, j, 0, ff // 2) for k in (2, 3) for j in (0, 1)]
    return WeightImport(blocks, [(3 * width, 5 * width)])


def spread_heads(w_ref, lanes_ref):
    rows = w_ref.shape[0]
    valid = lax.broadcasted_iota(jnp.int32, (rows, LANES), 1) < HD
    for head in range(3 * HEADS):
        kind, device, place = head // HEADS, head % HEADS // 4, head % 4
        start = head * HD // LANES * LANES
        stop = min(start + 2 * LANES, w_ref.shape[1])
        window = w_ref[:, start:stop].astype(F32)
        shift = head * HD - start
        if shift:
            window = pltpu.roll(window, window.shape[1] - shift, 1)
        target = (kind * 4 + place) * LANES
        lanes_ref[device, :, target : target + LANES] = jnp.where(
            valid, window[:, :LANES], 0.0
        ).astype(BF16)


def start_all(copies):
    for copy in copies:
        copy.start()


def wait_all(copies):
    for copy in copies:
        copy.wait()


def first_kernel(imports, *refs):
    (w_mod, w_qkv, condition, tokens, cotangent, embed, share, bias, positions), refs = refs[:9], refs[9:]
    (mod_out, qkv_out, scale_a, gate_a, gate_b), refs = refs[:5], refs[5:]
    (hidden_all, lifted_all, grads, lifted, positions_all), refs = refs[:5], refs[5:]
    (mod_all, lanes, hidden, mod_sem, spot_send, spot_recv), refs = refs[:6], refs[6:]
    imports.bind({0: w_mod, 1: lanes}, {0: mod_all, 1: qkv_out}, refs[:3])
    gather = RowGather(hidden, hidden_all, *refs[3:6])
    gather_lifted = RowGather(lifted, lifted_all, *refs[6:9])
    item, column = lax.axis_index("dp"), lax.axis_index("seq")
    width = tokens.shape[1]
    greet(imports.partners())
    imports.over(0).start()
    start_all(imports.own(0))
    start_all(imports.beside(0))
    peers = [(item, lax.rem(column + k, 4)) for k in range(1, 4)]
    spot_copies = [
        pltpu.make_async_remote_copy(
            src_ref=positions,
            dst_ref=positions_all.at[column],
            send_sem=spot_send.at[k],
            recv_sem=spot_recv.at[k],
            device_id=peer,
            device_id_type=MESH,
        )
        for k, peer in enumerate(peers)
    ]
    start_all(spot_copies)
    positions_all[column] = positions[...]
    spread_heads(w_qkv, lanes)
    for block in range(1, len(imports.blocks)):
        imports.over(block).start()
    start_all(imports.own(1))
    start_all(imports.beside(1))
    values = condition[...].astype(F32) + embed[...]
    lifted[...] = (values * jax.nn.sigmoid(values)).astype(BF16)
    imports.arrive(0)
    imports.pass_on(0)
    imports.arrive(1)
    imports.complete(0)
    wait_all(imports.own(0))
    for copy in imports.beside(0):
        copy.wait_recv()

    def modulate(block):
        imports.share(block).wait_recv()
        start = imports.blocks[block][2]
        weights = mod_all[:, :, start : start + 2 * width].reshape(-1, 2 * width)
        modulation = jnp.dot(lifted[...], weights, preferred_element_type=F32)
        return [
            modulation[:, k * width : (k + 1) * width]
            + bias[:, pl.ds(imports.source_column(start + k * width), width)]
            for k in range(2)
        ]

    shift, scale = modulate(0)
    scale_a[...] = scale
    values = tokens[...].astype(F32)
    normed = values * inverse_rms(values)
    hidden[...] = (normed * (1.0 + scale) + shift).astype(BF16)
    gather.start()
    gather_lifted.start()
    imports.pass_on(1)
    imports.arrive(2)
    imports.complete(1)
    imports.arrive(3)
    store = pltpu.make_async_copy(mod_all, mod_out, mod_sem)
    gate_a[...], gate = modulate(1)
    store.start()
    gate_b[...] = gate
    grads[...] = (cotangent[...].astype(F32) * share[...] * gate).astype(BF16)
    imports.pass_on(2)
    imports.pass_on(3)
    gather.pass_on()
    imports.complete(2)
    imports.complete(3)
    gather_lifted.pass_on()
    imports.end()
    for copy in imports.beside(0):
        copy.wait_send()
    wait_all(imports.beside(1))
    wait_all(imports.own(1))
    gather.end()
    gather_lifted.end()
    wait_all(spot_copies)
    store.wait()


def first_stage(w_mod, w_qkv, condition, tokens, cotangent, embed, share, bias, positions):
    rows, width = tokens.shape
    depth, lanes = w_mod.shape[0], 3 * HEADS // 4 * LANES
    imports = first_import(width)
    vmem, anywhere = pl.BlockSpec(memory_space=pltpu.VMEM), pl.BlockSpec(memory_space=pl.ANY)

    def kernel(*refs):
        first_kernel(imports, *refs)

    return pl.pallas_call(
        kernel,
        out_shape=[
            jax.ShapeDtypeStruct((4, depth, 4 * width), BF16),
            jax.ShapeDtypeStruct((4, depth, lanes), BF16),
            jax.ShapeDtypeStruct((rows, width), F32),
            jax.ShapeDtypeStruct((rows, width), F32),
            jax.ShapeDtypeStruct((rows, width), F32),
            jax.ShapeDtypeStruct((4, rows, width), BF16),
            jax.ShapeDtypeStruct((4, rows, width), BF16),
            jax.ShapeDtypeStruct((rows, width), BF16),
            jax.ShapeDtypeStruct((rows, width), BF16),
            jax.ShapeDtypeStruct((4,) + positions.shape, jnp.int32),
        ],
        in_specs=[anywhere] + [vmem] * 8,
        out_specs=[anywhere, anywhere] + [vmem] * 8,
        scratch_shapes=[
            pltpu.VMEM((4, depth, 4 * width), BF16),
            pltpu.VMEM((4, depth, lanes), BF16),
            pltpu.VMEM((rows, width), BF16),
            pltpu.SemaphoreType.DMA,
            pltpu.SemaphoreType.DMA((3,)),
            pltpu.SemaphoreType.DMA((3,)),
        ]
        + imports.scratch()
        + RowGather.scratch() * 2,
        compiler_params=pltpu.CompilerParams(
            collective_id=WEIGHT_ID, has_side_effects=True, vmem_limit_bytes=60 * 2**20
        ),
        name="first_stage",
    )(w_mod, w_qkv, condition, tokens, cotangent, embed, share, bias, positions)


def rotated(values, tables, sign):
    cosine, ahead, behind = tables
    turned = pltpu.roll(values, LANES - QUARTER, 1) * ahead + pltpu.roll(values, QUARTER, 1) * behind
    return values * cosine + turned if sign > 0 else values * cosine - turned


def lane_tables(positions):
    cosine, sine = rope_tables(positions, HD)
    cosine, sine = cosine[:, 0], sine[:, 0]
    takes_ahead = (jnp.arange(HD) // QUARTER % 2 == 0)[None, :]
    tables = (cosine, jnp.where(takes_ahead, -sine, 0.0), jnp.where(takes_ahead, 0.0, sine))
    return [jnp.pad(table, ((0, 0), (0, LANES - HD))) for table in tables]


def head_inverse(values):
    return lax.rsqrt(jnp.sum(values * values, axis=-1, keepdims=True) * (1.0 / HD) + EPSILON)


def over_rows(left, right):
    return lax.dot_general(left, right, (((1,), (1,)), ((), ())), preferred_element_type=F32)


def over_first(left, right):
    return lax.dot_general(left, right, (((0,), (0,)), ((), ())), preferred_element_type=F32)


class RowSums:
    def __init__(self, blocks, near, low, far, send_sem, recv_sem):
        column = lax.axis_index("seq")
        self.column = column
        self.core, self.chip = lax.rem(column, 2), column // 2
        self.sibling, self.across = group_partners()
        self.blocks, self.near, self.low, self.far = blocks, near, low, far
        self.send_sem, self.recv_sem = send_sem, recv_sem
        self.order = [
            (1 - self.chip) * 2 + 1 - self.core,
            (1 - self.chip) * 2 + self.core,
            self.chip * 2 + 1 - self.core,
            column,
        ]

    def copy(self, source, target_ref, index, target):
        return pltpu.make_async_remote_copy(
            src_ref=source,
            dst_ref=target_ref,
            send_sem=self.send_sem.at[index],
            recv_sem=self.recv_sem.at[index],
            device_id=target,
            device_id_type=MESH,
        )

    def beside(self, index):
        return self.copy(self.blocks.at[index], self.near.at[index], index, self.sibling)

    def over(self):
        return self.copy(self.low, self.far, 2, self.across)

    def put(self, index, values):
        if index == 0 or index == 2:
            self.blocks[index // 2] = values.astype(BF16)
            self.beside(index // 2).start()
        elif index == 1:
            self.beside(0).wait_recv()
            self.low[...] = (values + self.near[0].astype(F32)).astype(BF16)
            self.over().start()
        else:
            self.own = values

    def sums(self):
        self.beside(1).wait_recv()
        total = self.own + self.near[1].astype(F32)
        self.over().wait()
        total = total + self.far[...].astype(F32)
        self.beside(0).wait_send()
        self.beside(1).wait_send()
        return total

    @staticmethod
    def scratch(rows, columns):
        return [
            pltpu.VMEM((2, rows, columns), BF16),
            pltpu.VMEM((2, rows, columns), BF16),
            pltpu.VMEM((rows, columns), BF16),
            pltpu.VMEM((rows, columns), BF16),
            pltpu.SemaphoreType.DMA((3,)),
            pltpu.SemaphoreType.DMA((3,)),
        ]


def attend_kernel(imports, *refs):
    (hidden, w_qkv, w_out, cosine, ahead, behind, q_gain, k_gain), refs = refs[:8], refs[8:]
    (w_mod, w_gate, w_up, lifted, bias, tokens, gate_a, grads), refs = refs[:8], refs[8:]
    (heads_out, rows_out, attended_out, branch_out), refs = refs[:4], refs[4:]
    (mod_out, gate_out, up_out, scale_out, middle_out, hidden_out, grads_all), refs = refs[:7], refs[7:]
    (mod_all, gate_own, up_own, mod_sem, load_sem), refs = refs[:5], refs[5:]
    sums = RowSums(*refs[:6])
    imports.bind({0: w_mod, 2: w_gate, 3: w_up}, {0: mod_all, 2: gate_out, 3: up_out}, refs[6:9])
    gather = RowGather(grads, grads_all, *refs[9:])
    greet(imports.partners())
    for block in range(len(imports.blocks)):
        imports.over(block).start()
    start_all(imports.own(0))
    loads = [
        pltpu.make_async_copy(imports.whole(k, sums.column), ref, load_sem.at[k - 2])
        for k, ref in ((2, gate_own), (3, up_own))
    ]
    stores = [
        pltpu.make_async_copy(ref, imports.outs[k].at[sums.column], load_sem.at[k])
        for k, ref in ((2, gate_own), (3, up_own))
    ]
    for copy in loads:
        copy.start()
    for array in imports.arrays:
        start_all(imports.beside(array))
    gather.start()
    todo = imports.steps()

    def aside(number):
        for _ in range(min(number, len(todo))):
            todo.pop(0)()

    factor = HD ** (-0.5)
    rows = branch_out.shape[0]
    heads = attended_out.shape[1] // LANES
    tables = cosine[...], ahead[...], behind[...]
    for pair in range(3 * heads // 2):
        span = slice(pair * 2 * LANES, (pair + 1) * 2 * LANES)
        projected = jnp.dot(hidden[...], w_qkv[:, span], preferred_element_type=F32)
        if pair >= heads:
            rows_out[:, span] = projected.astype(BF16)
            continue
        heads_out[:, span] = projected
        gain = (q_gain if pair < heads // 2 else k_gain)[...]
        for half in range(2):
            values = projected[:, half * LANES : (half + 1) * LANES]
            values = values * head_inverse(values) * gain
            start = pair * 2 * LANES + half * LANES
            rows_out[:, start : start + LANES] = rotated(values, tables, 1).astype(BF16)
    aside(1)
    for copy in loads:
        copy.wait()
    for copy in stores:
        copy.start()
    for index in range(4):
        block = pl.ds(pl.multiple_of(sums.order[index] * rows, rows), rows)
        for head in range(heads):
            spans = [slice((k * heads + head) * LANES, (k * heads + head + 1) * LANES) for k in range(3)]
            exp_scores = jnp.exp(over_rows(rows_out[block, spans[0]], rows_out[:, spans[1]]) * factor)
            scale = 1.0 / jnp.sum(exp_scores, axis=1, keepdims=True)
            mixed = jnp.dot(
                (exp_scores * scale).astype(BF16),
                rows_out[:, spans[2]],
                preferred_element_type=F32,
            )
            attended_out[block, spans[0]] = mixed.astype(BF16)
        sums.put(index, jnp.dot(attended_out[block, :], w_out[...], preferred_element_type=F32))
        aside((1, 3, 4, len(todo))[index])
    gather.pass_on()
    wait_all(imports.own(0))
    for copy in imports.beside(0):
        copy.wait_recv()
    imports.share(0).wait_recv()
    store = pltpu.make_async_copy(mod_all, mod_out, mod_sem)
    store.start()
    width = tokens.shape[1]
    weights = mod_all[...].reshape(-1, 2 * width)
    modulation = jnp.dot(lifted[...], weights, preferred_element_type=F32)
    modulation = modulation + bias[:, pl.ds(imports.source_column(0), 2 * width)]
    scale = modulation[:, width:]
    scale_out[...] = scale
    branch = sums.sums()
    branch_out[...] = branch
    middle = tokens[...].astype(F32) + gate_a[...] * branch
    middle_out[...] = middle
    hidden_out[...] = (middle * inverse_rms(middle) * (1.0 + scale) + modulation[:, :width]).astype(BF16)
    imports.end()
    for copy in imports.beside(0):
        copy.wait_send()
    for array in imports.arrays[1:]:
        wait_all(imports.beside(array))
    gather.end()
    for copy in stores:
        copy.wait()
    store.wait()


def attend(hidden, w_qkv, w_out, tables, q_gain, k_gain, w_mod, w_gate, w_up, lifted, bias, tokens, gate_a, grads):
    patches, wide = hidden.shape[0], w_qkv.shape[1]
    rows, width = patches // 4, hidden.shape[1]
    depth, ff = w_mod.shape[0], w_gate.shape[1] // 4
    imports = second_import(width, ff)
    vmem, anywhere = pl.BlockSpec(memory_space=pltpu.VMEM), pl.BlockSpec(memory_space=pl.ANY)

    def kernel(*refs):
        attend_kernel(imports, *refs)

    return pl.pallas_call(
        kernel,
        out_shape=[
            jax.ShapeDtypeStruct((patches, wide * 2 // 3), F32),
            jax.ShapeDtypeStruct((patches, wide), BF16),
            jax.ShapeDtypeStruct((patches, wide // 3), BF16),
            jax.ShapeDtypeStruct((rows, width), F32),
            jax.ShapeDtypeStruct((4, depth, 2 * width), BF16),
            jax.ShapeDtypeStruct((4, depth, ff), BF16),
            jax.ShapeDtypeStruct((4, depth, ff), BF16),
            jax.ShapeDtypeStruct((rows, width), F32),
            jax.ShapeDtypeStruct((rows, width), F32),
            jax.ShapeDtypeStruct((rows, width), BF16),
            jax.ShapeDtypeStruct((4, rows, width), BF16),
        ],
        in_specs=[vmem] * 8 + [anywhere] * 3 + [vmem] * 5,
        out_specs=[vmem] * 4 + [anywhere] * 3 + [vmem] * 4,
        scratch_shapes=[
            pltpu.VMEM((4, depth, 2 * width), BF16),
            pltpu.VMEM((depth, ff), BF16),
            pltpu.VMEM((depth, ff), BF16),
            pltpu.SemaphoreType.DMA,
            pltpu.SemaphoreType.DMA((4,)),
        ]
        + RowSums.scratch(rows, width)
        + imports.scratch()
        + RowGather.scratch(),
        compiler_params=pltpu.CompilerParams(
            collective_id=ATTEND_ID, has_side_effects=True, vmem_limit_bytes=63 * 2**20
        ),
        name="attend",
    )(hidden, w_qkv, w_out, *tables, q_gain, k_gain, w_mod, w_gate, w_up, lifted, bias, tokens, gate_a, grads)


def mlp_kernel(sums, *refs):
    (hidden, grads_all, w_gate, w_up, w_down), refs = refs[:5], refs[5:]
    (middle, scale, gate_a, gate_b, branch_a, cotangent, share), refs = refs[:7], refs[7:]
    (hidden_all, inner, grad_gate, grad_up), refs = refs[:4], refs[4:]
    (block_out, middle_out, branch_grad_out, mod_out), refs = refs[:4], refs[4:]
    handed_out, refs = refs[: len(sums.leaving)], refs[len(sums.leaving) :]
    if sums.parts:
        sums.bind([], [], None, [], None, [], handed_out, refs[30:])
    sums.others = {
        "inner": (inner, lambda: None),
        "grad_branch_b": (grads_all, lambda: None),
        "hidden_b": (hidden_all, lambda: None),
        "grad_gate_in": (grad_gate, lambda: None),
    }
    gather = RowGather(hidden, hidden_all, *refs[:3])
    halves = [RowSums(*refs[3 + 6 * k : 9 + 6 * k]) for k in range(4)]
    sums_grad, sums_branch = halves[:2], halves[2:]
    first = sums_grad[0]
    greet([first.sibling, first.across] + (sums.partners[:2] if sums.parts else []))
    gather.start()
    rows, width = hidden.shape
    near, far = first.chip * 2, (1 - first.chip) * 2
    depth = w_gate.shape[0] * w_gate.shape[1]
    gate_weights, up_weights = (ref[...].reshape(depth, ref.shape[2]) for ref in (w_gate, w_up))

    def block(ref, pair, start, count):
        return jnp.concatenate([ref[pair + k, start : start + count] for k in range(2)], axis=0)

    def process(pair, start, count):
        values = block(hidden_all, pair, start, count)
        gate_in = jnp.dot(values, gate_weights, preferred_element_type=F32)
        up_in = jnp.dot(values, up_weights, preferred_element_type=F32)
        grad_inner = over_rows(block(grads_all, pair, start, count), w_down[...])
        logistic = jax.nn.sigmoid(gate_in)
        activated = gate_in * logistic
        slope = logistic * (1.0 + gate_in * (1.0 - logistic))
        results = (
            (activated * up_in).astype(BF16),
            (grad_inner * up_in * slope).astype(BF16),
            (grad_inner * activated).astype(BF16),
        )
        for ref, result in zip((inner, grad_gate, grad_up), results, strict=True):
            for k in range(2):
                at = pl.multiple_of((pair + k) * rows + start, 16)
                ref[pl.ds(at, count), :] = result[k * count : (k + 1) * count]
        return over_rows(results[1], gate_weights) + over_rows(results[2], up_weights)

    def put(sums, partial, count, far_rows):
        @pl.when(first.core == 0)
        def _():
            held[0, :count], held[1, :count] = partial[count:], partial[:count]

        @pl.when(first.core == 1)
        def _():
            held[0, :count], held[1, :count] = partial[:count], partial[count:]

        if far_rows:
            sums.put(0, held[0, :count])
            sums.put(1, held[1, :count])
        else:
            sums.put(2, held[0, :count])
            return held[1, :count]

    held, own_grad, own_branch = refs[27:30]
    half = rows // 2
    for piece in range(GATHER_PIECES):
        gather.beside(piece).wait_recv()
    gather.local().wait()
    partial = process(near, 0, rows)
    for k in range(2):
        part = slice(k * half, (k + 1) * half)
        both = jnp.concatenate([partial[part], partial[rows + k * half : rows + (k + 1) * half]], axis=0)
        own_grad[part] = put(sums_grad[k], both, half, False)
    for k in range(2):
        pieces = range(k * GATHER_PIECES // 2, (k + 1) * GATHER_PIECES // 2)
        for piece in pieces:
            gather.over(piece).wait_recv()
            gather.onward(piece).start()
        for piece in pieces:
            gather.onward(piece).wait_recv()
        put(sums_grad[k], process(far, k * half, half), half, True)
    sums.do(*["b0", "b1"][: len(sums.parts)])
    for k in range(2):
        at = [pl.ds(pl.multiple_of((far + j) * rows + k * half, 16), half) for j in range(2)]
        values = jnp.concatenate([inner[part, :] for part in at], axis=0)
        put(sums_branch[k], jnp.dot(values, w_down[...], preferred_element_type=F32), half, True)
    sums.do(*["b2", "b3"][: len(sums.parts)])
    for k in range(2):
        at = [pl.ds(pl.multiple_of((near + j) * rows + k * half, 16), half) for j in range(2)]
        values = jnp.concatenate([inner[part, :] for part in at], axis=0)
        partial = jnp.dot(values, w_down[...], preferred_element_type=F32)
        own_branch[k * half : (k + 1) * half] = put(sums_branch[k], partial, half, False)
    sums.do(*["f0", "f1"][: len(sums.parts)])
    for k in range(2):
        part = slice(k * half, (k + 1) * half)
        sums_grad[k].put(3, own_grad[part])
        grad_hidden = sums_grad[k].sums()
        values = middle[part]
        inverse = inverse_rms(values)
        normed = values * inverse
        grad_out = cotangent[part].astype(F32) * share[...]
        grad_middle = grad_out + rms_back(grad_hidden * (1.0 + scale[part]), normed, inverse)
        middle_out[part] = grad_middle
        branch_grad_out[part] = (grad_middle * gate_a[part]).astype(BF16)
        mod_out[part, :width] = (grad_middle * branch_a[part]).astype(BF16)
        mod_out[part, width : 2 * width] = grad_hidden.astype(BF16)
        mod_out[part, 2 * width : 3 * width] = (grad_hidden * normed).astype(BF16)
    sums.do(*["f2", "f3"][: len(sums.parts)])
    for k in range(2):
        part = slice(k * half, (k + 1) * half)
        sums_branch[k].put(3, own_branch[part])
        branch = sums_branch[k].sums()
        block_out[part] = (middle[part] + gate_b[part] * branch).astype(BF16)
        grad_out = cotangent[part].astype(F32) * share[...]
        mod_out[part, 3 * width :] = (grad_out * branch).astype(BF16)
    for piece in range(GATHER_PIECES):
        gather.over(piece).wait_send()
        gather.beside(piece).wait_send()
        gather.onward(piece).wait_send()
    sums.end()


def mlp(hidden, grads_all, w_gate, w_up, w_down, rest, parts):
    rows, width = hidden.shape
    ff = w_down.shape[0]
    sums = GradSums(parts, (), [], (16, LANES))
    vmem, anywhere = pl.BlockSpec(memory_space=pltpu.VMEM), pl.BlockSpec(memory_space=pl.ANY)

    def kernel(*refs):
        mlp_kernel(sums, *refs)

    return pl.pallas_call(
        kernel,
        out_shape=[
            jax.ShapeDtypeStruct((4, rows, width), BF16),
            jax.ShapeDtypeStruct((4 * rows, ff), BF16),
            jax.ShapeDtypeStruct((4 * rows, ff), BF16),
            jax.ShapeDtypeStruct((4 * rows, ff), BF16),
            jax.ShapeDtypeStruct((rows, width), BF16),
            jax.ShapeDtypeStruct((rows, width), F32),
            jax.ShapeDtypeStruct((rows, width), BF16),
            jax.ShapeDtypeStruct((rows, 4 * width), BF16),
        ]
        + [jax.ShapeDtypeStruct(part.handed(), BF16) for part in parts],
        in_specs=[vmem] * 12,
        out_specs=[vmem] * 8 + [anywhere] * len(parts),
        scratch_shapes=RowGather.scratch()
        + RowSums.scratch(rows // 2, width) * 4
        + [
            pltpu.VMEM((2, rows // 2, width), F32),
            pltpu.VMEM((rows, width), F32),
            pltpu.VMEM((rows, width), F32),
        ]
        + (sums.scratch([]) if parts else []),
        compiler_params=pltpu.CompilerParams(
            collective_id=MLP_ID, has_side_effects=True, vmem_limit_bytes=63 * 2**20
        ),
        name="mlp",
    )(hidden, grads_all, w_gate, w_up, w_down, *rest)


def rows_to_columns(values, blocks):
    rows, columns = values.shape
    ways = lax.axis_size("seq")
    values = values.reshape(rows, blocks, ways, columns // (blocks * ways))
    moved = lax.all_to_all(values, "seq", split_axis=2, concat_axis=0, tiled=True)
    return moved.reshape(rows * ways, columns // ways)


def columns_to_rows(values, blocks):
    rows, columns = values.shape
    ways = lax.axis_size("seq")
    values = values.reshape(rows, blocks, 1, columns // blocks)
    moved = lax.all_to_all(values, "seq", split_axis=0, concat_axis=2, tiled=True)
    return moved.reshape(rows // ways, columns * ways)


def first_tile(place, tiles):
    return (tiles * place) // 4


def padded_rows(rows):
    return -(-rows // 16) * 16


class Part:
    def __init__(self, left, right, rows, span, out, order, at=None, **kinds):
        self.left, self.right, self.rows = left, right, rows
        self.start, self.columns, self.out = span[0], span[1] - span[0], out
        self.at = self.start if at is None else at
        self.order = order
        for kind in ("by_rows", "in_lanes", "bias", "enter", "leave"):
            setattr(self, kind, kinds.get(kind, False))
        self.slab = padded_rows(rows)

    def handed(self):
        return (2, 2, self.slab, self.columns)


def split_part(left, right, rows, columns, out, order, **kinds):
    middle = -(-columns // (2 * TILE)) * TILE
    return [
        Part(left, right, rows, span, out, order, **kinds)
        for span in ((0, middle), (middle, columns))
    ]


class GradSums:
    def __init__(self, parts, names, shared_shapes, small_shape, after=()):
        self.parts, self.names = parts, names
        self.after = dict(after)
        self.shared_shapes, self.small_shape = shared_shapes, small_shape
        self.has_rows = any(part.by_rows and not part.leave for part in parts)
        self.entering = [index for index, part in enumerate(parts) if part.enter]
        self.leaving = [index for index, part in enumerate(parts) if part.leave]

    def scratch(self, array_shapes):
        parts, count, groups = self.parts, len(self.parts), len(self.shared_shapes)
        none = pltpu.VMEM((16, LANES), BF16)
        shapes = [
            none if name in self.after else pltpu.VMEM(shape, BF16)
            for name, shape in zip(self.names, array_shapes, strict=True)
        ]
        shapes += [pltpu.VMEM((4, rows, columns), BF16) for rows, _, _, columns in self.shared_shapes]

        def each(lead, needed):
            return [
                pltpu.VMEM(lead(part) + (part.slab, part.columns), BF16) if needed(part) else none
                for part in parts
            ]

        shapes += each(lambda part: (2, 2) if part.enter else (2, 2, 2), lambda part: True)
        shapes += each(lambda part: (2, 2), lambda part: not part.enter)
        shapes += each(lambda part: (2,), lambda part: not part.leave)
        shapes += each(lambda part: (), lambda part: not part.leave)
        for _ in range(2):
            for part in parts:
                if part.leave:
                    shapes.append(none)
                elif part.by_rows:
                    shapes.append(pltpu.VMEM((part.slab, part.columns), BF16))
                else:
                    shapes.append(pltpu.VMEM((4, padded_rows(part.rows // 4), part.columns), BF16))
        widest = max(part.columns for part in parts)
        tallest = max(4 * LANES if part.in_lanes else part.rows for part in parts)
        return shapes + [
            pltpu.VMEM((tallest, widest), F32),
            pltpu.VMEM((4,) + self.small_shape, F32),
            pltpu.VMEM((3,) + self.small_shape, F32),
            pltpu.SemaphoreType.DMA((max(len(self.names), 1),)),
            pltpu.SemaphoreType.DMA((max(groups, 1), 3)),
            pltpu.SemaphoreType.DMA((max(groups, 1), 3)),
            pltpu.SemaphoreType.DMA((max(groups, 1),)),
            pltpu.SemaphoreType.DMA((count,)),
            pltpu.SemaphoreType.DMA((count, 3)),
            pltpu.SemaphoreType.DMA((count, 3)),
            pltpu.SemaphoreType.DMA((count, 3)),
            pltpu.SemaphoreType.DMA((count, 3)),
            pltpu.SemaphoreType.DMA((6,)),
            pltpu.SemaphoreType.DMA((6,)),
        ]

    def bind(self, ins, shared, small_in, outs, small_out, handed_in, handed_out, scratch):
        count, groups, names = len(self.parts), len(self.shared_shapes), self.names
        refs = list(scratch)

        def take(number):
            taken = refs[:number]
            del refs[:number]
            return taken

        self.shared, self.small_in, self.outs, self.small_out = shared, small_in, outs, small_out
        self.held = dict(zip(names, take(len(names)), strict=True))
        for name, place in self.after.items():
            self.held[name] = self.held[place]
        self.gathered = take(groups)
        self.own, self.first_in = take(count), take(count)
        self.second_in, self.third_in = take(count), take(count)
        self.slabs, self.slab_in = take(count), take(count)
        self.total, self.small, self.small_came = take(3)
        load_sem, self.share_send, self.share_recv, own_sem, hand_sem = take(5)
        self.send_sem, self.recv_sem = take(2)
        self.last_send, self.last_recv, self.small_send, self.small_recv = take(4)
        item, column = lax.axis_index("dp"), lax.axis_index("seq")
        self.column = column
        self.bits = [lax.rem(item, 2), lax.rem(item // 2, 2), item // 4]
        self.partners = [(item + (1 - 2 * self.bits[k]) * (1 << k), column) for k in range(3)]
        self.peers = [(item, lax.rem(column + k, 4)) for k in range(1, 4)]
        self.owner = (2 * column + item // 4, lax.rem(item, 4))
        self.feeder = (4 * lax.rem(item, 2) + column, item // 2)
        self.elsewhere = jnp.logical_or(self.owner[0] != item, self.owner[1] != column)
        self.loads = {
            name: pltpu.make_async_copy(ins[i], self.held[name], load_sem.at[i])
            for i, name in enumerate(names)
        }
        self.own_shares = [
            pltpu.make_async_copy(
                self.columns_of(g, column), self.gathered[g].at[column], own_sem.at[g]
            )
            for g in range(groups)
        ]
        self.ready = set()
        self.others = {}
        self.handing = {
            index: pltpu.make_async_copy(ref, self.own[index], hand_sem.at[index])
            for index, ref in zip(self.entering, handed_in, strict=True)
        }
        for index, ref in zip(self.leaving, handed_out, strict=True):
            half = self.own[index].at[self.half(index, True)]
            self.handing[index] = pltpu.make_async_copy(half, ref, hand_sem.at[index])

    def greet(self):
        barrier = pltpu.get_barrier_semaphore()
        for partner in self.partners + self.peers:
            pl.semaphore_signal(barrier, inc=1, device_id=partner, device_id_type=MESH)
        waits = 6
        if self.has_rows:
            waits = 6 + self.elsewhere.astype(jnp.int32)

            @pl.when(self.elsewhere)
            def _():
                pl.semaphore_signal(barrier, inc=1, device_id=self.feeder, device_id_type=MESH)

        pl.semaphore_wait(barrier, waits)

    def load(self):
        for index in self.entering:
            self.handing[index].start()
        for name in self.names:
            if name not in self.after:
                self.loads[name].start()

    def remote(self, source, target_ref, send, recv, target):
        return pltpu.make_async_remote_copy(
            src_ref=source,
            dst_ref=target_ref,
            send_sem=send,
            recv_sem=recv,
            device_id=target,
            device_id_type=MESH,
        )

    def columns_of(self, group, place):
        _, wide, first, narrow = self.shared_shapes[group]
        start = first_tile(place, wide // TILE) * TILE + first
        return self.shared[group].at[:, pl.ds(pl.multiple_of(start, TILE), narrow)]

    def shares(self, group):
        return [
            self.remote(
                self.columns_of(group, peer[1]),
                self.gathered[group].at[self.column],
                self.share_send.at[group, k],
                self.share_recv.at[group, k],
                peer,
            )
            for k, peer in enumerate(self.peers)
        ]

    def share(self):
        for group in range(len(self.shared_shapes)):
            self.own_shares[group].start()
            for copy in self.shares(group):
                copy.start()

    def operand(self, name):
        if isinstance(name, int):
            if name not in self.ready:
                self.own_shares[name].wait()
                for copy in self.shares(name):
                    copy.wait()
            self.ready.add(name)
            ref = self.gathered[name]
            return ref[...].reshape(4 * ref.shape[1], ref.shape[2])
        first = name not in self.ready
        self.ready.add(name)
        if name in self.others:
            ref, wait = self.others[name]
            if first:
                wait()
            return ref[...].reshape(-1, ref.shape[-1])
        if first:
            self.loads[name].wait()
        return self.held[name][...]

    def multiply(self, index):
        part = self.parts[index]
        left, right = self.operand(part.left), self.operand(part.right)
        right = right[:, part.start : part.start + part.columns]
        if part.bias:
            sums = jnp.sum(right.astype(F32), axis=0, keepdims=True)
            for tile in range(part.columns // TILE):
                row = part.at // TILE + tile
                self.small[0, row : row + 1] = sums[:, tile * TILE : (tile + 1) * TILE]
        own, rows = self.own[index], part.rows
        if part.in_lanes:
            self.total[: left.shape[1], : part.columns] = over_first(left, right)
            for d in range(8):
                start = d // 2 * LANES + d % 2 * rows
                own[d // 4, d // 2 % 2, d % 2] = self.cut(start, rows, part.slab, part.columns)
            return
        step = 3 * TILE
        for start in range(0, left.shape[1], step):
            product = over_first(left[:, start : start + step], right).astype(BF16)
            for d in range(8):
                low, high = max(start, d * rows), min(start + step, (d + 1) * rows)
                if low < high:
                    place = slice(low - d * rows, high - d * rows)
                    own[d // 4, d // 2 % 2, d % 2, place] = product[low - start : high - start]

    def cut(self, start, rows, padded, columns):
        values = self.total[start : start + rows, :columns]
        if padded > rows:
            values = jnp.concatenate([values, jnp.zeros((padded - rows, columns), F32)], axis=0)
        return values.astype(BF16)

    def half(self, index, mine):
        order = self.parts[index].order
        pick = self.bits[order] if mine else 1 - self.bits[order]
        return (slice(None), slice(None), pick) if order == 0 else (slice(None), pick)

    def place(self, index, high, low):
        if self.parts[index].enter:
            return (high, low)
        if self.parts[index].order == 0:
            return (high, low, self.bits[0])
        return (high, self.bits[1], low)

    def stage(self, index, step):
        order = self.parts[index].order
        other = 1 - order
        sems = self.send_sem.at[index, step], self.recv_sem.at[index, step]
        own = self.own[index]
        if step == 0:
            source = own.at[self.half(index, False)]
            return self.remote(source, self.first_in[index], *sems, self.partners[order])
        if step == 1:
            place = self.place(index, slice(None), 1 - self.bits[other])
            return self.remote(own.at[place], self.second_in[index], *sems, self.partners[other])
        place = self.place(index, 1 - self.bits[2], self.bits[other])
        return self.remote(own.at[place], self.third_in[index], *sems, self.partners[2])

    def begin(self, index):
        if self.parts[index].enter:
            self.handing[index].wait()
            self.stage(index, 1).start()
            return
        self.multiply(index)
        self.stage(index, 0).start()

    def end_first(self, index):
        self.stage(index, 0).wait()
        for high in range(2):
            for low in range(2):
                place = self.place(index, high, low)
                came = self.first_in[index][high, low].astype(F32)
                self.own[index][place] = (self.own[index][place].astype(F32) + came).astype(BF16)
        if self.parts[index].leave:
            self.handing[index].start()
        else:
            self.stage(index, 1).start()

    def end_second(self, index):
        self.stage(index, 1).wait()
        for high in range(2):
            place = self.place(index, high, self.bits[1 - self.parts[index].order])
            came = self.second_in[index][high].astype(F32)
            self.own[index][place] = (self.own[index][place].astype(F32) + came).astype(BF16)
        self.stage(index, 2).start()

    def last(self, index):
        if self.parts[index].by_rows:
            sems = self.last_send.at[index, 0], self.last_recv.at[index, 0]
            return [self.remote(self.slabs[index], self.slab_in[index], *sems, self.owner)]
        return [
            self.remote(
                self.slabs[index].at[peer[1]],
                self.slab_in[index].at[self.column],
                self.last_send.at[index, k],
                self.last_recv.at[index, k],
                peer,
            )
            for k, peer in enumerate(self.peers)
        ]

    def end_third(self, index):
        part = self.parts[index]
        self.stage(index, 2).wait()
        place = self.place(index, self.bits[2], self.bits[1 - part.order])
        sums = self.own[index][place].astype(F32) + self.third_in[index][...].astype(F32)
        if part.by_rows:
            self.slabs[index][...] = sums.astype(BF16)

            @pl.when(self.elsewhere)
            def _():
                self.last(index)[0].start()

            @pl.when(jnp.logical_not(self.elsewhere))
            def _():
                self.slab_in[index][...] = self.slabs[index][...]

            return
        self.total[: part.rows, : part.columns] = sums
        rows = part.rows // 4
        for k in range(4):
            self.slabs[index][k] = self.cut(k * rows, rows, padded_rows(rows), part.columns)
        for copy in self.last(index):
            copy.start()
        self.slab_in[index][self.column] = self.slabs[index][self.column]

    def end_last(self, index):
        part = self.parts[index]
        out, stop = self.outs[part.out], part.at + part.columns
        if part.by_rows:

            @pl.when(self.elsewhere)
            def _():
                self.last(index)[0].wait()

            out[:, part.at : stop] = self.slab_in[index][...].astype(F32)[: part.rows]
            return
        for copy in self.last(index):
            copy.wait()
        rows = part.rows // 4
        wide = out.shape[-1]
        for k in range(4):
            values = self.slab_in[index][k].astype(F32)[:rows]
            if len(out.shape) == 3:
                out[k, :, part.at : stop] = values
            else:
                start = first_tile(k, wide // TILE) * TILE
                out[:, start + part.at : start + stop] = values

    def small_step(self, step):
        if step < 3:
            sems = self.small_send.at[step], self.small_recv.at[step]
            return [
                self.remote(self.small.at[step], self.small_came.at[step], *sems, self.partners[step])
            ]
        return [
            self.remote(
                self.small.at[3],
                self.small_out.at[self.column],
                self.small_send.at[3 + k],
                self.small_recv.at[3 + k],
                peer,
            )
            for k, peer in enumerate(self.peers)
        ]

    def end_small(self, at):
        self.small_step(at - 1)[0].wait()
        self.small[at] = self.small[at - 1] + self.small_came[at - 1]
        for copy in self.small_step(at):
            copy.start()

    def do(self, *steps):
        kinds = {
            "b": self.begin,
            "f": self.end_first,
            "s": self.end_second,
            "t": self.end_third,
            "l": self.end_last,
            "x": self.small_exchange,
            "r": lambda number: self.loads[self.names[number]].start(),
        }
        for step in steps:
            kinds[step[0]](int(step[1:]))

    def small_exchange(self, at):
        if at == 0:
            self.small_step(0)[0].start()
        elif at < 4:
            self.end_small(at)
        else:
            self.small_out[self.column] = self.small[3]
            for copy in self.small_step(3):
                copy.wait()

    def end(self):
        for index in self.leaving:
            self.handing[index].wait()


def split(refs, *counts):
    groups, start = [], 0
    for number in counts:
        groups.append(refs[start : start + number])
        start += number
    return groups + [refs[start:]]


LAST_STEPS = (
    ("b0", "b1", "b2", "b3", "b4"),
    ("s0", "s3", "s1"),
    ("b5", "s4", "t0", "s2"),
    ("t3", "b6", "t1", "f5"),
    ("t4", "l0", "l3", "t2", "x0", "l1"),
    ("f6", "x1", "l4", "s5", "l2", "x2", "t5", "x3", "s6", "l5", "t6", "x4", "l6"),
)


def last_grads(parts, arrays, shared, small, handed, out_shapes, condition, embed, rows_a, rows_b, mods):
    names = tuple(arrays)
    shapes = [value.shape + (first, columns) for value, first, columns in shared]
    sums = GradSums(parts, names, shapes, small.shape)
    count = len(out_shapes)
    width = condition.shape[1]

    def kernel(*refs):
        ins, given, handed_in, given_mods, (small_in, seen, embed_in, low, high), outs, lasts, refs = split(
            refs, len(names), len(shared), len(handed), len(mods), 5, count, 2
        )
        (small_out, condition_out), held, (mod_sem,), scratch = lasts, refs[:2], refs[2:3], refs[3:]
        sums.bind(ins, given, small_in, outs, small_out, handed_in, [], scratch)
        sums.load()
        loads = [
            pltpu.make_async_copy(source, target, mod_sem.at[k])
            for k, (source, target) in enumerate(zip(given_mods, held, strict=True))
        ]
        start_all(loads)
        sums.greet()
        sums.share()
        sums.small[0] = small_in[...]
        first, rest = held
        condition_out[...] = jnp.zeros_like(condition_out)
        work = [
            (low, 0, first, 0, 2 * width),
            (high, 0, first, 2 * width, width),
            (high, width, rest, 0, 2 * width),
            (high, 3 * width, first, 3 * width, width),
        ]
        for number, steps in enumerate(LAST_STEPS):
            sums.do(*steps)
            if number == 0:
                wait_all(loads)
            if number < 4:
                rows, at, weights, start, columns = work[number]
                condition_out[...] += over_rows(
                    rows[:, at : at + columns], weights[:, start : start + columns]
                )
            if number == 4:
                values = seen[...].astype(F32) + embed_in[...]
                condition_out[...] = condition_out[...] * silu_slope(values)
        sums.end()

    vmem, anywhere = pl.BlockSpec(memory_space=pltpu.VMEM), pl.BlockSpec(memory_space=pl.ANY)
    return pl.pallas_call(
        kernel,
        out_shape=[jax.ShapeDtypeStruct(shape, F32) for shape in out_shapes]
        + [
            jax.ShapeDtypeStruct((4,) + small.shape, F32),
            jax.ShapeDtypeStruct(condition.shape, F32),
        ],
        in_specs=[anywhere] * (len(names) + len(shared) + len(handed) + len(mods)) + [vmem] * 5,
        out_specs=[vmem] * (count + 2),
        scratch_shapes=[pltpu.VMEM(value.shape, BF16) for value in mods]
        + [pltpu.SemaphoreType.DMA((len(mods),))]
        + sums.scratch([value.shape for value in arrays.values()]),
        compiler_params=pltpu.CompilerParams(
            collective_id=SUM_ID, has_side_effects=True, vmem_limit_bytes=63 * 2**20
        ),
        name="last_grads",
    )(
        *arrays.values(),
        *[value for value, _, _ in shared],
        *handed,
        *mods,
        small,
        condition,
        embed,
        rows_a,
        rows_b,
    )


BACK_STEPS = {
    "start": ("b0", "b1", "b2", "b3", "b4", "b5", "r3", "s1", "s0", "s3", "t1"),
    "gathered": ("b6", "b7"),
    "head0": ("f2", "l1", "t0", "t3"),
    "head1": ("s2", "s4", "f5", "f6", "l0", "l3"),
    "head2": ("f7", "t4", "b8", "s5"),
    "head3": ("b11", "b12", "t2", "l4", "b9"),
    "put1": ("b10", "s6", "s7", "x0"),
    "put3": ("t5", "f8", "l2", "x1", "t6", "t7", "l5", "f11", "x2"),
    "end": ("f9", "x3", "l6", "l7", "f12", "f10", "x4"),
}


def pack_heads(lanes_ref, packed_ref):
    rows, count = lanes_ref.shape[0], lanes_ref.shape[1] // LANES
    lane = lax.broadcasted_iota(jnp.int32, (rows, LANES), 1)
    for tile in range(packed_ref.shape[1] // LANES):
        values = jnp.zeros((rows, LANES), F32)
        for head in range(count):
            start = head * HD - tile * LANES
            if -HD < start < LANES:
                one = lanes_ref[:, head * LANES : (head + 1) * LANES].astype(F32)
                one = pltpu.roll(one, start % LANES, 1) if start else one
                values = jnp.where(jnp.logical_and(lane >= start, lane < start + HD), one, values)
        packed_ref[:, tile * LANES : (tile + 1) * LANES] = values.astype(BF16)


def back_kernel(sums, own, outs, refs):
    grad_in, rows_in, heads_in, w_qkv_in, w_out_in, cosine, ahead, behind, q_gain, k_gain = own[:10]
    grad_middle, tokens, scale = own[10:]
    tokens_out, mod_out, gains_out = outs
    (branch_all, rows, heads, w_qkv, w_out, grad_heads, packed, load_sem), refs = refs[:8], refs[8:]
    gather = RowGather(grad_in, branch_all, *refs[:3])
    row_sums = RowSums(*refs[3:])
    local_rows = grad_in.shape[0]
    count = grad_heads.shape[1] // LANES
    factor = HD ** (-0.5)
    loads = [
        pltpu.make_async_copy(source, target, load_sem.at[k])
        for k, (source, target) in enumerate(
            ((rows_in, rows), (w_out_in, w_out), (w_qkv_in, w_qkv))
        )
    ]

    def load_head(head):
        return [
            pltpu.make_async_copy(
                heads_in.at[:, pl.ds((k * count + head) * LANES, LANES)],
                heads.at[head % 2, k],
                load_sem.at[3 + 2 * (head % 2) + k],
            )
            for k in range(2)
        ]

    for k in (1, 0, 2):
        loads[k].start()
    start_all(load_head(0))
    sums.load()
    sums.greet()
    gather.start()
    sums.share()
    sums.small[0] = jnp.zeros_like(sums.small[0])
    sums.others["grad_branch_a"] = (branch_all, lambda: None)
    sums.others["grad_project"] = (packed, lambda: None)
    sums.do(*BACK_STEPS["start"])
    gather.pass_on()
    gather.end()
    loads[1].wait()
    grad_branch = branch_all[...].reshape(4 * local_rows, branch_all.shape[2])
    grad_heads[...] = over_rows(grad_branch, w_out[...]).astype(BF16)
    sums.do(*BACK_STEPS["gathered"])
    loads[0].wait()
    tables = cosine[...], ahead[...], behind[...]
    block = 256
    gain_sums = [jnp.zeros((1, LANES), F32), jnp.zeros((1, LANES), F32)]
    for head in range(count):
        spans = [slice((k * count + head) * LANES, (k * count + head + 1) * LANES) for k in range(3)]
        if head + 1 < count:
            start_all(load_head(head + 1))
        keys, values = rows[:, spans[1]], rows[:, spans[2]]
        grad_query, grad_key, grad_value = [], None, None
        for start in range(0, rows.shape[0], block):
            queries = rows[start : start + block, spans[0]]
            grads = grad_heads[start : start + block, spans[0]]
            exp_scores = jnp.exp(over_rows(keys, queries) * factor)
            probs = exp_scores * (1.0 / jnp.sum(exp_scores, axis=0, keepdims=True))
            grad_probs = over_rows(values, grads)
            inner = jnp.sum(probs * grad_probs, axis=0, keepdims=True)
            grad_scores = (probs * (grad_probs - inner)).astype(BF16)
            grad_query.append(over_first(grad_scores, keys))
            key_term = jnp.dot(grad_scores, queries, preferred_element_type=F32)
            value_term = jnp.dot(probs.astype(BF16), grads, preferred_element_type=F32)
            grad_key = key_term if grad_key is None else grad_key + key_term
            grad_value = value_term if grad_value is None else grad_value + value_term
        rows[:, spans[2]] = grad_value.astype(BF16)
        terms = (jnp.concatenate(grad_query, axis=0) * factor, grad_key * factor)
        wait_all(load_head(head))
        for k, (term, gain) in enumerate(zip(terms, (q_gain, k_gain), strict=True)):
            raw = heads[head % 2, k]
            inverse = head_inverse(raw)
            normed = raw * inverse
            back = rotated(term, tables, -1)
            gain_sums[k] = gain_sums[k] + jnp.sum(back * normed, axis=0, keepdims=True)
            back = back * gain[...]
            mean = jnp.sum(back * normed, axis=-1, keepdims=True) * (1.0 / HD)
            rows[:, spans[k]] = (inverse * (back - normed * mean)).astype(BF16)
        if head == count - 1:
            pack_heads(rows, packed)
        sums.do(*BACK_STEPS["head%d" % head])
    gains_out[...] = jnp.concatenate(gain_sums + [jnp.zeros((6, LANES), F32)], axis=0)
    loads[2].wait()
    for index in range(4):
        part = pl.ds(pl.multiple_of(row_sums.order[index] * local_rows, local_rows), local_rows)
        row_sums.put(index, over_rows(rows[part, :], w_qkv[...]))
        sums.do(*BACK_STEPS.get("put%d" % index, ()))
    grad_hidden = row_sums.sums()
    values = tokens[...].astype(F32)
    inverse = inverse_rms(values)
    normed = values * inverse
    tokens_out[...] = grad_middle[...] + rms_back(grad_hidden * (1.0 + scale[...]), normed, inverse)
    width = values.shape[1]
    mod_out[:, :width] = grad_hidden.astype(BF16)
    mod_out[:, width:] = (grad_hidden * normed).astype(BF16)
    sums.do(*BACK_STEPS["end"])
    sums.end()


def attention_back(own, parts, arrays, shared, small_shape, handed, out_shapes):
    names = tuple(arrays)
    shapes = [value.shape + (first, columns) for value, first, columns in shared]
    sums = GradSums(parts, names, shapes, small_shape, {"hidden_a": "hidden_b"})
    count = len(out_shapes)
    rows, width = own[0].shape
    kept, heads, w_qkv, w_out = own[1:5]
    leaving = [parts[index].handed() for index in sums.leaving]
    vmem, anywhere = pl.BlockSpec(memory_space=pltpu.VMEM), pl.BlockSpec(memory_space=pl.ANY)
    own_scratch = [
        pltpu.VMEM((4, rows, width), BF16),
        pltpu.VMEM(kept.shape, BF16),
        pltpu.VMEM((2, 2, 4 * rows, LANES), F32),
        pltpu.VMEM(w_qkv.shape, BF16),
        pltpu.VMEM(w_out.shape, BF16),
        pltpu.VMEM((4 * rows, w_out.shape[0]), BF16),
        pltpu.VMEM((4 * rows, -(-3 * width // 4 // LANES) * LANES), BF16),
        pltpu.SemaphoreType.DMA((7,)),
        *RowGather.scratch(),
        *RowSums.scratch(rows, width),
    ]

    def kernel(*refs):
        ins, exchanged, handed_in, given, outs, handed_out, (small_out,), results, mine, scratch = split(
            refs,
            len(names),
            len(shared),
            len(handed),
            len(own),
            count,
            len(leaving),
            1,
            3,
            len(own_scratch),
        )
        sums.bind(ins, exchanged, None, outs, small_out, handed_in, handed_out, scratch)
        back_kernel(sums, given, results, mine)

    return pl.pallas_call(
        kernel,
        out_shape=[jax.ShapeDtypeStruct(shape, F32) for shape in out_shapes]
        + [jax.ShapeDtypeStruct(shape, BF16) for shape in leaving]
        + [
            jax.ShapeDtypeStruct((4,) + small_shape, F32),
            jax.ShapeDtypeStruct((rows, width), F32),
            jax.ShapeDtypeStruct((rows, 2 * width), BF16),
            jax.ShapeDtypeStruct((8, LANES), F32),
        ],
        in_specs=[anywhere] * (len(names) + len(shared) + len(handed))
        + [vmem]
        + [anywhere] * 4
        + [vmem] * 8,
        out_specs=[vmem] * count + [anywhere] * len(leaving) + [vmem] * 4,
        scratch_shapes=own_scratch + sums.scratch([value.shape for value in arrays.values()]),
        compiler_params=pltpu.CompilerParams(
            collective_id=BACK_ID, has_side_effects=True, vmem_limit_bytes=63 * 2**20
        ),
        name="attention_back",
    )(*arrays.values(), *[value for value, _, _ in shared], *handed, *own)


def to_owners(rows):
    n_dp, n_seq = lax.axis_size("dp"), lax.axis_size("seq")
    pairs = []
    for d in range(n_dp):
        for s in range(n_seq):
            pairs.append((d * n_seq + s, s * n_dp + d))
    return lax.ppermute(rows, ("dp", "seq"), pairs)


def plain_sums(left, right, blocks):
    mine = lax.psum_scatter(outer_sum(left, right).astype(BF16), "dp", scatter_dimension=0, tiled=True)
    return (columns_to_rows(mine, blocks) if blocks else to_owners(mine)).astype(F32)


def padded_small(values):
    values = jnp.pad(values, ((0, 8 - values.shape[0]), (0, TILE - values.shape[1])))
    return jnp.concatenate([jnp.zeros((8, TILE), F32), values])


def again(part):
    span = (part.start, part.start + part.columns)
    kinds = {"by_rows": part.by_rows, "enter": True}
    return Part(None, None, part.rows, span, part.out, part.order, at=part.at, **kinds)


def bias_columns(small, tiles):
    edges = [first_tile(k, tiles) for k in range(4)] + [tiles]
    sums = small.reshape(4, -1)
    return [sums[k, : (edges[k + 1] - edges[k]) * TILE] for k in range(4)]


def in_lanes(values, axis):
    shape = values.shape
    values = values.reshape(shape[:axis] + (shape[axis] // HD, HD) + shape[axis + 1 :])
    pads = [(0, 0)] * len(values.shape)
    pads[axis + 1] = (0, LANES - HD)
    return jnp.pad(values, pads).reshape(shape[:axis] + (-1,) + shape[axis + 1 :])


def out_of_lanes(values):
    return values.reshape(values.shape[0], -1, LANES)[:, :, :HD]


def plain_back(grad_branch_a, given):
    kept, projected, w_qkv, w_out, cosine, ahead, behind, q_gain, k_gain = given
    patches, count = kept.shape[0], w_out.shape[0] // LANES
    factor = HD ** (-0.5)
    tables = [table[:, None, :] for table in (cosine, ahead, behind)]

    def turn(values):
        turned = jnp.roll(values, -QUARTER, -1) * tables[1] + jnp.roll(values, QUARTER, -1) * tables[2]
        return values * tables[0] - turned

    query, key, value = jnp.split(kept.reshape(patches, 3 * count, LANES), 3, axis=1)
    grads = times_transpose(grad_branch_a, w_out).astype(BF16).reshape(patches, count, LANES)
    scores = jnp.einsum("qhd,khd->hqk", query, key, preferred_element_type=F32) * factor
    exp_scores = jnp.exp(scores)
    probs = exp_scores / jnp.sum(exp_scores, axis=-1, keepdims=True)
    grad_probs = jnp.einsum("qhd,khd->hqk", grads, value, preferred_element_type=F32)
    inner = jnp.sum(probs * grad_probs, axis=-1, keepdims=True)
    grad_scores = (probs * (grad_probs - inner)).astype(BF16)
    terms = (
        jnp.einsum("hqk,khd->qhd", grad_scores, key, preferred_element_type=F32) * factor,
        jnp.einsum("hqk,qhd->khd", grad_scores, query, preferred_element_type=F32) * factor,
    )
    grad_value = jnp.einsum("hqk,qhd->khd", probs.astype(BF16), grads, preferred_element_type=F32)
    raws = jnp.split(projected.reshape(patches, 2 * count, LANES), 2, axis=1)
    results, gains = [], []
    for term, raw, gain in zip(terms, raws, (q_gain, k_gain), strict=True):
        inverse = head_inverse(raw)
        normed = raw * inverse
        back = turn(term)
        gains.append(jnp.sum(back * normed, axis=(0, 1)))
        back = back * gain[0]
        mean = jnp.sum(back * normed, axis=-1, keepdims=True) * (1.0 / HD)
        results.append(inverse * (back - normed * mean))
    grad_lanes = jnp.concatenate(results + [grad_value], axis=1).reshape(kept.shape).astype(BF16)
    return grad_lanes, times_transpose(grad_lanes, w_qkv), jnp.stack(gains)


def shards(
    tokens,
    condition,
    cotangent,
    w_qkv,
    w_out,
    w_gate,
    w_up,
    w_down,
    w_mod,
    b_mod,
    q_gain,
    k_gain,
    noise_counts,
    time_steps,
    positions,
):
    local_rows, width = tokens.shape[1:]
    ways = lax.axis_size("seq")
    patches = local_rows * ways
    local_heads = HEADS // ways
    item = lax.axis_index("dp")
    running = jnp.cumsum(noise_counts)
    image_id = jnp.sum((running <= item).astype(jnp.int32))
    chosen = jnp.arange(noise_counts.shape[0], dtype=jnp.int32) == image_id
    share = 1.0 / jnp.sum(jnp.where(chosen, noise_counts, 0)).astype(F32)

    embed = time_embed(time_steps, width)
    bias_row = b_mod[None]
    share_row = jnp.full((1, width), share)
    (
        mod_first,
        w_qkv_lanes,
        scale_a,
        gate_a,
        gate_b,
        hidden_a,
        lifted_full,
        own_branch_b,
        lifted_low,
        all_positions,
    ) = first_stage(
        w_mod, w_qkv, condition[0], tokens[0], cotangent[0], embed, share_row, bias_row, positions[:, 0]
    )
    hidden_a = hidden_a.reshape(patches, width)
    lifted_full = lifted_full.reshape(patches, width)
    w_qkv_lanes = w_qkv_lanes.reshape(width, w_qkv_lanes.shape[2])
    tables = lane_tables(jnp.transpose(all_positions, (1, 0, 2)).reshape(2, patches))
    w_out_lanes = in_lanes(w_out, 0)
    gain_lanes = [jnp.pad(gain, (0, LANES - HD))[None] for gain in (q_gain, k_gain)]
    (
        projected_lanes,
        rows_lanes,
        attended_lanes,
        branch_a,
        mod_rest,
        gate_cols,
        up_cols,
        scale_b,
        middle,
        hidden_b,
        grads_all,
    ) = attend(
        hidden_a,
        w_qkv_lanes,
        w_out_lanes,
        tables,
        *gain_lanes,
        w_mod,
        w_gate,
        w_up,
        lifted_low,
        bias_row,
        tokens[0],
        gate_a,
        own_branch_b,
    )
    grad_branch_b = grads_all.reshape(patches, width)
    pieces = lax.axis_size("dp") == 8
    ff, heads_wide, own_rows = w_down.shape[0], local_heads * HD, width // 8
    handed_mlp = [
        split_part("inner", "grad_branch_b", ff // 8, width, 0, 0, by_rows=True, leave=True),
        split_part("hidden_b", "grad_gate_in", own_rows, ff, 1, 1, leave=True),
    ]
    handed_mlp = [handed_mlp[k % 2][k // 2] for k in range(4)] if pieces else []
    hidden_b, inner, grad_gate_in, grad_up_in, block_out, grad_middle, own_branch_a, grad_mod_b, *handed = mlp(
        hidden_b,
        grads_all,
        gate_cols,
        up_cols,
        w_down,
        (middle, scale_b, gate_a, gate_b, branch_a, cotangent[0], share_row),
        handed_mlp,
    )
    hidden_b = hidden_b.reshape(patches, width)
    mod_first, mod_rest = mod_first.reshape(width, -1), mod_rest.reshape(width, -1)
    given = [rows_lanes, projected_lanes, w_qkv_lanes, w_out_lanes, *tables, *gain_lanes]
    if pieces:
        tiles_b, tiles_a = grad_mod_b.shape[1] // TILE, 2 * width // TILE
        mod_b, mod_a = -(-tiles_b // 4) * TILE, -(-tiles_a // 4) * TILE
        third = mod_b // 3
        late_a = mod_a // 2 // TILE * TILE
        ups = split_part("hidden_b", "grad_up_in", own_rows, ff, 2, 0)
        lasts = split_part("hidden_a", "grad_project", own_rows, 3 * heads_wide, 1, 1, leave=True)
        mods = [
            Part("lifted", k, own_rows, (0, third), 0, 0, at=k * third, bias=True, leave=True)
            for k in range(3)
        ]
        downs, gates = handed_mlp[0::2], handed_mlp[1::2]
        parts_b = [
            again(downs[0]),
            again(gates[0]),
            ups[0],
            again(downs[1]),
            again(gates[1]),
            ups[1],
            *split_part("attended", "grad_branch_a", heads_wide // 8, width, 3, 1, by_rows=True, in_lanes=True),
            *mods,
            *lasts,
        ]
        arrays_b = {
            "hidden_b": hidden_b,
            "grad_up_in": grad_up_in,
            "attended": attended_lanes,
            "hidden_a": hidden_a,
            "lifted": lifted_full,
        }
        shapes_b = [
            (ff // 8, width),
            (own_rows // 4, 4 * ff),
            (own_rows // 4, 4 * ff),
            (heads_wide // 8, width),
        ]
        own = [own_branch_a, *given, grad_middle, tokens[0], scale_a]
        (
            grad_w_down,
            grad_w_gate,
            grad_w_up,
            grad_w_out,
            *handed,
            small_b,
            grad_tokens,
            grad_mod_a,
            gain_sums,
        ) = attention_back(
            own,
            parts_b,
            arrays_b,
            [(grad_mod_b, k * third, third) for k in range(3)],
            (16, LANES),
            [handed[k] for k in (0, 1, 2, 3)],
            shapes_b,
        )
        parts_a = [again(part) for part in mods + lasts]
        spans = ((0, mod_a - late_a), (mod_a - late_a, mod_a))
        parts_a += [
            Part("lifted", k, own_rows, (0, span[1] - span[0]), 2, 0, at=span[0], bias=True)
            for k, span in enumerate(spans)
        ]
        shapes_a = [
            (own_rows // 4, tiles_b * TILE),
            (4, own_rows // 4, 3 * heads_wide),
            (own_rows // 4, tiles_a * TILE),
        ]
        sum_b, qkv_sum, sum_a, small_a, grad_condition = last_grads(
            parts_a,
            {"lifted": lifted_full},
            [(grad_mod_a, span[0], span[1] - span[0]) for span in spans],
            padded_small(gain_sums[:2]),
            handed,
            shapes_a,
            condition[0],
            embed,
            grad_mod_a,
            grad_mod_b,
            [mod_first, mod_rest],
        )
        grad_w_qkv = jnp.transpose(
            qkv_sum.reshape(4, own_rows // 4, 3, heads_wide), (1, 2, 0, 3)
        ).reshape(own_rows // 4, 3 * width)
        grad_w_mod = jnp.concatenate([sum_a, sum_b], axis=1)
        bias = jnp.concatenate(bias_columns(small_a, tiles_a) + bias_columns(small_b, tiles_b))
        own_bias = bias.shape[0] // (8 * ways)
        sum_bias = lax.dynamic_slice(
            bias, ((item * ways + lax.axis_index("seq")) * own_bias,), (own_bias,)
        )
        gains = jnp.sum(small_a[:, 8:10, :HD], axis=0)
    else:
        tokens_f = tokens[0].astype(F32)
        inverse_a = inverse_rms(tokens_f)
        normed_a = tokens_f * inverse_a
        grad_branch_a = gather_rows(own_branch_a)
        grad_lanes, partial, gain_sums = plain_back(grad_branch_a, given)
        grad_hidden_a = scatter_rows(partial)
        grad_tokens = grad_middle + rms_back(grad_hidden_a * (1.0 + scale_a), normed_a, inverse_a)
        grad_mod_a = jnp.concatenate([grad_hidden_a, grad_hidden_a * normed_a], axis=-1).astype(BF16)
        grad_mod_first = jnp.concatenate([grad_mod_a, grad_mod_b[:, :width], grad_mod_b[:, 3 * width :]], axis=1)
        grad_condition = (
            times_transpose(grad_mod_first, mod_first)
            + times_transpose(grad_mod_b[:, width : 3 * width], mod_rest)
        ) * silu_slope(condition[0].astype(F32) + embed)
        grad_project = out_of_lanes(grad_lanes).reshape(patches, 3 * heads_wide)
        gain_sums = gain_sums[:2, :HD]
        mod_rows = jnp.concatenate([grad_mod_a, grad_mod_b], axis=1)
        grad_w_down = plain_sums(inner, grad_branch_b, 0)
        grad_w_gate = plain_sums(hidden_b, grad_gate_in, 1)
        grad_w_up = plain_sums(hidden_b, grad_up_in, 1)
        grad_w_qkv = plain_sums(hidden_a, grad_project, 3)
        attended = out_of_lanes(attended_lanes).reshape(patches, heads_wide)
        grad_w_out = plain_sums(attended, grad_branch_a, 0)
        grad_w_mod = plain_sums(lifted_full, rows_to_columns(mod_rows, 6), 6)
        bias_rows = jnp.sum(mod_rows, axis=0, dtype=F32)
        sum_bias = lax.psum_scatter(bias_rows, ("dp", "seq"), scatter_dimension=0, tiled=True)
        gains = lax.psum(gain_sums, ("dp", "seq"))
    sum_q_gain, sum_k_gain = gains[0], gains[1]
    return (
        block_out[None],
        grad_tokens[None],
        grad_condition[None],
        grad_w_qkv,
        grad_w_out,
        grad_w_gate,
        grad_w_up,
        grad_w_down,
        grad_w_mod,
        sum_bias,
        sum_q_gain,
        sum_k_gain,
    )


def solution(mesh):
    placed = (
        P("dp", "seq", None),
        P("dp", "seq", None),
        P("dp", "seq", None),
        P("seq", None),
        P("seq", None),
        P("seq", None),
        P("seq", None),
        P("seq", None),
        P("seq", None),
        P(),
        P(),
        P(),
        P(),
        P("dp"),
        P(None, "dp", "seq"),
    )
    return jax.shard_map(
        shards,
        mesh=mesh,
        in_specs=placed,
        out_specs=(
            P("dp", "seq", None),
            P("dp", "seq", None),
            P("dp", "seq", None),
            P(("dp", "seq"), None),
            P(("dp", "seq"), None),
            P(("dp", "seq"), None),
            P(("dp", "seq"), None),
            P(("dp", "seq"), None),
            P(("dp", "seq"), None),
            P(("dp", "seq")),
            P(),
            P(),
        ),
        check_vma=False,
    )
```

```python
import math

import jax
import jax.numpy as jnp
from jax import lax
from jax.experimental import pallas as pl
from jax.experimental.pallas import tpu as pltpu
from jax.sharding import PartitionSpec as P

HEADS = 16
HD = 72
EPSILON = 1e-06
BF16 = jnp.bfloat16
F32 = jnp.float32


def inverse_rms(values):
    return lax.rsqrt(jnp.mean(values * values, axis=-1, keepdims=True) + EPSILON)


def rms_back(grad_in, normed, inverse):
    return inverse * (grad_in - normed * jnp.mean(grad_in * normed, axis=-1, keepdims=True))


def silu_slope(values):
    logistic = jax.nn.sigmoid(values)
    return logistic * (1.0 + values * (1.0 - logistic))


def time_embed(steps, width):
    half_width = width // 2
    frequency = jnp.exp(-math.log(10000.0) * jnp.arange(half_width, dtype=F32) / half_width)
    angles = steps.astype(F32)[:, None] * frequency[None, :]
    return jnp.concatenate([jnp.cos(angles), jnp.sin(angles)], axis=-1)


def rope_tables(positions, head_size):
    quarter = head_size // 4
    frequency = jnp.exp(-math.log(10000.0) * jnp.arange(quarter, dtype=F32) / quarter)
    along_rows = positions[0].astype(F32)[..., None] * frequency
    along_cols = positions[1].astype(F32)[..., None] * frequency
    angles = jnp.concatenate([along_rows, along_rows, along_cols, along_cols], axis=-1)
    return (jnp.cos(angles)[..., None, :], jnp.sin(angles)[..., None, :])


def quarter_turn(values):
    first, second, third, fourth = jnp.split(values, 4, axis=-1)
    return jnp.concatenate([-second, first, -fourth, third], axis=-1)


def rotate_heads(values, cosine, sine):
    return values * cosine + quarter_turn(values) * sine


def unrotate(grad_in, cosine, sine):
    return grad_in * cosine - quarter_turn(grad_in * sine)


def matmul(left, right):
    return jnp.dot(left, right, preferred_element_type=F32)


def outer_sum(left, right):
    return jnp.einsum("ra,rb->ab", left, right, preferred_element_type=F32)


def times_transpose(left, right):
    return jnp.einsum("rb,ab->ra", left, right, preferred_element_type=F32)


MESH = pl.DeviceIdType.MESH
SUM_ID, GATHER_ID, SCATTER_ID, WEIGHT_ID, ATTEND_ID, BACK_ID, MLP_ID = 1, 2, 3, 4, 5, 6, 7


def greet(partners):
    barrier = pltpu.get_barrier_semaphore()
    for partner in partners:
        pl.semaphore_signal(barrier, inc=1, device_id=partner, device_id_type=MESH)
    pl.semaphore_wait(barrier, len(partners))


def group_partners():
    item, column = lax.axis_index("dp"), lax.axis_index("seq")
    core = lax.rem(column, 2)
    return (item, column + 1 - 2 * core), (item, lax.rem(column + 2, 4))


GATHER_PIECES = 4


def gather_kernel(own_ref, out_ref, local_sem, send_sem, recv_sem):
    column = lax.axis_index("seq")
    sibling, across = group_partners()
    greet([sibling, across])
    local = pltpu.make_async_copy(own_ref, out_ref.at[column], local_sem)
    local.start()
    rows = own_ref.shape[0] // GATHER_PIECES

    def remote(source, place, piece, kind, target):
        part = pl.ds(piece * rows, rows)
        return pltpu.make_async_remote_copy(
            src_ref=source.at[part],
            dst_ref=out_ref.at[place, part],
            send_sem=send_sem.at[kind, piece],
            recv_sem=recv_sem.at[kind, piece],
            device_id=target,
            device_id_type=MESH,
        )

    far = lax.rem(column + 2, 4)
    pieces = range(GATHER_PIECES)
    over = [remote(own_ref, column, piece, 0, across) for piece in pieces]
    beside = [remote(own_ref, column, piece, 1, sibling) for piece in pieces]
    onward = [remote(out_ref.at[far], far, piece, 2, sibling) for piece in pieces]
    for copy in over:
        copy.start()
    for copy in beside:
        copy.start()
    for piece in pieces:
        over[piece].wait_recv()
        onward[piece].start()
    for piece in pieces:
        over[piece].wait_send()
        beside[piece].wait()
        onward[piece].wait()
    local.wait()


def gather_rows(values):
    rows, columns = values.shape
    gathered = pl.pallas_call(
        gather_kernel,
        out_shape=jax.ShapeDtypeStruct((4, rows, columns), values.dtype),
        in_specs=[pl.BlockSpec(memory_space=pltpu.VMEM)],
        out_specs=pl.BlockSpec(memory_space=pltpu.VMEM),
        scratch_shapes=[
            pltpu.SemaphoreType.DMA,
            pltpu.SemaphoreType.DMA((3, GATHER_PIECES)),
            pltpu.SemaphoreType.DMA((3, GATHER_PIECES)),
        ],
        compiler_params=pltpu.CompilerParams(
            collective_id=GATHER_ID, has_side_effects=True, vmem_limit_bytes=48 * 2**20
        ),
        name="gather_rows",
    )(values)
    return gathered.reshape(4 * rows, columns)


def scatter_kernel(parts_ref, out_ref, near, low, far, send_sem, recv_sem):
    column = lax.axis_index("seq")
    core, chip = lax.rem(column, 2), column // 2
    sibling, across = group_partners()
    greet([sibling, across])
    rows = out_ref.shape[0] // 2

    def remote(source, target_ref, index, target):
        return pltpu.make_async_remote_copy(
            src_ref=source,
            dst_ref=target_ref,
            send_sem=send_sem.at[index],
            recv_sem=recv_sem.at[index],
            device_id=target,
            device_id_type=MESH,
        )

    parts = [pl.ds(piece * rows, rows) for piece in range(2)]
    beside = [
        remote(parts_ref.at[1 - chip, 1 - core, part], near.at[0, part], i, sibling)
        for i, part in enumerate(parts)
    ]
    beside.append(remote(parts_ref.at[chip, 1 - core], near.at[1], 2, sibling))
    for copy in beside:
        copy.start()
    over = [remote(low.at[part], far.at[part], 3 + i, across) for i, part in enumerate(parts)]
    for i, part in enumerate(parts):
        beside[i].wait_recv()
        pair = parts_ref[1 - chip, core, part].astype(F32) + near[0, part].astype(F32)
        low[part] = pair.astype(BF16)
        over[i].start()
    beside[2].wait_recv()
    out_ref[...] = parts_ref[chip, core].astype(F32) + near[1].astype(F32)
    for i, part in enumerate(parts):
        over[i].wait()
        out_ref[part] += far[part].astype(F32)
    for copy in beside:
        copy.wait_send()


def scatter_rows(partial):
    rows, columns = partial.shape[0] // 4, partial.shape[1]
    return pl.pallas_call(
        scatter_kernel,
        out_shape=jax.ShapeDtypeStruct((rows, columns), F32),
        in_specs=[pl.BlockSpec(memory_space=pltpu.VMEM)],
        out_specs=pl.BlockSpec(memory_space=pltpu.VMEM),
        scratch_shapes=[
            pltpu.VMEM((2, rows, columns), BF16),
            pltpu.VMEM((rows, columns), BF16),
            pltpu.VMEM((rows, columns), BF16),
            pltpu.SemaphoreType.DMA((5,)),
            pltpu.SemaphoreType.DMA((5,)),
        ],
        compiler_params=pltpu.CompilerParams(
            collective_id=SCATTER_ID, has_side_effects=True, vmem_limit_bytes=48 * 2**20
        ),
        name="scatter_rows",
    )(partial.astype(BF16).reshape(2, 2, rows, columns))


TILE = 128
LANES = 128
QUARTER = HD // 4
FIRST_ROWS = 80


class WeightImport:
    def __init__(self, blocks, ranges):
        self.blocks, self.ranges = blocks, ranges
        self.arrays = sorted({block[0] for block in blocks})

    def scratch(self):
        count = len(self.blocks)
        return [
            pltpu.SemaphoreType.DMA((8,)),
            pltpu.SemaphoreType.DMA((count, 7)),
            pltpu.SemaphoreType.DMA((count, 7)),
        ]

    def bind(self, ins, outs, scratch):
        self.ins, self.outs = ins, outs
        self.own_sem, self.send_sem, self.recv_sem = scratch
        item, column = lax.axis_index("dp"), lax.axis_index("seq")
        core, chip = lax.rem(column, 2), column // 2
        self.item, self.column = item, column
        self.y_bit, self.z_bit = lax.rem(item, 2), lax.rem(item // 2, 2)
        self.sibling = (item, column + 1 - 2 * core)
        self.y_near = (item + 1 - 2 * self.y_bit, column)
        self.z_near = (item + 2 - 4 * self.z_bit, column)
        self.far = [(1 - chip) * 2 + k for k in (core, 1 - core)]
        self.half_rows = ins[0].shape[0] // 2

    def partners(self):
        across = [(self.item, place) for place in self.far]
        return across + [self.sibling, self.y_near, self.z_near]

    def copy(self, source, target_ref, block, kind, target):
        return pltpu.make_async_remote_copy(
            src_ref=source,
            dst_ref=target_ref,
            send_sem=self.send_sem.at[block, kind],
            recv_sem=self.recv_sem.at[block, kind],
            device_id=target,
            device_id_type=MESH,
        )

    def source_column(self, column):
        for start, stop in self.ranges:
            if column < stop - start:
                return start + column
            column -= stop - start

    def piece(self, ref, block, y_pick, z_pick, first_row=0, rows=None, base=0, outside=False):
        array, _, start, columns = self.blocks[block]
        step = columns
        if array == 0 and outside:
            step = self.source_column(start + columns) - self.source_column(start)
            start = self.source_column(start)
        rows = self.half_rows if rows is None else rows
        return ref.at[
            pl.ds(pl.multiple_of(z_pick * self.half_rows + first_row, 16), rows),
            pl.ds(pl.multiple_of(base + start + y_pick * step, TILE), columns),
        ]

    def mine_for(self, array, place):
        ref = self.ins[array]
        if len(ref.shape) == 3:
            return ref.at[place], 0
        return ref, 0 if array == 0 else place * self.outs[array].shape[2]

    def whole(self, array, place):
        ref, base = self.mine_for(array, place)
        columns = self.outs[array].shape[2]
        if ref.shape[-1] == columns:
            return ref
        return ref.at[:, pl.ds(pl.multiple_of(base, TILE), columns)]

    def over(self, block):
        array, offset, _, _ = self.blocks[block]
        goal = self.far[offset or 0]
        ref, base = self.mine_for(array, goal)
        source = self.piece(ref, block, self.y_bit, self.z_bit, base=base, outside=True)
        target = self.piece(self.outs[array].at[self.column], block, self.y_bit, self.z_bit)
        return self.copy(source, target, block, 0, (self.item, goal))

    def onward(self, block, kind):
        array, offset, _, _ = self.blocks[block]
        ref = self.outs[array].at[self.far[offset or 0]]
        if kind == 1:
            part, target = self.piece(ref, block, self.y_bit, self.z_bit), self.y_near
        elif kind == 2:
            part, target = self.piece(ref, block, self.y_bit, self.z_bit), self.z_near
        elif kind == 3:
            part = self.piece(ref, block, 1 - self.y_bit, self.z_bit, 0, FIRST_ROWS)
            target = self.z_near
        else:
            rest = self.half_rows - FIRST_ROWS
            part = self.piece(ref, block, self.y_bit, 1 - self.z_bit, FIRST_ROWS, rest)
            target = self.y_near
        return self.copy(part, part, block, kind, target)

    def share(self, block):
        _, _, start, columns = self.blocks[block]
        part = self.outs[0].at[self.far[0], :, pl.ds(start, 2 * columns)]
        return self.copy(part, part, block, 5, self.sibling)

    def spans(self, array, place):
        target = self.outs[array].at[self.column]
        if array:
            return [(self.whole(array, place), target)]
        pairs, at = [], 0
        for start, stop in self.ranges:
            columns = stop - start
            pairs.append((self.ins[0].at[:, pl.ds(start, columns)], target.at[:, pl.ds(at, columns)]))
            at += columns
        return pairs

    def beside(self, array):
        index = self.arrays.index(array)
        return [
            self.copy(source, target, index + 2 * k, 6, self.sibling)
            for k, (source, target) in enumerate(self.spans(array, self.sibling[1]))
        ]

    def own(self, array):
        return [
            pltpu.make_async_copy(source, target, self.own_sem.at[array + 4 * k])
            for k, (source, target) in enumerate(self.spans(array, self.column))
        ]

    def steps(self):
        count = len(self.blocks)
        todo = []
        for step in range(count + 3):
            if step < count:
                todo.append(lambda step=step: self.arrive(step))
            if 0 <= step - 1 < count:
                todo.append(lambda step=step: self.pass_on(step - 1))
            if 0 <= step - 2 < count:
                todo.append(lambda step=step: self.complete(step - 2))
        return todo

    def arrive(self, step):
        self.over(step).wait_recv()
        self.onward(step, 1).start()
        self.onward(step, 2).start()

    def pass_on(self, step):
        self.onward(step, 1).wait_recv()
        self.onward(step, 3).start()
        self.onward(step, 2).wait_recv()
        self.onward(step, 4).start()

    def complete(self, step):
        self.onward(step, 3).wait_recv()
        self.onward(step, 4).wait_recv()
        if self.blocks[step][0] == 0:
            self.share(step).start()

    def end(self):
        for block in range(len(self.blocks)):
            self.over(block).wait_send()
            for kind in range(1, 5):
                self.onward(block, kind).wait_send()
            if self.blocks[block][0] == 0:
                self.share(block).wait_send()


class RowGather:
    def __init__(self, own, everyone, local_sem, send_sem, recv_sem):
        self.own, self.everyone = own, everyone
        self.local_sem, self.send_sem, self.recv_sem = local_sem, send_sem, recv_sem
        self.column = lax.axis_index("seq")
        self.far = lax.rem(self.column + 2, 4)
        self.sibling, self.across = group_partners()

    def remote(self, source, place, piece, kind, target):
        rows = self.own.shape[0] // GATHER_PIECES
        part = pl.ds(piece * rows, rows)
        return pltpu.make_async_remote_copy(
            src_ref=source.at[part],
            dst_ref=self.everyone.at[place, part],
            send_sem=self.send_sem.at[kind, piece],
            recv_sem=self.recv_sem.at[kind, piece],
            device_id=target,
            device_id_type=MESH,
        )

    def over(self, piece):
        return self.remote(self.own, self.column, piece, 0, self.across)

    def beside(self, piece):
        return self.remote(self.own, self.column, piece, 1, self.sibling)

    def onward(self, piece):
        return self.remote(self.everyone.at[self.far], self.far, piece, 2, self.sibling)

    def local(self):
        return pltpu.make_async_copy(self.own, self.everyone.at[self.column], self.local_sem)

    def start(self):
        for piece in range(GATHER_PIECES):
            self.over(piece).start()
        for piece in range(GATHER_PIECES):
            self.beside(piece).start()
        self.local().start()

    def pass_on(self):
        for piece in range(GATHER_PIECES):
            self.over(piece).wait_recv()
            self.onward(piece).start()

    def end(self):
        for piece in range(GATHER_PIECES):
            self.over(piece).wait_send()
            self.beside(piece).wait()
            self.onward(piece).wait()
        self.local().wait()

    @staticmethod
    def scratch():
        return [
            pltpu.SemaphoreType.DMA,
            pltpu.SemaphoreType.DMA((3, GATHER_PIECES)),
            pltpu.SemaphoreType.DMA((3, GATHER_PIECES)),
        ]


def first_import(width):
    wide = 3 * HEADS // 4 * LANES
    blocks = [(0, None, 0, width), (0, None, 2 * width, width), (1, 0, 0, wide // 2), (1, 1, 0, wide // 2)]
    return WeightImport(blocks, [(0, 3 * width), (5 * width, 6 * width)])


def second_import(width, ff):
    blocks = [(0, None, 0, width)] + [(k, j, 0, ff // 2) for k in (2, 3) for j in (0, 1)]
    return WeightImport(blocks, [(3 * width, 5 * width)])


def spread_heads(w_ref, lanes_ref):
    rows = w_ref.shape[0]
    valid = lax.broadcasted_iota(jnp.int32, (rows, LANES), 1) < HD
    for head in range(3 * HEADS):
        kind, device, place = head // HEADS, head % HEADS // 4, head % 4
        start = head * HD // LANES * LANES
        stop = min(start + 2 * LANES, w_ref.shape[1])
        window = w_ref[:, start:stop].astype(F32)
        shift = head * HD - start
        if shift:
            window = pltpu.roll(window, window.shape[1] - shift, 1)
        target = (kind * 4 + place) * LANES
        lanes_ref[device, :, target : target + LANES] = jnp.where(
            valid, window[:, :LANES], 0.0
        ).astype(BF16)


def start_all(copies):
    for copy in copies:
        copy.start()


def wait_all(copies):
    for copy in copies:
        copy.wait()


def first_kernel(imports, *refs):
    (w_mod, w_qkv, condition, tokens, cotangent, embed, share, bias, positions), refs = refs[:9], refs[9:]
    (mod_out, qkv_out, scale_a, gate_a, gate_b), refs = refs[:5], refs[5:]
    (hidden_all, lifted_all, grads, lifted, positions_all), refs = refs[:5], refs[5:]
    (mod_all, lanes, hidden, mod_sem, spot_send, spot_recv), refs = refs[:6], refs[6:]
    imports.bind({0: w_mod, 1: lanes}, {0: mod_all, 1: qkv_out}, refs[:3])
    gather = RowGather(hidden, hidden_all, *refs[3:6])
    gather_lifted = RowGather(lifted, lifted_all, *refs[6:9])
    item, column = lax.axis_index("dp"), lax.axis_index("seq")
    width = tokens.shape[1]
    greet(imports.partners())
    imports.over(0).start()
    start_all(imports.own(0))
    start_all(imports.beside(0))
    peers = [(item, lax.rem(column + k, 4)) for k in range(1, 4)]
    spot_copies = [
        pltpu.make_async_remote_copy(
            src_ref=positions,
            dst_ref=positions_all.at[column],
            send_sem=spot_send.at[k],
            recv_sem=spot_recv.at[k],
            device_id=peer,
            device_id_type=MESH,
        )
        for k, peer in enumerate(peers)
    ]
    start_all(spot_copies)
    positions_all[column] = positions[...]
    spread_heads(w_qkv, lanes)
    for block in range(1, len(imports.blocks)):
        imports.over(block).start()
    start_all(imports.own(1))
    start_all(imports.beside(1))
    values = condition[...].astype(F32) + embed[...]
    lifted[...] = (values * jax.nn.sigmoid(values)).astype(BF16)
    imports.arrive(0)
    imports.pass_on(0)
    imports.arrive(1)
    imports.complete(0)
    wait_all(imports.own(0))
    for copy in imports.beside(0):
        copy.wait_recv()

    def modulate(block):
        imports.share(block).wait_recv()
        start = imports.blocks[block][2]
        weights = mod_all[:, :, start : start + 2 * width].reshape(-1, 2 * width)
        modulation = jnp.dot(lifted[...], weights, preferred_element_type=F32)
        return [
            modulation[:, k * width : (k + 1) * width]
            + bias[:, pl.ds(imports.source_column(start + k * width), width)]
            for k in range(2)
        ]

    shift, scale = modulate(0)
    scale_a[...] = scale
    values = tokens[...].astype(F32)
    normed = values * inverse_rms(values)
    hidden[...] = (normed * (1.0 + scale) + shift).astype(BF16)
    gather.start()
    gather_lifted.start()
    imports.pass_on(1)
    imports.arrive(2)
    imports.complete(1)
    imports.arrive(3)
    store = pltpu.make_async_copy(mod_all, mod_out, mod_sem)
    gate_a[...], gate = modulate(1)
    store.start()
    gate_b[...] = gate
    grads[...] = (cotangent[...].astype(F32) * share[...] * gate).astype(BF16)
    imports.pass_on(2)
    imports.pass_on(3)
    gather.pass_on()
    imports.complete(2)
    imports.complete(3)
    gather_lifted.pass_on()
    imports.end()
    for copy in imports.beside(0):
        copy.wait_send()
    wait_all(imports.beside(1))
    wait_all(imports.own(1))
    gather.end()
    gather_lifted.end()
    wait_all(spot_copies)
    store.wait()


def first_stage(w_mod, w_qkv, condition, tokens, cotangent, embed, share, bias, positions):
    rows, width = tokens.shape
    depth, lanes = w_mod.shape[0], 3 * HEADS // 4 * LANES
    imports = first_import(width)
    vmem, anywhere = pl.BlockSpec(memory_space=pltpu.VMEM), pl.BlockSpec(memory_space=pl.ANY)

    def kernel(*refs):
        first_kernel(imports, *refs)

    return pl.pallas_call(
        kernel,
        out_shape=[
            jax.ShapeDtypeStruct((4, depth, 4 * width), BF16),
            jax.ShapeDtypeStruct((4, depth, lanes), BF16),
            jax.ShapeDtypeStruct((rows, width), F32),
            jax.ShapeDtypeStruct((rows, width), F32),
            jax.ShapeDtypeStruct((rows, width), F32),
            jax.ShapeDtypeStruct((4, rows, width), BF16),
            jax.ShapeDtypeStruct((4, rows, width), BF16),
            jax.ShapeDtypeStruct((rows, width), BF16),
            jax.ShapeDtypeStruct((rows, width), BF16),
            jax.ShapeDtypeStruct((4,) + positions.shape, jnp.int32),
        ],
        in_specs=[anywhere] + [vmem] * 8,
        out_specs=[anywhere, anywhere] + [vmem] * 8,
        scratch_shapes=[
            pltpu.VMEM((4, depth, 4 * width), BF16),
            pltpu.VMEM((4, depth, lanes), BF16),
            pltpu.VMEM((rows, width), BF16),
            pltpu.SemaphoreType.DMA,
            pltpu.SemaphoreType.DMA((3,)),
            pltpu.SemaphoreType.DMA((3,)),
        ]
        + imports.scratch()
        + RowGather.scratch() * 2,
        compiler_params=pltpu.CompilerParams(
            collective_id=WEIGHT_ID, has_side_effects=True, vmem_limit_bytes=60 * 2**20
        ),
        name="first_stage",
    )(w_mod, w_qkv, condition, tokens, cotangent, embed, share, bias, positions)


def rotated(values, tables, sign):
    cosine, ahead, behind = tables
    turned = pltpu.roll(values, LANES - QUARTER, 1) * ahead + pltpu.roll(values, QUARTER, 1) * behind
    return values * cosine + turned if sign > 0 else values * cosine - turned


def lane_tables(positions):
    lane = jnp.arange(LANES)[None, :]
    frequency = jnp.exp(-math.log(10000.0) * (lane % QUARTER).astype(F32) / QUARTER)
    places = jnp.where(lane < 2 * QUARTER, positions[0][:, None], positions[1][:, None])
    angles = places.astype(F32) * frequency
    valid, takes_ahead = lane < HD, lane // QUARTER % 2 == 0
    cosine, sine = jnp.where(valid, jnp.cos(angles), 0.0), jnp.where(valid, jnp.sin(angles), 0.0)
    return [cosine, jnp.where(takes_ahead, -sine, 0.0), jnp.where(takes_ahead, 0.0, sine)]


def head_inverse(values):
    return lax.rsqrt(jnp.sum(values * values, axis=-1, keepdims=True) * (1.0 / HD) + EPSILON)


def over_rows(left, right):
    return lax.dot_general(left, right, (((1,), (1,)), ((), ())), preferred_element_type=F32)


def over_first(left, right):
    return lax.dot_general(left, right, (((0,), (0,)), ((), ())), preferred_element_type=F32)


class RowSums:
    def __init__(self, blocks, near, low, far, send_sem, recv_sem):
        column = lax.axis_index("seq")
        self.column = column
        self.core, self.chip = lax.rem(column, 2), column // 2
        self.sibling, self.across = group_partners()
        self.blocks, self.near, self.low, self.far = blocks, near, low, far
        self.send_sem, self.recv_sem = send_sem, recv_sem
        self.order = [
            (1 - self.chip) * 2 + 1 - self.core,
            (1 - self.chip) * 2 + self.core,
            self.chip * 2 + 1 - self.core,
            column,
        ]

    def copy(self, source, target_ref, index, target):
        return pltpu.make_async_remote_copy(
            src_ref=source,
            dst_ref=target_ref,
            send_sem=self.send_sem.at[index],
            recv_sem=self.recv_sem.at[index],
            device_id=target,
            device_id_type=MESH,
        )

    def beside(self, index):
        return self.copy(self.blocks.at[index], self.near.at[index], index, self.sibling)

    def over(self):
        return self.copy(self.low, self.far, 2, self.across)

    def put(self, index, values):
        if index == 0 or index == 2:
            self.blocks[index // 2] = values.astype(BF16)
            self.beside(index // 2).start()
        elif index == 1:
            self.beside(0).wait_recv()
            self.low[...] = (values + self.near[0].astype(F32)).astype(BF16)
            self.over().start()
        else:
            self.own = values

    def sums(self):
        self.beside(1).wait_recv()
        total = self.own + self.near[1].astype(F32)
        self.over().wait()
        total = total + self.far[...].astype(F32)
        self.beside(0).wait_send()
        self.beside(1).wait_send()
        return total

    @staticmethod
    def scratch(rows, columns):
        return [
            pltpu.VMEM((2, rows, columns), BF16),
            pltpu.VMEM((2, rows, columns), BF16),
            pltpu.VMEM((rows, columns), BF16),
            pltpu.VMEM((rows, columns), BF16),
            pltpu.SemaphoreType.DMA((3,)),
            pltpu.SemaphoreType.DMA((3,)),
        ]


def attend_kernel(imports, *refs):
    (hidden, w_qkv, w_out, cosine, ahead, behind, q_gain, k_gain), refs = refs[:8], refs[8:]
    (w_mod, w_gate, w_up, lifted, bias, tokens, gate_a, grads), refs = refs[:8], refs[8:]
    (heads_out, rows_out, attended_out, branch_out), refs = refs[:4], refs[4:]
    (mod_out, gate_out, up_out, scale_out, middle_out, hidden_out, grads_all), refs = refs[:7], refs[7:]
    (mod_all, gate_own, up_own, mod_sem, load_sem), refs = refs[:5], refs[5:]
    sums = RowSums(*refs[:6])
    imports.bind({0: w_mod, 2: w_gate, 3: w_up}, {0: mod_all, 2: gate_out, 3: up_out}, refs[6:9])
    gather = RowGather(grads, grads_all, *refs[9:])
    greet(imports.partners())
    for block in range(len(imports.blocks)):
        imports.over(block).start()
    start_all(imports.own(0))
    loads = [
        pltpu.make_async_copy(imports.whole(k, sums.column), ref, load_sem.at[k - 2])
        for k, ref in ((2, gate_own), (3, up_own))
    ]
    stores = [
        pltpu.make_async_copy(ref, imports.outs[k].at[sums.column], load_sem.at[k])
        for k, ref in ((2, gate_own), (3, up_own))
    ]
    for copy in loads:
        copy.start()
    for array in imports.arrays:
        start_all(imports.beside(array))
    gather.start()
    todo = imports.steps()

    def aside(number):
        for _ in range(min(number, len(todo))):
            todo.pop(0)()

    factor = HD ** (-0.5)
    rows = branch_out.shape[0]
    heads = attended_out.shape[1] // LANES
    tables = cosine[...], ahead[...], behind[...]
    for pair in range(3 * heads // 2):
        span = slice(pair * 2 * LANES, (pair + 1) * 2 * LANES)
        projected = jnp.dot(hidden[...], w_qkv[:, span], preferred_element_type=F32)
        if pair >= heads:
            rows_out[:, span] = projected.astype(BF16)
            continue
        heads_out[:, span] = projected
        gain = (q_gain if pair < heads // 2 else k_gain)[...]
        for half in range(2):
            values = projected[:, half * LANES : (half + 1) * LANES]
            values = values * head_inverse(values) * gain
            start = pair * 2 * LANES + half * LANES
            rows_out[:, start : start + LANES] = rotated(values, tables, 1).astype(BF16)
    aside(1)
    for copy in loads:
        copy.wait()
    for copy in stores:
        copy.start()
    for index in range(4):
        block = pl.ds(pl.multiple_of(sums.order[index] * rows, rows), rows)
        for head in range(heads):
            spans = [slice((k * heads + head) * LANES, (k * heads + head + 1) * LANES) for k in range(3)]
            exp_scores = jnp.exp(over_rows(rows_out[block, spans[0]], rows_out[:, spans[1]]) * factor)
            scale = 1.0 / jnp.sum(exp_scores, axis=1, keepdims=True)
            mixed = jnp.dot(
                (exp_scores * scale).astype(BF16),
                rows_out[:, spans[2]],
                preferred_element_type=F32,
            )
            attended_out[block, spans[0]] = mixed.astype(BF16)
        sums.put(index, jnp.dot(attended_out[block, :], w_out[...], preferred_element_type=F32))
        aside((1, 3, 4, len(todo))[index])
    gather.pass_on()
    wait_all(imports.own(0))
    for copy in imports.beside(0):
        copy.wait_recv()
    imports.share(0).wait_recv()
    store = pltpu.make_async_copy(mod_all, mod_out, mod_sem)
    store.start()
    width = tokens.shape[1]
    weights = mod_all[...].reshape(-1, 2 * width)
    modulation = jnp.dot(lifted[...], weights, preferred_element_type=F32)
    modulation = modulation + bias[:, pl.ds(imports.source_column(0), 2 * width)]
    scale = modulation[:, width:]
    scale_out[...] = scale
    branch = sums.sums()
    branch_out[...] = branch
    middle = tokens[...].astype(F32) + gate_a[...] * branch
    middle_out[...] = middle
    hidden_out[...] = (middle * inverse_rms(middle) * (1.0 + scale) + modulation[:, :width]).astype(BF16)
    imports.end()
    for copy in imports.beside(0):
        copy.wait_send()
    for array in imports.arrays[1:]:
        wait_all(imports.beside(array))
    gather.end()
    for copy in stores:
        copy.wait()
    store.wait()


def attend(hidden, w_qkv, w_out, tables, q_gain, k_gain, w_mod, w_gate, w_up, lifted, bias, tokens, gate_a, grads):
    patches, wide = hidden.shape[0], w_qkv.shape[1]
    rows, width = patches // 4, hidden.shape[1]
    depth, ff = w_mod.shape[0], w_gate.shape[1] // 4
    imports = second_import(width, ff)
    vmem, anywhere = pl.BlockSpec(memory_space=pltpu.VMEM), pl.BlockSpec(memory_space=pl.ANY)

    def kernel(*refs):
        attend_kernel(imports, *refs)

    return pl.pallas_call(
        kernel,
        out_shape=[
            jax.ShapeDtypeStruct((patches, wide * 2 // 3), F32),
            jax.ShapeDtypeStruct((patches, wide), BF16),
            jax.ShapeDtypeStruct((patches, wide // 3), BF16),
            jax.ShapeDtypeStruct((rows, width), F32),
            jax.ShapeDtypeStruct((4, depth, 2 * width), BF16),
            jax.ShapeDtypeStruct((4, depth, ff), BF16),
            jax.ShapeDtypeStruct((4, depth, ff), BF16),
            jax.ShapeDtypeStruct((rows, width), F32),
            jax.ShapeDtypeStruct((rows, width), F32),
            jax.ShapeDtypeStruct((rows, width), BF16),
            jax.ShapeDtypeStruct((4, rows, width), BF16),
        ],
        in_specs=[vmem] * 8 + [anywhere] * 3 + [vmem] * 5,
        out_specs=[vmem] * 4 + [anywhere] * 3 + [vmem] * 4,
        scratch_shapes=[
            pltpu.VMEM((4, depth, 2 * width), BF16),
            pltpu.VMEM((depth, ff), BF16),
            pltpu.VMEM((depth, ff), BF16),
            pltpu.SemaphoreType.DMA,
            pltpu.SemaphoreType.DMA((4,)),
        ]
        + RowSums.scratch(rows, width)
        + imports.scratch()
        + RowGather.scratch(),
        compiler_params=pltpu.CompilerParams(
            collective_id=ATTEND_ID, has_side_effects=True, vmem_limit_bytes=63 * 2**20
        ),
        name="attend",
    )(hidden, w_qkv, w_out, *tables, q_gain, k_gain, w_mod, w_gate, w_up, lifted, bias, tokens, gate_a, grads)


def mlp_kernel(sums, *refs):
    (hidden, grads_all, w_gate, w_up, w_down), refs = refs[:5], refs[5:]
    (middle, scale, gate_a, gate_b, branch_a, cotangent, share), refs = refs[:7], refs[7:]
    (hidden_all, inner, grad_gate, grad_up), refs = refs[:4], refs[4:]
    (block_out, middle_out, branch_grad_out, mod_out), refs = refs[:4], refs[4:]
    handed_out, refs = refs[: len(sums.leaving)], refs[len(sums.leaving) :]
    if sums.parts:
        sums.bind([], [], None, [], None, [], handed_out, refs[30:])
    sums.others = {
        "inner": (inner, lambda: None),
        "grad_branch_b": (grads_all, lambda: None),
        "hidden_b": (hidden_all, lambda: None),
        "grad_gate_in": (grad_gate, lambda: None),
    }
    gather = RowGather(hidden, hidden_all, *refs[:3])
    halves = [RowSums(*refs[3 + 6 * k : 9 + 6 * k]) for k in range(4)]
    sums_grad, sums_branch = halves[:2], halves[2:]
    first = sums_grad[0]
    greet([first.sibling, first.across] + (sums.partners[:2] if sums.parts else []))
    gather.start()
    rows, width = hidden.shape
    near, far = first.chip * 2, (1 - first.chip) * 2
    depth = w_gate.shape[0] * w_gate.shape[1]
    gate_weights, up_weights = (ref[...].reshape(depth, ref.shape[2]) for ref in (w_gate, w_up))

    def block(ref, pair, start, count):
        return jnp.concatenate([ref[pair + k, start : start + count] for k in range(2)], axis=0)

    def process(pair, start, count):
        values = block(hidden_all, pair, start, count)
        gate_in = jnp.dot(values, gate_weights, preferred_element_type=F32)
        up_in = jnp.dot(values, up_weights, preferred_element_type=F32)
        grad_inner = over_rows(block(grads_all, pair, start, count), w_down[...])
        logistic = jax.nn.sigmoid(gate_in)
        activated = gate_in * logistic
        slope = logistic * (1.0 + gate_in * (1.0 - logistic))
        results = (
            (activated * up_in).astype(BF16),
            (grad_inner * up_in * slope).astype(BF16),
            (grad_inner * activated).astype(BF16),
        )
        for ref, result in zip((inner, grad_gate, grad_up), results, strict=True):
            for k in range(2):
                at = pl.multiple_of((pair + k) * rows + start, 16)
                ref[pl.ds(at, count), :] = result[k * count : (k + 1) * count]
        return over_rows(results[1], gate_weights) + over_rows(results[2], up_weights)

    def put(sums, partial, count, far_rows):
        @pl.when(first.core == 0)
        def _():
            held[0, :count], held[1, :count] = partial[count:], partial[:count]

        @pl.when(first.core == 1)
        def _():
            held[0, :count], held[1, :count] = partial[:count], partial[count:]

        if far_rows:
            sums.put(0, held[0, :count])
            sums.put(1, held[1, :count])
        else:
            sums.put(2, held[0, :count])
            return held[1, :count]

    held, own_grad, own_branch = refs[27:30]
    half = rows // 2
    for piece in range(GATHER_PIECES):
        gather.beside(piece).wait_recv()
    gather.local().wait()
    partial = process(near, 0, rows)
    for k in range(2):
        part = slice(k * half, (k + 1) * half)
        both = jnp.concatenate([partial[part], partial[rows + k * half : rows + (k + 1) * half]], axis=0)
        own_grad[part] = put(sums_grad[k], both, half, False)
    for k in range(2):
        pieces = range(k * GATHER_PIECES // 2, (k + 1) * GATHER_PIECES // 2)
        for piece in pieces:
            gather.over(piece).wait_recv()
            gather.onward(piece).start()
        for piece in pieces:
            gather.onward(piece).wait_recv()
        put(sums_grad[k], process(far, k * half, half), half, True)
    sums.do(*["b0", "b1"][: len(sums.parts)])
    for k in range(2):
        at = [pl.ds(pl.multiple_of((far + j) * rows + k * half, 16), half) for j in range(2)]
        values = jnp.concatenate([inner[part, :] for part in at], axis=0)
        put(sums_branch[k], jnp.dot(values, w_down[...], preferred_element_type=F32), half, True)
    sums.do(*["b2", "b3"][: len(sums.parts)])
    for k in range(2):
        at = [pl.ds(pl.multiple_of((near + j) * rows + k * half, 16), half) for j in range(2)]
        values = jnp.concatenate([inner[part, :] for part in at], axis=0)
        partial = jnp.dot(values, w_down[...], preferred_element_type=F32)
        own_branch[k * half : (k + 1) * half] = put(sums_branch[k], partial, half, False)
    sums.do(*["f0", "f1"][: len(sums.parts)])
    for k in range(2):
        part = slice(k * half, (k + 1) * half)
        sums_grad[k].put(3, own_grad[part])
        grad_hidden = sums_grad[k].sums()
        values = middle[part]
        inverse = inverse_rms(values)
        normed = values * inverse
        grad_out = cotangent[part].astype(F32) * share[...]
        grad_middle = grad_out + rms_back(grad_hidden * (1.0 + scale[part]), normed, inverse)
        middle_out[part] = grad_middle
        branch_grad_out[part] = (grad_middle * gate_a[part]).astype(BF16)
        mod_out[part, :width] = (grad_middle * branch_a[part]).astype(BF16)
        mod_out[part, width : 2 * width] = grad_hidden.astype(BF16)
        mod_out[part, 2 * width : 3 * width] = (grad_hidden * normed).astype(BF16)
    sums.do(*["f2", "f3"][: len(sums.parts)])
    for k in range(2):
        part = slice(k * half, (k + 1) * half)
        sums_branch[k].put(3, own_branch[part])
        branch = sums_branch[k].sums()
        block_out[part] = (middle[part] + gate_b[part] * branch).astype(BF16)
        grad_out = cotangent[part].astype(F32) * share[...]
        mod_out[part, 3 * width :] = (grad_out * branch).astype(BF16)
    for piece in range(GATHER_PIECES):
        gather.over(piece).wait_send()
        gather.beside(piece).wait_send()
        gather.onward(piece).wait_send()
    sums.end()


def mlp(hidden, grads_all, w_gate, w_up, w_down, rest, parts):
    rows, width = hidden.shape
    ff = w_down.shape[0]
    sums = GradSums(parts, (), [], (16, LANES))
    vmem, anywhere = pl.BlockSpec(memory_space=pltpu.VMEM), pl.BlockSpec(memory_space=pl.ANY)

    def kernel(*refs):
        mlp_kernel(sums, *refs)

    return pl.pallas_call(
        kernel,
        out_shape=[
            jax.ShapeDtypeStruct((4, rows, width), BF16),
            jax.ShapeDtypeStruct((4 * rows, ff), BF16),
            jax.ShapeDtypeStruct((4 * rows, ff), BF16),
            jax.ShapeDtypeStruct((4 * rows, ff), BF16),
            jax.ShapeDtypeStruct((rows, width), BF16),
            jax.ShapeDtypeStruct((rows, width), F32),
            jax.ShapeDtypeStruct((rows, width), BF16),
            jax.ShapeDtypeStruct((rows, 4 * width), BF16),
        ]
        + [jax.ShapeDtypeStruct(part.handed(), BF16) for part in parts],
        in_specs=[vmem] * 12,
        out_specs=[vmem] * 8 + [anywhere] * len(parts),
        scratch_shapes=RowGather.scratch()
        + RowSums.scratch(rows // 2, width) * 4
        + [
            pltpu.VMEM((2, rows // 2, width), F32),
            pltpu.VMEM((rows, width), F32),
            pltpu.VMEM((rows, width), F32),
        ]
        + (sums.scratch([]) if parts else []),
        compiler_params=pltpu.CompilerParams(
            collective_id=MLP_ID, has_side_effects=True, vmem_limit_bytes=63 * 2**20
        ),
        name="mlp",
    )(hidden, grads_all, w_gate, w_up, w_down, *rest)


def rows_to_columns(values, blocks):
    rows, columns = values.shape
    ways = lax.axis_size("seq")
    values = values.reshape(rows, blocks, ways, columns // (blocks * ways))
    moved = lax.all_to_all(values, "seq", split_axis=2, concat_axis=0, tiled=True)
    return moved.reshape(rows * ways, columns // ways)


def columns_to_rows(values, blocks):
    rows, columns = values.shape
    ways = lax.axis_size("seq")
    values = values.reshape(rows, blocks, 1, columns // blocks)
    moved = lax.all_to_all(values, "seq", split_axis=0, concat_axis=2, tiled=True)
    return moved.reshape(rows // ways, columns * ways)


def first_tile(place, tiles):
    return (tiles * place) // 4


def padded_rows(rows):
    return -(-rows // 16) * 16


class Part:
    def __init__(self, left, right, rows, span, out, order, at=None, **kinds):
        self.left, self.right, self.rows = left, right, rows
        self.start, self.columns, self.out = span[0], span[1] - span[0], out
        self.at = self.start if at is None else at
        self.order = order
        for kind in ("by_rows", "in_lanes", "bias", "enter", "leave"):
            setattr(self, kind, kinds.get(kind, False))
        self.slab = padded_rows(rows)

    def handed(self):
        return (2, 2, self.slab, self.columns)


def split_part(left, right, rows, columns, out, order, **kinds):
    middle = -(-columns // (2 * TILE)) * TILE
    return [
        Part(left, right, rows, span, out, order, **kinds)
        for span in ((0, middle), (middle, columns))
    ]


class GradSums:
    def __init__(self, parts, names, shared_shapes, small_shape, after=()):
        self.parts, self.names = parts, names
        self.after = dict(after)
        self.shared_shapes, self.small_shape = shared_shapes, small_shape
        self.has_rows = any(part.by_rows and not part.leave for part in parts)
        self.entering = [index for index, part in enumerate(parts) if part.enter]
        self.leaving = [index for index, part in enumerate(parts) if part.leave]

    def scratch(self, array_shapes):
        parts, count, groups = self.parts, len(self.parts), len(self.shared_shapes)
        none = pltpu.VMEM((16, LANES), BF16)
        shapes = [
            none if name in self.after else pltpu.VMEM(shape, BF16)
            for name, shape in zip(self.names, array_shapes, strict=True)
        ]
        shapes += [pltpu.VMEM((4, rows, columns), BF16) for rows, _, _, columns in self.shared_shapes]

        def each(lead, needed):
            return [
                pltpu.VMEM(lead(part) + (part.slab, part.columns), BF16) if needed(part) else none
                for part in parts
            ]

        shapes += each(lambda part: (2, 2) if part.enter else (2, 2, 2), lambda part: True)
        shapes += each(lambda part: (2, 2), lambda part: not part.enter)
        shapes += each(lambda part: (2,), lambda part: not part.leave)
        shapes += each(lambda part: (), lambda part: not part.leave)
        for _ in range(2):
            for part in parts:
                if part.leave:
                    shapes.append(none)
                elif part.by_rows:
                    shapes.append(pltpu.VMEM((part.slab, part.columns), BF16))
                else:
                    shapes.append(pltpu.VMEM((4, padded_rows(part.rows // 4), part.columns), BF16))
        widest = max(part.columns for part in parts)
        tallest = max(4 * LANES if part.in_lanes else part.rows for part in parts)
        return shapes + [
            pltpu.VMEM((tallest, widest), F32),
            pltpu.VMEM((4,) + self.small_shape, F32),
            pltpu.VMEM((3,) + self.small_shape, F32),
            pltpu.SemaphoreType.DMA((max(len(self.names), 1),)),
            pltpu.SemaphoreType.DMA((max(groups, 1), 3)),
            pltpu.SemaphoreType.DMA((max(groups, 1), 3)),
            pltpu.SemaphoreType.DMA((max(groups, 1),)),
            pltpu.SemaphoreType.DMA((count,)),
            pltpu.SemaphoreType.DMA((count, 3)),
            pltpu.SemaphoreType.DMA((count, 3)),
            pltpu.SemaphoreType.DMA((count, 3)),
            pltpu.SemaphoreType.DMA((count, 3)),
            pltpu.SemaphoreType.DMA((6,)),
            pltpu.SemaphoreType.DMA((6,)),
        ]

    def bind(self, ins, shared, small_in, outs, small_out, handed_in, handed_out, scratch):
        count, groups, names = len(self.parts), len(self.shared_shapes), self.names
        refs = list(scratch)

        def take(number):
            taken = refs[:number]
            del refs[:number]
            return taken

        self.shared, self.small_in, self.outs, self.small_out = shared, small_in, outs, small_out
        self.held = dict(zip(names, take(len(names)), strict=True))
        for name, place in self.after.items():
            self.held[name] = self.held[place]
        self.gathered = take(groups)
        self.own, self.first_in = take(count), take(count)
        self.second_in, self.third_in = take(count), take(count)
        self.slabs, self.slab_in = take(count), take(count)
        self.total, self.small, self.small_came = take(3)
        load_sem, self.share_send, self.share_recv, own_sem, hand_sem = take(5)
        self.send_sem, self.recv_sem = take(2)
        self.last_send, self.last_recv, self.small_send, self.small_recv = take(4)
        item, column = lax.axis_index("dp"), lax.axis_index("seq")
        self.column = column
        self.bits = [lax.rem(item, 2), lax.rem(item // 2, 2), item // 4]
        self.partners = [(item + (1 - 2 * self.bits[k]) * (1 << k), column) for k in range(3)]
        self.peers = [(item, lax.rem(column + k, 4)) for k in range(1, 4)]
        self.owner = (2 * column + item // 4, lax.rem(item, 4))
        self.feeder = (4 * lax.rem(item, 2) + column, item // 2)
        self.elsewhere = jnp.logical_or(self.owner[0] != item, self.owner[1] != column)
        self.loads = {
            name: pltpu.make_async_copy(ins[i], self.held[name], load_sem.at[i])
            for i, name in enumerate(names)
        }
        self.own_shares = [
            pltpu.make_async_copy(
                self.columns_of(g, column), self.gathered[g].at[column], own_sem.at[g]
            )
            for g in range(groups)
        ]
        self.ready = set()
        self.others = {}
        self.handing = {
            index: pltpu.make_async_copy(ref, self.own[index], hand_sem.at[index])
            for index, ref in zip(self.entering, handed_in, strict=True)
        }
        for index, ref in zip(self.leaving, handed_out, strict=True):
            half = self.own[index].at[self.half(index, True)]
            self.handing[index] = pltpu.make_async_copy(half, ref, hand_sem.at[index])

    def greet(self):
        barrier = pltpu.get_barrier_semaphore()
        for partner in self.partners + self.peers:
            pl.semaphore_signal(barrier, inc=1, device_id=partner, device_id_type=MESH)
        waits = 6
        if self.has_rows:
            waits = 6 + self.elsewhere.astype(jnp.int32)

            @pl.when(self.elsewhere)
            def _():
                pl.semaphore_signal(barrier, inc=1, device_id=self.feeder, device_id_type=MESH)

        pl.semaphore_wait(barrier, waits)

    def load(self):
        for index in self.entering:
            self.handing[index].start()
        for name in self.names:
            if name not in self.after:
                self.loads[name].start()

    def remote(self, source, target_ref, send, recv, target):
        return pltpu.make_async_remote_copy(
            src_ref=source,
            dst_ref=target_ref,
            send_sem=send,
            recv_sem=recv,
            device_id=target,
            device_id_type=MESH,
        )

    def columns_of(self, group, place):
        _, wide, first, narrow = self.shared_shapes[group]
        start = first_tile(place, wide // TILE) * TILE + first
        return self.shared[group].at[:, pl.ds(pl.multiple_of(start, TILE), narrow)]

    def shares(self, group):
        return [
            self.remote(
                self.columns_of(group, peer[1]),
                self.gathered[group].at[self.column],
                self.share_send.at[group, k],
                self.share_recv.at[group, k],
                peer,
            )
            for k, peer in enumerate(self.peers)
        ]

    def share(self):
        for group in range(len(self.shared_shapes)):
            self.own_shares[group].start()
            for copy in self.shares(group):
                copy.start()

    def operand(self, name):
        if isinstance(name, int):
            if name not in self.ready:
                self.own_shares[name].wait()
                for copy in self.shares(name):
                    copy.wait()
            self.ready.add(name)
            ref = self.gathered[name]
            return ref[...].reshape(4 * ref.shape[1], ref.shape[2])
        first = name not in self.ready
        self.ready.add(name)
        if name in self.others:
            ref, wait = self.others[name]
            if first:
                wait()
            return ref[...].reshape(-1, ref.shape[-1])
        if first:
            self.loads[name].wait()
        return self.held[name][...]

    def multiply(self, index):
        part = self.parts[index]
        left, right = self.operand(part.left), self.operand(part.right)
        right = right[:, part.start : part.start + part.columns]
        if part.bias:
            sums = jnp.sum(right.astype(F32), axis=0, keepdims=True)
            for tile in range(part.columns // TILE):
                row = part.at // TILE + tile
                self.small[0, row : row + 1] = sums[:, tile * TILE : (tile + 1) * TILE]
        own, rows = self.own[index], part.rows
        if part.in_lanes:
            self.total[: left.shape[1], : part.columns] = over_first(left, right)
            for d in range(8):
                start = d // 2 * LANES + d % 2 * rows
                own[d // 4, d // 2 % 2, d % 2] = self.cut(start, rows, part.slab, part.columns)
            return
        step = 3 * TILE
        for start in range(0, left.shape[1], step):
            product = over_first(left[:, start : start + step], right).astype(BF16)
            for d in range(8):
                low, high = max(start, d * rows), min(start + step, (d + 1) * rows)
                if low < high:
                    place = slice(low - d * rows, high - d * rows)
                    own[d // 4, d // 2 % 2, d % 2, place] = product[low - start : high - start]

    def cut(self, start, rows, padded, columns):
        values = self.total[start : start + rows, :columns]
        if padded > rows:
            values = jnp.concatenate([values, jnp.zeros((padded - rows, columns), F32)], axis=0)
        return values.astype(BF16)

    def half(self, index, mine):
        order = self.parts[index].order
        pick = self.bits[order] if mine else 1 - self.bits[order]
        return (slice(None), slice(None), pick) if order == 0 else (slice(None), pick)

    def place(self, index, high, low):
        if self.parts[index].enter:
            return (high, low)
        if self.parts[index].order == 0:
            return (high, low, self.bits[0])
        return (high, self.bits[1], low)

    def stage(self, index, step):
        order = self.parts[index].order
        other = 1 - order
        sems = self.send_sem.at[index, step], self.recv_sem.at[index, step]
        own = self.own[index]
        if step == 0:
            source = own.at[self.half(index, False)]
            return self.remote(source, self.first_in[index], *sems, self.partners[order])
        if step == 1:
            place = self.place(index, slice(None), 1 - self.bits[other])
            return self.remote(own.at[place], self.second_in[index], *sems, self.partners[other])
        place = self.place(index, 1 - self.bits[2], self.bits[other])
        return self.remote(own.at[place], self.third_in[index], *sems, self.partners[2])

    def begin(self, index):
        if self.parts[index].enter:
            self.handing[index].wait()
            self.stage(index, 1).start()
            return
        self.multiply(index)
        self.stage(index, 0).start()

    def end_first(self, index):
        self.stage(index, 0).wait()
        for high in range(2):
            for low in range(2):
                place = self.place(index, high, low)
                came = self.first_in[index][high, low].astype(F32)
                self.own[index][place] = (self.own[index][place].astype(F32) + came).astype(BF16)
        if self.parts[index].leave:
            self.handing[index].start()
        else:
            self.stage(index, 1).start()

    def end_second(self, index):
        self.stage(index, 1).wait()
        for high in range(2):
            place = self.place(index, high, self.bits[1 - self.parts[index].order])
            came = self.second_in[index][high].astype(F32)
            self.own[index][place] = (self.own[index][place].astype(F32) + came).astype(BF16)
        self.stage(index, 2).start()

    def last(self, index):
        if self.parts[index].by_rows:
            sems = self.last_send.at[index, 0], self.last_recv.at[index, 0]
            return [self.remote(self.slabs[index], self.slab_in[index], *sems, self.owner)]
        return [
            self.remote(
                self.slabs[index].at[peer[1]],
                self.slab_in[index].at[self.column],
                self.last_send.at[index, k],
                self.last_recv.at[index, k],
                peer,
            )
            for k, peer in enumerate(self.peers)
        ]

    def end_third(self, index):
        part = self.parts[index]
        self.stage(index, 2).wait()
        place = self.place(index, self.bits[2], self.bits[1 - part.order])
        sums = self.own[index][place].astype(F32) + self.third_in[index][...].astype(F32)
        if part.by_rows:
            self.slabs[index][...] = sums.astype(BF16)

            @pl.when(self.elsewhere)
            def _():
                self.last(index)[0].start()

            @pl.when(jnp.logical_not(self.elsewhere))
            def _():
                self.slab_in[index][...] = self.slabs[index][...]

            return
        self.total[: part.rows, : part.columns] = sums
        rows = part.rows // 4
        for k in range(4):
            self.slabs[index][k] = self.cut(k * rows, rows, padded_rows(rows), part.columns)
        for copy in self.last(index):
            copy.start()
        self.slab_in[index][self.column] = self.slabs[index][self.column]

    def end_last(self, index):
        part = self.parts[index]
        out, stop = self.outs[part.out], part.at + part.columns
        if part.by_rows:

            @pl.when(self.elsewhere)
            def _():
                self.last(index)[0].wait()

            out[:, part.at : stop] = self.slab_in[index][...].astype(F32)[: part.rows]
            return
        for copy in self.last(index):
            copy.wait()
        rows = part.rows // 4
        wide = out.shape[-1]
        for k in range(4):
            values = self.slab_in[index][k].astype(F32)[:rows]
            if len(out.shape) == 3:
                out[k, :, part.at : stop] = values
            else:
                start = first_tile(k, wide // TILE) * TILE
                out[:, start + part.at : start + stop] = values

    def small_step(self, step):
        if step < 3:
            sems = self.small_send.at[step], self.small_recv.at[step]
            return [
                self.remote(self.small.at[step], self.small_came.at[step], *sems, self.partners[step])
            ]
        return [
            self.remote(
                self.small.at[3],
                self.small_out.at[self.column],
                self.small_send.at[3 + k],
                self.small_recv.at[3 + k],
                peer,
            )
            for k, peer in enumerate(self.peers)
        ]

    def end_small(self, at):
        self.small_step(at - 1)[0].wait()
        self.small[at] = self.small[at - 1] + self.small_came[at - 1]
        for copy in self.small_step(at):
            copy.start()

    def do(self, *steps):
        kinds = {
            "b": self.begin,
            "f": self.end_first,
            "s": self.end_second,
            "t": self.end_third,
            "l": self.end_last,
            "x": self.small_exchange,
            "r": lambda number: self.loads[self.names[number]].start(),
        }
        for step in steps:
            kinds[step[0]](int(step[1:]))

    def small_exchange(self, at):
        if at == 0:
            self.small_step(0)[0].start()
        elif at < 4:
            self.end_small(at)
        else:
            self.small_out[self.column] = self.small[3]
            for copy in self.small_step(3):
                copy.wait()

    def end(self):
        for index in self.leaving:
            self.handing[index].wait()


def split(refs, *counts):
    groups, start = [], 0
    for number in counts:
        groups.append(refs[start : start + number])
        start += number
    return groups + [refs[start:]]


LAST_STEPS = (
    ("b0", "b1", "b2", "b3", "b4"),
    ("s0", "b5"),
    ("s1",),
    ("b6", "f3", "s2", "t0", "t1"),
    ("f4", "t2", "s3", "x0", "l0", "l1"),
    ("l2", "s4", "x1", "f5", "t3", "x2", "t4", "f6", "l3", "s5", "x3", "l4", "s6", "t5", "t6", "x4", "l5", "l6"),
)


def last_grads(parts, arrays, shared, small, handed, out_shapes, condition, embed, rows_a, rows_b, mods):
    names = tuple(arrays)
    shapes = [value.shape + (first, columns) for value, first, columns in shared]
    sums = GradSums(parts, names, shapes, small.shape)
    count = len(out_shapes)
    width = condition.shape[1]

    def kernel(*refs):
        ins, given, handed_in, given_mods, (small_in, seen, embed_in, low, high), outs, lasts, refs = split(
            refs, len(names), len(shared), len(handed), len(mods), 5, count, 2
        )
        (small_out, condition_out), held, (mod_sem,), scratch = lasts, refs[:2], refs[2:3], refs[3:]
        sums.bind(ins, given, small_in, outs, small_out, handed_in, [], scratch)
        sums.load()
        loads = [
            pltpu.make_async_copy(source, target, mod_sem.at[k])
            for k, (source, target) in enumerate(zip(given_mods, held, strict=True))
        ]
        start_all(loads)
        sums.greet()
        sums.share()
        sums.small[0] = small_in[...]
        first, rest = held
        condition_out[...] = jnp.zeros_like(condition_out)
        work = [
            (low, 0, first, 0, 2 * width),
            (high, 0, first, 2 * width, width),
            (high, width, rest, 0, 2 * width),
            (high, 3 * width, first, 3 * width, width),
        ]
        for number, steps in enumerate(LAST_STEPS):
            sums.do(*steps)
            if number == 0:
                wait_all(loads)
            if number < 4:
                rows, at, weights, start, columns = work[number]
                condition_out[...] += over_rows(
                    rows[:, at : at + columns], weights[:, start : start + columns]
                )
            if number == 4:
                values = seen[...].astype(F32) + embed_in[...]
                condition_out[...] = condition_out[...] * silu_slope(values)
        sums.end()

    vmem, anywhere = pl.BlockSpec(memory_space=pltpu.VMEM), pl.BlockSpec(memory_space=pl.ANY)
    return pl.pallas_call(
        kernel,
        out_shape=[jax.ShapeDtypeStruct(shape, F32) for shape in out_shapes]
        + [
            jax.ShapeDtypeStruct((4,) + small.shape, F32),
            jax.ShapeDtypeStruct(condition.shape, F32),
        ],
        in_specs=[anywhere] * (len(names) + len(shared) + len(handed) + len(mods)) + [vmem] * 5,
        out_specs=[vmem] * (count + 2),
        scratch_shapes=[pltpu.VMEM(value.shape, BF16) for value in mods]
        + [pltpu.SemaphoreType.DMA((len(mods),))]
        + sums.scratch([value.shape for value in arrays.values()]),
        compiler_params=pltpu.CompilerParams(
            collective_id=SUM_ID, has_side_effects=True, vmem_limit_bytes=63 * 2**20
        ),
        name="last_grads",
    )(
        *arrays.values(),
        *[value for value, _, _ in shared],
        *handed,
        *mods,
        small,
        condition,
        embed,
        rows_a,
        rows_b,
    )


BACK_STEPS = {
    "start": ("b0", "b1", "b2", "b3", "b4", "b5"),
    "gathered": ("b6", "b7", "s1", "s0", "s3"),
    "head0": ("b8", "s4", "f2"),
    "head1": ("b9", "f5", "f6", "f7", "s2", "t1", "t0", "t3"),
    "head2": ("b10", "s5", "f8", "t4"),
    "head3": ("s6", "s7", "f9", "t2", "x0"),
    "put3": ("t5", "x1", "t6", "t7", "f10", "x2", "l0", "l1", "l3", "l4"),
    "end": ("x3", "l2", "l5", "l6", "l7", "x4"),
}


def pack_heads(lanes_ref, packed_ref):
    rows, count = lanes_ref.shape[0], lanes_ref.shape[1] // LANES
    lane = lax.broadcasted_iota(jnp.int32, (rows, LANES), 1)
    for tile in range(packed_ref.shape[1] // LANES):
        values = jnp.zeros((rows, LANES), F32)
        for head in range(count):
            start = head * HD - tile * LANES
            if -HD < start < LANES:
                one = lanes_ref[:, head * LANES : (head + 1) * LANES].astype(F32)
                one = pltpu.roll(one, start % LANES, 1) if start else one
                values = jnp.where(jnp.logical_and(lane >= start, lane < start + HD), one, values)
        packed_ref[:, tile * LANES : (tile + 1) * LANES] = values.astype(BF16)


def back_kernel(sums, own, outs, refs):
    grad_in, rows_in, heads_in, w_qkv_in, w_out_in, cosine, ahead, behind, q_gain, k_gain = own[:10]
    grad_middle, tokens, scale = own[10:]
    tokens_out, mod_out, gains_out, packed = outs
    (branch_all, rows, heads, w_qkv, w_out, grad_heads, load_sem), refs = refs[:7], refs[7:]
    gather = RowGather(grad_in, branch_all, *refs[:3])
    row_sums = RowSums(*refs[3:])
    local_rows = grad_in.shape[0]
    count = grad_heads.shape[1] // LANES
    factor = HD ** (-0.5)
    loads = [
        pltpu.make_async_copy(source, target, load_sem.at[k])
        for k, (source, target) in enumerate(
            ((rows_in, rows), (w_out_in, w_out), (w_qkv_in, w_qkv))
        )
    ]

    def load_head(head):
        return [
            pltpu.make_async_copy(
                heads_in.at[:, pl.ds((k * count + head) * LANES, LANES)],
                heads.at[head % 2, k],
                load_sem.at[3 + 2 * (head % 2) + k],
            )
            for k in range(2)
        ]

    for k in (1, 0, 2):
        loads[k].start()
    start_all(load_head(0))
    sums.load()
    sums.greet()
    gather.start()
    sums.share()
    sums.small[0] = jnp.zeros_like(sums.small[0])
    sums.others["grad_branch_a"] = (branch_all, lambda: None)
    sums.do(*BACK_STEPS["start"])
    gather.pass_on()
    gather.end()
    loads[1].wait()
    grad_branch = branch_all[...].reshape(4 * local_rows, branch_all.shape[2])
    grad_heads[...] = over_rows(grad_branch, w_out[...]).astype(BF16)
    sums.do(*BACK_STEPS["gathered"])
    loads[0].wait()
    tables = cosine[...], ahead[...], behind[...]
    block = 256
    gain_sums = [jnp.zeros((1, LANES), F32), jnp.zeros((1, LANES), F32)]
    for head in range(count):
        spans = [slice((k * count + head) * LANES, (k * count + head + 1) * LANES) for k in range(3)]
        if head + 1 < count:
            start_all(load_head(head + 1))
        keys, values = rows[:, spans[1]], rows[:, spans[2]]
        grad_query, grad_key, grad_value = [], None, None
        for start in range(0, rows.shape[0], block):
            queries = rows[start : start + block, spans[0]]
            grads = grad_heads[start : start + block, spans[0]]
            exp_scores = jnp.exp(over_rows(keys, queries) * factor)
            probs = exp_scores * (1.0 / jnp.sum(exp_scores, axis=0, keepdims=True))
            grad_probs = over_rows(values, grads)
            inner = jnp.sum(probs * grad_probs, axis=0, keepdims=True)
            grad_scores = (probs * (grad_probs - inner)).astype(BF16)
            grad_query.append(over_first(grad_scores, keys))
            key_term = jnp.dot(grad_scores, queries, preferred_element_type=F32)
            value_term = jnp.dot(probs.astype(BF16), grads, preferred_element_type=F32)
            grad_key = key_term if grad_key is None else grad_key + key_term
            grad_value = value_term if grad_value is None else grad_value + value_term
        rows[:, spans[2]] = grad_value.astype(BF16)
        terms = (jnp.concatenate(grad_query, axis=0) * factor, grad_key * factor)
        wait_all(load_head(head))
        for k, (term, gain) in enumerate(zip(terms, (q_gain, k_gain), strict=True)):
            raw = heads[head % 2, k]
            inverse = head_inverse(raw)
            normed = raw * inverse
            back = rotated(term, tables, -1)
            gain_sums[k] = gain_sums[k] + jnp.sum(back * normed, axis=0, keepdims=True)
            back = back * gain[...]
            mean = jnp.sum(back * normed, axis=-1, keepdims=True) * (1.0 / HD)
            rows[:, spans[k]] = (inverse * (back - normed * mean)).astype(BF16)
        if head == count - 1:
            pack_heads(rows, packed)
        sums.do(*BACK_STEPS["head%d" % head])
    gains_out[...] = jnp.concatenate(gain_sums + [jnp.zeros((6, LANES), F32)], axis=0)
    loads[2].wait()
    for index in range(4):
        part = pl.ds(pl.multiple_of(row_sums.order[index] * local_rows, local_rows), local_rows)
        row_sums.put(index, over_rows(rows[part, :], w_qkv[...]))
        sums.do(*BACK_STEPS.get("put%d" % index, ()))
    grad_hidden = row_sums.sums()
    values = tokens[...].astype(F32)
    inverse = inverse_rms(values)
    normed = values * inverse
    tokens_out[...] = grad_middle[...] + rms_back(grad_hidden * (1.0 + scale[...]), normed, inverse)
    width = values.shape[1]
    mod_out[:, :width] = grad_hidden.astype(BF16)
    mod_out[:, width:] = (grad_hidden * normed).astype(BF16)
    sums.do(*BACK_STEPS["end"])
    sums.end()


def attention_back(own, parts, arrays, shared, small_shape, handed, out_shapes):
    names = tuple(arrays)
    shapes = [value.shape + (first, columns) for value, first, columns in shared]
    sums = GradSums(parts, names, shapes, small_shape)
    count = len(out_shapes)
    rows, width = own[0].shape
    kept, heads, w_qkv, w_out = own[1:5]
    leaving = [parts[index].handed() for index in sums.leaving]
    vmem, anywhere = pl.BlockSpec(memory_space=pltpu.VMEM), pl.BlockSpec(memory_space=pl.ANY)
    own_scratch = [
        pltpu.VMEM((4, rows, width), BF16),
        pltpu.VMEM(kept.shape, BF16),
        pltpu.VMEM((2, 2, 4 * rows, LANES), F32),
        pltpu.VMEM(w_qkv.shape, BF16),
        pltpu.VMEM(w_out.shape, BF16),
        pltpu.VMEM((4 * rows, w_out.shape[0]), BF16),
        pltpu.SemaphoreType.DMA((7,)),
        *RowGather.scratch(),
        *RowSums.scratch(rows, width),
    ]

    def kernel(*refs):
        ins, exchanged, handed_in, given, outs, handed_out, (small_out,), results, mine, scratch = split(
            refs,
            len(names),
            len(shared),
            len(handed),
            len(own),
            count,
            len(leaving),
            1,
            4,
            len(own_scratch),
        )
        sums.bind(ins, exchanged, None, outs, small_out, handed_in, handed_out, scratch)
        back_kernel(sums, given, results, mine)

    return pl.pallas_call(
        kernel,
        out_shape=[jax.ShapeDtypeStruct(shape, F32) for shape in out_shapes]
        + [jax.ShapeDtypeStruct(shape, BF16) for shape in leaving]
        + [
            jax.ShapeDtypeStruct((4,) + small_shape, F32),
            jax.ShapeDtypeStruct((rows, width), F32),
            jax.ShapeDtypeStruct((rows, 2 * width), BF16),
            jax.ShapeDtypeStruct((8, LANES), F32),
            jax.ShapeDtypeStruct((4 * rows, -(-3 * width // 4 // LANES) * LANES), BF16),
        ],
        in_specs=[anywhere] * (len(names) + len(shared) + len(handed))
        + [vmem]
        + [anywhere] * 4
        + [vmem] * 8,
        out_specs=[vmem] * count + [anywhere] * len(leaving) + [vmem] * 5,
        scratch_shapes=own_scratch + sums.scratch([value.shape for value in arrays.values()]),
        compiler_params=pltpu.CompilerParams(
            collective_id=BACK_ID, has_side_effects=True, vmem_limit_bytes=63 * 2**20
        ),
        name="attention_back",
    )(*arrays.values(), *[value for value, _, _ in shared], *handed, *own)


def to_owners(rows):
    n_dp, n_seq = lax.axis_size("dp"), lax.axis_size("seq")
    pairs = []
    for d in range(n_dp):
        for s in range(n_seq):
            pairs.append((d * n_seq + s, s * n_dp + d))
    return lax.ppermute(rows, ("dp", "seq"), pairs)


def plain_sums(left, right, blocks):
    mine = lax.psum_scatter(outer_sum(left, right).astype(BF16), "dp", scatter_dimension=0, tiled=True)
    return (columns_to_rows(mine, blocks) if blocks else to_owners(mine)).astype(F32)


def padded_small(values):
    values = jnp.pad(values, ((0, 8 - values.shape[0]), (0, TILE - values.shape[1])))
    return jnp.concatenate([jnp.zeros((8, TILE), F32), values])


def again(part):
    span = (part.start, part.start + part.columns)
    kinds = {"by_rows": part.by_rows, "enter": True}
    return Part(None, None, part.rows, span, part.out, part.order, at=part.at, **kinds)


def bias_columns(small, tiles):
    edges = [first_tile(k, tiles) for k in range(4)] + [tiles]
    sums = small.reshape(4, -1)
    return [sums[k, : (edges[k + 1] - edges[k]) * TILE] for k in range(4)]


def in_lanes(values, axis):
    shape = values.shape
    values = values.reshape(shape[:axis] + (shape[axis] // HD, HD) + shape[axis + 1 :])
    pads = [(0, 0)] * len(values.shape)
    pads[axis + 1] = (0, LANES - HD)
    return jnp.pad(values, pads).reshape(shape[:axis] + (-1,) + shape[axis + 1 :])


def out_of_lanes(values):
    return values.reshape(values.shape[0], -1, LANES)[:, :, :HD]


def plain_back(grad_branch_a, given):
    kept, projected, w_qkv, w_out, cosine, ahead, behind, q_gain, k_gain = given
    patches, count = kept.shape[0], w_out.shape[0] // LANES
    factor = HD ** (-0.5)
    tables = [table[:, None, :] for table in (cosine, ahead, behind)]

    def turn(values):
        turned = jnp.roll(values, -QUARTER, -1) * tables[1] + jnp.roll(values, QUARTER, -1) * tables[2]
        return values * tables[0] - turned

    query, key, value = jnp.split(kept.reshape(patches, 3 * count, LANES), 3, axis=1)
    grads = times_transpose(grad_branch_a, w_out).astype(BF16).reshape(patches, count, LANES)
    scores = jnp.einsum("qhd,khd->hqk", query, key, preferred_element_type=F32) * factor
    exp_scores = jnp.exp(scores)
    probs = exp_scores / jnp.sum(exp_scores, axis=-1, keepdims=True)
    grad_probs = jnp.einsum("qhd,khd->hqk", grads, value, preferred_element_type=F32)
    inner = jnp.sum(probs * grad_probs, axis=-1, keepdims=True)
    grad_scores = (probs * (grad_probs - inner)).astype(BF16)
    terms = (
        jnp.einsum("hqk,khd->qhd", grad_scores, key, preferred_element_type=F32) * factor,
        jnp.einsum("hqk,qhd->khd", grad_scores, query, preferred_element_type=F32) * factor,
    )
    grad_value = jnp.einsum("hqk,qhd->khd", probs.astype(BF16), grads, preferred_element_type=F32)
    raws = jnp.split(projected.reshape(patches, 2 * count, LANES), 2, axis=1)
    results, gains = [], []
    for term, raw, gain in zip(terms, raws, (q_gain, k_gain), strict=True):
        inverse = head_inverse(raw)
        normed = raw * inverse
        back = turn(term)
        gains.append(jnp.sum(back * normed, axis=(0, 1)))
        back = back * gain[0]
        mean = jnp.sum(back * normed, axis=-1, keepdims=True) * (1.0 / HD)
        results.append(inverse * (back - normed * mean))
    grad_lanes = jnp.concatenate(results + [grad_value], axis=1).reshape(kept.shape).astype(BF16)
    return grad_lanes, times_transpose(grad_lanes, w_qkv), jnp.stack(gains)


def shards(
    tokens,
    condition,
    cotangent,
    w_qkv,
    w_out,
    w_gate,
    w_up,
    w_down,
    w_mod,
    b_mod,
    q_gain,
    k_gain,
    noise_counts,
    time_steps,
    positions,
):
    local_rows, width = tokens.shape[1:]
    ways = lax.axis_size("seq")
    patches = local_rows * ways
    local_heads = HEADS // ways
    item = lax.axis_index("dp")
    image = jnp.arange(noise_counts.shape[0], dtype=jnp.int32)
    running = jnp.sum(jnp.where(image[None, :] <= image[:, None], noise_counts[None, :], 0), axis=1)
    image_id = jnp.sum((running <= item).astype(jnp.int32))
    chosen = jnp.arange(noise_counts.shape[0], dtype=jnp.int32) == image_id
    share = 1.0 / jnp.sum(jnp.where(chosen, noise_counts, 0)).astype(F32)

    embed = time_embed(time_steps, width)
    bias_row = b_mod[None]
    share_row = jnp.full((1, width), share)
    (
        mod_first,
        w_qkv_lanes,
        scale_a,
        gate_a,
        gate_b,
        hidden_a,
        lifted_full,
        own_branch_b,
        lifted_low,
        all_positions,
    ) = first_stage(
        w_mod, w_qkv, condition[0], tokens[0], cotangent[0], embed, share_row, bias_row, positions[:, 0]
    )
    hidden_a = hidden_a.reshape(patches, width)
    lifted_full = lifted_full.reshape(patches, width)
    w_qkv_lanes = w_qkv_lanes.reshape(width, w_qkv_lanes.shape[2])
    tables = lane_tables(jnp.transpose(all_positions, (1, 0, 2)).reshape(2, patches))
    w_out_lanes = in_lanes(w_out, 0)
    gain_lanes = [jnp.pad(gain, (0, LANES - HD))[None] for gain in (q_gain, k_gain)]
    (
        projected_lanes,
        rows_lanes,
        attended_lanes,
        branch_a,
        mod_rest,
        gate_cols,
        up_cols,
        scale_b,
        middle,
        hidden_b,
        grads_all,
    ) = attend(
        hidden_a,
        w_qkv_lanes,
        w_out_lanes,
        tables,
        *gain_lanes,
        w_mod,
        w_gate,
        w_up,
        lifted_low,
        bias_row,
        tokens[0],
        gate_a,
        own_branch_b,
    )
    grad_branch_b = grads_all.reshape(patches, width)
    pieces = lax.axis_size("dp") == 8
    ff, heads_wide, own_rows = w_down.shape[0], local_heads * HD, width // 8
    handed_mlp = [
        split_part("inner", "grad_branch_b", ff // 8, width, 0, 0, by_rows=True, leave=True),
        split_part("hidden_b", "grad_gate_in", own_rows, ff, 1, 1, leave=True),
    ]
    handed_mlp = [handed_mlp[k % 2][k // 2] for k in range(4)] if pieces else []
    hidden_b, inner, grad_gate_in, grad_up_in, block_out, grad_middle, own_branch_a, grad_mod_b, *handed = mlp(
        hidden_b,
        grads_all,
        gate_cols,
        up_cols,
        w_down,
        (middle, scale_b, gate_a, gate_b, branch_a, cotangent[0], share_row),
        handed_mlp,
    )
    hidden_b = hidden_b.reshape(patches, width)
    mod_first, mod_rest = mod_first.reshape(width, -1), mod_rest.reshape(width, -1)
    given = [rows_lanes, projected_lanes, w_qkv_lanes, w_out_lanes, *tables, *gain_lanes]
    if pieces:
        tiles_b, tiles_a = grad_mod_b.shape[1] // TILE, 2 * width // TILE
        mod_b, mod_a = -(-tiles_b // 4) * TILE, -(-tiles_a // 4) * TILE
        third = mod_b // 3
        late_a = mod_a // 2 // TILE * TILE
        ups = split_part("hidden_b", "grad_up_in", own_rows, ff, 2, 0)
        lasts = split_part("hidden_a", "grad_project", own_rows, 3 * heads_wide, 1, 0)
        mods = [
            Part("lifted", k, own_rows, (0, third), 0, 0, at=k * third, bias=True, leave=True)
            for k in range(3)
        ]
        downs, gates = handed_mlp[0::2], handed_mlp[1::2]
        parts_b = [
            again(downs[0]),
            again(gates[0]),
            ups[0],
            again(downs[1]),
            again(gates[1]),
            ups[1],
            *split_part("attended", "grad_branch_a", heads_wide // 8, width, 3, 1, by_rows=True, in_lanes=True),
            *mods,
        ]
        arrays_b = {
            "hidden_b": hidden_b,
            "grad_up_in": grad_up_in,
            "attended": attended_lanes,
            "lifted": lifted_full,
        }
        shapes_b = [
            (ff // 8, width),
            (own_rows // 4, 4 * ff),
            (own_rows // 4, 4 * ff),
            (heads_wide // 8, width),
        ]
        own = [own_branch_a, *given, grad_middle, tokens[0], scale_a]
        (
            grad_w_down,
            grad_w_gate,
            grad_w_up,
            grad_w_out,
            *handed,
            small_b,
            grad_tokens,
            grad_mod_a,
            gain_sums,
            grad_project,
        ) = attention_back(
            own,
            parts_b,
            arrays_b,
            [(grad_mod_b, k * third, third) for k in range(3)],
            (16, LANES),
            [handed[k] for k in (0, 1, 2, 3)],
            shapes_b,
        )
        parts_a = [again(part) for part in mods] + lasts
        spans = ((0, mod_a - late_a), (mod_a - late_a, mod_a))
        parts_a += [
            Part("lifted", k, own_rows, (0, span[1] - span[0]), 2, 0, at=span[0], bias=True)
            for k, span in enumerate(spans)
        ]
        shapes_a = [
            (own_rows // 4, tiles_b * TILE),
            (4, own_rows // 4, 3 * heads_wide),
            (own_rows // 4, tiles_a * TILE),
        ]
        sum_b, qkv_sum, sum_a, small_a, grad_condition = last_grads(
            parts_a,
            {"hidden_a": hidden_a, "grad_project": grad_project, "lifted": lifted_full},
            [(grad_mod_a, span[0], span[1] - span[0]) for span in spans],
            padded_small(gain_sums[:2]),
            handed,
            shapes_a,
            condition[0],
            embed,
            grad_mod_a,
            grad_mod_b,
            [mod_first, mod_rest],
        )
        grad_w_qkv = jnp.transpose(
            qkv_sum.reshape(4, own_rows // 4, 3, heads_wide), (1, 2, 0, 3)
        ).reshape(own_rows // 4, 3 * width)
        grad_w_mod = jnp.concatenate([sum_a, sum_b], axis=1)
        bias = jnp.concatenate(bias_columns(small_a, tiles_a) + bias_columns(small_b, tiles_b))
        own_bias = bias.shape[0] // (8 * ways)
        sum_bias = lax.dynamic_slice(
            bias, ((item * ways + lax.axis_index("seq")) * own_bias,), (own_bias,)
        )
        gains = jnp.sum(small_a[:, 8:10, :HD], axis=0)
    else:
        tokens_f = tokens[0].astype(F32)
        inverse_a = inverse_rms(tokens_f)
        normed_a = tokens_f * inverse_a
        grad_branch_a = gather_rows(own_branch_a)
        grad_lanes, partial, gain_sums = plain_back(grad_branch_a, given)
        grad_hidden_a = scatter_rows(partial)
        grad_tokens = grad_middle + rms_back(grad_hidden_a * (1.0 + scale_a), normed_a, inverse_a)
        grad_mod_a = jnp.concatenate([grad_hidden_a, grad_hidden_a * normed_a], axis=-1).astype(BF16)
        grad_mod_first = jnp.concatenate([grad_mod_a, grad_mod_b[:, :width], grad_mod_b[:, 3 * width :]], axis=1)
        grad_condition = (
            times_transpose(grad_mod_first, mod_first)
            + times_transpose(grad_mod_b[:, width : 3 * width], mod_rest)
        ) * silu_slope(condition[0].astype(F32) + embed)
        grad_project = out_of_lanes(grad_lanes).reshape(patches, 3 * heads_wide)
        gain_sums = gain_sums[:2, :HD]
        mod_rows = jnp.concatenate([grad_mod_a, grad_mod_b], axis=1)
        grad_w_down = plain_sums(inner, grad_branch_b, 0)
        grad_w_gate = plain_sums(hidden_b, grad_gate_in, 1)
        grad_w_up = plain_sums(hidden_b, grad_up_in, 1)
        grad_w_qkv = plain_sums(hidden_a, grad_project, 3)
        attended = out_of_lanes(attended_lanes).reshape(patches, heads_wide)
        grad_w_out = plain_sums(attended, grad_branch_a, 0)
        grad_w_mod = plain_sums(lifted_full, rows_to_columns(mod_rows, 6), 6)
        bias_rows = jnp.sum(mod_rows, axis=0, dtype=F32)
        sum_bias = lax.psum_scatter(bias_rows, ("dp", "seq"), scatter_dimension=0, tiled=True)
        gains = lax.psum(gain_sums, ("dp", "seq"))
    sum_q_gain, sum_k_gain = gains[0], gains[1]
    return (
        block_out[None],
        grad_tokens[None],
        grad_condition[None],
        grad_w_qkv,
        grad_w_out,
        grad_w_gate,
        grad_w_up,
        grad_w_down,
        grad_w_mod,
        sum_bias,
        sum_q_gain,
        sum_k_gain,
    )


def solution(mesh):
    placed = (
        P("dp", "seq", None),
        P("dp", "seq", None),
        P("dp", "seq", None),
        P("seq", None),
        P("seq", None),
        P("seq", None),
        P("seq", None),
        P("seq", None),
        P("seq", None),
        P(),
        P(),
        P(),
        P(),
        P("dp"),
        P(None, "dp", "seq"),
    )
    return jax.shard_map(
        shards,
        mesh=mesh,
        in_specs=placed,
        out_specs=(
            P("dp", "seq", None),
            P("dp", "seq", None),
            P("dp", "seq", None),
            P(("dp", "seq"), None),
            P(("dp", "seq"), None),
            P(("dp", "seq"), None),
            P(("dp", "seq"), None),
            P(("dp", "seq"), None),
            P(("dp", "seq"), None),
            P(("dp", "seq")),
            P(),
            P(),
        ),
        check_vma=False,
    )
```

```python
import math

import jax
import jax.numpy as jnp
from jax import lax
from jax.experimental import pallas as pl
from jax.experimental.pallas import tpu as pltpu
from jax.sharding import PartitionSpec as P

HEADS = 16
HD = 72
EPSILON = 1e-06
BF16 = jnp.bfloat16
F32 = jnp.float32


def inverse_rms(values):
    return lax.rsqrt(jnp.mean(values * values, axis=-1, keepdims=True) + EPSILON)


def rms_back(grad_in, normed, inverse):
    return inverse * (grad_in - normed * jnp.mean(grad_in * normed, axis=-1, keepdims=True))


def silu_slope(values):
    logistic = jax.nn.sigmoid(values)
    return logistic * (1.0 + values * (1.0 - logistic))


def time_embed(steps, width):
    half_width = width // 2
    frequency = jnp.exp(-math.log(10000.0) * jnp.arange(half_width, dtype=F32) / half_width)
    angles = steps.astype(F32)[:, None] * frequency[None, :]
    return jnp.concatenate([jnp.cos(angles), jnp.sin(angles)], axis=-1)


def rope_tables(positions, head_size):
    quarter = head_size // 4
    frequency = jnp.exp(-math.log(10000.0) * jnp.arange(quarter, dtype=F32) / quarter)
    along_rows = positions[0].astype(F32)[..., None] * frequency
    along_cols = positions[1].astype(F32)[..., None] * frequency
    angles = jnp.concatenate([along_rows, along_rows, along_cols, along_cols], axis=-1)
    return (jnp.cos(angles)[..., None, :], jnp.sin(angles)[..., None, :])


def quarter_turn(values):
    first, second, third, fourth = jnp.split(values, 4, axis=-1)
    return jnp.concatenate([-second, first, -fourth, third], axis=-1)


def rotate_heads(values, cosine, sine):
    return values * cosine + quarter_turn(values) * sine


def unrotate(grad_in, cosine, sine):
    return grad_in * cosine - quarter_turn(grad_in * sine)


def matmul(left, right):
    return jnp.dot(left, right, preferred_element_type=F32)


def outer_sum(left, right):
    return jnp.einsum("ra,rb->ab", left, right, preferred_element_type=F32)


def times_transpose(left, right):
    return jnp.einsum("rb,ab->ra", left, right, preferred_element_type=F32)


MESH = pl.DeviceIdType.MESH
SUM_ID, GATHER_ID, SCATTER_ID, WEIGHT_ID, ATTEND_ID, BACK_ID, MLP_ID = 1, 2, 3, 4, 5, 6, 7


def greet(partners):
    barrier = pltpu.get_barrier_semaphore()
    for partner in partners:
        pl.semaphore_signal(barrier, inc=1, device_id=partner, device_id_type=MESH)
    pl.semaphore_wait(barrier, len(partners))


def group_partners():
    item, column = lax.axis_index("dp"), lax.axis_index("seq")
    core = lax.rem(column, 2)
    return (item, column + 1 - 2 * core), (item, lax.rem(column + 2, 4))


GATHER_PIECES = 4


def gather_kernel(own_ref, out_ref, local_sem, send_sem, recv_sem):
    column = lax.axis_index("seq")
    sibling, across = group_partners()
    greet([sibling, across])
    local = pltpu.make_async_copy(own_ref, out_ref.at[column], local_sem)
    local.start()
    rows = own_ref.shape[0] // GATHER_PIECES

    def remote(source, place, piece, kind, target):
        part = pl.ds(piece * rows, rows)
        return pltpu.make_async_remote_copy(
            src_ref=source.at[part],
            dst_ref=out_ref.at[place, part],
            send_sem=send_sem.at[kind, piece],
            recv_sem=recv_sem.at[kind, piece],
            device_id=target,
            device_id_type=MESH,
        )

    far = lax.rem(column + 2, 4)
    pieces = range(GATHER_PIECES)
    over = [remote(own_ref, column, piece, 0, across) for piece in pieces]
    beside = [remote(own_ref, column, piece, 1, sibling) for piece in pieces]
    onward = [remote(out_ref.at[far], far, piece, 2, sibling) for piece in pieces]
    for copy in over:
        copy.start()
    for copy in beside:
        copy.start()
    for piece in pieces:
        over[piece].wait_recv()
        onward[piece].start()
    for piece in pieces:
        over[piece].wait_send()
        beside[piece].wait()
        onward[piece].wait()
    local.wait()


def gather_rows(values):
    rows, columns = values.shape
    gathered = pl.pallas_call(
        gather_kernel,
        out_shape=jax.ShapeDtypeStruct((4, rows, columns), values.dtype),
        in_specs=[pl.BlockSpec(memory_space=pltpu.VMEM)],
        out_specs=pl.BlockSpec(memory_space=pltpu.VMEM),
        scratch_shapes=[
            pltpu.SemaphoreType.DMA,
            pltpu.SemaphoreType.DMA((3, GATHER_PIECES)),
            pltpu.SemaphoreType.DMA((3, GATHER_PIECES)),
        ],
        compiler_params=pltpu.CompilerParams(
            collective_id=GATHER_ID, has_side_effects=True, vmem_limit_bytes=48 * 2**20
        ),
        name="gather_rows",
    )(values)
    return gathered.reshape(4 * rows, columns)


def scatter_kernel(parts_ref, out_ref, near, low, far, send_sem, recv_sem):
    column = lax.axis_index("seq")
    core, chip = lax.rem(column, 2), column // 2
    sibling, across = group_partners()
    greet([sibling, across])
    rows = out_ref.shape[0] // 2

    def remote(source, target_ref, index, target):
        return pltpu.make_async_remote_copy(
            src_ref=source,
            dst_ref=target_ref,
            send_sem=send_sem.at[index],
            recv_sem=recv_sem.at[index],
            device_id=target,
            device_id_type=MESH,
        )

    parts = [pl.ds(piece * rows, rows) for piece in range(2)]
    beside = [
        remote(parts_ref.at[1 - chip, 1 - core, part], near.at[0, part], i, sibling)
        for i, part in enumerate(parts)
    ]
    beside.append(remote(parts_ref.at[chip, 1 - core], near.at[1], 2, sibling))
    for copy in beside:
        copy.start()
    over = [remote(low.at[part], far.at[part], 3 + i, across) for i, part in enumerate(parts)]
    for i, part in enumerate(parts):
        beside[i].wait_recv()
        pair = parts_ref[1 - chip, core, part].astype(F32) + near[0, part].astype(F32)
        low[part] = pair.astype(BF16)
        over[i].start()
    beside[2].wait_recv()
    out_ref[...] = parts_ref[chip, core].astype(F32) + near[1].astype(F32)
    for i, part in enumerate(parts):
        over[i].wait()
        out_ref[part] += far[part].astype(F32)
    for copy in beside:
        copy.wait_send()


def scatter_rows(partial):
    rows, columns = partial.shape[0] // 4, partial.shape[1]
    return pl.pallas_call(
        scatter_kernel,
        out_shape=jax.ShapeDtypeStruct((rows, columns), F32),
        in_specs=[pl.BlockSpec(memory_space=pltpu.VMEM)],
        out_specs=pl.BlockSpec(memory_space=pltpu.VMEM),
        scratch_shapes=[
            pltpu.VMEM((2, rows, columns), BF16),
            pltpu.VMEM((rows, columns), BF16),
            pltpu.VMEM((rows, columns), BF16),
            pltpu.SemaphoreType.DMA((5,)),
            pltpu.SemaphoreType.DMA((5,)),
        ],
        compiler_params=pltpu.CompilerParams(
            collective_id=SCATTER_ID, has_side_effects=True, vmem_limit_bytes=48 * 2**20
        ),
        name="scatter_rows",
    )(partial.astype(BF16).reshape(2, 2, rows, columns))


TILE = 128
LANES = 128
QUARTER = HD // 4
FIRST_ROWS = 80


class WeightImport:
    def __init__(self, blocks, ranges):
        self.blocks, self.ranges = blocks, ranges
        self.arrays = sorted({block[0] for block in blocks})

    def scratch(self):
        count = len(self.blocks)
        return [
            pltpu.SemaphoreType.DMA((8,)),
            pltpu.SemaphoreType.DMA((count, 7)),
            pltpu.SemaphoreType.DMA((count, 7)),
        ]

    def bind(self, ins, outs, scratch):
        self.ins, self.outs = ins, outs
        self.own_sem, self.send_sem, self.recv_sem = scratch
        item, column = lax.axis_index("dp"), lax.axis_index("seq")
        core, chip = lax.rem(column, 2), column // 2
        self.item, self.column = item, column
        self.y_bit, self.z_bit = lax.rem(item, 2), lax.rem(item // 2, 2)
        self.sibling = (item, column + 1 - 2 * core)
        self.y_near = (item + 1 - 2 * self.y_bit, column)
        self.z_near = (item + 2 - 4 * self.z_bit, column)
        self.far = [(1 - chip) * 2 + k for k in (core, 1 - core)]
        self.half_rows = ins[0].shape[0] // 2

    def partners(self):
        across = [(self.item, place) for place in self.far]
        return across + [self.sibling, self.y_near, self.z_near]

    def copy(self, source, target_ref, block, kind, target):
        return pltpu.make_async_remote_copy(
            src_ref=source,
            dst_ref=target_ref,
            send_sem=self.send_sem.at[block, kind],
            recv_sem=self.recv_sem.at[block, kind],
            device_id=target,
            device_id_type=MESH,
        )

    def source_column(self, column):
        for start, stop in self.ranges:
            if column < stop - start:
                return start + column
            column -= stop - start

    def piece(self, ref, block, y_pick, z_pick, first_row=0, rows=None, base=0, outside=False):
        array, _, start, columns = self.blocks[block]
        step = columns
        if array == 0 and outside:
            step = self.source_column(start + columns) - self.source_column(start)
            start = self.source_column(start)
        rows = self.half_rows if rows is None else rows
        return ref.at[
            pl.ds(pl.multiple_of(z_pick * self.half_rows + first_row, 16), rows),
            pl.ds(pl.multiple_of(base + start + y_pick * step, TILE), columns),
        ]

    def mine_for(self, array, place):
        ref = self.ins[array]
        if len(ref.shape) == 3:
            return ref.at[place], 0
        return ref, 0 if array == 0 else place * self.outs[array].shape[2]

    def whole(self, array, place):
        ref, base = self.mine_for(array, place)
        columns = self.outs[array].shape[2]
        if ref.shape[-1] == columns:
            return ref
        return ref.at[:, pl.ds(pl.multiple_of(base, TILE), columns)]

    def over(self, block):
        array, offset, _, _ = self.blocks[block]
        goal = self.far[offset or 0]
        ref, base = self.mine_for(array, goal)
        source = self.piece(ref, block, self.y_bit, self.z_bit, base=base, outside=True)
        target = self.piece(self.outs[array].at[self.column], block, self.y_bit, self.z_bit)
        return self.copy(source, target, block, 0, (self.item, goal))

    def onward(self, block, kind):
        array, offset, _, _ = self.blocks[block]
        ref = self.outs[array].at[self.far[offset or 0]]
        if kind == 1:
            part, target = self.piece(ref, block, self.y_bit, self.z_bit), self.y_near
        elif kind == 2:
            part, target = self.piece(ref, block, self.y_bit, self.z_bit), self.z_near
        elif kind == 3:
            part = self.piece(ref, block, 1 - self.y_bit, self.z_bit, 0, FIRST_ROWS)
            target = self.z_near
        else:
            rest = self.half_rows - FIRST_ROWS
            part = self.piece(ref, block, self.y_bit, 1 - self.z_bit, FIRST_ROWS, rest)
            target = self.y_near
        return self.copy(part, part, block, kind, target)

    def share(self, block):
        _, _, start, columns = self.blocks[block]
        part = self.outs[0].at[self.far[0], :, pl.ds(start, 2 * columns)]
        return self.copy(part, part, block, 5, self.sibling)

    def spans(self, array, place):
        target = self.outs[array].at[self.column]
        if array:
            return [(self.whole(array, place), target)]
        pairs, at = [], 0
        for start, stop in self.ranges:
            columns = stop - start
            pairs.append((self.ins[0].at[:, pl.ds(start, columns)], target.at[:, pl.ds(at, columns)]))
            at += columns
        return pairs

    def beside(self, array):
        index = self.arrays.index(array)
        return [
            self.copy(source, target, index + 2 * k, 6, self.sibling)
            for k, (source, target) in enumerate(self.spans(array, self.sibling[1]))
        ]

    def own(self, array):
        return [
            pltpu.make_async_copy(source, target, self.own_sem.at[array + 4 * k])
            for k, (source, target) in enumerate(self.spans(array, self.column))
        ]

    def do(self, *steps):
        kinds = {"a": self.arrive, "p": self.pass_on, "c": self.complete}
        for step in steps:
            kinds[step[0]](int(step[1:]))

    def arrive(self, step):
        self.over(step).wait_recv()
        self.onward(step, 1).start()
        self.onward(step, 2).start()

    def pass_on(self, step):
        self.onward(step, 1).wait_recv()
        self.onward(step, 3).start()
        self.onward(step, 2).wait_recv()
        self.onward(step, 4).start()

    def complete(self, step):
        self.onward(step, 3).wait_recv()
        self.onward(step, 4).wait_recv()
        if self.blocks[step][0] == 0:
            self.share(step).start()

    def end(self):
        for block in range(len(self.blocks)):
            self.over(block).wait_send()
            for kind in range(1, 5):
                self.onward(block, kind).wait_send()
            if self.blocks[block][0] == 0:
                self.share(block).wait_send()


class RowGather:
    def __init__(self, own, everyone, local_sem, send_sem, recv_sem):
        self.own, self.everyone = own, everyone
        self.local_sem, self.send_sem, self.recv_sem = local_sem, send_sem, recv_sem
        self.column = lax.axis_index("seq")
        self.far = lax.rem(self.column + 2, 4)
        self.sibling, self.across = group_partners()

    def remote(self, source, place, piece, kind, target):
        rows = self.own.shape[0] // GATHER_PIECES
        part = pl.ds(piece * rows, rows)
        return pltpu.make_async_remote_copy(
            src_ref=source.at[part],
            dst_ref=self.everyone.at[place, part],
            send_sem=self.send_sem.at[kind, piece],
            recv_sem=self.recv_sem.at[kind, piece],
            device_id=target,
            device_id_type=MESH,
        )

    def over(self, piece):
        return self.remote(self.own, self.column, piece, 0, self.across)

    def beside(self, piece):
        return self.remote(self.own, self.column, piece, 1, self.sibling)

    def onward(self, piece):
        return self.remote(self.everyone.at[self.far], self.far, piece, 2, self.sibling)

    def local(self):
        return pltpu.make_async_copy(self.own, self.everyone.at[self.column], self.local_sem)

    def start(self):
        for piece in range(GATHER_PIECES):
            self.over(piece).start()
        for piece in range(GATHER_PIECES):
            self.beside(piece).start()
        self.local().start()

    def pass_on(self):
        for piece in range(GATHER_PIECES):
            self.over(piece).wait_recv()
            self.onward(piece).start()

    def end(self):
        for piece in range(GATHER_PIECES):
            self.over(piece).wait_send()
            self.beside(piece).wait()
            self.onward(piece).wait()
        self.local().wait()

    @staticmethod
    def scratch():
        return [
            pltpu.SemaphoreType.DMA,
            pltpu.SemaphoreType.DMA((3, GATHER_PIECES)),
            pltpu.SemaphoreType.DMA((3, GATHER_PIECES)),
        ]


def first_import(width):
    wide = 3 * HEADS // 4 * LANES
    blocks = [(0, None, 0, width), (0, None, 2 * width, width), (1, 0, 0, wide // 2), (1, 1, 0, wide // 2)]
    return WeightImport(blocks, [(0, 3 * width), (5 * width, 6 * width)])


def second_import(width, ff):
    blocks = [(0, None, 0, width)] + [(k, j, 0, ff // 2) for k in (2, 3) for j in (0, 1)]
    return WeightImport(blocks, [(3 * width, 5 * width)])


def spread_heads(w_ref, lanes_ref):
    rows = w_ref.shape[0]
    valid = lax.broadcasted_iota(jnp.int32, (rows, LANES), 1) < HD
    for head in range(3 * HEADS):
        kind, device, place = head // HEADS, head % HEADS // 4, head % 4
        start = head * HD // LANES * LANES
        stop = min(start + 2 * LANES, w_ref.shape[1])
        window = w_ref[:, start:stop].astype(F32)
        shift = head * HD - start
        if shift:
            window = pltpu.roll(window, window.shape[1] - shift, 1)
        target = (kind * 4 + place) * LANES
        lanes_ref[device, :, target : target + LANES] = jnp.where(
            valid, window[:, :LANES], 0.0
        ).astype(BF16)


def start_all(copies):
    for copy in copies:
        copy.start()


def wait_all(copies):
    for copy in copies:
        copy.wait()


def row_of(ref, start, columns):
    rows = range(start // LANES, (start + columns) // LANES)
    return jnp.concatenate([ref[row : row + 1, :] for row in rows], axis=1)


def first_kernel(imports, *refs):
    (w_mod, w_qkv, condition, tokens, cotangent, embed, share, bias, positions), refs = refs[:9], refs[9:]
    (mod_out, qkv_out, scale_a, gate_a, gate_b), refs = refs[:5], refs[5:]
    (hidden_all, grads, lifted, positions_all), refs = refs[:4], refs[4:]
    (mod_all, lanes, hidden, mod_sem, spot_send, spot_recv), refs = refs[:6], refs[6:]
    imports.bind({0: w_mod, 1: lanes}, {0: mod_all, 1: qkv_out}, refs[:3])
    gather = RowGather(hidden, hidden_all, *refs[3:6])
    item, column = lax.axis_index("dp"), lax.axis_index("seq")
    width = tokens.shape[1]
    greet(imports.partners())
    imports.over(0).start()
    start_all(imports.own(0))
    start_all(imports.beside(0))
    peers = [(item, lax.rem(column + k, 4)) for k in range(1, 4)]
    spot_copies = [
        pltpu.make_async_remote_copy(
            src_ref=positions,
            dst_ref=positions_all.at[column],
            send_sem=spot_send.at[k],
            recv_sem=spot_recv.at[k],
            device_id=peer,
            device_id_type=MESH,
        )
        for k, peer in enumerate(peers)
    ]
    start_all(spot_copies)
    positions_all[column] = positions[...]
    spread_heads(w_qkv, lanes)
    for block in range(1, len(imports.blocks)):
        imports.over(block).start()
    start_all(imports.own(1))
    start_all(imports.beside(1))
    values = condition[...].astype(F32) + embed[...]
    lifted[...] = (values * jax.nn.sigmoid(values)).astype(BF16)
    imports.arrive(0)
    imports.pass_on(0)
    imports.arrive(1)
    imports.complete(0)
    wait_all(imports.own(0))
    for copy in imports.beside(0):
        copy.wait_recv()

    def modulate(block):
        imports.share(block).wait_recv()
        start = imports.blocks[block][2]
        weights = mod_all[:, :, start : start + 2 * width].reshape(-1, 2 * width)
        modulation = jnp.dot(lifted[...], weights, preferred_element_type=F32)
        return [
            modulation[:, k * width : (k + 1) * width]
            + row_of(bias, imports.source_column(start + k * width), width)
            for k in range(2)
        ]

    shift, scale = modulate(0)
    scale_a[...] = scale
    values = tokens[...].astype(F32)
    normed = values * inverse_rms(values)
    hidden[...] = (normed * (1.0 + scale) + shift).astype(BF16)
    gather.start()
    imports.pass_on(1)
    imports.arrive(2)
    imports.complete(1)
    imports.arrive(3)
    store = pltpu.make_async_copy(mod_all, mod_out, mod_sem)
    gate_a[...], gate = modulate(1)
    store.start()
    gate_b[...] = gate
    grads[...] = (cotangent[...].astype(F32) * share[...] * gate).astype(BF16)
    imports.pass_on(2)
    imports.pass_on(3)
    gather.pass_on()
    imports.complete(2)
    imports.complete(3)
    imports.end()
    for copy in imports.beside(0):
        copy.wait_send()
    wait_all(imports.beside(1))
    wait_all(imports.own(1))
    gather.end()
    wait_all(spot_copies)
    store.wait()


def first_stage(w_mod, w_qkv, condition, tokens, cotangent, embed, share, bias, positions):
    rows, width = tokens.shape
    depth, lanes = w_mod.shape[0], 3 * HEADS // 4 * LANES
    imports = first_import(width)
    vmem, anywhere = pl.BlockSpec(memory_space=pltpu.VMEM), pl.BlockSpec(memory_space=pl.ANY)

    def kernel(*refs):
        first_kernel(imports, *refs)

    return pl.pallas_call(
        kernel,
        out_shape=[
            jax.ShapeDtypeStruct((4, depth, 4 * width), BF16),
            jax.ShapeDtypeStruct((4, depth, lanes), BF16),
            jax.ShapeDtypeStruct((rows, width), F32),
            jax.ShapeDtypeStruct((rows, width), F32),
            jax.ShapeDtypeStruct((rows, width), F32),
            jax.ShapeDtypeStruct((4, rows, width), BF16),
            jax.ShapeDtypeStruct((rows, width), BF16),
            jax.ShapeDtypeStruct((rows, width), BF16),
            jax.ShapeDtypeStruct((4,) + positions.shape, jnp.int32),
        ],
        in_specs=[anywhere] + [vmem] * 8,
        out_specs=[anywhere, anywhere] + [vmem] * 7,
        scratch_shapes=[
            pltpu.VMEM((4, depth, 4 * width), BF16),
            pltpu.VMEM((4, depth, lanes), BF16),
            pltpu.VMEM((rows, width), BF16),
            pltpu.SemaphoreType.DMA,
            pltpu.SemaphoreType.DMA((3,)),
            pltpu.SemaphoreType.DMA((3,)),
        ]
        + imports.scratch()
        + RowGather.scratch(),
        compiler_params=pltpu.CompilerParams(
            collective_id=WEIGHT_ID, has_side_effects=True, vmem_limit_bytes=60 * 2**20
        ),
        name="first_stage",
    )(w_mod, w_qkv, condition, tokens, cotangent, embed, share, bias, positions)


def rotated(values, tables, sign):
    cosine, ahead, behind = tables
    turned = pltpu.roll(values, LANES - QUARTER, 1) * ahead + pltpu.roll(values, QUARTER, 1) * behind
    return values * cosine + turned if sign > 0 else values * cosine - turned


def lane_tables(positions):
    lane = jnp.arange(LANES)[None, :]
    frequency = jnp.exp(-math.log(10000.0) * (lane % QUARTER).astype(F32) / QUARTER)
    places = jnp.where(lane < 2 * QUARTER, positions[0][:, None], positions[1][:, None])
    angles = places.astype(F32) * frequency
    valid, takes_ahead = lane < HD, lane // QUARTER % 2 == 0
    cosine, sine = jnp.where(valid, jnp.cos(angles), 0.0), jnp.where(valid, jnp.sin(angles), 0.0)
    return [cosine, jnp.where(takes_ahead, -sine, 0.0), jnp.where(takes_ahead, 0.0, sine)]


def head_inverse(values):
    return lax.rsqrt(jnp.sum(values * values, axis=-1, keepdims=True) * (1.0 / HD) + EPSILON)


def over_rows(left, right):
    return lax.dot_general(left, right, (((1,), (1,)), ((), ())), preferred_element_type=F32)


def over_first(left, right):
    return lax.dot_general(left, right, (((0,), (0,)), ((), ())), preferred_element_type=F32)


class RowSums:
    def __init__(self, blocks, near, low, far, send_sem, recv_sem):
        column = lax.axis_index("seq")
        self.column = column
        self.core, self.chip = lax.rem(column, 2), column // 2
        self.sibling, self.across = group_partners()
        self.blocks, self.near, self.low, self.far = blocks, near, low, far
        self.send_sem, self.recv_sem = send_sem, recv_sem
        self.order = [
            (1 - self.chip) * 2 + 1 - self.core,
            (1 - self.chip) * 2 + self.core,
            self.chip * 2 + 1 - self.core,
            column,
        ]

    def copy(self, source, target_ref, index, target):
        return pltpu.make_async_remote_copy(
            src_ref=source,
            dst_ref=target_ref,
            send_sem=self.send_sem.at[index],
            recv_sem=self.recv_sem.at[index],
            device_id=target,
            device_id_type=MESH,
        )

    def beside(self, index):
        return self.copy(self.blocks.at[index], self.near.at[index], index, self.sibling)

    def over(self):
        return self.copy(self.low, self.far, 2, self.across)

    def put(self, index, values):
        if index == 0 or index == 2:
            self.blocks[index // 2] = values.astype(BF16)
            self.beside(index // 2).start()
        elif index == 1:
            self.beside(0).wait_recv()
            self.low[...] = (values + self.near[0].astype(F32)).astype(BF16)
            self.over().start()
        else:
            self.own = values

    def sums(self):
        self.beside(1).wait_recv()
        total = self.own + self.near[1].astype(F32)
        self.over().wait()
        total = total + self.far[...].astype(F32)
        self.beside(0).wait_send()
        self.beside(1).wait_send()
        return total

    @staticmethod
    def scratch(rows, columns):
        return [
            pltpu.VMEM((2, rows, columns), BF16),
            pltpu.VMEM((2, rows, columns), BF16),
            pltpu.VMEM((rows, columns), BF16),
            pltpu.VMEM((rows, columns), BF16),
            pltpu.SemaphoreType.DMA((3,)),
            pltpu.SemaphoreType.DMA((3,)),
        ]


IMPORT_STEPS = (
    ("a0",),
    ("a1", "a2", "p0"),
    ("a3", "a4", "c0", "p1"),
    ("p2", "p3", "c1"),
    ("p4", "c2", "c3", "c4"),
)


def attend_kernel(imports, *refs):
    (hidden, w_qkv, w_out, cosine, ahead, behind, q_gain, k_gain), refs = refs[:8], refs[8:]
    (w_mod, w_gate, w_up, lifted, bias, tokens, gate_a, grads), refs = refs[:8], refs[8:]
    (heads_out, rows_out, attended_out, branch_out), refs = refs[:4], refs[4:]
    (mod_out, gate_out, up_out, scale_out, middle_out, hidden_out, grads_all), refs = refs[:7], refs[7:]
    (mod_all, gate_own, up_own, mod_sem, load_sem), refs = refs[:5], refs[5:]
    sums = RowSums(*refs[:6])
    imports.bind({0: w_mod, 2: w_gate, 3: w_up}, {0: mod_all, 2: gate_out, 3: up_out}, refs[6:9])
    gather = RowGather(grads, grads_all, *refs[9:])
    greet(imports.partners())
    for block in range(len(imports.blocks)):
        imports.over(block).start()
    start_all(imports.own(0))
    loads = [
        pltpu.make_async_copy(imports.whole(k, sums.column), ref, load_sem.at[k - 2])
        for k, ref in ((2, gate_own), (3, up_own))
    ]
    stores = [
        pltpu.make_async_copy(ref, imports.outs[k].at[sums.column], load_sem.at[k])
        for k, ref in ((2, gate_own), (3, up_own))
    ]
    for copy in loads:
        copy.start()
    for array in imports.arrays:
        start_all(imports.beside(array))
    gather.start()
    factor = HD ** (-0.5)
    rows = branch_out.shape[0]
    heads = attended_out.shape[1] // LANES
    tables = cosine[...], ahead[...], behind[...]
    for pair in range(3 * heads // 2):
        span = slice(pair * 2 * LANES, (pair + 1) * 2 * LANES)
        projected = jnp.dot(hidden[...], w_qkv[:, span], preferred_element_type=F32)
        if pair >= heads:
            rows_out[:, span] = projected.astype(BF16)
            continue
        heads_out[:, span] = projected
        gain = (q_gain if pair < heads // 2 else k_gain)[...]
        for half in range(2):
            values = projected[:, half * LANES : (half + 1) * LANES]
            values = values * head_inverse(values) * gain
            start = pair * 2 * LANES + half * LANES
            rows_out[:, start : start + LANES] = rotated(values, tables, 1).astype(BF16)
    imports.do(*IMPORT_STEPS[0])
    for copy in loads:
        copy.wait()
    for copy in stores:
        copy.start()
    for index in range(4):
        block = pl.ds(pl.multiple_of(sums.order[index] * rows, rows), rows)
        for head in range(heads):
            spans = [slice((k * heads + head) * LANES, (k * heads + head + 1) * LANES) for k in range(3)]
            exp_scores = jnp.exp(over_rows(rows_out[block, spans[0]], rows_out[:, spans[1]]) * factor)
            scale = 1.0 / jnp.sum(exp_scores, axis=1, keepdims=True)
            mixed = jnp.dot(
                (exp_scores * scale).astype(BF16),
                rows_out[:, spans[2]],
                preferred_element_type=F32,
            )
            attended_out[block, spans[0]] = mixed.astype(BF16)
        sums.put(index, jnp.dot(attended_out[block, :], w_out[...], preferred_element_type=F32))
        imports.do(*IMPORT_STEPS[1 + index])
    gather.pass_on()
    wait_all(imports.own(0))
    for copy in imports.beside(0):
        copy.wait_recv()
    imports.share(0).wait_recv()
    store = pltpu.make_async_copy(mod_all, mod_out, mod_sem)
    store.start()
    width = tokens.shape[1]
    weights = mod_all[...].reshape(-1, 2 * width)
    modulation = jnp.dot(lifted[...], weights, preferred_element_type=F32)
    modulation = modulation + row_of(bias, imports.source_column(0), 2 * width)
    scale = modulation[:, width:]
    scale_out[...] = scale
    branch = sums.sums()
    branch_out[...] = branch
    middle = tokens[...].astype(F32) + gate_a[...] * branch
    middle_out[...] = middle
    hidden_out[...] = (middle * inverse_rms(middle) * (1.0 + scale) + modulation[:, :width]).astype(BF16)
    imports.end()
    for copy in imports.beside(0):
        copy.wait_send()
    for array in imports.arrays[1:]:
        wait_all(imports.beside(array))
    gather.end()
    for copy in stores:
        copy.wait()
    store.wait()


def attend(hidden, w_qkv, w_out, tables, q_gain, k_gain, w_mod, w_gate, w_up, lifted, bias, tokens, gate_a, grads):
    patches, wide = hidden.shape[0], w_qkv.shape[1]
    rows, width = patches // 4, hidden.shape[1]
    depth, ff = w_mod.shape[0], w_gate.shape[1] // 4
    imports = second_import(width, ff)
    vmem, anywhere = pl.BlockSpec(memory_space=pltpu.VMEM), pl.BlockSpec(memory_space=pl.ANY)

    def kernel(*refs):
        attend_kernel(imports, *refs)

    return pl.pallas_call(
        kernel,
        out_shape=[
            jax.ShapeDtypeStruct((patches, wide * 2 // 3), F32),
            jax.ShapeDtypeStruct((patches, wide), BF16),
            jax.ShapeDtypeStruct((patches, wide // 3), BF16),
            jax.ShapeDtypeStruct((rows, width), F32),
            jax.ShapeDtypeStruct((4, depth, 2 * width), BF16),
            jax.ShapeDtypeStruct((4, depth, ff), BF16),
            jax.ShapeDtypeStruct((4, depth, ff), BF16),
            jax.ShapeDtypeStruct((rows, width), F32),
            jax.ShapeDtypeStruct((rows, width), F32),
            jax.ShapeDtypeStruct((rows, width), BF16),
            jax.ShapeDtypeStruct((4, rows, width), BF16),
        ],
        in_specs=[vmem] * 8 + [anywhere] * 3 + [vmem] * 5,
        out_specs=[vmem] * 4 + [anywhere] * 3 + [vmem] * 4,
        scratch_shapes=[
            pltpu.VMEM((4, depth, 2 * width), BF16),
            pltpu.VMEM((depth, ff), BF16),
            pltpu.VMEM((depth, ff), BF16),
            pltpu.SemaphoreType.DMA,
            pltpu.SemaphoreType.DMA((4,)),
        ]
        + RowSums.scratch(rows, width)
        + imports.scratch()
        + RowGather.scratch(),
        compiler_params=pltpu.CompilerParams(
            collective_id=ATTEND_ID, has_side_effects=True, vmem_limit_bytes=63 * 2**20
        ),
        name="attend",
    )(hidden, w_qkv, w_out, *tables, q_gain, k_gain, w_mod, w_gate, w_up, lifted, bias, tokens, gate_a, grads)


def mlp_kernel(sums, *refs):
    (hidden, grads_all, w_gate, w_up, w_down), refs = refs[:5], refs[5:]
    (middle, scale, gate_a, gate_b, branch_a, cotangent, share), refs = refs[:7], refs[7:]
    (hidden_all, inner, grad_gate, grad_up), refs = refs[:4], refs[4:]
    (block_out, middle_out, branch_grad_out, mod_out), refs = refs[:4], refs[4:]
    handed_out, refs = refs[: len(sums.leaving)], refs[len(sums.leaving) :]
    if sums.parts:
        sums.bind([], [], None, [], None, [], handed_out, refs[30:])
    sums.others = {
        "inner": (inner, lambda: None),
        "grad_branch_b": (grads_all, lambda: None),
        "hidden_b": (hidden_all, lambda: None),
        "grad_gate_in": (grad_gate, lambda: None),
    }
    gather = RowGather(hidden, hidden_all, *refs[:3])
    halves = [RowSums(*refs[3 + 6 * k : 9 + 6 * k]) for k in range(4)]
    sums_grad, sums_branch = halves[:2], halves[2:]
    first = sums_grad[0]
    greet([first.sibling, first.across] + (sums.partners[:2] if sums.parts else []))
    gather.start()
    rows, width = hidden.shape
    near, far = first.chip * 2, (1 - first.chip) * 2
    depth = w_gate.shape[0] * w_gate.shape[1]
    gate_weights, up_weights = (ref[...].reshape(depth, ref.shape[2]) for ref in (w_gate, w_up))

    def block(ref, pair, start, count):
        return jnp.concatenate([ref[pair + k, start : start + count] for k in range(2)], axis=0)

    def process(pair, start, count):
        values = block(hidden_all, pair, start, count)
        gate_in = jnp.dot(values, gate_weights, preferred_element_type=F32)
        up_in = jnp.dot(values, up_weights, preferred_element_type=F32)
        grad_inner = over_rows(block(grads_all, pair, start, count), w_down[...])
        logistic = jax.nn.sigmoid(gate_in)
        activated = gate_in * logistic
        slope = logistic * (1.0 + gate_in * (1.0 - logistic))
        results = (
            (activated * up_in).astype(BF16),
            (grad_inner * up_in * slope).astype(BF16),
            (grad_inner * activated).astype(BF16),
        )
        for ref, result in zip((inner, grad_gate, grad_up), results, strict=True):
            for k in range(2):
                at = pl.multiple_of((pair + k) * rows + start, 16)
                ref[pl.ds(at, count), :] = result[k * count : (k + 1) * count]
        return over_rows(results[1], gate_weights) + over_rows(results[2], up_weights)

    def put(sums, partial, count, far_rows):
        @pl.when(first.core == 0)
        def _():
            held[0, :count], held[1, :count] = partial[count:], partial[:count]

        @pl.when(first.core == 1)
        def _():
            held[0, :count], held[1, :count] = partial[:count], partial[count:]

        if far_rows:
            sums.put(0, held[0, :count])
            sums.put(1, held[1, :count])
        else:
            sums.put(2, held[0, :count])
            return held[1, :count]

    held, own_grad, own_branch = refs[27:30]
    half = rows // 2
    for piece in range(GATHER_PIECES):
        gather.beside(piece).wait_recv()
    gather.local().wait()
    partial = process(near, 0, rows)
    for k in range(2):
        part = slice(k * half, (k + 1) * half)
        both = jnp.concatenate([partial[part], partial[rows + k * half : rows + (k + 1) * half]], axis=0)
        own_grad[part] = put(sums_grad[k], both, half, False)
    for k in range(2):
        pieces = range(k * GATHER_PIECES // 2, (k + 1) * GATHER_PIECES // 2)
        for piece in pieces:
            gather.over(piece).wait_recv()
            gather.onward(piece).start()
        for piece in pieces:
            gather.onward(piece).wait_recv()
        put(sums_grad[k], process(far, k * half, half), half, True)
    sums.do(*["b0", "b1"][: len(sums.parts)])
    for k in range(2):
        at = [pl.ds(pl.multiple_of((far + j) * rows + k * half, 16), half) for j in range(2)]
        values = jnp.concatenate([inner[part, :] for part in at], axis=0)
        put(sums_branch[k], jnp.dot(values, w_down[...], preferred_element_type=F32), half, True)
    sums.do(*["b2", "b3"][: len(sums.parts)])
    for k in range(2):
        at = [pl.ds(pl.multiple_of((near + j) * rows + k * half, 16), half) for j in range(2)]
        values = jnp.concatenate([inner[part, :] for part in at], axis=0)
        partial = jnp.dot(values, w_down[...], preferred_element_type=F32)
        own_branch[k * half : (k + 1) * half] = put(sums_branch[k], partial, half, False)
    sums.do(*["f0", "f1"][: len(sums.parts)])
    for k in range(2):
        part = slice(k * half, (k + 1) * half)
        sums_grad[k].put(3, own_grad[part])
        grad_hidden = sums_grad[k].sums()
        values = middle[part]
        inverse = inverse_rms(values)
        normed = values * inverse
        grad_out = cotangent[part].astype(F32) * share[...]
        grad_middle = grad_out + rms_back(grad_hidden * (1.0 + scale[part]), normed, inverse)
        middle_out[part] = grad_middle
        branch_grad_out[part] = (grad_middle * gate_a[part]).astype(BF16)
        mod_out[part, :width] = (grad_middle * branch_a[part]).astype(BF16)
        mod_out[part, width : 2 * width] = grad_hidden.astype(BF16)
        mod_out[part, 2 * width : 3 * width] = (grad_hidden * normed).astype(BF16)
    sums.do(*["f2", "f3"][: len(sums.parts)])
    for k in range(2):
        part = slice(k * half, (k + 1) * half)
        sums_branch[k].put(3, own_branch[part])
        branch = sums_branch[k].sums()
        block_out[part] = (middle[part] + gate_b[part] * branch).astype(BF16)
        grad_out = cotangent[part].astype(F32) * share[...]
        mod_out[part, 3 * width :] = (grad_out * branch).astype(BF16)
    for piece in range(GATHER_PIECES):
        gather.over(piece).wait_send()
        gather.beside(piece).wait_send()
        gather.onward(piece).wait_send()
    sums.end()


def mlp(hidden, grads_all, w_gate, w_up, w_down, rest, parts):
    rows, width = hidden.shape
    ff = w_down.shape[0]
    sums = GradSums(parts, (), [], (16, LANES))
    vmem, anywhere = pl.BlockSpec(memory_space=pltpu.VMEM), pl.BlockSpec(memory_space=pl.ANY)

    def kernel(*refs):
        mlp_kernel(sums, *refs)

    return pl.pallas_call(
        kernel,
        out_shape=[
            jax.ShapeDtypeStruct((4, rows, width), BF16),
            jax.ShapeDtypeStruct((4 * rows, ff), BF16),
            jax.ShapeDtypeStruct((4 * rows, ff), BF16),
            jax.ShapeDtypeStruct((4 * rows, ff), BF16),
            jax.ShapeDtypeStruct((rows, width), BF16),
            jax.ShapeDtypeStruct((rows, width), F32),
            jax.ShapeDtypeStruct((rows, width), BF16),
            jax.ShapeDtypeStruct((rows, 4 * width), BF16),
        ]
        + [jax.ShapeDtypeStruct(part.handed(), BF16) for part in parts],
        in_specs=[vmem] * 12,
        out_specs=[vmem] * 8 + [anywhere] * len(parts),
        scratch_shapes=RowGather.scratch()
        + RowSums.scratch(rows // 2, width) * 4
        + [
            pltpu.VMEM((2, rows // 2, width), F32),
            pltpu.VMEM((rows, width), F32),
            pltpu.VMEM((rows, width), F32),
        ]
        + (sums.scratch([]) if parts else []),
        compiler_params=pltpu.CompilerParams(
            collective_id=MLP_ID, has_side_effects=True, vmem_limit_bytes=63 * 2**20
        ),
        name="mlp",
    )(hidden, grads_all, w_gate, w_up, w_down, *rest)


def rows_to_columns(values, blocks):
    rows, columns = values.shape
    ways = lax.axis_size("seq")
    values = values.reshape(rows, blocks, ways, columns // (blocks * ways))
    moved = lax.all_to_all(values, "seq", split_axis=2, concat_axis=0, tiled=True)
    return moved.reshape(rows * ways, columns // ways)


def columns_to_rows(values, blocks):
    rows, columns = values.shape
    ways = lax.axis_size("seq")
    values = values.reshape(rows, blocks, 1, columns // blocks)
    moved = lax.all_to_all(values, "seq", split_axis=0, concat_axis=2, tiled=True)
    return moved.reshape(rows // ways, columns * ways)


def first_tile(place, tiles):
    return (tiles * place) // 4


def padded_rows(rows):
    return -(-rows // 16) * 16


class Part:
    def __init__(self, left, right, rows, span, out, order, at=None, **kinds):
        self.left, self.right, self.rows = left, right, rows
        self.start, self.columns, self.out = span[0], span[1] - span[0], out
        self.at = self.start if at is None else at
        self.order = order
        for kind in ("by_rows", "in_lanes", "bias", "enter", "leave"):
            setattr(self, kind, kinds.get(kind, False))
        self.slab = padded_rows(rows)

    def handed(self):
        return (2, 2, self.slab, self.columns)


def split_part(left, right, rows, columns, out, order, **kinds):
    middle = -(-columns // (2 * TILE)) * TILE
    return [
        Part(left, right, rows, span, out, order, **kinds)
        for span in ((0, middle), (middle, columns))
    ]


class GradSums:
    def __init__(self, parts, names, shared_shapes, small_shape, after=()):
        self.parts, self.names = parts, names
        self.after = dict(after)
        self.shared_shapes, self.small_shape = shared_shapes, small_shape
        self.has_rows = any(part.by_rows and not part.leave for part in parts)
        self.entering = [index for index, part in enumerate(parts) if part.enter]
        self.leaving = [index for index, part in enumerate(parts) if part.leave]

    def scratch(self, array_shapes):
        parts, count, groups = self.parts, len(self.parts), len(self.shared_shapes)
        none = pltpu.VMEM((16, LANES), BF16)
        shapes = [
            none if name in self.after else pltpu.VMEM(shape, BF16)
            for name, shape in zip(self.names, array_shapes, strict=True)
        ]
        shapes += [pltpu.VMEM((4, rows, columns), BF16) for rows, _, _, columns in self.shared_shapes]

        def each(lead, needed):
            return [
                pltpu.VMEM(lead(part) + (part.slab, part.columns), BF16) if needed(part) else none
                for part in parts
            ]

        shapes += each(lambda part: (2, 2) if part.enter else (2, 2, 2), lambda part: True)
        shapes += each(lambda part: (2, 2), lambda part: not part.enter)
        shapes += each(lambda part: (2,), lambda part: not part.leave)
        shapes += each(lambda part: (), lambda part: not part.leave)
        for _ in range(2):
            for part in parts:
                if part.leave:
                    shapes.append(none)
                elif part.by_rows:
                    shapes.append(pltpu.VMEM((part.slab, part.columns), BF16))
                else:
                    shapes.append(pltpu.VMEM((4, padded_rows(part.rows // 4), part.columns), BF16))
        widest = max(part.columns for part in parts)
        tallest = max(4 * LANES if part.in_lanes else part.rows for part in parts)
        return shapes + [
            pltpu.VMEM((tallest, widest), F32),
            pltpu.VMEM((4,) + self.small_shape, F32),
            pltpu.VMEM((3,) + self.small_shape, F32),
            pltpu.SemaphoreType.DMA((max(len(self.names), 1),)),
            pltpu.SemaphoreType.DMA((max(groups, 1), 3)),
            pltpu.SemaphoreType.DMA((max(groups, 1), 3)),
            pltpu.SemaphoreType.DMA((max(groups, 1),)),
            pltpu.SemaphoreType.DMA((count,)),
            pltpu.SemaphoreType.DMA((count, 3)),
            pltpu.SemaphoreType.DMA((count, 3)),
            pltpu.SemaphoreType.DMA((count, 3)),
            pltpu.SemaphoreType.DMA((count, 3)),
            pltpu.SemaphoreType.DMA((6,)),
            pltpu.SemaphoreType.DMA((6,)),
        ]

    def bind(self, ins, shared, small_in, outs, small_out, handed_in, handed_out, scratch):
        count, groups, names = len(self.parts), len(self.shared_shapes), self.names
        refs = list(scratch)

        def take(number):
            taken = refs[:number]
            del refs[:number]
            return taken

        self.shared, self.small_in, self.outs, self.small_out = shared, small_in, outs, small_out
        self.held = dict(zip(names, take(len(names)), strict=True))
        for name, place in self.after.items():
            self.held[name] = self.held[place]
        self.gathered = take(groups)
        self.own, self.first_in = take(count), take(count)
        self.second_in, self.third_in = take(count), take(count)
        self.slabs, self.slab_in = take(count), take(count)
        self.total, self.small, self.small_came = take(3)
        load_sem, self.share_send, self.share_recv, own_sem, hand_sem = take(5)
        self.send_sem, self.recv_sem = take(2)
        self.last_send, self.last_recv, self.small_send, self.small_recv = take(4)
        item, column = lax.axis_index("dp"), lax.axis_index("seq")
        self.column = column
        self.bits = [lax.rem(item, 2), lax.rem(item // 2, 2), item // 4]
        self.partners = [(item + (1 - 2 * self.bits[k]) * (1 << k), column) for k in range(3)]
        self.peers = [(item, lax.rem(column + k, 4)) for k in range(1, 4)]
        self.owner = (2 * column + item // 4, lax.rem(item, 4))
        self.feeder = (4 * lax.rem(item, 2) + column, item // 2)
        self.elsewhere = jnp.logical_or(self.owner[0] != item, self.owner[1] != column)
        self.loads = {
            name: pltpu.make_async_copy(ins[i], self.held[name], load_sem.at[i])
            for i, name in enumerate(names)
        }
        self.own_shares = [
            pltpu.make_async_copy(
                self.columns_of(g, column), self.gathered[g].at[column], own_sem.at[g]
            )
            for g in range(groups)
        ]
        self.ready = set()
        self.others = {}
        self.handing = {
            index: pltpu.make_async_copy(ref, self.own[index], hand_sem.at[index])
            for index, ref in zip(self.entering, handed_in, strict=True)
        }
        for index, ref in zip(self.leaving, handed_out, strict=True):
            half = self.own[index].at[self.half(index, True)]
            self.handing[index] = pltpu.make_async_copy(half, ref, hand_sem.at[index])

    def greet(self):
        barrier = pltpu.get_barrier_semaphore()
        for partner in self.partners + self.peers:
            pl.semaphore_signal(barrier, inc=1, device_id=partner, device_id_type=MESH)
        waits = 6
        if self.has_rows:
            waits = 6 + self.elsewhere.astype(jnp.int32)

            @pl.when(self.elsewhere)
            def _():
                pl.semaphore_signal(barrier, inc=1, device_id=self.feeder, device_id_type=MESH)

        pl.semaphore_wait(barrier, waits)

    def load(self):
        for index in self.entering:
            self.handing[index].start()
        for name in self.names:
            if name not in self.after:
                self.loads[name].start()

    def remote(self, source, target_ref, send, recv, target):
        return pltpu.make_async_remote_copy(
            src_ref=source,
            dst_ref=target_ref,
            send_sem=send,
            recv_sem=recv,
            device_id=target,
            device_id_type=MESH,
        )

    def columns_of(self, group, place):
        _, wide, first, narrow = self.shared_shapes[group]
        start = first_tile(place, wide // TILE) * TILE + first
        return self.shared[group].at[:, pl.ds(pl.multiple_of(start, TILE), narrow)]

    def shares(self, group):
        return [
            self.remote(
                self.columns_of(group, peer[1]),
                self.gathered[group].at[self.column],
                self.share_send.at[group, k],
                self.share_recv.at[group, k],
                peer,
            )
            for k, peer in enumerate(self.peers)
        ]

    def share(self):
        for group in range(len(self.shared_shapes)):
            self.own_shares[group].start()
            for copy in self.shares(group):
                copy.start()

    def operand(self, name):
        if isinstance(name, int):
            if name not in self.ready:
                self.own_shares[name].wait()
                for copy in self.shares(name):
                    copy.wait()
            self.ready.add(name)
            ref = self.gathered[name]
            return ref[...].reshape(4 * ref.shape[1], ref.shape[2])
        first = name not in self.ready
        self.ready.add(name)
        if name in self.others:
            ref, wait = self.others[name]
            if first:
                wait()
            return ref[...].reshape(-1, ref.shape[-1])
        if first:
            self.loads[name].wait()
        return self.held[name][...]

    def multiply(self, index):
        part = self.parts[index]
        left, right = self.operand(part.left), self.operand(part.right)
        right = right[:, part.start : part.start + part.columns]
        if part.bias:
            sums = jnp.sum(right.astype(F32), axis=0, keepdims=True)
            for tile in range(part.columns // TILE):
                row = part.at // TILE + tile
                self.small[0, row : row + 1] = sums[:, tile * TILE : (tile + 1) * TILE]
        own, rows = self.own[index], part.rows
        if part.in_lanes:
            self.total[: left.shape[1], : part.columns] = over_first(left, right)
            for d in range(8):
                start = d // 2 * LANES + d % 2 * rows
                own[d // 4, d // 2 % 2, d % 2] = self.cut(start, rows, part.slab, part.columns)
            return
        step = 3 * TILE
        for start in range(0, left.shape[1], step):
            product = over_first(left[:, start : start + step], right).astype(BF16)
            for d in range(8):
                low, high = max(start, d * rows), min(start + step, (d + 1) * rows)
                if low < high:
                    place = slice(low - d * rows, high - d * rows)
                    own[d // 4, d // 2 % 2, d % 2, place] = product[low - start : high - start]

    def cut(self, start, rows, padded, columns):
        values = self.total[start : start + rows, :columns]
        if padded > rows:
            values = jnp.concatenate([values, jnp.zeros((padded - rows, columns), F32)], axis=0)
        return values.astype(BF16)

    def half(self, index, mine):
        order = self.parts[index].order
        pick = self.bits[order] if mine else 1 - self.bits[order]
        return (slice(None), slice(None), pick) if order == 0 else (slice(None), pick)

    def place(self, index, high, low):
        if self.parts[index].enter:
            return (high, low)
        if self.parts[index].order == 0:
            return (high, low, self.bits[0])
        return (high, self.bits[1], low)

    def stage(self, index, step):
        order = self.parts[index].order
        other = 1 - order
        sems = self.send_sem.at[index, step], self.recv_sem.at[index, step]
        own = self.own[index]
        if step == 0:
            source = own.at[self.half(index, False)]
            return self.remote(source, self.first_in[index], *sems, self.partners[order])
        if step == 1:
            place = self.place(index, slice(None), 1 - self.bits[other])
            return self.remote(own.at[place], self.second_in[index], *sems, self.partners[other])
        place = self.place(index, 1 - self.bits[2], self.bits[other])
        return self.remote(own.at[place], self.third_in[index], *sems, self.partners[2])

    def begin(self, index):
        if self.parts[index].enter:
            self.handing[index].wait()
            self.stage(index, 1).start()
            return
        self.multiply(index)
        self.stage(index, 0).start()

    def end_first(self, index):
        self.stage(index, 0).wait()
        for high in range(2):
            for low in range(2):
                place = self.place(index, high, low)
                came = self.first_in[index][high, low].astype(F32)
                self.own[index][place] = (self.own[index][place].astype(F32) + came).astype(BF16)
        if self.parts[index].leave:
            self.handing[index].start()
        else:
            self.stage(index, 1).start()

    def end_second(self, index):
        self.stage(index, 1).wait()
        for high in range(2):
            place = self.place(index, high, self.bits[1 - self.parts[index].order])
            came = self.second_in[index][high].astype(F32)
            self.own[index][place] = (self.own[index][place].astype(F32) + came).astype(BF16)
        self.stage(index, 2).start()

    def last(self, index):
        if self.parts[index].by_rows:
            sems = self.last_send.at[index, 0], self.last_recv.at[index, 0]
            return [self.remote(self.slabs[index], self.slab_in[index], *sems, self.owner)]
        return [
            self.remote(
                self.slabs[index].at[peer[1]],
                self.slab_in[index].at[self.column],
                self.last_send.at[index, k],
                self.last_recv.at[index, k],
                peer,
            )
            for k, peer in enumerate(self.peers)
        ]

    def end_third(self, index):
        part = self.parts[index]
        self.stage(index, 2).wait()
        place = self.place(index, self.bits[2], self.bits[1 - part.order])
        sums = self.own[index][place].astype(F32) + self.third_in[index][...].astype(F32)
        if part.by_rows:
            self.slabs[index][...] = sums.astype(BF16)

            @pl.when(self.elsewhere)
            def _():
                self.last(index)[0].start()

            @pl.when(jnp.logical_not(self.elsewhere))
            def _():
                self.slab_in[index][...] = self.slabs[index][...]

            return
        self.total[: part.rows, : part.columns] = sums
        rows = part.rows // 4
        for k in range(4):
            self.slabs[index][k] = self.cut(k * rows, rows, padded_rows(rows), part.columns)
        for copy in self.last(index):
            copy.start()
        self.slab_in[index][self.column] = self.slabs[index][self.column]

    def end_last(self, index):
        part = self.parts[index]
        out, stop = self.outs[part.out], part.at + part.columns
        if part.by_rows:

            @pl.when(self.elsewhere)
            def _():
                self.last(index)[0].wait()

            out[:, part.at : stop] = self.slab_in[index][...].astype(F32)[: part.rows]
            return
        for copy in self.last(index):
            copy.wait()
        rows = part.rows // 4
        wide = out.shape[-1]
        for k in range(4):
            values = self.slab_in[index][k].astype(F32)[:rows]
            if len(out.shape) == 3:
                out[k, :, part.at : stop] = values
            else:
                start = first_tile(k, wide // TILE) * TILE
                out[:, start + part.at : start + stop] = values

    def small_step(self, step):
        if step < 3:
            sems = self.small_send.at[step], self.small_recv.at[step]
            return [
                self.remote(self.small.at[step], self.small_came.at[step], *sems, self.partners[step])
            ]
        return [
            self.remote(
                self.small.at[3],
                self.small_out.at[self.column],
                self.small_send.at[3 + k],
                self.small_recv.at[3 + k],
                peer,
            )
            for k, peer in enumerate(self.peers)
        ]

    def end_small(self, at):
        self.small_step(at - 1)[0].wait()
        self.small[at] = self.small[at - 1] + self.small_came[at - 1]
        for copy in self.small_step(at):
            copy.start()

    def do(self, *steps):
        kinds = {
            "b": self.begin,
            "f": self.end_first,
            "s": self.end_second,
            "t": self.end_third,
            "l": self.end_last,
            "x": self.small_exchange,
            "r": lambda number: self.loads[self.names[number]].start(),
        }
        for step in steps:
            kinds[step[0]](int(step[1:]))

    def small_exchange(self, at):
        if at == 0:
            self.small_step(0)[0].start()
        elif at < 4:
            self.end_small(at)
        else:
            self.small_out[self.column] = self.small[3]
            for copy in self.small_step(3):
                copy.wait()

    def end(self):
        for index in self.leaving:
            self.handing[index].wait()


def split(refs, *counts):
    groups, start = [], 0
    for number in counts:
        groups.append(refs[start : start + number])
        start += number
    return groups + [refs[start:]]


LAST_STEPS = (
    ("b0", "b1", "b2", "b3", "b4"),
    ("b5",),
    ("b6", "s0", "s1"),
    ("s2", "f3"),
    ("f4", "s3", "x0", "t0", "t1", "t2"),
    ("s4", "f5", "x1", "f6", "s5", "x2", "t3", "s6", "x3", "t4", "l0", "l1", "l2", "t5", "t6", "l3", "l4", "l5", "l6", "x4"),
)


def last_grads(parts, arrays, shared, small, handed, out_shapes, condition, embed, rows_a, rows_b, mods):
    names = tuple(arrays)
    shapes = [value.shape + (first, columns) for value, first, columns in shared]
    sums = GradSums(parts, names, shapes, small.shape)
    count = len(out_shapes)
    width = condition.shape[1]

    def kernel(*refs):
        ins, given, handed_in, given_mods, (small_in, seen, embed_in, low, high), outs, lasts, refs = split(
            refs, len(names), len(shared), len(handed), len(mods), 5, count, 2
        )
        (small_out, condition_out), held, (mod_sem,), scratch = lasts, refs[:2], refs[2:3], refs[3:]
        sums.bind(ins, given, small_in, outs, small_out, handed_in, [], scratch)
        sums.load()
        loads = [
            pltpu.make_async_copy(source, target, mod_sem.at[k])
            for k, (source, target) in enumerate(zip(given_mods, held, strict=True))
        ]
        start_all(loads)
        sums.greet()
        sums.share()
        sums.small[0] = small_in[...]
        first, rest = held
        condition_out[...] = jnp.zeros_like(condition_out)
        work = [
            (low, 0, first, 0, 2 * width),
            (high, 0, first, 2 * width, width),
            (high, width, rest, 0, 2 * width),
            (high, 3 * width, first, 3 * width, width),
        ]
        for number, steps in enumerate(LAST_STEPS):
            sums.do(*steps)
            if number == 0:
                wait_all(loads)
            if number < 4:
                rows, at, weights, start, columns = work[number]
                condition_out[...] += over_rows(
                    rows[:, at : at + columns], weights[:, start : start + columns]
                )
            if number == 4:
                values = seen[...].astype(F32) + embed_in[...]
                condition_out[...] = condition_out[...] * silu_slope(values)
        sums.end()

    vmem, anywhere = pl.BlockSpec(memory_space=pltpu.VMEM), pl.BlockSpec(memory_space=pl.ANY)
    return pl.pallas_call(
        kernel,
        out_shape=[jax.ShapeDtypeStruct(shape, F32) for shape in out_shapes]
        + [
            jax.ShapeDtypeStruct((4,) + small.shape, F32),
            jax.ShapeDtypeStruct(condition.shape, F32),
        ],
        in_specs=[anywhere] * (len(names) + len(shared) + len(handed) + len(mods)) + [vmem] * 5,
        out_specs=[vmem] * (count + 2),
        scratch_shapes=[pltpu.VMEM(value.shape, BF16) for value in mods]
        + [pltpu.SemaphoreType.DMA((len(mods),))]
        + sums.scratch([value.shape for value in arrays.values()]),
        compiler_params=pltpu.CompilerParams(
            collective_id=SUM_ID, has_side_effects=True, vmem_limit_bytes=63 * 2**20
        ),
        name="last_grads",
    )(
        *arrays.values(),
        *[value for value, _, _ in shared],
        *handed,
        *mods,
        small,
        condition,
        embed,
        rows_a,
        rows_b,
    )


BACK_STEPS = {
    "start": ("b0", "b1", "b2", "b3", "b4", "b5"),
    "gathered": ("b6", "b7", "s1", "s0", "s3"),
    "head0": ("s4", "f2"),
    "head1": ("b8", "f5", "f6", "f7", "s2", "t1", "t0", "t3"),
    "head2": ("b9", "s5", "t4"),
    "head3": ("b10", "s6", "s7", "f8", "t2", "x0"),
    "put3": ("t5", "x1", "t6", "t7", "f9", "x2", "l0", "l1", "l3", "l4"),
    "end": ("f10", "x3", "l2", "l5", "l6", "l7", "x4"),
}


def pack_heads(lanes_ref, packed_ref):
    rows, count = lanes_ref.shape[0], lanes_ref.shape[1] // LANES
    lane = lax.broadcasted_iota(jnp.int32, (rows, LANES), 1)
    for tile in range(packed_ref.shape[1] // LANES):
        values = jnp.zeros((rows, LANES), F32)
        for head in range(count):
            start = head * HD - tile * LANES
            if -HD < start < LANES:
                one = lanes_ref[:, head * LANES : (head + 1) * LANES].astype(F32)
                one = pltpu.roll(one, start % LANES, 1) if start else one
                values = jnp.where(jnp.logical_and(lane >= start, lane < start + HD), one, values)
        packed_ref[:, tile * LANES : (tile + 1) * LANES] = values.astype(BF16)


def back_kernel(sums, own, outs, refs):
    grad_in, rows_in, heads_in, w_qkv_in, w_out_in, cosine, ahead, behind, q_gain, k_gain = own[:10]
    grad_middle, tokens, scale, lifted = own[10:]
    tokens_out, mod_out, gains_out, packed, lifted_all = outs
    (branch_all, rows, heads, w_qkv, w_out, grad_heads, load_sem), refs = refs[:7], refs[7:]
    gather = RowGather(grad_in, branch_all, *refs[:3])
    gather_lifted = RowGather(lifted, lifted_all, *refs[3:6])
    row_sums = RowSums(*refs[6:])
    local_rows = grad_in.shape[0]
    count = grad_heads.shape[1] // LANES
    factor = HD ** (-0.5)
    loads = [
        pltpu.make_async_copy(source, target, load_sem.at[k])
        for k, (source, target) in enumerate(
            ((rows_in, rows), (w_out_in, w_out), (w_qkv_in, w_qkv))
        )
    ]

    def load_head(head):
        return [
            pltpu.make_async_copy(
                heads_in.at[:, pl.ds((k * count + head) * LANES, LANES)],
                heads.at[head % 2, k],
                load_sem.at[3 + 2 * (head % 2) + k],
            )
            for k in range(2)
        ]

    for k in (1, 0, 2):
        loads[k].start()
    start_all(load_head(0))
    sums.load()
    sums.greet()
    gather.start()
    gather_lifted.start()
    sums.share()
    sums.small[0] = jnp.zeros_like(sums.small[0])
    sums.others["grad_branch_a"] = (branch_all, lambda: None)
    sums.others["lifted"] = (lifted_all, gather_lifted.end)
    sums.do(*BACK_STEPS["start"])
    gather.pass_on()
    gather.end()
    loads[1].wait()
    grad_branch = branch_all[...].reshape(4 * local_rows, branch_all.shape[2])
    grad_heads[...] = over_rows(grad_branch, w_out[...]).astype(BF16)
    sums.do(*BACK_STEPS["gathered"])
    loads[0].wait()
    tables = cosine[...], ahead[...], behind[...]
    block = 256
    gain_sums = [jnp.zeros((1, LANES), F32), jnp.zeros((1, LANES), F32)]
    for head in range(count):
        spans = [slice((k * count + head) * LANES, (k * count + head + 1) * LANES) for k in range(3)]
        if head + 1 < count:
            start_all(load_head(head + 1))
        keys, values = rows[:, spans[1]], rows[:, spans[2]]
        grad_query, grad_key, grad_value = [], None, None
        for start in range(0, rows.shape[0], block):
            queries = rows[start : start + block, spans[0]]
            grads = grad_heads[start : start + block, spans[0]]
            exp_scores = jnp.exp(over_rows(keys, queries) * factor)
            probs = exp_scores * (1.0 / jnp.sum(exp_scores, axis=0, keepdims=True))
            grad_probs = over_rows(values, grads)
            inner = jnp.sum(probs * grad_probs, axis=0, keepdims=True)
            grad_scores = (probs * (grad_probs - inner)).astype(BF16)
            grad_query.append(over_first(grad_scores, keys))
            key_term = jnp.dot(grad_scores, queries, preferred_element_type=F32)
            value_term = jnp.dot(probs.astype(BF16), grads, preferred_element_type=F32)
            grad_key = key_term if grad_key is None else grad_key + key_term
            grad_value = value_term if grad_value is None else grad_value + value_term
        rows[:, spans[2]] = grad_value.astype(BF16)
        terms = (jnp.concatenate(grad_query, axis=0) * factor, grad_key * factor)
        wait_all(load_head(head))
        for k, (term, gain) in enumerate(zip(terms, (q_gain, k_gain), strict=True)):
            raw = heads[head % 2, k]
            inverse = head_inverse(raw)
            normed = raw * inverse
            back = rotated(term, tables, -1)
            gain_sums[k] = gain_sums[k] + jnp.sum(back * normed, axis=0, keepdims=True)
            back = back * gain[...]
            mean = jnp.sum(back * normed, axis=-1, keepdims=True) * (1.0 / HD)
            rows[:, spans[k]] = (inverse * (back - normed * mean)).astype(BF16)
        if head == count - 1:
            pack_heads(rows, packed)
        if head == 0:
            gather_lifted.pass_on()
        sums.do(*BACK_STEPS["head%d" % head])
    gains_out[...] = jnp.concatenate(gain_sums + [jnp.zeros((6, LANES), F32)], axis=0)
    loads[2].wait()
    for index in range(4):
        part = pl.ds(pl.multiple_of(row_sums.order[index] * local_rows, local_rows), local_rows)
        row_sums.put(index, over_rows(rows[part, :], w_qkv[...]))
        sums.do(*BACK_STEPS.get("put%d" % index, ()))
    grad_hidden = row_sums.sums()
    values = tokens[...].astype(F32)
    inverse = inverse_rms(values)
    normed = values * inverse
    tokens_out[...] = grad_middle[...] + rms_back(grad_hidden * (1.0 + scale[...]), normed, inverse)
    width = values.shape[1]
    mod_out[:, :width] = grad_hidden.astype(BF16)
    mod_out[:, width:] = (grad_hidden * normed).astype(BF16)
    sums.do(*BACK_STEPS["end"])
    sums.end()


def attention_back(own, parts, arrays, shared, small_shape, handed, out_shapes):
    names = tuple(arrays)
    shapes = [value.shape + (first, columns) for value, first, columns in shared]
    sums = GradSums(parts, names, shapes, small_shape)
    count = len(out_shapes)
    rows, width = own[0].shape
    kept, heads, w_qkv, w_out = own[1:5]
    leaving = [parts[index].handed() for index in sums.leaving]
    vmem, anywhere = pl.BlockSpec(memory_space=pltpu.VMEM), pl.BlockSpec(memory_space=pl.ANY)
    own_scratch = [
        pltpu.VMEM((4, rows, width), BF16),
        pltpu.VMEM(kept.shape, BF16),
        pltpu.VMEM((2, 2, 4 * rows, LANES), F32),
        pltpu.VMEM(w_qkv.shape, BF16),
        pltpu.VMEM(w_out.shape, BF16),
        pltpu.VMEM((4 * rows, w_out.shape[0]), BF16),
        pltpu.SemaphoreType.DMA((7,)),
        *RowGather.scratch(),
        *RowGather.scratch(),
        *RowSums.scratch(rows, width),
    ]

    def kernel(*refs):
        ins, exchanged, handed_in, given, outs, handed_out, (small_out,), results, mine, scratch = split(
            refs,
            len(names),
            len(shared),
            len(handed),
            len(own),
            count,
            len(leaving),
            1,
            5,
            len(own_scratch),
        )
        sums.bind(ins, exchanged, None, outs, small_out, handed_in, handed_out, scratch)
        back_kernel(sums, given, results, mine)

    return pl.pallas_call(
        kernel,
        out_shape=[jax.ShapeDtypeStruct(shape, F32) for shape in out_shapes]
        + [jax.ShapeDtypeStruct(shape, BF16) for shape in leaving]
        + [
            jax.ShapeDtypeStruct((4,) + small_shape, F32),
            jax.ShapeDtypeStruct((rows, width), F32),
            jax.ShapeDtypeStruct((rows, 2 * width), BF16),
            jax.ShapeDtypeStruct((8, LANES), F32),
            jax.ShapeDtypeStruct((4 * rows, -(-3 * width // 4 // LANES) * LANES), BF16),
            jax.ShapeDtypeStruct((4, rows, width), BF16),
        ],
        in_specs=[anywhere] * (len(names) + len(shared) + len(handed))
        + [vmem]
        + [anywhere] * 4
        + [vmem] * 9,
        out_specs=[vmem] * count + [anywhere] * len(leaving) + [vmem] * 6,
        scratch_shapes=own_scratch + sums.scratch([value.shape for value in arrays.values()]),
        compiler_params=pltpu.CompilerParams(
            collective_id=BACK_ID, has_side_effects=True, vmem_limit_bytes=63 * 2**20
        ),
        name="attention_back",
    )(*arrays.values(), *[value for value, _, _ in shared], *handed, *own)


def to_owners(rows):
    n_dp, n_seq = lax.axis_size("dp"), lax.axis_size("seq")
    pairs = []
    for d in range(n_dp):
        for s in range(n_seq):
            pairs.append((d * n_seq + s, s * n_dp + d))
    return lax.ppermute(rows, ("dp", "seq"), pairs)


def plain_sums(left, right, blocks):
    mine = lax.psum_scatter(outer_sum(left, right).astype(BF16), "dp", scatter_dimension=0, tiled=True)
    return (columns_to_rows(mine, blocks) if blocks else to_owners(mine)).astype(F32)


def padded_small(values):
    values = jnp.pad(values, ((0, 8 - values.shape[0]), (0, TILE - values.shape[1])))
    return jnp.concatenate([jnp.zeros((8, TILE), F32), values])


def again(part):
    span = (part.start, part.start + part.columns)
    kinds = {"by_rows": part.by_rows, "enter": True}
    return Part(None, None, part.rows, span, part.out, part.order, at=part.at, **kinds)


def bias_columns(small, tiles):
    edges = [first_tile(k, tiles) for k in range(4)] + [tiles]
    sums = small.reshape(4, -1)
    return [sums[k, : (edges[k + 1] - edges[k]) * TILE] for k in range(4)]


def in_lanes(values, axis):
    shape = values.shape
    values = values.reshape(shape[:axis] + (shape[axis] // HD, HD) + shape[axis + 1 :])
    pads = [(0, 0)] * len(values.shape)
    pads[axis + 1] = (0, LANES - HD)
    return jnp.pad(values, pads).reshape(shape[:axis] + (-1,) + shape[axis + 1 :])


def out_of_lanes(values):
    return values.reshape(values.shape[0], -1, LANES)[:, :, :HD]


def plain_back(grad_branch_a, given):
    kept, projected, w_qkv, w_out, cosine, ahead, behind, q_gain, k_gain = given
    patches, count = kept.shape[0], w_out.shape[0] // LANES
    factor = HD ** (-0.5)
    tables = [table[:, None, :] for table in (cosine, ahead, behind)]

    def turn(values):
        turned = jnp.roll(values, -QUARTER, -1) * tables[1] + jnp.roll(values, QUARTER, -1) * tables[2]
        return values * tables[0] - turned

    query, key, value = jnp.split(kept.reshape(patches, 3 * count, LANES), 3, axis=1)
    grads = times_transpose(grad_branch_a, w_out).astype(BF16).reshape(patches, count, LANES)
    scores = jnp.einsum("qhd,khd->hqk", query, key, preferred_element_type=F32) * factor
    exp_scores = jnp.exp(scores)
    probs = exp_scores / jnp.sum(exp_scores, axis=-1, keepdims=True)
    grad_probs = jnp.einsum("qhd,khd->hqk", grads, value, preferred_element_type=F32)
    inner = jnp.sum(probs * grad_probs, axis=-1, keepdims=True)
    grad_scores = (probs * (grad_probs - inner)).astype(BF16)
    terms = (
        jnp.einsum("hqk,khd->qhd", grad_scores, key, preferred_element_type=F32) * factor,
        jnp.einsum("hqk,qhd->khd", grad_scores, query, preferred_element_type=F32) * factor,
    )
    grad_value = jnp.einsum("hqk,qhd->khd", probs.astype(BF16), grads, preferred_element_type=F32)
    raws = jnp.split(projected.reshape(patches, 2 * count, LANES), 2, axis=1)
    results, gains = [], []
    for term, raw, gain in zip(terms, raws, (q_gain, k_gain), strict=True):
        inverse = head_inverse(raw)
        normed = raw * inverse
        back = turn(term)
        gains.append(jnp.sum(back * normed, axis=(0, 1)))
        back = back * gain[0]
        mean = jnp.sum(back * normed, axis=-1, keepdims=True) * (1.0 / HD)
        results.append(inverse * (back - normed * mean))
    grad_lanes = jnp.concatenate(results + [grad_value], axis=1).reshape(kept.shape).astype(BF16)
    return grad_lanes, times_transpose(grad_lanes, w_qkv), jnp.stack(gains)


def shards(
    tokens,
    condition,
    cotangent,
    w_qkv,
    w_out,
    w_gate,
    w_up,
    w_down,
    w_mod,
    b_mod,
    q_gain,
    k_gain,
    noise_counts,
    time_steps,
    positions,
):
    local_rows, width = tokens.shape[1:]
    ways = lax.axis_size("seq")
    patches = local_rows * ways
    local_heads = HEADS // ways
    item = lax.axis_index("dp")
    image = jnp.arange(noise_counts.shape[0], dtype=jnp.int32)
    running = jnp.sum(jnp.where(image[None, :] <= image[:, None], noise_counts[None, :], 0), axis=1)
    image_id = jnp.sum((running <= item).astype(jnp.int32))
    chosen = jnp.arange(noise_counts.shape[0], dtype=jnp.int32) == image_id
    share = 1.0 / jnp.sum(jnp.where(chosen, noise_counts, 0)).astype(F32)

    embed = time_embed(time_steps, width)
    bias_row = b_mod.reshape(-1, LANES)
    share_row = jnp.full((1, width), share)
    (
        mod_first,
        w_qkv_lanes,
        scale_a,
        gate_a,
        gate_b,
        hidden_a,
        own_branch_b,
        lifted_low,
        all_positions,
    ) = first_stage(
        w_mod, w_qkv, condition[0], tokens[0], cotangent[0], embed, share_row, bias_row, positions
    )
    hidden_a = hidden_a.reshape(patches, width)
    w_qkv_lanes = w_qkv_lanes.reshape(width, w_qkv_lanes.shape[2])
    tables = lane_tables(jnp.transpose(all_positions[:, :, 0], (1, 0, 2)).reshape(2, patches))
    w_out_lanes = in_lanes(w_out, 0)
    gain_lanes = [jnp.pad(gain, (0, LANES - HD))[None] for gain in (q_gain, k_gain)]
    (
        projected_lanes,
        rows_lanes,
        attended_lanes,
        branch_a,
        mod_rest,
        gate_cols,
        up_cols,
        scale_b,
        middle,
        hidden_b,
        grads_all,
    ) = attend(
        hidden_a,
        w_qkv_lanes,
        w_out_lanes,
        tables,
        *gain_lanes,
        w_mod,
        w_gate,
        w_up,
        lifted_low,
        bias_row,
        tokens[0],
        gate_a,
        own_branch_b,
    )
    grad_branch_b = grads_all.reshape(patches, width)
    pieces = lax.axis_size("dp") == 8
    ff, heads_wide, own_rows = w_down.shape[0], local_heads * HD, width // 8
    handed_mlp = [
        split_part("inner", "grad_branch_b", ff // 8, width, 0, 0, by_rows=True, leave=True),
        split_part("hidden_b", "grad_gate_in", own_rows, ff, 1, 1, leave=True),
    ]
    handed_mlp = [handed_mlp[k % 2][k // 2] for k in range(4)] if pieces else []
    hidden_b, inner, grad_gate_in, grad_up_in, block_out, grad_middle, own_branch_a, grad_mod_b, *handed = mlp(
        hidden_b,
        grads_all,
        gate_cols,
        up_cols,
        w_down,
        (middle, scale_b, gate_a, gate_b, branch_a, cotangent[0], share_row),
        handed_mlp,
    )
    hidden_b = hidden_b.reshape(patches, width)
    mod_first, mod_rest = mod_first.reshape(width, -1), mod_rest.reshape(width, -1)
    given = [rows_lanes, projected_lanes, w_qkv_lanes, w_out_lanes, *tables, *gain_lanes]
    if pieces:
        tiles_b, tiles_a = grad_mod_b.shape[1] // TILE, 2 * width // TILE
        mod_b, mod_a = -(-tiles_b // 4) * TILE, -(-tiles_a // 4) * TILE
        third = mod_b // 3
        late_a = mod_a // 2 // TILE * TILE
        ups = split_part("hidden_b", "grad_up_in", own_rows, ff, 2, 0)
        lasts = split_part("hidden_a", "grad_project", own_rows, 3 * heads_wide, 1, 0)
        mods = [
            Part("lifted", k, own_rows, (0, third), 0, 0, at=k * third, bias=True, leave=True)
            for k in range(3)
        ]
        downs, gates = handed_mlp[0::2], handed_mlp[1::2]
        parts_b = [
            again(downs[0]),
            again(gates[0]),
            ups[0],
            again(downs[1]),
            again(gates[1]),
            ups[1],
            *split_part("attended", "grad_branch_a", heads_wide // 8, width, 3, 1, by_rows=True, in_lanes=True),
            *mods,
        ]
        arrays_b = {
            "hidden_b": hidden_b,
            "grad_up_in": grad_up_in,
            "attended": attended_lanes,
        }
        shapes_b = [
            (ff // 8, width),
            (own_rows // 4, 4 * ff),
            (own_rows // 4, 4 * ff),
            (heads_wide // 8, width),
        ]
        own = [own_branch_a, *given, grad_middle, tokens[0], scale_a, lifted_low]
        (
            grad_w_down,
            grad_w_gate,
            grad_w_up,
            grad_w_out,
            *handed,
            small_b,
            grad_tokens,
            grad_mod_a,
            gain_sums,
            grad_project,
            lifted_full,
        ) = attention_back(
            own,
            parts_b,
            arrays_b,
            [(grad_mod_b, k * third, third) for k in range(3)],
            (16, LANES),
            [handed[k] for k in (0, 1, 2, 3)],
            shapes_b,
        )
        lifted_full = lifted_full.reshape(patches, width)
        parts_a = [again(part) for part in mods] + lasts
        spans = ((0, mod_a - late_a), (mod_a - late_a, mod_a))
        parts_a += [
            Part("lifted", k, own_rows, (0, span[1] - span[0]), 2, 0, at=span[0], bias=True)
            for k, span in enumerate(spans)
        ]
        shapes_a = [
            (own_rows // 4, tiles_b * TILE),
            (4, own_rows // 4, 3 * heads_wide),
            (own_rows // 4, tiles_a * TILE),
        ]
        sum_b, qkv_sum, sum_a, small_a, grad_condition = last_grads(
            parts_a,
            {"hidden_a": hidden_a, "grad_project": grad_project, "lifted": lifted_full},
            [(grad_mod_a, span[0], span[1] - span[0]) for span in spans],
            padded_small(gain_sums[:2]),
            handed,
            shapes_a,
            condition[0],
            embed,
            grad_mod_a,
            grad_mod_b,
            [mod_first, mod_rest],
        )
        grad_w_qkv = jnp.transpose(
            qkv_sum.reshape(4, own_rows // 4, 3, heads_wide), (1, 2, 0, 3)
        ).reshape(own_rows // 4, 3 * width)
        grad_w_mod = jnp.concatenate([sum_a, sum_b], axis=1)
        bias = jnp.concatenate(bias_columns(small_a, tiles_a) + bias_columns(small_b, tiles_b))
        own_bias = bias.shape[0] // (8 * ways)
        sum_bias = lax.dynamic_slice(
            bias, ((item * ways + lax.axis_index("seq")) * own_bias,), (own_bias,)
        )
        gains = jnp.sum(small_a[:, 8:10, :HD], axis=0)
    else:
        tokens_f = tokens[0].astype(F32)
        inverse_a = inverse_rms(tokens_f)
        normed_a = tokens_f * inverse_a
        grad_branch_a = gather_rows(own_branch_a)
        grad_lanes, partial, gain_sums = plain_back(grad_branch_a, given)
        grad_hidden_a = scatter_rows(partial)
        grad_tokens = grad_middle + rms_back(grad_hidden_a * (1.0 + scale_a), normed_a, inverse_a)
        grad_mod_a = jnp.concatenate([grad_hidden_a, grad_hidden_a * normed_a], axis=-1).astype(BF16)
        grad_mod_first = jnp.concatenate([grad_mod_a, grad_mod_b[:, :width], grad_mod_b[:, 3 * width :]], axis=1)
        grad_condition = (
            times_transpose(grad_mod_first, mod_first)
            + times_transpose(grad_mod_b[:, width : 3 * width], mod_rest)
        ) * silu_slope(condition[0].astype(F32) + embed)
        grad_project = out_of_lanes(grad_lanes).reshape(patches, 3 * heads_wide)
        gain_sums = gain_sums[:2, :HD]
        mod_rows = jnp.concatenate([grad_mod_a, grad_mod_b], axis=1)
        grad_w_down = plain_sums(inner, grad_branch_b, 0)
        grad_w_gate = plain_sums(hidden_b, grad_gate_in, 1)
        grad_w_up = plain_sums(hidden_b, grad_up_in, 1)
        grad_w_qkv = plain_sums(hidden_a, grad_project, 3)
        attended = out_of_lanes(attended_lanes).reshape(patches, heads_wide)
        grad_w_out = plain_sums(attended, grad_branch_a, 0)
        grad_w_mod = plain_sums(gather_rows(lifted_low), rows_to_columns(mod_rows, 6), 6)
        bias_rows = jnp.sum(mod_rows, axis=0, dtype=F32)
        sum_bias = lax.psum_scatter(bias_rows, ("dp", "seq"), scatter_dimension=0, tiled=True)
        gains = lax.psum(gain_sums, ("dp", "seq"))
    sum_q_gain, sum_k_gain = gains[0], gains[1]
    return (
        block_out[None],
        grad_tokens[None],
        grad_condition[None],
        grad_w_qkv,
        grad_w_out,
        grad_w_gate,
        grad_w_up,
        grad_w_down,
        grad_w_mod,
        sum_bias,
        sum_q_gain,
        sum_k_gain,
    )


def solution(mesh):
    placed = (
        P("dp", "seq", None),
        P("dp", "seq", None),
        P("dp", "seq", None),
        P("seq", None),
        P("seq", None),
        P("seq", None),
        P("seq", None),
        P("seq", None),
        P("seq", None),
        P(),
        P(),
        P(),
        P(),
        P("dp"),
        P(None, "dp", "seq"),
    )
    return jax.shard_map(
        shards,
        mesh=mesh,
        in_specs=placed,
        out_specs=(
            P("dp", "seq", None),
            P("dp", "seq", None),
            P("dp", "seq", None),
            P(("dp", "seq"), None),
            P(("dp", "seq"), None),
            P(("dp", "seq"), None),
            P(("dp", "seq"), None),
            P(("dp", "seq"), None),
            P(("dp", "seq"), None),
            P(("dp", "seq")),
            P(),
            P(),
        ),
        check_vma=False,
    )
```

```python
import math

import jax
import jax.numpy as jnp
from jax import lax
from jax.experimental import pallas as pl
from jax.experimental.pallas import tpu as pltpu
from jax.sharding import PartitionSpec as P

HEADS = 16
HD = 72
EPSILON = 1e-06
BF16 = jnp.bfloat16
F32 = jnp.float32


def inverse_rms(values):
    return lax.rsqrt(jnp.mean(values * values, axis=-1, keepdims=True) + EPSILON)


def rms_back(grad_in, normed, inverse):
    return inverse * (grad_in - normed * jnp.mean(grad_in * normed, axis=-1, keepdims=True))


def silu_slope(values):
    logistic = jax.nn.sigmoid(values)
    return logistic * (1.0 + values * (1.0 - logistic))


def time_embed(steps, width):
    half_width = width // 2
    frequency = jnp.exp(-math.log(10000.0) * jnp.arange(half_width, dtype=F32) / half_width)
    angles = steps.astype(F32)[:, None] * frequency[None, :]
    return jnp.concatenate([jnp.cos(angles), jnp.sin(angles)], axis=-1)


def rope_tables(positions, head_size):
    quarter = head_size // 4
    frequency = jnp.exp(-math.log(10000.0) * jnp.arange(quarter, dtype=F32) / quarter)
    along_rows = positions[0].astype(F32)[..., None] * frequency
    along_cols = positions[1].astype(F32)[..., None] * frequency
    angles = jnp.concatenate([along_rows, along_rows, along_cols, along_cols], axis=-1)
    return (jnp.cos(angles)[..., None, :], jnp.sin(angles)[..., None, :])


def quarter_turn(values):
    first, second, third, fourth = jnp.split(values, 4, axis=-1)
    return jnp.concatenate([-second, first, -fourth, third], axis=-1)


def rotate_heads(values, cosine, sine):
    return values * cosine + quarter_turn(values) * sine


def unrotate(grad_in, cosine, sine):
    return grad_in * cosine - quarter_turn(grad_in * sine)


def matmul(left, right):
    return jnp.dot(left, right, preferred_element_type=F32)


def outer_sum(left, right):
    return jnp.einsum("ra,rb->ab", left, right, preferred_element_type=F32)


def times_transpose(left, right):
    return jnp.einsum("rb,ab->ra", left, right, preferred_element_type=F32)


MESH = pl.DeviceIdType.MESH
SUM_ID, GATHER_ID, SCATTER_ID, WEIGHT_ID, ATTEND_ID, BACK_ID, MLP_ID = 1, 2, 3, 4, 5, 6, 7


def greet(partners):
    barrier = pltpu.get_barrier_semaphore()
    for partner in partners:
        pl.semaphore_signal(barrier, inc=1, device_id=partner, device_id_type=MESH)
    pl.semaphore_wait(barrier, len(partners))


def group_partners():
    item, column = lax.axis_index("dp"), lax.axis_index("seq")
    core = lax.rem(column, 2)
    return (item, column + 1 - 2 * core), (item, lax.rem(column + 2, 4))


GATHER_PIECES = 4


def gather_kernel(own_ref, out_ref, local_sem, send_sem, recv_sem):
    column = lax.axis_index("seq")
    sibling, across = group_partners()
    greet([sibling, across])
    local = pltpu.make_async_copy(own_ref, out_ref.at[column], local_sem)
    local.start()
    rows = own_ref.shape[0] // GATHER_PIECES

    def remote(source, place, piece, kind, target):
        part = pl.ds(piece * rows, rows)
        return pltpu.make_async_remote_copy(
            src_ref=source.at[part],
            dst_ref=out_ref.at[place, part],
            send_sem=send_sem.at[kind, piece],
            recv_sem=recv_sem.at[kind, piece],
            device_id=target,
            device_id_type=MESH,
        )

    far = lax.rem(column + 2, 4)
    pieces = range(GATHER_PIECES)
    over = [remote(own_ref, column, piece, 0, across) for piece in pieces]
    beside = [remote(own_ref, column, piece, 1, sibling) for piece in pieces]
    onward = [remote(out_ref.at[far], far, piece, 2, sibling) for piece in pieces]
    for copy in over:
        copy.start()
    for copy in beside:
        copy.start()
    for piece in pieces:
        over[piece].wait_recv()
        onward[piece].start()
    for piece in pieces:
        over[piece].wait_send()
        beside[piece].wait()
        onward[piece].wait()
    local.wait()


def gather_rows(values):
    rows, columns = values.shape
    gathered = pl.pallas_call(
        gather_kernel,
        out_shape=jax.ShapeDtypeStruct((4, rows, columns), values.dtype),
        in_specs=[pl.BlockSpec(memory_space=pltpu.VMEM)],
        out_specs=pl.BlockSpec(memory_space=pltpu.VMEM),
        scratch_shapes=[
            pltpu.SemaphoreType.DMA,
            pltpu.SemaphoreType.DMA((3, GATHER_PIECES)),
            pltpu.SemaphoreType.DMA((3, GATHER_PIECES)),
        ],
        compiler_params=pltpu.CompilerParams(
            collective_id=GATHER_ID, has_side_effects=True, vmem_limit_bytes=48 * 2**20
        ),
        name="gather_rows",
    )(values)
    return gathered.reshape(4 * rows, columns)


def scatter_kernel(parts_ref, out_ref, near, low, far, send_sem, recv_sem):
    column = lax.axis_index("seq")
    core, chip = lax.rem(column, 2), column // 2
    sibling, across = group_partners()
    greet([sibling, across])
    rows = out_ref.shape[0] // 2

    def remote(source, target_ref, index, target):
        return pltpu.make_async_remote_copy(
            src_ref=source,
            dst_ref=target_ref,
            send_sem=send_sem.at[index],
            recv_sem=recv_sem.at[index],
            device_id=target,
            device_id_type=MESH,
        )

    parts = [pl.ds(piece * rows, rows) for piece in range(2)]
    beside = [
        remote(parts_ref.at[1 - chip, 1 - core, part], near.at[0, part], i, sibling)
        for i, part in enumerate(parts)
    ]
    beside.append(remote(parts_ref.at[chip, 1 - core], near.at[1], 2, sibling))
    for copy in beside:
        copy.start()
    over = [remote(low.at[part], far.at[part], 3 + i, across) for i, part in enumerate(parts)]
    for i, part in enumerate(parts):
        beside[i].wait_recv()
        pair = parts_ref[1 - chip, core, part].astype(F32) + near[0, part].astype(F32)
        low[part] = pair.astype(BF16)
        over[i].start()
    beside[2].wait_recv()
    out_ref[...] = parts_ref[chip, core].astype(F32) + near[1].astype(F32)
    for i, part in enumerate(parts):
        over[i].wait()
        out_ref[part] += far[part].astype(F32)
    for copy in beside:
        copy.wait_send()


def scatter_rows(partial):
    rows, columns = partial.shape[0] // 4, partial.shape[1]
    return pl.pallas_call(
        scatter_kernel,
        out_shape=jax.ShapeDtypeStruct((rows, columns), F32),
        in_specs=[pl.BlockSpec(memory_space=pltpu.VMEM)],
        out_specs=pl.BlockSpec(memory_space=pltpu.VMEM),
        scratch_shapes=[
            pltpu.VMEM((2, rows, columns), BF16),
            pltpu.VMEM((rows, columns), BF16),
            pltpu.VMEM((rows, columns), BF16),
            pltpu.SemaphoreType.DMA((5,)),
            pltpu.SemaphoreType.DMA((5,)),
        ],
        compiler_params=pltpu.CompilerParams(
            collective_id=SCATTER_ID, has_side_effects=True, vmem_limit_bytes=48 * 2**20
        ),
        name="scatter_rows",
    )(partial.astype(BF16).reshape(2, 2, rows, columns))


TILE = 128
LANES = 128
QUARTER = HD // 4
FIRST_ROWS = 80


class WeightImport:
    def __init__(self, blocks, ranges):
        self.blocks, self.ranges = blocks, ranges
        self.arrays = sorted({block[0] for block in blocks})

    def scratch(self):
        count = len(self.blocks)
        return [
            pltpu.SemaphoreType.DMA((8,)),
            pltpu.SemaphoreType.DMA((count, 7)),
            pltpu.SemaphoreType.DMA((count, 7)),
        ]

    def bind(self, ins, outs, scratch):
        self.ins, self.outs = ins, outs
        self.own_sem, self.send_sem, self.recv_sem = scratch
        item, column = lax.axis_index("dp"), lax.axis_index("seq")
        core, chip = lax.rem(column, 2), column // 2
        self.item, self.column = item, column
        self.y_bit, self.z_bit = lax.rem(item, 2), lax.rem(item // 2, 2)
        self.sibling = (item, column + 1 - 2 * core)
        self.y_near = (item + 1 - 2 * self.y_bit, column)
        self.z_near = (item + 2 - 4 * self.z_bit, column)
        self.far = [(1 - chip) * 2 + k for k in (core, 1 - core)]
        self.half_rows = ins[0].shape[0] // 2

    def partners(self):
        across = [(self.item, place) for place in self.far]
        return across + [self.sibling, self.y_near, self.z_near]

    def copy(self, source, target_ref, block, kind, target):
        return pltpu.make_async_remote_copy(
            src_ref=source,
            dst_ref=target_ref,
            send_sem=self.send_sem.at[block, kind],
            recv_sem=self.recv_sem.at[block, kind],
            device_id=target,
            device_id_type=MESH,
        )

    def source_column(self, column):
        for start, stop in self.ranges:
            if column < stop - start:
                return start + column
            column -= stop - start

    def piece(self, ref, block, y_pick, z_pick, first_row=0, rows=None, base=0, outside=False):
        array, _, start, columns = self.blocks[block]
        step = columns
        if array == 0 and outside:
            step = self.source_column(start + columns) - self.source_column(start)
            start = self.source_column(start)
        rows = self.half_rows if rows is None else rows
        return ref.at[
            pl.ds(pl.multiple_of(z_pick * self.half_rows + first_row, 16), rows),
            pl.ds(pl.multiple_of(base + start + y_pick * step, TILE), columns),
        ]

    def mine_for(self, array, place):
        ref = self.ins[array]
        if len(ref.shape) == 3:
            return ref.at[place], 0
        return ref, 0 if array == 0 else place * self.outs[array].shape[2]

    def whole(self, array, place):
        ref, base = self.mine_for(array, place)
        columns = self.outs[array].shape[2]
        if ref.shape[-1] == columns:
            return ref
        return ref.at[:, pl.ds(pl.multiple_of(base, TILE), columns)]

    def over(self, block):
        array, offset, _, _ = self.blocks[block]
        goal = self.far[offset or 0]
        ref, base = self.mine_for(array, goal)
        source = self.piece(ref, block, self.y_bit, self.z_bit, base=base, outside=True)
        target = self.piece(self.outs[array].at[self.column], block, self.y_bit, self.z_bit)
        return self.copy(source, target, block, 0, (self.item, goal))

    def onward(self, block, kind):
        array, offset, _, _ = self.blocks[block]
        ref = self.outs[array].at[self.far[offset or 0]]
        if kind == 1:
            part, target = self.piece(ref, block, self.y_bit, self.z_bit), self.y_near
        elif kind == 2:
            part, target = self.piece(ref, block, self.y_bit, self.z_bit), self.z_near
        elif kind == 3:
            part = self.piece(ref, block, 1 - self.y_bit, self.z_bit, 0, FIRST_ROWS)
            target = self.z_near
        else:
            rest = self.half_rows - FIRST_ROWS
            part = self.piece(ref, block, self.y_bit, 1 - self.z_bit, FIRST_ROWS, rest)
            target = self.y_near
        return self.copy(part, part, block, kind, target)

    def share(self, block):
        _, _, start, columns = self.blocks[block]
        part = self.outs[0].at[self.far[0], :, pl.ds(start, 2 * columns)]
        return self.copy(part, part, block, 5, self.sibling)

    def spans(self, array, place):
        target = self.outs[array].at[self.column]
        if array:
            return [(self.whole(array, place), target)]
        pairs, at = [], 0
        for start, stop in self.ranges:
            columns = stop - start
            pairs.append((self.ins[0].at[:, pl.ds(start, columns)], target.at[:, pl.ds(at, columns)]))
            at += columns
        return pairs

    def beside(self, array):
        index = self.arrays.index(array)
        return [
            self.copy(source, target, index + 2 * k, 6, self.sibling)
            for k, (source, target) in enumerate(self.spans(array, self.sibling[1]))
        ]

    def own(self, array):
        return [
            pltpu.make_async_copy(source, target, self.own_sem.at[array + 4 * k])
            for k, (source, target) in enumerate(self.spans(array, self.column))
        ]

    def do(self, *steps):
        kinds = {"a": self.arrive, "p": self.pass_on, "c": self.complete}
        for step in steps:
            kinds[step[0]](int(step[1:]))

    def arrive(self, step):
        self.over(step).wait_recv()
        self.onward(step, 1).start()
        self.onward(step, 2).start()

    def pass_on(self, step):
        self.onward(step, 1).wait_recv()
        self.onward(step, 3).start()
        self.onward(step, 2).wait_recv()
        self.onward(step, 4).start()

    def complete(self, step):
        self.onward(step, 3).wait_recv()
        self.onward(step, 4).wait_recv()
        if self.blocks[step][0] == 0:
            self.share(step).start()

    def end(self):
        for block in range(len(self.blocks)):
            self.over(block).wait_send()
            for kind in range(1, 5):
                self.onward(block, kind).wait_send()
            if self.blocks[block][0] == 0:
                self.share(block).wait_send()


class RowGather:
    def __init__(self, own, everyone, local_sem, send_sem, recv_sem):
        self.own, self.everyone = own, everyone
        self.local_sem, self.send_sem, self.recv_sem = local_sem, send_sem, recv_sem
        self.column = lax.axis_index("seq")
        self.far = lax.rem(self.column + 2, 4)
        self.sibling, self.across = group_partners()

    def remote(self, source, place, piece, kind, target):
        rows = self.own.shape[0] // GATHER_PIECES
        part = pl.ds(piece * rows, rows)
        return pltpu.make_async_remote_copy(
            src_ref=source.at[part],
            dst_ref=self.everyone.at[place, part],
            send_sem=self.send_sem.at[kind, piece],
            recv_sem=self.recv_sem.at[kind, piece],
            device_id=target,
            device_id_type=MESH,
        )

    def over(self, piece):
        return self.remote(self.own, self.column, piece, 0, self.across)

    def beside(self, piece):
        return self.remote(self.own, self.column, piece, 1, self.sibling)

    def onward(self, piece):
        return self.remote(self.everyone.at[self.far], self.far, piece, 2, self.sibling)

    def local(self):
        return pltpu.make_async_copy(self.own, self.everyone.at[self.column], self.local_sem)

    def start(self):
        for piece in range(GATHER_PIECES):
            self.over(piece).start()
        for piece in range(GATHER_PIECES):
            self.beside(piece).start()
        self.local().start()

    def pass_on(self):
        for piece in range(GATHER_PIECES):
            self.over(piece).wait_recv()
            self.onward(piece).start()

    def end(self):
        for piece in range(GATHER_PIECES):
            self.over(piece).wait_send()
            self.beside(piece).wait()
            self.onward(piece).wait()
        self.local().wait()

    @staticmethod
    def scratch():
        return [
            pltpu.SemaphoreType.DMA,
            pltpu.SemaphoreType.DMA((3, GATHER_PIECES)),
            pltpu.SemaphoreType.DMA((3, GATHER_PIECES)),
        ]


def first_import(width):
    wide = 3 * HEADS // 4 * LANES
    blocks = [(0, None, 0, width), (0, None, 2 * width, width), (1, 0, 0, wide // 2), (1, 1, 0, wide // 2)]
    return WeightImport(blocks, [(0, 3 * width), (5 * width, 6 * width)])


def second_import(width, ff):
    blocks = [(0, None, 0, width)] + [(k, j, 0, ff // 2) for k in (2, 3) for j in (0, 1)]
    return WeightImport(blocks, [(3 * width, 5 * width)])


def spread_heads(w_ref, lanes_ref):
    rows = w_ref.shape[0]
    valid = lax.broadcasted_iota(jnp.int32, (rows, LANES), 1) < HD
    for head in range(3 * HEADS):
        kind, device, place = head // HEADS, head % HEADS // 4, head % 4
        start = head * HD // LANES * LANES
        stop = min(start + 2 * LANES, w_ref.shape[1])
        window = w_ref[:, start:stop].astype(F32)
        shift = head * HD - start
        if shift:
            window = pltpu.roll(window, window.shape[1] - shift, 1)
        target = (kind * 4 + place) * LANES
        lanes_ref[device, :, target : target + LANES] = jnp.where(
            valid, window[:, :LANES], 0.0
        ).astype(BF16)


def start_all(copies):
    for copy in copies:
        copy.start()


def wait_all(copies):
    for copy in copies:
        copy.wait()


def row_of(ref, start, columns):
    rows = range(start // LANES, (start + columns) // LANES)
    return jnp.concatenate([ref[row : row + 1, :] for row in rows], axis=1)


def first_kernel(imports, *refs):
    (w_mod, w_qkv, condition, tokens, cotangent, embed, share, bias, positions), refs = refs[:9], refs[9:]
    (mod_out, qkv_out, scale_a, gate_a, gate_b), refs = refs[:5], refs[5:]
    (hidden_all, grads, lifted, positions_all), refs = refs[:4], refs[4:]
    (mod_all, lanes, hidden, mod_sem, spot_send, spot_recv), refs = refs[:6], refs[6:]
    imports.bind({0: w_mod, 1: lanes}, {0: mod_all, 1: qkv_out}, refs[:3])
    gather = RowGather(hidden, hidden_all, *refs[3:6])
    item, column = lax.axis_index("dp"), lax.axis_index("seq")
    width = tokens.shape[1]
    greet(imports.partners())
    imports.over(0).start()
    start_all(imports.own(0))
    start_all(imports.beside(0))
    peers = [(item, lax.rem(column + k, 4)) for k in range(1, 4)]
    spot_copies = [
        pltpu.make_async_remote_copy(
            src_ref=positions,
            dst_ref=positions_all.at[column],
            send_sem=spot_send.at[k],
            recv_sem=spot_recv.at[k],
            device_id=peer,
            device_id_type=MESH,
        )
        for k, peer in enumerate(peers)
    ]
    start_all(spot_copies)
    positions_all[column] = positions[...]
    spread_heads(w_qkv, lanes)
    for block in range(1, len(imports.blocks)):
        imports.over(block).start()
    start_all(imports.own(1))
    start_all(imports.beside(1))
    values = condition[...].astype(F32) + embed[...]
    lifted[...] = (values * jax.nn.sigmoid(values)).astype(BF16)
    imports.arrive(0)
    imports.pass_on(0)
    imports.arrive(1)
    imports.complete(0)
    wait_all(imports.own(0))
    for copy in imports.beside(0):
        copy.wait_recv()

    def modulate(block):
        imports.share(block).wait_recv()
        start = imports.blocks[block][2]
        weights = mod_all[:, :, start : start + 2 * width].reshape(-1, 2 * width)
        modulation = jnp.dot(lifted[...], weights, preferred_element_type=F32)
        return [
            modulation[:, k * width : (k + 1) * width]
            + row_of(bias, imports.source_column(start + k * width), width)
            for k in range(2)
        ]

    shift, scale = modulate(0)
    scale_a[...] = scale
    values = tokens[...].astype(F32)
    normed = values * inverse_rms(values)
    hidden[...] = (normed * (1.0 + scale) + shift).astype(BF16)
    gather.start()
    imports.pass_on(1)
    imports.arrive(2)
    imports.complete(1)
    imports.arrive(3)
    store = pltpu.make_async_copy(mod_all, mod_out, mod_sem)
    gate_a[...], gate = modulate(1)
    store.start()
    gate_b[...] = gate
    grads[...] = (cotangent[...].astype(F32) * share[...] * gate).astype(BF16)
    imports.pass_on(2)
    imports.pass_on(3)
    gather.pass_on()
    imports.complete(2)
    imports.complete(3)
    imports.end()
    for copy in imports.beside(0):
        copy.wait_send()
    wait_all(imports.beside(1))
    wait_all(imports.own(1))
    gather.end()
    wait_all(spot_copies)
    store.wait()


def first_stage(w_mod, w_qkv, condition, tokens, cotangent, embed, share, bias, positions):
    rows, width = tokens.shape
    depth, lanes = w_mod.shape[0], 3 * HEADS // 4 * LANES
    imports = first_import(width)
    vmem, anywhere = pl.BlockSpec(memory_space=pltpu.VMEM), pl.BlockSpec(memory_space=pl.ANY)

    def kernel(*refs):
        first_kernel(imports, *refs)

    return pl.pallas_call(
        kernel,
        out_shape=[
            jax.ShapeDtypeStruct((4, depth, 4 * width), BF16),
            jax.ShapeDtypeStruct((4, depth, lanes), BF16),
            jax.ShapeDtypeStruct((rows, width), F32),
            jax.ShapeDtypeStruct((rows, width), F32),
            jax.ShapeDtypeStruct((rows, width), F32),
            jax.ShapeDtypeStruct((4, rows, width), BF16),
            jax.ShapeDtypeStruct((rows, width), BF16),
            jax.ShapeDtypeStruct((rows, width), BF16),
            jax.ShapeDtypeStruct((4,) + positions.shape, jnp.int32),
        ],
        in_specs=[anywhere] + [vmem] * 8,
        out_specs=[anywhere, anywhere] + [vmem] * 7,
        scratch_shapes=[
            pltpu.VMEM((4, depth, 4 * width), BF16),
            pltpu.VMEM((4, depth, lanes), BF16),
            pltpu.VMEM((rows, width), BF16),
            pltpu.SemaphoreType.DMA,
            pltpu.SemaphoreType.DMA((3,)),
            pltpu.SemaphoreType.DMA((3,)),
        ]
        + imports.scratch()
        + RowGather.scratch(),
        compiler_params=pltpu.CompilerParams(
            collective_id=WEIGHT_ID, has_side_effects=True, vmem_limit_bytes=60 * 2**20
        ),
        name="first_stage",
    )(w_mod, w_qkv, condition, tokens, cotangent, embed, share, bias, positions)


def rotated(values, tables, sign):
    cosine, ahead, behind = tables
    turned = pltpu.roll(values, LANES - QUARTER, 1) * ahead + pltpu.roll(values, QUARTER, 1) * behind
    return values * cosine + turned if sign > 0 else values * cosine - turned


def lane_tables(positions):
    lane = jnp.arange(LANES)[None, :]
    frequency = jnp.exp(-math.log(10000.0) * (lane % QUARTER).astype(F32) / QUARTER)
    places = jnp.where(lane < 2 * QUARTER, positions[0][:, None], positions[1][:, None])
    angles = places.astype(F32) * frequency
    valid, takes_ahead = lane < HD, lane // QUARTER % 2 == 0
    cosine, sine = jnp.where(valid, jnp.cos(angles), 0.0), jnp.where(valid, jnp.sin(angles), 0.0)
    return [cosine, jnp.where(takes_ahead, -sine, 0.0), jnp.where(takes_ahead, 0.0, sine)]


def head_inverse(values):
    return lax.rsqrt(jnp.sum(values * values, axis=-1, keepdims=True) * (1.0 / HD) + EPSILON)


def over_rows(left, right):
    return lax.dot_general(left, right, (((1,), (1,)), ((), ())), preferred_element_type=F32)


def over_first(left, right):
    return lax.dot_general(left, right, (((0,), (0,)), ((), ())), preferred_element_type=F32)


class RowSums:
    def __init__(self, blocks, near, low, far, send_sem, recv_sem):
        column = lax.axis_index("seq")
        self.column = column
        self.core, self.chip = lax.rem(column, 2), column // 2
        self.sibling, self.across = group_partners()
        self.blocks, self.near, self.low, self.far = blocks, near, low, far
        self.send_sem, self.recv_sem = send_sem, recv_sem
        self.order = [
            (1 - self.chip) * 2 + 1 - self.core,
            (1 - self.chip) * 2 + self.core,
            self.chip * 2 + 1 - self.core,
            column,
        ]

    def copy(self, source, target_ref, index, target):
        return pltpu.make_async_remote_copy(
            src_ref=source,
            dst_ref=target_ref,
            send_sem=self.send_sem.at[index],
            recv_sem=self.recv_sem.at[index],
            device_id=target,
            device_id_type=MESH,
        )

    def beside(self, index):
        return self.copy(self.blocks.at[index], self.near.at[index], index, self.sibling)

    def over(self):
        return self.copy(self.low, self.far, 2, self.across)

    def put(self, index, values):
        if index == 0 or index == 2:
            self.blocks[index // 2] = values.astype(BF16)
            self.beside(index // 2).start()
        elif index == 1:
            self.beside(0).wait_recv()
            self.low[...] = (values + self.near[0].astype(F32)).astype(BF16)
            self.over().start()
        else:
            self.own = values

    def sums(self):
        self.beside(1).wait_recv()
        total = self.own + self.near[1].astype(F32)
        self.over().wait()
        total = total + self.far[...].astype(F32)
        self.beside(0).wait_send()
        self.beside(1).wait_send()
        return total

    @staticmethod
    def scratch(rows, columns):
        return [
            pltpu.VMEM((2, rows, columns), BF16),
            pltpu.VMEM((2, rows, columns), BF16),
            pltpu.VMEM((rows, columns), BF16),
            pltpu.VMEM((rows, columns), BF16),
            pltpu.SemaphoreType.DMA((3,)),
            pltpu.SemaphoreType.DMA((3,)),
        ]


IMPORT_STEPS = (
    ("a0",),
    ("a1", "a2", "p0"),
    ("a3", "a4", "c0", "p1"),
    ("p2", "p3", "c1"),
    ("p4", "c2", "c3", "c4"),
)


def attend_kernel(imports, *refs):
    (hidden, w_qkv, w_out, cosine, ahead, behind, q_gain, k_gain), refs = refs[:8], refs[8:]
    (w_mod, w_gate, w_up, lifted, bias, tokens, gate_a, grads), refs = refs[:8], refs[8:]
    (heads_out, rows_out, attended_out, branch_out), refs = refs[:4], refs[4:]
    (mod_out, gate_out, up_out, scale_out, middle_out, hidden_out, grads_all), refs = refs[:7], refs[7:]
    (mod_all, gate_own, up_own, mod_sem, load_sem), refs = refs[:5], refs[5:]
    sums = RowSums(*refs[:6])
    imports.bind({0: w_mod, 2: w_gate, 3: w_up}, {0: mod_all, 2: gate_out, 3: up_out}, refs[6:9])
    gather = RowGather(grads, grads_all, *refs[9:])
    greet(imports.partners())
    for block in range(len(imports.blocks)):
        imports.over(block).start()
    start_all(imports.own(0))
    loads = [
        pltpu.make_async_copy(imports.whole(k, sums.column), ref, load_sem.at[k - 2])
        for k, ref in ((2, gate_own), (3, up_own))
    ]
    stores = [
        pltpu.make_async_copy(ref, imports.outs[k].at[sums.column], load_sem.at[k])
        for k, ref in ((2, gate_own), (3, up_own))
    ]
    for copy in loads:
        copy.start()
    for array in imports.arrays:
        start_all(imports.beside(array))
    gather.start()
    factor = HD ** (-0.5)
    rows = branch_out.shape[0]
    heads = attended_out.shape[1] // LANES
    tables = cosine[...], ahead[...], behind[...]
    for pair in range(3 * heads // 2):
        span = slice(pair * 2 * LANES, (pair + 1) * 2 * LANES)
        projected = jnp.dot(hidden[...], w_qkv[:, span], preferred_element_type=F32)
        if pair >= heads:
            rows_out[:, span] = projected.astype(BF16)
            continue
        heads_out[:, span] = projected
        gain = (q_gain if pair < heads // 2 else k_gain)[...]
        for half in range(2):
            values = projected[:, half * LANES : (half + 1) * LANES]
            values = values * head_inverse(values) * gain
            start = pair * 2 * LANES + half * LANES
            rows_out[:, start : start + LANES] = rotated(values, tables, 1).astype(BF16)
    imports.do(*IMPORT_STEPS[0])
    for copy in loads:
        copy.wait()
    for copy in stores:
        copy.start()
    for index in range(4):
        block = pl.ds(pl.multiple_of(sums.order[index] * rows, rows), rows)
        for head in range(heads):
            spans = [slice((k * heads + head) * LANES, (k * heads + head + 1) * LANES) for k in range(3)]
            exp_scores = jnp.exp(over_rows(rows_out[block, spans[0]], rows_out[:, spans[1]]) * factor)
            scale = 1.0 / jnp.sum(exp_scores, axis=1, keepdims=True)
            mixed = jnp.dot(
                (exp_scores * scale).astype(BF16),
                rows_out[:, spans[2]],
                preferred_element_type=F32,
            )
            attended_out[block, spans[0]] = mixed.astype(BF16)
        sums.put(index, jnp.dot(attended_out[block, :], w_out[...], preferred_element_type=F32))
        imports.do(*IMPORT_STEPS[1 + index])
    gather.pass_on()
    wait_all(imports.own(0))
    for copy in imports.beside(0):
        copy.wait_recv()
    imports.share(0).wait_recv()
    store = pltpu.make_async_copy(mod_all, mod_out, mod_sem)
    store.start()
    width = tokens.shape[1]
    weights = mod_all[...].reshape(-1, 2 * width)
    modulation = jnp.dot(lifted[...], weights, preferred_element_type=F32)
    modulation = modulation + row_of(bias, imports.source_column(0), 2 * width)
    scale = modulation[:, width:]
    scale_out[...] = scale
    branch = sums.sums()
    branch_out[...] = branch
    middle = tokens[...].astype(F32) + gate_a[...] * branch
    middle_out[...] = middle
    hidden_out[...] = (middle * inverse_rms(middle) * (1.0 + scale) + modulation[:, :width]).astype(BF16)
    imports.end()
    for copy in imports.beside(0):
        copy.wait_send()
    for array in imports.arrays[1:]:
        wait_all(imports.beside(array))
    gather.end()
    for copy in stores:
        copy.wait()
    store.wait()


def attend(hidden, w_qkv, w_out, tables, q_gain, k_gain, w_mod, w_gate, w_up, lifted, bias, tokens, gate_a, grads):
    patches, wide = hidden.shape[0], w_qkv.shape[1]
    rows, width = patches // 4, hidden.shape[1]
    depth, ff = w_mod.shape[0], w_gate.shape[1] // 4
    imports = second_import(width, ff)
    vmem, anywhere = pl.BlockSpec(memory_space=pltpu.VMEM), pl.BlockSpec(memory_space=pl.ANY)

    def kernel(*refs):
        attend_kernel(imports, *refs)

    return pl.pallas_call(
        kernel,
        out_shape=[
            jax.ShapeDtypeStruct((patches, wide * 2 // 3), F32),
            jax.ShapeDtypeStruct((patches, wide), BF16),
            jax.ShapeDtypeStruct((patches, wide // 3), BF16),
            jax.ShapeDtypeStruct((rows, width), F32),
            jax.ShapeDtypeStruct((4, depth, 2 * width), BF16),
            jax.ShapeDtypeStruct((4, depth, ff), BF16),
            jax.ShapeDtypeStruct((4, depth, ff), BF16),
            jax.ShapeDtypeStruct((rows, width), F32),
            jax.ShapeDtypeStruct((rows, width), F32),
            jax.ShapeDtypeStruct((rows, width), BF16),
            jax.ShapeDtypeStruct((4, rows, width), BF16),
        ],
        in_specs=[vmem] * 8 + [anywhere] * 3 + [vmem] * 5,
        out_specs=[vmem] * 4 + [anywhere] * 3 + [vmem] * 4,
        scratch_shapes=[
            pltpu.VMEM((4, depth, 2 * width), BF16),
            pltpu.VMEM((depth, ff), BF16),
            pltpu.VMEM((depth, ff), BF16),
            pltpu.SemaphoreType.DMA,
            pltpu.SemaphoreType.DMA((4,)),
        ]
        + RowSums.scratch(rows, width)
        + imports.scratch()
        + RowGather.scratch(),
        compiler_params=pltpu.CompilerParams(
            collective_id=ATTEND_ID, has_side_effects=True, vmem_limit_bytes=63 * 2**20
        ),
        name="attend",
    )(hidden, w_qkv, w_out, *tables, q_gain, k_gain, w_mod, w_gate, w_up, lifted, bias, tokens, gate_a, grads)


def mlp_kernel(sums, *refs):
    (hidden, grads_all, w_gate, w_up, w_down), refs = refs[:5], refs[5:]
    (middle, scale, gate_a, gate_b, branch_a, cotangent, share), refs = refs[:7], refs[7:]
    (hidden_all, inner, grad_gate, grad_up), refs = refs[:4], refs[4:]
    (block_out, middle_out, branch_grad_out, mod_out), refs = refs[:4], refs[4:]
    handed_out, refs = refs[: len(sums.leaving)], refs[len(sums.leaving) :]
    if sums.parts:
        sums.bind([], [], None, [], None, [], handed_out, refs[30:])
    sums.others = {
        "inner": (inner, lambda: None),
        "grad_branch_b": (grads_all, lambda: None),
        "hidden_b": (hidden_all, lambda: None),
        "grad_gate_in": (grad_gate, lambda: None),
    }
    gather = RowGather(hidden, hidden_all, *refs[:3])
    halves = [RowSums(*refs[3 + 6 * k : 9 + 6 * k]) for k in range(4)]
    sums_grad, sums_branch = halves[:2], halves[2:]
    first = sums_grad[0]
    greet([first.sibling, first.across] + (sums.partners[:2] if sums.parts else []))
    gather.start()
    rows, width = hidden.shape
    near, far = first.chip * 2, (1 - first.chip) * 2
    depth = w_gate.shape[0] * w_gate.shape[1]
    gate_weights, up_weights = (ref[...].reshape(depth, ref.shape[2]) for ref in (w_gate, w_up))

    def block(ref, pair, start, count):
        return jnp.concatenate([ref[pair + k, start : start + count] for k in range(2)], axis=0)

    def process(pair, start, count):
        values = block(hidden_all, pair, start, count)
        gate_in = jnp.dot(values, gate_weights, preferred_element_type=F32)
        up_in = jnp.dot(values, up_weights, preferred_element_type=F32)
        grad_inner = over_rows(block(grads_all, pair, start, count), w_down[...])
        logistic = jax.nn.sigmoid(gate_in)
        activated = gate_in * logistic
        slope = logistic * (1.0 + gate_in * (1.0 - logistic))
        results = (
            (activated * up_in).astype(BF16),
            (grad_inner * up_in * slope).astype(BF16),
            (grad_inner * activated).astype(BF16),
        )
        for ref, result in zip((inner, grad_gate, grad_up), results, strict=True):
            for k in range(2):
                at = pl.multiple_of((pair + k) * rows + start, 16)
                ref[pl.ds(at, count), :] = result[k * count : (k + 1) * count]
        return over_rows(results[1], gate_weights) + over_rows(results[2], up_weights)

    def put(sums, partial, count, far_rows):
        @pl.when(first.core == 0)
        def _():
            held[0, :count], held[1, :count] = partial[count:], partial[:count]

        @pl.when(first.core == 1)
        def _():
            held[0, :count], held[1, :count] = partial[:count], partial[count:]

        if far_rows:
            sums.put(0, held[0, :count])
            sums.put(1, held[1, :count])
        else:
            sums.put(2, held[0, :count])
            return held[1, :count]

    held, own_grad, own_branch = refs[27:30]
    half = rows // 2
    for piece in range(GATHER_PIECES):
        gather.beside(piece).wait_recv()
    gather.local().wait()
    partial = process(near, 0, rows)
    for k in range(2):
        part = slice(k * half, (k + 1) * half)
        both = jnp.concatenate([partial[part], partial[rows + k * half : rows + (k + 1) * half]], axis=0)
        own_grad[part] = put(sums_grad[k], both, half, False)
    for k in range(2):
        pieces = range(k * GATHER_PIECES // 2, (k + 1) * GATHER_PIECES // 2)
        for piece in pieces:
            gather.over(piece).wait_recv()
            gather.onward(piece).start()
        for piece in pieces:
            gather.onward(piece).wait_recv()
        put(sums_grad[k], process(far, k * half, half), half, True)
    sums.do(*["b0", "b1"][: len(sums.parts)])
    for k in range(2):
        at = [pl.ds(pl.multiple_of((far + j) * rows + k * half, 16), half) for j in range(2)]
        values = jnp.concatenate([inner[part, :] for part in at], axis=0)
        put(sums_branch[k], jnp.dot(values, w_down[...], preferred_element_type=F32), half, True)
    sums.do(*["b2", "b3"][: len(sums.parts)])
    for k in range(2):
        at = [pl.ds(pl.multiple_of((near + j) * rows + k * half, 16), half) for j in range(2)]
        values = jnp.concatenate([inner[part, :] for part in at], axis=0)
        partial = jnp.dot(values, w_down[...], preferred_element_type=F32)
        own_branch[k * half : (k + 1) * half] = put(sums_branch[k], partial, half, False)
    sums.do(*["f0", "f1"][: len(sums.parts)])
    for k in range(2):
        part = slice(k * half, (k + 1) * half)
        sums_grad[k].put(3, own_grad[part])
        grad_hidden = sums_grad[k].sums()
        values = middle[part]
        inverse = inverse_rms(values)
        normed = values * inverse
        grad_out = cotangent[part].astype(F32) * share[...]
        grad_middle = grad_out + rms_back(grad_hidden * (1.0 + scale[part]), normed, inverse)
        middle_out[part] = grad_middle
        branch_grad_out[part] = (grad_middle * gate_a[part]).astype(BF16)
        mod_out[part, :width] = (grad_middle * branch_a[part]).astype(BF16)
        mod_out[part, width : 2 * width] = grad_hidden.astype(BF16)
        mod_out[part, 2 * width : 3 * width] = (grad_hidden * normed).astype(BF16)
    sums.do(*["f2", "f3"][: len(sums.parts)])
    for k in range(2):
        part = slice(k * half, (k + 1) * half)
        sums_branch[k].put(3, own_branch[part])
        branch = sums_branch[k].sums()
        block_out[part] = (middle[part] + gate_b[part] * branch).astype(BF16)
        grad_out = cotangent[part].astype(F32) * share[...]
        mod_out[part, 3 * width :] = (grad_out * branch).astype(BF16)
    for piece in range(GATHER_PIECES):
        gather.over(piece).wait_send()
        gather.beside(piece).wait_send()
        gather.onward(piece).wait_send()
    sums.end()


def mlp(hidden, grads_all, w_gate, w_up, w_down, rest, parts):
    rows, width = hidden.shape
    ff = w_down.shape[0]
    sums = GradSums(parts, (), [], (16, LANES))
    vmem, anywhere = pl.BlockSpec(memory_space=pltpu.VMEM), pl.BlockSpec(memory_space=pl.ANY)

    def kernel(*refs):
        mlp_kernel(sums, *refs)

    return pl.pallas_call(
        kernel,
        out_shape=[
            jax.ShapeDtypeStruct((4, rows, width), BF16),
            jax.ShapeDtypeStruct((4 * rows, ff), BF16),
            jax.ShapeDtypeStruct((4 * rows, ff), BF16),
            jax.ShapeDtypeStruct((4 * rows, ff), BF16),
            jax.ShapeDtypeStruct((rows, width), BF16),
            jax.ShapeDtypeStruct((rows, width), F32),
            jax.ShapeDtypeStruct((rows, width), BF16),
            jax.ShapeDtypeStruct((rows, 4 * width), BF16),
        ]
        + [jax.ShapeDtypeStruct(part.handed(), BF16) for part in parts],
        in_specs=[vmem] * 12,
        out_specs=[vmem] * 8 + [anywhere] * len(parts),
        scratch_shapes=RowGather.scratch()
        + RowSums.scratch(rows // 2, width) * 4
        + [
            pltpu.VMEM((2, rows // 2, width), F32),
            pltpu.VMEM((rows, width), F32),
            pltpu.VMEM((rows, width), F32),
        ]
        + (sums.scratch([]) if parts else []),
        compiler_params=pltpu.CompilerParams(
            collective_id=MLP_ID, has_side_effects=True, vmem_limit_bytes=63 * 2**20
        ),
        name="mlp",
    )(hidden, grads_all, w_gate, w_up, w_down, *rest)


def rows_to_columns(values, blocks):
    rows, columns = values.shape
    ways = lax.axis_size("seq")
    values = values.reshape(rows, blocks, ways, columns // (blocks * ways))
    moved = lax.all_to_all(values, "seq", split_axis=2, concat_axis=0, tiled=True)
    return moved.reshape(rows * ways, columns // ways)


def columns_to_rows(values, blocks):
    rows, columns = values.shape
    ways = lax.axis_size("seq")
    values = values.reshape(rows, blocks, 1, columns // blocks)
    moved = lax.all_to_all(values, "seq", split_axis=0, concat_axis=2, tiled=True)
    return moved.reshape(rows // ways, columns * ways)


def first_tile(place, tiles):
    return (tiles * place) // 4


def padded_rows(rows):
    return -(-rows // 16) * 16


class Part:
    def __init__(self, left, right, rows, span, out, order, at=None, **kinds):
        self.left, self.right, self.rows = left, right, rows
        self.start, self.columns, self.out = span[0], span[1] - span[0], out
        self.at = self.start if at is None else at
        self.order = order
        for kind in ("by_rows", "in_lanes", "bias", "enter", "leave"):
            setattr(self, kind, kinds.get(kind, False))
        self.region = kinds.get("region")
        self.slab = padded_rows(rows)

    def handed(self):
        return (2, 2, self.slab, self.columns)


def split_part(left, right, rows, columns, out, order, **kinds):
    middle = -(-columns // (2 * TILE)) * TILE
    return [
        Part(left, right, rows, span, out, order, **kinds)
        for span in ((0, middle), (middle, columns))
    ]


class GradSums:
    def __init__(self, parts, names, shared_shapes, small_shape, after=()):
        self.parts, self.names = parts, names
        self.after = dict(after)
        self.shared_shapes, self.small_shape = shared_shapes, small_shape
        self.has_rows = any(part.by_rows and not part.leave for part in parts)
        self.entering = [index for index, part in enumerate(parts) if part.enter]
        self.leaving = [index for index, part in enumerate(parts) if part.leave]

    def scratch(self, array_shapes):
        parts, count, groups = self.parts, len(self.parts), len(self.shared_shapes)
        none = pltpu.VMEM((16, LANES), BF16)
        shapes = [
            none if name in self.after else pltpu.VMEM(shape, BF16)
            for name, shape in zip(self.names, array_shapes, strict=True)
        ]
        shapes += [pltpu.VMEM((4, rows, columns), BF16) for rows, _, _, columns in self.shared_shapes]

        def each(lead, needed):
            return [
                pltpu.VMEM(lead(part) + (part.slab, part.columns), BF16) if needed(part) else none
                for part in parts
            ]

        shapes += each(lambda part: (2, 2) if part.enter else (2, 2, 2), lambda part: True)
        shapes += each(lambda part: (2, 2), lambda part: not part.enter)
        shapes += each(lambda part: (2,), lambda part: not part.leave)
        shapes += each(lambda part: (), lambda part: not part.leave)
        for _ in range(2):
            for part in parts:
                if part.leave:
                    shapes.append(none)
                elif part.by_rows:
                    shapes.append(pltpu.VMEM((part.slab, part.columns), BF16))
                else:
                    shapes.append(pltpu.VMEM((4, padded_rows(part.rows // 4), part.columns), BF16))
        widest = max(part.columns for part in parts)
        tallest = max(4 * LANES if part.in_lanes else part.rows for part in parts)
        return shapes + [
            pltpu.VMEM((tallest, widest), F32),
            pltpu.VMEM((4,) + self.small_shape, F32),
            pltpu.VMEM((3,) + self.small_shape, F32),
            pltpu.SemaphoreType.DMA((max(len(self.names), 1),)),
            pltpu.SemaphoreType.DMA((max(groups, 1), 3)),
            pltpu.SemaphoreType.DMA((max(groups, 1), 3)),
            pltpu.SemaphoreType.DMA((max(groups, 1),)),
            pltpu.SemaphoreType.DMA((count,)),
            pltpu.SemaphoreType.DMA((count, 3)),
            pltpu.SemaphoreType.DMA((count, 3)),
            pltpu.SemaphoreType.DMA((count, 3)),
            pltpu.SemaphoreType.DMA((count, 3)),
            pltpu.SemaphoreType.DMA((6,)),
            pltpu.SemaphoreType.DMA((6,)),
        ]

    def bind(self, ins, shared, small_in, outs, small_out, handed_in, handed_out, scratch):
        count, groups, names = len(self.parts), len(self.shared_shapes), self.names
        refs = list(scratch)

        def take(number):
            taken = refs[:number]
            del refs[:number]
            return taken

        self.shared, self.small_in, self.outs, self.small_out = shared, small_in, outs, small_out
        self.held = dict(zip(names, take(len(names)), strict=True))
        for name, place in self.after.items():
            self.held[name] = self.held[place]
        self.gathered = take(groups)
        self.own, self.first_in = take(count), take(count)
        self.second_in, self.third_in = take(count), take(count)
        self.slabs, self.slab_in = take(count), take(count)
        self.total, self.small, self.small_came = take(3)
        load_sem, self.share_send, self.share_recv, own_sem, hand_sem = take(5)
        self.send_sem, self.recv_sem = take(2)
        self.last_send, self.last_recv, self.small_send, self.small_recv = take(4)
        item, column = lax.axis_index("dp"), lax.axis_index("seq")
        self.column = column
        self.bits = [lax.rem(item, 2), lax.rem(item // 2, 2), item // 4]
        self.partners = [(item + (1 - 2 * self.bits[k]) * (1 << k), column) for k in range(3)]
        self.peers = [(item, lax.rem(column + k, 4)) for k in range(1, 4)]
        self.owner = (2 * column + item // 4, lax.rem(item, 4))
        self.feeder = (4 * lax.rem(item, 2) + column, item // 2)
        self.elsewhere = jnp.logical_or(self.owner[0] != item, self.owner[1] != column)
        self.loads = {
            name: pltpu.make_async_copy(ins[i], self.held[name], load_sem.at[i])
            for i, name in enumerate(names)
        }
        self.own_shares = [
            pltpu.make_async_copy(
                self.columns_of(g, column), self.gathered[g].at[column], own_sem.at[g]
            )
            for g in range(groups)
        ]
        self.ready = set()
        self.others = {}
        self.handing = {
            index: pltpu.make_async_copy(ref, self.own[index], hand_sem.at[index])
            for index, ref in zip(self.entering, handed_in, strict=True)
        }
        for index, ref in zip(self.leaving, handed_out, strict=True):
            half = self.own[index].at[self.half(index, True)]
            self.handing[index] = pltpu.make_async_copy(half, ref, hand_sem.at[index])

    def greet(self):
        barrier = pltpu.get_barrier_semaphore()
        for partner in self.partners + self.peers:
            pl.semaphore_signal(barrier, inc=1, device_id=partner, device_id_type=MESH)
        waits = 6
        if self.has_rows:
            waits = 6 + self.elsewhere.astype(jnp.int32)

            @pl.when(self.elsewhere)
            def _():
                pl.semaphore_signal(barrier, inc=1, device_id=self.feeder, device_id_type=MESH)

        pl.semaphore_wait(barrier, waits)

    def load(self):
        for index in self.entering:
            self.handing[index].start()
        for name in self.names:
            if name not in self.after:
                self.loads[name].start()

    def remote(self, source, target_ref, send, recv, target):
        return pltpu.make_async_remote_copy(
            src_ref=source,
            dst_ref=target_ref,
            send_sem=send,
            recv_sem=recv,
            device_id=target,
            device_id_type=MESH,
        )

    def columns_of(self, group, place):
        _, wide, first, narrow = self.shared_shapes[group]
        start = first_tile(place, wide // TILE) * TILE + first
        return self.shared[group].at[:, pl.ds(pl.multiple_of(start, TILE), narrow)]

    def shares(self, group):
        return [
            self.remote(
                self.columns_of(group, peer[1]),
                self.gathered[group].at[self.column],
                self.share_send.at[group, k],
                self.share_recv.at[group, k],
                peer,
            )
            for k, peer in enumerate(self.peers)
        ]

    def share(self):
        for group in range(len(self.shared_shapes)):
            self.own_shares[group].start()
            for copy in self.shares(group):
                copy.start()

    def operand(self, name):
        if isinstance(name, int):
            if name not in self.ready:
                self.own_shares[name].wait()
                for copy in self.shares(name):
                    copy.wait()
            self.ready.add(name)
            ref = self.gathered[name]
            return ref[...].reshape(4 * ref.shape[1], ref.shape[2])
        first = name not in self.ready
        self.ready.add(name)
        if name in self.others:
            ref, wait = self.others[name]
            if first:
                wait()
            return ref[...].reshape(-1, ref.shape[-1])
        if first:
            self.loads[name].wait()
        return self.held[name][...]

    def multiply(self, index):
        part = self.parts[index]
        left, right = self.operand(part.left), self.operand(part.right)
        right = right[:, part.start : part.start + part.columns]
        if part.bias:
            sums = jnp.sum(right.astype(F32), axis=0, keepdims=True)
            for tile in range(part.columns // TILE):
                row = part.at // TILE + tile
                self.small[0, row : row + 1] = sums[:, tile * TILE : (tile + 1) * TILE]
        own, rows = self.own[index], part.rows
        if part.in_lanes:
            self.total[: left.shape[1], : part.columns] = over_first(left, right)
            for d in range(8):
                start = d // 2 * LANES + d % 2 * rows
                own[d // 4, d // 2 % 2, d % 2] = self.cut(start, rows, part.slab, part.columns)
            return
        step = 3 * TILE
        for start in range(0, left.shape[1], step):
            product = over_first(left[:, start : start + step], right).astype(BF16)
            for d in range(8):
                low, high = max(start, d * rows), min(start + step, (d + 1) * rows)
                if low < high:
                    place = slice(low - d * rows, high - d * rows)
                    own[d // 4, d // 2 % 2, d % 2, place] = product[low - start : high - start]

    def cut(self, start, rows, padded, columns):
        values = self.total[start : start + rows, :columns]
        if padded > rows:
            values = jnp.concatenate([values, jnp.zeros((padded - rows, columns), F32)], axis=0)
        return values.astype(BF16)

    def half(self, index, mine):
        order = self.parts[index].order
        pick = self.bits[order] if mine else 1 - self.bits[order]
        return (slice(None), slice(None), pick) if order == 0 else (slice(None), pick)

    def place(self, index, high, low):
        if self.parts[index].enter:
            return (high, low)
        if self.parts[index].order == 0:
            return (high, low, self.bits[0])
        return (high, self.bits[1], low)

    def stage(self, index, step):
        order = self.parts[index].order
        other = 1 - order
        sems = self.send_sem.at[index, step], self.recv_sem.at[index, step]
        own = self.own[index]
        if step == 0:
            source = own.at[self.half(index, False)]
            return self.remote(source, self.first_in[index], *sems, self.partners[order])
        if step == 1:
            place = self.place(index, slice(None), 1 - self.bits[other])
            return self.remote(own.at[place], self.second_in[index], *sems, self.partners[other])
        place = self.place(index, 1 - self.bits[2], self.bits[other])
        return self.remote(own.at[place], self.third_in[index], *sems, self.partners[2])

    def begin(self, index):
        if self.parts[index].enter:
            self.handing[index].wait()
            self.stage(index, 1).start()
            return
        self.multiply(index)
        self.stage(index, 0).start()

    def end_first(self, index):
        self.stage(index, 0).wait()
        for high in range(2):
            for low in range(2):
                place = self.place(index, high, low)
                came = self.first_in[index][high, low].astype(F32)
                self.own[index][place] = (self.own[index][place].astype(F32) + came).astype(BF16)
        if self.parts[index].leave:
            self.handing[index].start()
        else:
            self.stage(index, 1).start()

    def end_second(self, index):
        self.stage(index, 1).wait()
        for high in range(2):
            place = self.place(index, high, self.bits[1 - self.parts[index].order])
            came = self.second_in[index][high].astype(F32)
            self.own[index][place] = (self.own[index][place].astype(F32) + came).astype(BF16)
        self.stage(index, 2).start()

    def last(self, index):
        if self.parts[index].by_rows:
            sems = self.last_send.at[index, 0], self.last_recv.at[index, 0]
            return [self.remote(self.slabs[index], self.slab_in[index], *sems, self.owner)]
        return [
            self.remote(
                self.slabs[index].at[peer[1]],
                self.slab_in[index].at[self.column],
                self.last_send.at[index, k],
                self.last_recv.at[index, k],
                peer,
            )
            for k, peer in enumerate(self.peers)
        ]

    def end_third(self, index):
        part = self.parts[index]
        self.stage(index, 2).wait()
        place = self.place(index, self.bits[2], self.bits[1 - part.order])
        sums = self.own[index][place].astype(F32) + self.third_in[index][...].astype(F32)
        if part.by_rows:
            self.slabs[index][...] = sums.astype(BF16)

            @pl.when(self.elsewhere)
            def _():
                self.last(index)[0].start()

            @pl.when(jnp.logical_not(self.elsewhere))
            def _():
                self.slab_in[index][...] = self.slabs[index][...]

            return
        self.total[: part.rows, : part.columns] = sums
        rows = part.rows // 4
        for k in range(4):
            self.slabs[index][k] = self.cut(k * rows, rows, padded_rows(rows), part.columns)
        for copy in self.last(index):
            copy.start()
        self.slab_in[index][self.column] = self.slabs[index][self.column]

    def end_last(self, index):
        part = self.parts[index]
        out, stop = self.outs[part.out], part.at + part.columns
        if part.by_rows:

            @pl.when(self.elsewhere)
            def _():
                self.last(index)[0].wait()

            out[:, part.at : stop] = self.slab_in[index][...].astype(F32)[: part.rows]
            return
        for copy in self.last(index):
            copy.wait()
        rows = part.rows // 4
        base, wide = part.region or (0, out.shape[-1])
        for k in range(4):
            values = self.slab_in[index][k].astype(F32)[:rows]
            if len(out.shape) == 3:
                out[k, :, part.at : stop] = values
            else:
                start = base + first_tile(k, wide // TILE) * TILE
                out[:, start + part.at : start + stop] = values

    def small_step(self, step):
        if step < 3:
            sems = self.small_send.at[step], self.small_recv.at[step]
            return [
                self.remote(self.small.at[step], self.small_came.at[step], *sems, self.partners[step])
            ]
        return [
            self.remote(
                self.small.at[3],
                self.small_out.at[self.column],
                self.small_send.at[3 + k],
                self.small_recv.at[3 + k],
                peer,
            )
            for k, peer in enumerate(self.peers)
        ]

    def end_small(self, at):
        self.small_step(at - 1)[0].wait()
        self.small[at] = self.small[at - 1] + self.small_came[at - 1]
        for copy in self.small_step(at):
            copy.start()

    def do(self, *steps):
        kinds = {
            "b": self.begin,
            "f": self.end_first,
            "s": self.end_second,
            "t": self.end_third,
            "l": self.end_last,
            "x": self.small_exchange,
            "r": lambda number: self.loads[self.names[number]].start(),
        }
        for step in steps:
            kinds[step[0]](int(step[1:]))

    def small_exchange(self, at):
        if at == 0:
            self.small_step(0)[0].start()
        elif at < 4:
            self.end_small(at)
        else:
            self.small_out[self.column] = self.small[3]
            for copy in self.small_step(3):
                copy.wait()

    def end(self):
        for index in self.leaving:
            self.handing[index].wait()


def split(refs, *counts):
    groups, start = [], 0
    for number in counts:
        groups.append(refs[start : start + number])
        start += number
    return groups + [refs[start:]]


LAST_STEPS = (
    ("b0", "b1", "b2", "b3", "b4"),
    ("b5",),
    ("b6", "s0", "s1"),
    ("s2", "f3"),
    ("f4", "s3", "x0", "t0", "t1", "t2"),
    ("s4", "f5", "x1", "f6", "s5", "x2", "t3", "s6", "x3", "t4", "l0", "l1", "l2", "t5", "t6", "l3", "l4", "l5", "l6", "x4"),
)


def last_grads(parts, arrays, shared, small, handed, out_shapes, condition, embed, rows_a, rows_b, mods):
    names = tuple(arrays)
    shapes = [value.shape + (first, columns) for value, first, columns in shared]
    sums = GradSums(parts, names, shapes, small.shape)
    count = len(out_shapes)
    width = condition.shape[1]

    def kernel(*refs):
        ins, given, handed_in, given_mods, (small_in, seen, embed_in, low, high), outs, lasts, refs = split(
            refs, len(names), len(shared), len(handed), len(mods), 5, count, 2
        )
        (small_out, condition_out), held, (mod_sem,), scratch = lasts, refs[:2], refs[2:3], refs[3:]
        sums.bind(ins, given, small_in, outs, small_out, handed_in, [], scratch)
        sums.load()
        loads = [
            pltpu.make_async_copy(source, target, mod_sem.at[k])
            for k, (source, target) in enumerate(zip(given_mods, held, strict=True))
        ]
        start_all(loads)
        sums.greet()
        sums.share()
        sums.small[0] = small_in[...]
        first, rest = held
        condition_out[...] = jnp.zeros_like(condition_out)
        work = [
            (low, 0, first, 0, 2 * width),
            (high, 0, first, 2 * width, width),
            (high, width, rest, 0, 2 * width),
            (high, 3 * width, first, 3 * width, width),
        ]
        for number, steps in enumerate(LAST_STEPS):
            sums.do(*steps)
            if number == 0:
                wait_all(loads)
            if number < 4:
                rows, at, weights, start, columns = work[number]
                condition_out[...] += over_rows(
                    rows[:, at : at + columns], weights[:, start : start + columns]
                )
            if number == 4:
                values = seen[...].astype(F32) + embed_in[...]
                condition_out[...] = condition_out[...] * silu_slope(values)
        sums.end()

    vmem, anywhere = pl.BlockSpec(memory_space=pltpu.VMEM), pl.BlockSpec(memory_space=pl.ANY)
    return pl.pallas_call(
        kernel,
        out_shape=[jax.ShapeDtypeStruct(shape, F32) for shape in out_shapes]
        + [
            jax.ShapeDtypeStruct((4,) + small.shape, F32),
            jax.ShapeDtypeStruct(condition.shape, F32),
        ],
        in_specs=[anywhere] * (len(names) + len(shared) + len(handed) + len(mods)) + [vmem] * 5,
        out_specs=[vmem] * (count + 2),
        scratch_shapes=[pltpu.VMEM(value.shape, BF16) for value in mods]
        + [pltpu.SemaphoreType.DMA((len(mods),))]
        + sums.scratch([value.shape for value in arrays.values()]),
        compiler_params=pltpu.CompilerParams(
            collective_id=SUM_ID, has_side_effects=True, vmem_limit_bytes=63 * 2**20
        ),
        name="last_grads",
    )(
        *arrays.values(),
        *[value for value, _, _ in shared],
        *handed,
        *mods,
        small,
        condition,
        embed,
        rows_a,
        rows_b,
    )


BACK_STEPS = {
    "start": ("b0", "b1", "b2", "b3", "b4", "b5"),
    "gathered": ("b6", "b7", "s1", "s0", "s3"),
    "head0": ("s4", "f2"),
    "head1": ("b8", "f5", "f6", "f7", "s2", "t1", "t0", "t3"),
    "head2": ("b9", "s5", "t4"),
    "head3": ("b10", "s6", "s7", "f8", "t2", "x0"),
    "put3": ("t5", "x1", "t6", "t7", "f9", "x2", "l0", "l1", "l3", "l4"),
    "end": ("f10", "x3", "l2", "l5", "l6", "l7", "x4"),
}


def pack_heads(lanes_ref, packed_ref):
    rows, count = lanes_ref.shape[0], lanes_ref.shape[1] // LANES
    lane = lax.broadcasted_iota(jnp.int32, (rows, LANES), 1)
    for tile in range(packed_ref.shape[1] // LANES):
        values = jnp.zeros((rows, LANES), F32)
        for head in range(count):
            start = head * HD - tile * LANES
            if -HD < start < LANES:
                one = lanes_ref[:, head * LANES : (head + 1) * LANES].astype(F32)
                one = pltpu.roll(one, start % LANES, 1) if start else one
                values = jnp.where(jnp.logical_and(lane >= start, lane < start + HD), one, values)
        packed_ref[:, tile * LANES : (tile + 1) * LANES] = values.astype(BF16)


def back_kernel(sums, own, outs, refs):
    grad_in, rows_in, heads_in, w_qkv_in, w_out_in, cosine, ahead, behind, q_gain, k_gain = own[:10]
    grad_middle, tokens, scale, lifted = own[10:]
    tokens_out, mod_out, gains_out, packed, lifted_all = outs
    (branch_all, rows, heads, w_qkv, w_out, grad_heads, load_sem), refs = refs[:7], refs[7:]
    gather = RowGather(grad_in, branch_all, *refs[:3])
    gather_lifted = RowGather(lifted, lifted_all, *refs[3:6])
    row_sums = RowSums(*refs[6:])
    local_rows = grad_in.shape[0]
    count = grad_heads.shape[1] // LANES
    factor = HD ** (-0.5)
    loads = [
        pltpu.make_async_copy(source, target, load_sem.at[k])
        for k, (source, target) in enumerate(
            ((rows_in, rows), (w_out_in, w_out), (w_qkv_in, w_qkv))
        )
    ]

    def load_head(head):
        return [
            pltpu.make_async_copy(
                heads_in.at[:, pl.ds((k * count + head) * LANES, LANES)],
                heads.at[head % 2, k],
                load_sem.at[3 + 2 * (head % 2) + k],
            )
            for k in range(2)
        ]

    for k in (1, 0, 2):
        loads[k].start()
    start_all(load_head(0))
    sums.load()
    sums.greet()
    gather.start()
    gather_lifted.start()
    sums.share()
    sums.small[0] = jnp.zeros_like(sums.small[0])
    sums.others["grad_branch_a"] = (branch_all, lambda: None)
    sums.others["lifted"] = (lifted_all, gather_lifted.end)
    sums.do(*BACK_STEPS["start"])
    gather.pass_on()
    gather.end()
    loads[1].wait()
    grad_branch = branch_all[...].reshape(4 * local_rows, branch_all.shape[2])
    grad_heads[...] = over_rows(grad_branch, w_out[...]).astype(BF16)
    sums.do(*BACK_STEPS["gathered"])
    loads[0].wait()
    tables = cosine[...], ahead[...], behind[...]
    block = 256
    gain_sums = [jnp.zeros((1, LANES), F32), jnp.zeros((1, LANES), F32)]
    for head in range(count):
        spans = [slice((k * count + head) * LANES, (k * count + head + 1) * LANES) for k in range(3)]
        if head + 1 < count:
            start_all(load_head(head + 1))
        keys, values = rows[:, spans[1]], rows[:, spans[2]]
        grad_query, grad_key, grad_value = [], None, None
        for start in range(0, rows.shape[0], block):
            queries = rows[start : start + block, spans[0]]
            grads = grad_heads[start : start + block, spans[0]]
            exp_scores = jnp.exp(over_rows(keys, queries) * factor)
            probs = exp_scores * (1.0 / jnp.sum(exp_scores, axis=0, keepdims=True))
            grad_probs = over_rows(values, grads)
            inner = jnp.sum(probs * grad_probs, axis=0, keepdims=True)
            grad_scores = (probs * (grad_probs - inner)).astype(BF16)
            grad_query.append(over_first(grad_scores, keys))
            key_term = jnp.dot(grad_scores, queries, preferred_element_type=F32)
            value_term = jnp.dot(probs.astype(BF16), grads, preferred_element_type=F32)
            grad_key = key_term if grad_key is None else grad_key + key_term
            grad_value = value_term if grad_value is None else grad_value + value_term
        rows[:, spans[2]] = grad_value.astype(BF16)
        terms = (jnp.concatenate(grad_query, axis=0) * factor, grad_key * factor)
        wait_all(load_head(head))
        for k, (term, gain) in enumerate(zip(terms, (q_gain, k_gain), strict=True)):
            raw = heads[head % 2, k]
            inverse = head_inverse(raw)
            normed = raw * inverse
            back = rotated(term, tables, -1)
            gain_sums[k] = gain_sums[k] + jnp.sum(back * normed, axis=0, keepdims=True)
            back = back * gain[...]
            mean = jnp.sum(back * normed, axis=-1, keepdims=True) * (1.0 / HD)
            rows[:, spans[k]] = (inverse * (back - normed * mean)).astype(BF16)
        if head == count - 1:
            pack_heads(rows, packed)
        if head == 0:
            gather_lifted.pass_on()
        sums.do(*BACK_STEPS["head%d" % head])
    gains_out[...] = jnp.concatenate(gain_sums + [jnp.zeros((6, LANES), F32)], axis=0)
    loads[2].wait()
    for index in range(4):
        part = pl.ds(pl.multiple_of(row_sums.order[index] * local_rows, local_rows), local_rows)
        row_sums.put(index, over_rows(rows[part, :], w_qkv[...]))
        sums.do(*BACK_STEPS.get("put%d" % index, ()))
    grad_hidden = row_sums.sums()
    values = tokens[...].astype(F32)
    inverse = inverse_rms(values)
    normed = values * inverse
    tokens_out[...] = grad_middle[...] + rms_back(grad_hidden * (1.0 + scale[...]), normed, inverse)
    width = values.shape[1]
    mod_out[:, :width] = grad_hidden.astype(BF16)
    mod_out[:, width:] = (grad_hidden * normed).astype(BF16)
    sums.do(*BACK_STEPS["end"])
    sums.end()


def attention_back(own, parts, arrays, shared, small_shape, handed, out_shapes):
    names = tuple(arrays)
    shapes = [value.shape + (first, columns) for value, first, columns in shared]
    sums = GradSums(parts, names, shapes, small_shape)
    count = len(out_shapes)
    rows, width = own[0].shape
    kept, heads, w_qkv, w_out = own[1:5]
    leaving = [parts[index].handed() for index in sums.leaving]
    vmem, anywhere = pl.BlockSpec(memory_space=pltpu.VMEM), pl.BlockSpec(memory_space=pl.ANY)
    own_scratch = [
        pltpu.VMEM((4, rows, width), BF16),
        pltpu.VMEM(kept.shape, BF16),
        pltpu.VMEM((2, 2, 4 * rows, LANES), F32),
        pltpu.VMEM(w_qkv.shape, BF16),
        pltpu.VMEM(w_out.shape, BF16),
        pltpu.VMEM((4 * rows, w_out.shape[0]), BF16),
        pltpu.SemaphoreType.DMA((7,)),
        *RowGather.scratch(),
        *RowGather.scratch(),
        *RowSums.scratch(rows, width),
    ]

    def kernel(*refs):
        ins, exchanged, handed_in, given, outs, handed_out, (small_out,), results, mine, scratch = split(
            refs,
            len(names),
            len(shared),
            len(handed),
            len(own),
            count,
            len(leaving),
            1,
            5,
            len(own_scratch),
        )
        sums.bind(ins, exchanged, None, outs, small_out, handed_in, handed_out, scratch)
        back_kernel(sums, given, results, mine)

    return pl.pallas_call(
        kernel,
        out_shape=[jax.ShapeDtypeStruct(shape, F32) for shape in out_shapes]
        + [jax.ShapeDtypeStruct(shape, BF16) for shape in leaving]
        + [
            jax.ShapeDtypeStruct((4,) + small_shape, F32),
            jax.ShapeDtypeStruct((rows, width), F32),
            jax.ShapeDtypeStruct((rows, 2 * width), BF16),
            jax.ShapeDtypeStruct((8, LANES), F32),
            jax.ShapeDtypeStruct((4 * rows, -(-3 * width // 4 // LANES) * LANES), BF16),
            jax.ShapeDtypeStruct((4, rows, width), BF16),
        ],
        in_specs=[anywhere] * (len(names) + len(shared) + len(handed))
        + [vmem]
        + [anywhere] * 4
        + [vmem] * 9,
        out_specs=[vmem] * count + [anywhere] * len(leaving) + [vmem] * 6,
        scratch_shapes=own_scratch + sums.scratch([value.shape for value in arrays.values()]),
        compiler_params=pltpu.CompilerParams(
            collective_id=BACK_ID, has_side_effects=True, vmem_limit_bytes=63 * 2**20
        ),
        name="attention_back",
    )(*arrays.values(), *[value for value, _, _ in shared], *handed, *own)


def to_owners(rows):
    n_dp, n_seq = lax.axis_size("dp"), lax.axis_size("seq")
    pairs = []
    for d in range(n_dp):
        for s in range(n_seq):
            pairs.append((d * n_seq + s, s * n_dp + d))
    return lax.ppermute(rows, ("dp", "seq"), pairs)


def plain_sums(left, right, blocks):
    mine = lax.psum_scatter(outer_sum(left, right).astype(BF16), "dp", scatter_dimension=0, tiled=True)
    return (columns_to_rows(mine, blocks) if blocks else to_owners(mine)).astype(F32)


def padded_small(values):
    values = jnp.pad(values, ((0, 8 - values.shape[0]), (0, TILE - values.shape[1])))
    return jnp.concatenate([jnp.zeros((8, TILE), F32), values])


def again(part, region=None):
    span = (part.start, part.start + part.columns)
    kinds = {"by_rows": part.by_rows, "enter": True, "region": region}
    return Part(None, None, part.rows, span, part.out, part.order, at=part.at, **kinds)


def bias_columns(small, tiles):
    edges = [first_tile(k, tiles) for k in range(4)] + [tiles]
    sums = small.reshape(4, -1)
    return [sums[k, : (edges[k + 1] - edges[k]) * TILE] for k in range(4)]


def in_lanes(values, axis):
    shape = values.shape
    values = values.reshape(shape[:axis] + (shape[axis] // HD, HD) + shape[axis + 1 :])
    pads = [(0, 0)] * len(values.shape)
    pads[axis + 1] = (0, LANES - HD)
    return jnp.pad(values, pads).reshape(shape[:axis] + (-1,) + shape[axis + 1 :])


def out_of_lanes(values):
    return values.reshape(values.shape[0], -1, LANES)[:, :, :HD]


def plain_back(grad_branch_a, given):
    kept, projected, w_qkv, w_out, cosine, ahead, behind, q_gain, k_gain = given
    patches, count = kept.shape[0], w_out.shape[0] // LANES
    factor = HD ** (-0.5)
    tables = [table[:, None, :] for table in (cosine, ahead, behind)]

    def turn(values):
        turned = jnp.roll(values, -QUARTER, -1) * tables[1] + jnp.roll(values, QUARTER, -1) * tables[2]
        return values * tables[0] - turned

    query, key, value = jnp.split(kept.reshape(patches, 3 * count, LANES), 3, axis=1)
    grads = times_transpose(grad_branch_a, w_out).astype(BF16).reshape(patches, count, LANES)
    scores = jnp.einsum("qhd,khd->hqk", query, key, preferred_element_type=F32) * factor
    exp_scores = jnp.exp(scores)
    probs = exp_scores / jnp.sum(exp_scores, axis=-1, keepdims=True)
    grad_probs = jnp.einsum("qhd,khd->hqk", grads, value, preferred_element_type=F32)
    inner = jnp.sum(probs * grad_probs, axis=-1, keepdims=True)
    grad_scores = (probs * (grad_probs - inner)).astype(BF16)
    terms = (
        jnp.einsum("hqk,khd->qhd", grad_scores, key, preferred_element_type=F32) * factor,
        jnp.einsum("hqk,qhd->khd", grad_scores, query, preferred_element_type=F32) * factor,
    )
    grad_value = jnp.einsum("hqk,qhd->khd", probs.astype(BF16), grads, preferred_element_type=F32)
    raws = jnp.split(projected.reshape(patches, 2 * count, LANES), 2, axis=1)
    results, gains = [], []
    for term, raw, gain in zip(terms, raws, (q_gain, k_gain), strict=True):
        inverse = head_inverse(raw)
        normed = raw * inverse
        back = turn(term)
        gains.append(jnp.sum(back * normed, axis=(0, 1)))
        back = back * gain[0]
        mean = jnp.sum(back * normed, axis=-1, keepdims=True) * (1.0 / HD)
        results.append(inverse * (back - normed * mean))
    grad_lanes = jnp.concatenate(results + [grad_value], axis=1).reshape(kept.shape).astype(BF16)
    return grad_lanes, times_transpose(grad_lanes, w_qkv), jnp.stack(gains)


def shards(
    tokens,
    condition,
    cotangent,
    w_qkv,
    w_out,
    w_gate,
    w_up,
    w_down,
    w_mod,
    b_mod,
    q_gain,
    k_gain,
    noise_counts,
    time_steps,
    positions,
):
    local_rows, width = tokens.shape[1:]
    ways = lax.axis_size("seq")
    patches = local_rows * ways
    local_heads = HEADS // ways
    item = lax.axis_index("dp")
    image = jnp.arange(noise_counts.shape[0], dtype=jnp.int32)
    running = jnp.sum(jnp.where(image[None, :] <= image[:, None], noise_counts[None, :], 0), axis=1)
    image_id = jnp.sum((running <= item).astype(jnp.int32))
    chosen = jnp.arange(noise_counts.shape[0], dtype=jnp.int32) == image_id
    share = 1.0 / jnp.sum(jnp.where(chosen, noise_counts, 0)).astype(F32)

    embed = time_embed(time_steps, width)
    bias_row = b_mod.reshape(-1, LANES)
    share_row = jnp.full((1, width), share)
    (
        mod_first,
        w_qkv_lanes,
        scale_a,
        gate_a,
        gate_b,
        hidden_a,
        own_branch_b,
        lifted_low,
        all_positions,
    ) = first_stage(
        w_mod, w_qkv, condition[0], tokens[0], cotangent[0], embed, share_row, bias_row, positions
    )
    hidden_a = hidden_a.reshape(patches, width)
    w_qkv_lanes = w_qkv_lanes.reshape(width, w_qkv_lanes.shape[2])
    tables = lane_tables(jnp.transpose(all_positions[:, :, 0], (1, 0, 2)).reshape(2, patches))
    w_out_lanes = in_lanes(w_out, 0)
    gain_lanes = [jnp.pad(gain, (0, LANES - HD))[None] for gain in (q_gain, k_gain)]
    (
        projected_lanes,
        rows_lanes,
        attended_lanes,
        branch_a,
        mod_rest,
        gate_cols,
        up_cols,
        scale_b,
        middle,
        hidden_b,
        grads_all,
    ) = attend(
        hidden_a,
        w_qkv_lanes,
        w_out_lanes,
        tables,
        *gain_lanes,
        w_mod,
        w_gate,
        w_up,
        lifted_low,
        bias_row,
        tokens[0],
        gate_a,
        own_branch_b,
    )
    grad_branch_b = grads_all.reshape(patches, width)
    pieces = lax.axis_size("dp") == 8
    ff, heads_wide, own_rows = w_down.shape[0], local_heads * HD, width // 8
    handed_mlp = [
        split_part("inner", "grad_branch_b", ff // 8, width, 0, 0, by_rows=True, leave=True),
        split_part("hidden_b", "grad_gate_in", own_rows, ff, 1, 1, leave=True),
    ]
    handed_mlp = [handed_mlp[k % 2][k // 2] for k in range(4)] if pieces else []
    hidden_b, inner, grad_gate_in, grad_up_in, block_out, grad_middle, own_branch_a, grad_mod_b, *handed = mlp(
        hidden_b,
        grads_all,
        gate_cols,
        up_cols,
        w_down,
        (middle, scale_b, gate_a, gate_b, branch_a, cotangent[0], share_row),
        handed_mlp,
    )
    hidden_b = hidden_b.reshape(patches, width)
    mod_first, mod_rest = mod_first.reshape(width, -1), mod_rest.reshape(width, -1)
    given = [rows_lanes, projected_lanes, w_qkv_lanes, w_out_lanes, *tables, *gain_lanes]
    if pieces:
        tiles_b, tiles_a = grad_mod_b.shape[1] // TILE, 2 * width // TILE
        mod_b, mod_a = -(-tiles_b // 4) * TILE, -(-tiles_a // 4) * TILE
        third = mod_b // 3
        late_a = mod_a // 2 // TILE * TILE
        ups = split_part("hidden_b", "grad_up_in", own_rows, ff, 2, 0)
        lasts = split_part("hidden_a", "grad_project", own_rows, 3 * heads_wide, 1, 0)
        mods = [
            Part("lifted", k, own_rows, (0, third), 0, 0, at=k * third, bias=True, leave=True)
            for k in range(3)
        ]
        downs, gates = handed_mlp[0::2], handed_mlp[1::2]
        parts_b = [
            again(downs[0]),
            again(gates[0]),
            ups[0],
            again(downs[1]),
            again(gates[1]),
            ups[1],
            *split_part("attended", "grad_branch_a", heads_wide // 8, width, 3, 1, by_rows=True, in_lanes=True),
            *mods,
        ]
        arrays_b = {
            "hidden_b": hidden_b,
            "grad_up_in": grad_up_in,
            "attended": attended_lanes,
        }
        shapes_b = [
            (ff // 8, width),
            (own_rows // 4, 4 * ff),
            (own_rows // 4, 4 * ff),
            (heads_wide // 8, width),
        ]
        own = [own_branch_a, *given, grad_middle, tokens[0], scale_a, lifted_low]
        (
            grad_w_down,
            grad_w_gate,
            grad_w_up,
            grad_w_out,
            *handed,
            small_b,
            grad_tokens,
            grad_mod_a,
            gain_sums,
            grad_project,
            lifted_full,
        ) = attention_back(
            own,
            parts_b,
            arrays_b,
            [(grad_mod_b, k * third, third) for k in range(3)],
            (16, LANES),
            [handed[k] for k in (0, 1, 2, 3)],
            shapes_b,
        )
        lifted_full = lifted_full.reshape(patches, width)
        wide_a, wide_b = tiles_a * TILE, tiles_b * TILE
        parts_a = [again(part, (wide_a, wide_b)) for part in mods] + lasts
        spans = ((0, mod_a - late_a), (mod_a - late_a, mod_a))
        parts_a += [
            Part("lifted", k, own_rows, (0, span[1] - span[0]), 0, 0, at=span[0], bias=True, region=(0, wide_a))
            for k, span in enumerate(spans)
        ]
        shapes_a = [
            (own_rows // 4, wide_a + wide_b),
            (4, own_rows // 4, 3 * heads_wide),
        ]
        grad_w_mod, qkv_sum, small_a, grad_condition = last_grads(
            parts_a,
            {"hidden_a": hidden_a, "grad_project": grad_project, "lifted": lifted_full},
            [(grad_mod_a, span[0], span[1] - span[0]) for span in spans],
            padded_small(gain_sums[:2]),
            handed,
            shapes_a,
            condition[0],
            embed,
            grad_mod_a,
            grad_mod_b,
            [mod_first, mod_rest],
        )
        grad_w_qkv = jnp.transpose(
            qkv_sum.reshape(4, own_rows // 4, 3, heads_wide), (1, 2, 0, 3)
        ).reshape(own_rows // 4, 3 * width)
        bias = jnp.concatenate(bias_columns(small_a, tiles_a) + bias_columns(small_b, tiles_b))
        own_bias = bias.shape[0] // (8 * ways)
        sum_bias = lax.dynamic_slice(
            bias, ((item * ways + lax.axis_index("seq")) * own_bias,), (own_bias,)
        )
        gains = jnp.sum(small_a[:, 8:10, :HD], axis=0)
    else:
        tokens_f = tokens[0].astype(F32)
        inverse_a = inverse_rms(tokens_f)
        normed_a = tokens_f * inverse_a
        grad_branch_a = gather_rows(own_branch_a)
        grad_lanes, partial, gain_sums = plain_back(grad_branch_a, given)
        grad_hidden_a = scatter_rows(partial)
        grad_tokens = grad_middle + rms_back(grad_hidden_a * (1.0 + scale_a), normed_a, inverse_a)
        grad_mod_a = jnp.concatenate([grad_hidden_a, grad_hidden_a * normed_a], axis=-1).astype(BF16)
        grad_mod_first = jnp.concatenate([grad_mod_a, grad_mod_b[:, :width], grad_mod_b[:, 3 * width :]], axis=1)
        grad_condition = (
            times_transpose(grad_mod_first, mod_first)
            + times_transpose(grad_mod_b[:, width : 3 * width], mod_rest)
        ) * silu_slope(condition[0].astype(F32) + embed)
        grad_project = out_of_lanes(grad_lanes).reshape(patches, 3 * heads_wide)
        gain_sums = gain_sums[:2, :HD]
        mod_rows = jnp.concatenate([grad_mod_a, grad_mod_b], axis=1)
        grad_w_down = plain_sums(inner, grad_branch_b, 0)
        grad_w_gate = plain_sums(hidden_b, grad_gate_in, 1)
        grad_w_up = plain_sums(hidden_b, grad_up_in, 1)
        grad_w_qkv = plain_sums(hidden_a, grad_project, 3)
        attended = out_of_lanes(attended_lanes).reshape(patches, heads_wide)
        grad_w_out = plain_sums(attended, grad_branch_a, 0)
        grad_w_mod = plain_sums(gather_rows(lifted_low), rows_to_columns(mod_rows, 6), 6)
        bias_rows = jnp.sum(mod_rows, axis=0, dtype=F32)
        sum_bias = lax.psum_scatter(bias_rows, ("dp", "seq"), scatter_dimension=0, tiled=True)
        gains = lax.psum(gain_sums, ("dp", "seq"))
    sum_q_gain, sum_k_gain = gains[0], gains[1]
    return (
        block_out[None],
        grad_tokens[None],
        grad_condition[None],
        grad_w_qkv,
        grad_w_out,
        grad_w_gate,
        grad_w_up,
        grad_w_down,
        grad_w_mod,
        sum_bias,
        sum_q_gain,
        sum_k_gain,
    )


def solution(mesh):
    placed = (
        P("dp", "seq", None),
        P("dp", "seq", None),
        P("dp", "seq", None),
        P("seq", None),
        P("seq", None),
        P("seq", None),
        P("seq", None),
        P("seq", None),
        P("seq", None),
        P(),
        P(),
        P(),
        P(),
        P("dp"),
        P(None, "dp", "seq"),
    )
    return jax.shard_map(
        shards,
        mesh=mesh,
        in_specs=placed,
        out_specs=(
            P("dp", "seq", None),
            P("dp", "seq", None),
            P("dp", "seq", None),
            P(("dp", "seq"), None),
            P(("dp", "seq"), None),
            P(("dp", "seq"), None),
            P(("dp", "seq"), None),
            P(("dp", "seq"), None),
            P(("dp", "seq"), None),
            P(("dp", "seq")),
            P(),
            P(),
        ),
        check_vma=False,
    )
```
